128 devices in a mesh: dp: 32 (over y, z, core), tensor: 4 (over x).
Axes of the slice: x: 4, y: 4, z: 4, core: 2. Of those that a mesh axis runs over, the one named last changes fastest.
Arguments:
- tokens: bfloat16 [4096, 2048], P('dp'), may hold values from -6 to 6
- cotangent: bfloat16 [4096, 2048], P('dp'), may hold values from -6 to 6
- seq_lengths: int32 [4], replicated, may hold values from 1 to 2048, 4096 in all
- stretch_order: int32 [64], replicated, may hold values from 0 to 63, as said below
- attn_gain: float32 [2048], P('dp'), may hold values from 0.5 to 1.5
- w_query: float32 [2048, 16, 128], P('dp', 'tensor'), may hold values from -0.125 to 0.125
- w_key: float32 [2048, 16, 128], P('dp', 'tensor'), may hold values from -0.125 to 0.125
- w_value: float32 [2048, 16, 256], P('dp', 'tensor'), may hold values from -0.125 to 0.125
- w_alpha: float32 [2048, 16], P('dp', 'tensor'), may hold values from -0.125 to 0.125
- w_beta: float32 [2048, 16], P('dp', 'tensor'), may hold values from -0.125 to 0.125
- conv_query: float32 [4, 16, 128], P(None, 'tensor', 'dp'), may hold values from -2.5 to 2.5
- conv_key: float32 [4, 16, 128], P(None, 'tensor', 'dp'), may hold values from -2.5 to 2.5
- conv_value: float32 [4, 16, 256], P(None, 'tensor', 'dp'), may hold values from -2.5 to 2.5
- a_log: float32 [16], P('tensor'), may hold values from -5 to 1.5
- dt_bias: float32 [16], P('tensor'), may hold values from -6 to -2
- head_gain: float32 [256], P('dp'), may hold values from 0.5 to 1.5
- w_outgate: float32 [2048, 16, 256], P('dp', 'tensor'), may hold values from -0.125 to 0.125
- w_output: float32 [16, 256, 2048], P('tensor', None, 'dp'), may hold values from -0.1875 to 0.1875
- mlp_gain: float32 [2048], P('dp'), may hold values from 0.5 to 1.5
- w_gate: float32 [2048, 5504], P('dp', 'tensor'), may hold values from -0.125 to 0.125
- w_up: float32 [2048, 5504], P('dp', 'tensor'), may hold values from -0.125 to 0.125
- w_down: float32 [5504, 2048], P('tensor', 'dp'), may hold values from -0.078125 to 0.078125
Outputs:
- output: bfloat16 [4096, 2048], P('dp', 'tensor')
- d_tokens: bfloat16 [4096, 2048], P('dp', 'tensor')
- d_attn_gain: float32 [2048], P('dp')
- d_w_query: float32 [2048, 16, 128], P('dp', 'tensor')
- d_w_key: float32 [2048, 16, 128], P('dp', 'tensor')
- d_w_value: float32 [2048, 16, 256], P('dp', 'tensor')
- d_w_alpha: float32 [2048, 16], P('dp', 'tensor')
- d_w_beta: float32 [2048, 16], P('dp', 'tensor')
- d_conv_query: float32 [4, 16, 128], P(None, 'tensor', 'dp')
- d_conv_key: float32 [4, 16, 128], P(None, 'tensor', 'dp')
- d_conv_value: float32 [4, 16, 256], P(None, 'tensor', 'dp')
- d_a_log: float32 [16], P('tensor')
- d_dt_bias: float32 [16], P('tensor')
- d_head_gain: float32 [256], P('dp')
- d_w_outgate: float32 [2048, 16, 256], P('dp', 'tensor')
- d_w_output: float32 [16, 256, 2048], P('tensor', None, 'dp')
- d_mlp_gain: float32 [2048], P('dp')
- d_w_gate: float32 [2048, 5504], P('dp', 'tensor')
- d_w_up: float32 [2048, 5504], P('dp', 'tensor')
- d_w_down: float32 [5504, 2048], P('tensor', 'dp')
The draws below stay inside these ranges and needn't reach their ends.
Inputs may be any that keep to these rules, and one draw needn't show every extreme that they name: `seq_lengths`: sum to 4096; the longest is exactly 2048. `stretch_order`: names each of the 64 blocks once; at least one block arrives 64 // 2 blocks away, counted round, from its place.
All inputs are finite; a program needn't handle non-finite values.
Results may differ from the reference program's by a relative error of at most 0.03.
Values may be sent and summed in bfloat16 or wider, within the bound.
A program may use at most 256 MiB of HBM per device.

```python
import math
import jax
import jax.numpy as jnp
import numpy as np
from jax import lax

D = 2048
H = 16
DK = 128
DV = 256
FF = 5504
KW = 4
STRETCH = 64
NSEQ = 4
TOKENS = 4096
NCHUNK = 64
MOST_LEN = 2048


def draw_stretch_order(key, part):
    first_key = jax.random.fold_in(key, 11)
    second_key = jax.random.fold_in(key, 12)
    shuffled = jax.random.permutation(first_key, NCHUNK).astype(jnp.int32)
    chosen = jax.random.randint(second_key, (), 0, NCHUNK, dtype=jnp.int32)
    target = (chosen + NCHUNK // 2) % NCHUNK
    previous = jnp.sum(jnp.where(jnp.arange(NCHUNK, dtype=jnp.int32) == chosen, shuffled, 0)).astype(jnp.int32)
    places = jnp.arange(NCHUNK, dtype=jnp.int32)
    swapped = jnp.where(shuffled == target, previous, shuffled)
    return jnp.where(places == chosen, target, swapped).astype(jnp.int32)


def levels(stream_key, extent, pieces, smallest, largest):
    factor_of, own = 1.0, jax.random.fold_in(stream_key, 6)
    for axis_at, parts in pieces:
        draws = jnp.exp(jax.random.uniform(jax.random.fold_in(own, axis_at), (parts,), jnp.float32, smallest / len(pieces), largest / len(pieces)))
        factor_of = factor_of * jnp.repeat(draws, extent[axis_at] // parts).reshape([-1 if axis == axis_at else 1 for axis in range(len(extent))])
    return factor_of


def split_up(number_of, total, limit, skew):
    loads = [(1 << 20) // math.isqrt(grade ** skew) + 1 for grade in range(2, number_of + 1)]
    rest, given = total - limit - (number_of - 1), [1] * (number_of - 1)
    while rest > 0:
        movable = [i for i in range(number_of - 1) if given[i] < limit]
        pool, left = sum([loads[i] for i in movable]), rest
        for i in movable:
            more = min(limit - given[i], max(1, left * loads[i] // pool), rest)
            given[i] = given[i] + more
            rest = rest - more
    return np.array([limit] + given)


def uneven_parts(stream_key, count, total, limit, lean):
    if count == 2:
        one = jax.random.randint(stream_key, (), max(1, total - limit), min(limit, total - 1) + 1)
        return jnp.stack([one, total - one])
    tallies = jnp.asarray(split_up(count, total, limit, lean), jnp.int32)
    pairs = (count - 1) // 2
    donor, sink = tallies[1:1 + 2 * pairs:2], tallies[2:2 + 2 * pairs:2]
    slack = jnp.minimum(donor - 1, limit - sink)
    passed = jax.random.randint(jax.random.fold_in(stream_key, 1), (pairs,), 0, 1 << 20) % (slack + 1)
    tallies = tallies.at[1:1 + 2 * pairs:2].set(donor - passed).at[2:2 + 2 * pairs:2].set(sink + passed)
    return tallies[jax.random.permutation(jax.random.fold_in(stream_key, 2), count)]


def gaussian(own_key, dims, spread, reach, pieces=(), kind=jnp.bfloat16):
    values = jax.random.normal(own_key, dims, jnp.float32) * spread
    if len(pieces) > 0:
        values = levels(own_key, dims, pieces, -0.22, 0.18) * values
    return jnp.clip(values, min=-reach, max=reach).astype(kind)


def setup_inputs(seed: int = 0) -> dict:
    key_of = jax.random.split(jax.random.key(seed), 23)
    return {
        "tokens": gaussian(key_of[0], (TOKENS, D), 1.0, 6.0, ((0, 32),)),
        "cotangent": gaussian(key_of[1], (TOKENS, D), 1.0, 6.0, ((0, 32),)),
        "seq_lengths": uneven_parts(key_of[2], NSEQ, TOKENS, MOST_LEN, 2).astype(jnp.int32),
        "stretch_order": draw_stretch_order(jax.random.fold_in(key_of[22], 71), 0),
        "attn_gain": jnp.clip(1.0 + 0.1 * jax.random.normal(key_of[4], (D,), jnp.float32), 0.5, 1.5),
        "w_query": gaussian(key_of[5], (D, H, DK), D ** -0.5, 0.125, ((0, 32), (1, 4)), jnp.float32),
        "w_key": gaussian(key_of[6], (D, H, DK), D ** -0.5, 0.125, ((0, 32), (1, 4)), jnp.float32),
        "w_value": gaussian(key_of[7], (D, H, DV), D ** -0.5, 0.125, ((0, 32), (1, 4)), jnp.float32),
        "w_alpha": gaussian(key_of[8], (D, H), D ** -0.5, 0.125, ((0, 32), (1, 4)), jnp.float32),
        "w_beta": gaussian(key_of[9], (D, H), D ** -0.5, 0.125, ((0, 32), (1, 4)), jnp.float32),
        "conv_query": gaussian(key_of[10], (KW, H, DK), 0.5, 2.5, ((1, 4), (2, 32)), jnp.float32),
        "conv_key": gaussian(key_of[11], (KW, H, DK), 0.5, 2.5, ((1, 4), (2, 32)), jnp.float32),
        "conv_value": gaussian(key_of[12], (KW, H, DV), 0.5, 2.5, ((1, 4), (2, 32)), jnp.float32),
        "a_log": jnp.clip(-5.0 + 6.5 * jax.random.uniform(key_of[13], (H,), jnp.float32) ** levels(key_of[13], (H,), ((0, 4),), -0.2, 0.2), -5.0, 1.5),
        "dt_bias": jnp.clip(-6.0 + 4.0 * jax.random.uniform(key_of[14], (H,), jnp.float32) ** levels(key_of[14], (H,), ((0, 4),), -0.2, 0.2), -6.0, -2.0),
        "head_gain": jnp.clip(1.0 + 0.1 * jax.random.normal(key_of[15], (DV,), jnp.float32), 0.5, 1.5),
        "w_outgate": gaussian(key_of[16], (D, H, DV), D ** -0.5, 0.125, ((0, 32), (1, 4)), jnp.float32),
        "w_output": gaussian(key_of[17], (H, DV, D), (H * DV // 4) ** -0.5, 0.1875, ((0, 4), (2, 32)), jnp.float32),
        "mlp_gain": jnp.clip(1.0 + 0.1 * jax.random.normal(key_of[18], (D,), jnp.float32), 0.5, 1.5),
        "w_gate": gaussian(key_of[19], (D, FF), D ** -0.5, 0.125, ((0, 32), (1, 4)), jnp.float32),
        "w_up": gaussian(key_of[20], (D, FF), D ** -0.5, 0.125, ((0, 32), (1, 4)), jnp.float32),
        "w_down": gaussian(key_of[21], (FF, D), FF ** -0.5, 0.078125, ((0, 4), (1, 32)), jnp.float32),
    }


EPSILON = 1e-06
MAXIMUM_ACCURACY = lax.Precision.HIGHEST

@jax.custom_vjp
def low(v):
    return lax.optimization_barrier(v.astype(jnp.bfloat16)).astype(jnp.float32)

@jax.custom_vjp
def low_back(v):
    return v

def low_keep(v):
    return (low(v), None)

def low_pass(kept, grad):
    return (grad,)

def back_keep(v):
    return (v, None)

def back_low(kept, grad):
    return (low(grad),)
low.defvjp(low_keep, low_pass)
low_back.defvjp(back_keep, back_low)

def rms_norm(inputs, gain_vector):
    return inputs * lax.rsqrt(lax.optimization_barrier(jnp.mean(inputs * inputs, axis=-1, keepdims=True)) + EPSILON) * gain_vector

def causal_filter(current, before, weight, valid_taps):
    filter_taps = weight.shape[0]
    length = current.shape[0]
    extended = jnp.concatenate([before, current], axis=0)
    summed = jnp.zeros_like(current)
    for tap_index in range(filter_taps):
        summed = summed + valid_taps[:, tap_index:tap_index + 1] * weight[tap_index] * extended[tap_index:tap_index + length]
    return jax.nn.silu(summed)

def unit_heads(values, heads_count, factor):
    shaped = values.reshape(values.shape[0], heads_count, -1)
    return shaped * lax.rsqrt(lax.optimization_barrier(jnp.sum(shaped * shaped, axis=-1, keepdims=True)) + EPSILON) * factor

def gate_norm(mixed_out, gate_pre, gain_vector):
    gate_values = gate_pre.reshape(mixed_out.shape)
    normed = mixed_out * lax.rsqrt(lax.optimization_barrier(jnp.mean(mixed_out * mixed_out, axis=-1, keepdims=True)) + EPSILON) * gain_vector * jax.nn.silu(gate_values)
    return normed.reshape(mixed_out.shape[0], -1)

def delta_stretch(current_state, block):

    def token_step(passed_state, item):
        current_query, current_key, value_now, alpha_now, beta_now, reset_now = item
        passed_state = passed_state * (1.0 - reset_now)
        restore_saved = jnp.einsum('ug,ugo->uo', current_key, passed_state, precision=MAXIMUM_ACCURACY)
        passed_state = alpha_now[:, None, None] * (passed_state - beta_now[:, None, None] * current_key[:, :, None] * restore_saved[:, None, :]) + beta_now[:, None, None] * current_key[:, :, None] * value_now[:, None, :]
        return (passed_state, jnp.einsum('ug,ugo->uo', current_query, passed_state, precision=MAXIMUM_ACCURACY))
    return lax.scan(token_step, current_state, block)

def block_forward(inputs, attn_gain, w_query, w_key, w_value, w_alpha, w_beta, conv_query, conv_key, conv_value, a_log, dt_bias, head_gain, w_outgate, w_output, mlp_gain, w_gate, w_up, w_down, valid_taps, resets):
    length = inputs.shape[0]
    heads_all = w_query.shape[1]
    normed = low(rms_norm(inputs, low(attn_gain)))

    def project(weight):
        return jnp.dot(normed, low(weight).reshape(weight.shape[0], -1), precision=MAXIMUM_ACCURACY)
    query_pre = low_back(project(w_query))
    key_pre = low_back(project(w_key))
    value_pre = low_back(project(w_value))
    gate_pre = low_back(project(w_outgate))
    alpha_pre = low_back(project(w_alpha))
    beta_pre = low_back(project(w_beta))
    filter_taps = conv_query.shape[0]

    def filtered(pre_values, weight):
        return causal_filter(pre_values, jnp.zeros((filter_taps - 1, pre_values.shape[1]), jnp.float32), low(weight).reshape(filter_taps, -1), valid_taps)
    queries = low(unit_heads(filtered(query_pre, conv_query), heads_all, w_query.shape[2] ** (-0.5)))
    key_rows = low(unit_heads(filtered(key_pre, conv_key), heads_all, 1.0))
    value_rows = low(filtered(value_pre, conv_value).reshape(length, heads_all, -1))
    beta_rows = jax.nn.sigmoid(beta_pre)
    alphas = jnp.exp(-jnp.exp(a_log) * jax.nn.softplus(alpha_pre + dt_bias))
    stretches = length // STRETCH

    def blocked(values):
        return values.reshape((stretches, STRETCH) + values.shape[1:])
    start_state = jnp.zeros((heads_all, w_query.shape[2], w_value.shape[2]), jnp.float32)
    final_state, mixed_out = lax.scan(jax.checkpoint(delta_stretch), start_state, (blocked(queries), blocked(key_rows), blocked(value_rows), blocked(alphas), blocked(beta_rows), blocked(resets)))
    mixed_out = mixed_out.reshape(length, heads_all, -1)
    head_flat = low(gate_norm(mixed_out, gate_pre, low(head_gain)))
    attn_out = low_back(jnp.dot(head_flat, low(w_output).reshape(-1, w_output.shape[2]), precision=MAXIMUM_ACCURACY))
    middle = inputs + attn_out
    normed_two = low(rms_norm(middle, low(mlp_gain)))
    gate_mlp = low_back(jnp.dot(normed_two, low(w_gate), precision=MAXIMUM_ACCURACY))
    up_mlp = low_back(jnp.dot(normed_two, low(w_up), precision=MAXIMUM_ACCURACY))
    hidden = low(jax.nn.silu(gate_mlp) * up_mlp)
    mlp_out = low_back(jnp.dot(hidden, low(w_down), precision=MAXIMUM_ACCURACY))
    return middle + mlp_out

def reference(tokens, cotangent, seq_lengths, stretch_order, attn_gain, w_query, w_key, w_value, w_alpha, w_beta, conv_query, conv_key, conv_value, a_log, dt_bias, head_gain, w_outgate, w_output, mlp_gain, w_gate, w_up, w_down):
    stretches = stretch_order.shape[0]
    model_width = tokens.shape[1]
    length = tokens.shape[0]
    inverse = jnp.zeros((stretches,), jnp.int32).at[stretch_order].set(jnp.arange(stretches, dtype=jnp.int32))

    def to_whole(values):
        return values.reshape(stretches, STRETCH, model_width)[inverse].reshape(length, model_width)

    def to_arrival(values):
        return values.reshape(stretches, STRETCH, model_width)[stretch_order].reshape(length, model_width)
    positions = jnp.arange(length, dtype=jnp.int32)
    seq_ends = jnp.cumsum(seq_lengths, dtype=jnp.int32)
    begins = seq_ends - seq_lengths
    inside = (positions[:, None] >= begins[None, :]) & (positions[:, None] < seq_ends[None, :])
    seq_begin = lax.optimization_barrier(jnp.sum(jnp.where(inside, begins[None, :], 0), axis=1, dtype=jnp.int32))
    filter_taps = conv_query.shape[0]
    valid_taps = (positions[:, None] - (filter_taps - 1) + jnp.arange(filter_taps, dtype=jnp.int32)[None, :] >= seq_begin[:, None]).astype(jnp.float32)
    resets = (positions == seq_begin).astype(jnp.float32)

    def forward(inputs, attn_gain, w_query, w_key, w_value, w_alpha, w_beta, conv_query, conv_key, conv_value, a_log, dt_bias, head_gain, w_outgate, w_output, mlp_gain, w_gate, w_up, w_down):
        return block_forward(inputs, attn_gain, w_query, w_key, w_value, w_alpha, w_beta, conv_query, conv_key, conv_value, a_log, dt_bias, head_gain, w_outgate, w_output, mlp_gain, w_gate, w_up, w_down, valid_taps, resets)
    result, pullback = jax.vjp(forward, to_whole(tokens).astype(jnp.float32), attn_gain, w_query, w_key, w_value, w_alpha, w_beta, conv_query, conv_key, conv_value, a_log, dt_bias, head_gain, w_outgate, w_output, mlp_gain, w_gate, w_up, w_down)
    gradients = pullback(to_whole(cotangent).astype(jnp.float32))
    return (to_arrival(result).astype(jnp.bfloat16), to_arrival(gradients[0]).astype(jnp.bfloat16), gradients[1], gradients[2], gradients[3], gradients[4], gradients[5], gradients[6], gradients[7], gradients[8], gradients[9], gradients[10], gradients[11], gradients[12], gradients[13], gradients[14], gradients[15], gradients[16], gradients[17], gradients[18])
```

```python
import functools
import math

import jax
import jax.numpy as jnp
from jax import lax
from jax.experimental import pallas as pl
from jax.experimental.pallas import tpu as pltpu
from jax.sharding import Mesh
from jax.sharding import PartitionSpec as P

MESH = pl.DeviceIdType.MESH
bf16, f32, i32 = jnp.bfloat16, jnp.float32, jnp.int32
HI = lax.Precision.HIGHEST
EPS = 1e-6
STRETCH = 64
D, DK, DV, FFP, HALO = 2048, 128, 256, 384, 16
SEG = 512
ROWS = SEG + HALO
CH = 128
NCH = SEG // CH
NA, NB = 1152, 1152
VLIM = 58 * 1024 * 1024


def at(axis, k):
    n = lax.axis_size(axis)
    return lax.rem(lax.axis_index(axis) + k + n, n)


def greet(peers):
    b = pltpu.get_barrier_semaphore()
    for p in peers:
        pl.semaphore_signal(b, inc=1, device_id=p, device_id_type=MESH)
    pl.semaphore_wait(b, len(peers))


def send(src, dst, ss, rs, who):
    cp = pltpu.make_async_remote_copy(
        src_ref=src, dst_ref=dst, send_sem=ss, recv_sem=rs, device_id=who, device_id_type=MESH
    )
    cp.start()
    return cp


def run(flows):
    flows = list(flows)
    while flows:
        left = []
        for f in flows:
            try:
                next(f)
                left.append(f)
            except StopIteration:
                pass
        flows = left


def peers(**steps):
    return [{ax: at(ax, k)} for ax, ks in steps.items() for k in ks]


def zc_gather(slot, halves, ss, rs):
    z, c = lax.axis_index("z"), lax.axis_index("c")
    other = {"c": 1 - c}
    zp, zm, zf = at("z", 1), at("z", -1), at("z", 2)
    own = slot(z, c)
    a = send(own, own, ss.at[0], rs.at[0], {"z": zp})
    b = send(own, own, ss.at[1], rs.at[1], {"z": zm})
    d0 = send(own, own, ss.at[4], rs.at[4], other)
    yield
    a.wait_recv()
    lo = halves(zm, c)[0]
    e = send(lo, lo, ss.at[2], rs.at[2], {"z": zp})
    m = slot(zm, c)
    d1 = send(m, m, ss.at[5], rs.at[5], other)
    b.wait_recv()
    hi = halves(zp, c)[1]
    f = send(hi, hi, ss.at[3], rs.at[3], {"z": zm})
    p = slot(zp, c)
    d2 = send(p, p, ss.at[6], rs.at[6], other)
    yield
    e.wait_recv()
    fl = halves(zf, c)[0]
    d3 = send(fl, fl, ss.at[7], rs.at[7], other)
    f.wait_recv()
    fh = halves(zf, c)[1]
    d4 = send(fh, fh, ss.at[8], rs.at[8], other)
    yield
    for cp in (d0, d1, d2, d3, d4):
        cp.wait_recv()
    for cp in (a, b, e, f, d0, d1, d2, d3, d4):
        cp.wait_send()


def exchange_flow(src_of, out, ss, rs):
    y, z, c = (lax.axis_index(a) for a in "yzc")
    loc = pltpu.make_async_copy(src_of(y), out.at[y, z, c], ss.at[12])
    loc.start()
    sends = [
        send(src_of(at("y", k)), out.at[y, z, c], ss.at[8 + k], rs.at[8 + k], {"y": at("y", k)})
        for k in (2, 1, 3)
    ]
    yield
    loc.wait()
    for cp in sends:
        cp.wait_recv()
    yield from zc_gather(
        lambda zz, cc: out.at[:, zz, cc],
        lambda zz, cc: (out.at[0:2, zz, cc], out.at[2:4, zz, cc]),
        ss,
        rs,
    )
    for cp in sends:
        cp.wait_send()


def ring_gather(axis, slot, halves, ss, rs):
    i = lax.axis_index(axis)
    p, m = at(axis, 1), at(axis, -1)
    a = send(slot(i), slot(i), ss.at[0], rs.at[0], {axis: p})
    b = send(slot(i), slot(i), ss.at[1], rs.at[1], {axis: m})
    yield
    a.wait_recv()
    lo = halves(m)[0]
    e = send(lo, lo, ss.at[2], rs.at[2], {axis: p})
    b.wait_recv()
    hi = halves(p)[1]
    f = send(hi, hi, ss.at[3], rs.at[3], {axis: m})
    yield
    e.wait_recv()
    f.wait_recv()
    for cp in (a, b, e, f):
        cp.wait_send()


def plane_gather(out, order, lo, mid, hi, ss, rs):
    x, y = lax.axis_index("x"), lax.axis_index("y")
    one, two = slice(lo, hi), (slice(lo, mid), slice(mid, hi))
    if order == "xy":
        yield from ring_gather(
            "x", lambda i: out.at[i, y, one], lambda i: [out.at[i, y, t] for t in two], ss.at[0], rs.at[0]
        )
        yield from ring_gather(
            "y",
            lambda i: out.at[:, i, one],
            lambda i: (out.at[0:2, i, one], out.at[2:4, i, one]),
            ss.at[1],
            rs.at[1],
        )
    else:
        yield from ring_gather(
            "y", lambda i: out.at[x, i, one], lambda i: [out.at[x, i, t] for t in two], ss.at[0], rs.at[0]
        )
        yield from ring_gather(
            "x",
            lambda i: out.at[i, :, one],
            lambda i: (out.at[i, 0:2, one], out.at[i, 2:4, one]),
            ss.at[1],
            rs.at[1],
        )


def ring_scatter(axis, piece, bufs, emit, ss, rs):
    me, p, m, fr = (at(axis, k) for k in (0, 1, -1, 2))
    a = send(piece(fr, 0), bufs.at[0], ss.at[0], rs.at[0], {axis: p})
    c = send(piece(fr, 1), bufs.at[1], ss.at[1], rs.at[1], {axis: m})
    b = send(piece(p, 1), bufs.at[2], ss.at[2], rs.at[2], {axis: p})
    d = send(piece(m, 0), bufs.at[3], ss.at[3], rs.at[3], {axis: m})
    yield
    a.wait_recv()
    bufs[0] = (bufs[0].astype(f32) + piece(p, 0)[...].astype(f32)).astype(bf16)
    e = send(bufs.at[0], bufs.at[4], ss.at[4], rs.at[4], {axis: p})
    c.wait_recv()
    bufs[1] = (bufs[1].astype(f32) + piece(m, 1)[...].astype(f32)).astype(bf16)
    f = send(bufs.at[1], bufs.at[5], ss.at[5], rs.at[5], {axis: m})
    yield
    d.wait_recv()
    e.wait_recv()
    emit(0, piece(me, 0)[...].astype(f32) + bufs[3].astype(f32) + bufs[4].astype(f32))
    b.wait_recv()
    f.wait_recv()
    emit(1, piece(me, 1)[...].astype(f32) + bufs[2].astype(f32) + bufs[5].astype(f32))
    for cp in (a, b, c, d, e, f):
        cp.wait_send()


def plane_scatter(part, res, big, mid, small, h, ss, rs):
    base, q = h * 1024, 512

    def keep(s, v):
        mid[:, :, s * q : (s + 1) * q] = v.astype(bf16)

    def final(s, v):
        res[:, base + s * q : base + (s + 1) * q] = v

    cols = [slice(base + s * q, base + (s + 1) * q) for s in (0, 1)]
    sub = [slice(s * q, (s + 1) * q) for s in (0, 1)]
    if h == 0:
        yield from ring_scatter("x", lambda i, s: part.at[i, :, :, cols[s]], big, keep, ss.at[0], rs.at[0])
        yield from ring_scatter("y", lambda i, s: mid.at[i, :, sub[s]], small, final, ss.at[1], rs.at[1])
    else:
        yield from ring_scatter("y", lambda i, s: part.at[:, i, :, cols[s]], big, keep, ss.at[0], rs.at[0])
        yield from ring_scatter("x", lambda i, s: mid.at[i, :, sub[s]], small, final, ss.at[1], rs.at[1])


SCATTER_SCRATCH = [
    pltpu.VMEM((2, 6, 4, 32, 512), bf16),
    pltpu.VMEM((2, 4, 32, 1024), bf16),
    pltpu.VMEM((2, 6, 32, 512), bf16),
    pltpu.SemaphoreType.DMA((2, 2, 6)),
    pltpu.SemaphoreType.DMA((2, 2, 6)),
]
VM = pl.BlockSpec(memory_space=pltpu.VMEM)
SM = pl.BlockSpec(memory_space=pltpu.SMEM)
HB = pl.BlockSpec(memory_space=pl.ANY)


def shape(dims, kind=f32):
    return jax.ShapeDtypeStruct(dims, kind)


def remote_params(cid):
    return pltpu.CompilerParams(collective_id=cid, has_side_effects=True, vmem_limit_bytes=VLIM)


def exchange(tokens, cotangent, packs, cid):
    n = 2 + len(packs)

    def kernel(*refs):
        ins, outs = refs[:n], refs[n : 2 * n]
        ss, rs = refs[2 * n :]
        x = lax.axis_index("x")
        greet(peers(y=(1, 2, 3), z=(1, 3), c=(1,)))

        def columns(r):
            return lambda yy: r.at[:, pl.ds(pl.multiple_of((x * 4 + yy) * 128, 128), 128)]

        def slots(r):
            return lambda yy: r.at[yy]

        run(
            exchange_flow(columns(ins[i]) if i < 2 else slots(ins[i]), outs[i], ss.at[i], rs.at[i])
            for i in range(n)
        )

    return pl.pallas_call(
        kernel,
        out_shape=[shape((4, 4, 2, 128, 128), bf16)] * 2
        + [shape((4, 4, 2) + p.shape[1:], p.dtype) for p in packs],
        in_specs=[HB] * n,
        out_specs=[HB] * n,
        scratch_shapes=[pltpu.SemaphoreType.DMA((n, 13)), pltpu.SemaphoreType.DMA((n, 12))],
        compiler_params=remote_params(cid),
    )(tokens, cotangent, *packs)


def pick_and_gather(index, tok, cot, cid):
    def kernel(index, tok, cot, xo, do, ss, rs):
        x, y = lax.axis_index("x"), lax.axis_index("y")
        xo[x, y, 0:HALO] = tok[index[0], STRETCH - HALO : STRETCH]
        for j in range(8):
            xo[x, y, HALO + 64 * j : HALO + 64 * (j + 1)] = tok[index[j + 1]]
            do[x, y, 64 * j : 64 * (j + 1)] = cot[index[j + 1]]
        greet(peers(x=(1, 3), y=(1, 3)))
        run(
            [
                plane_gather(xo, "xy", 0, 144, 272, ss.at[0], rs.at[0]),
                plane_gather(xo, "yx", 272, 400, 528, ss.at[1], rs.at[1]),
                plane_gather(do, "xy", 0, 128, 256, ss.at[2], rs.at[2]),
                plane_gather(do, "yx", 256, 384, 512, ss.at[3], rs.at[3]),
            ]
        )

    return pl.pallas_call(
        kernel,
        out_shape=[shape((4, 4, ROWS, 128), bf16), shape((4, 4, SEG, 128), bf16)],
        in_specs=[SM, VM, VM],
        out_specs=[VM, VM],
        scratch_shapes=[pltpu.SemaphoreType.DMA((4, 2, 4)), pltpu.SemaphoreType.DMA((4, 2, 4))],
        compiler_params=remote_params(cid),
    )(index, tok, cot)


def zc_all(a, cid):
    def kernel(a, out, ss, rs):
        z, c = lax.axis_index("z"), lax.axis_index("c")
        out[z, c] = a[...]
        h = a.shape[0] // 2
        greet(peers(z=(1, 3), c=(1,)))
        run(
            [
                zc_gather(
                    lambda zz, cc: out.at[zz, cc],
                    lambda zz, cc: (out.at[zz, cc, 0:h], out.at[zz, cc, h : 2 * h]),
                    ss,
                    rs,
                )
            ]
        )

    return pl.pallas_call(
        kernel,
        out_shape=shape((4, 2) + a.shape, a.dtype),
        in_specs=[VM],
        out_specs=VM,
        scratch_shapes=[pltpu.SemaphoreType.DMA((9,)), pltpu.SemaphoreType.DMA((9,))],
        compiler_params=remote_params(cid),
    )(a)


def gather_rows(out, ss, rs):
    x, y = lax.axis_index("x"), lax.axis_index("y")
    a, b = slice(0, 1024), slice(1024, 2048)
    a2, b2 = (slice(0, 512), slice(512, 1024)), (slice(1024, 1536), slice(1536, 2048))

    def first():
        yield from ring_gather(
            "x", lambda i: out.at[i, y, :, a], lambda i: [out.at[i, y, :, t] for t in a2], ss.at[0, 0], rs.at[0, 0]
        )
        yield from ring_gather(
            "y", lambda i: out.at[:, i, :, a], lambda i: [out.at[:, i, :, t] for t in a2], ss.at[0, 1], rs.at[0, 1]
        )

    def second():
        yield from ring_gather(
            "y", lambda i: out.at[x, i, :, b], lambda i: [out.at[x, i, :, t] for t in b2], ss.at[1, 0], rs.at[1, 0]
        )
        yield from ring_gather(
            "x", lambda i: out.at[i, :, :, b], lambda i: [out.at[i, :, :, t] for t in b2], ss.at[1, 1], rs.at[1, 1]
        )

    return [first(), second()]


def sum_norm_gather(part, xrows, gain, cid):
    def kernel(part, xr, gain, m_out, h_out, acc, big, mid, small, ss, rs, gs, gr):
        x, y = lax.axis_index("x"), lax.axis_index("y")
        greet(peers(x=(1, 3), y=(1, 3)))
        run(
            plane_scatter(part, acc, big.at[h], mid.at[h], small.at[h], h, ss.at[h], rs.at[h]) for h in (0, 1)
        )
        m = xr[...].astype(f32) + acc[...]
        m_out[...] = m
        r = lax.rsqrt(jnp.mean(m * m, axis=-1, keepdims=True) + EPS)
        h_out[x, y] = (m * r * gain[...]).astype(bf16)
        run(gather_rows(h_out, gs, gr))

    return pl.pallas_call(
        kernel,
        out_shape=[shape((32, D)), shape((4, 4, 32, D), bf16)],
        in_specs=[VM] * 3,
        out_specs=[VM] * 2,
        scratch_shapes=[pltpu.VMEM((32, D), f32)]
        + SCATTER_SCRATCH
        + [pltpu.SemaphoreType.DMA((2, 2, 4)), pltpu.SemaphoreType.DMA((2, 2, 4))],
        compiler_params=remote_params(cid),
    )(part, xrows, gain)


def norm_back(v, gain, dh):
    r = lax.rsqrt(jnp.mean(v * v, axis=-1, keepdims=True) + EPS)
    t = gain * dh
    dv = r * t - v * (r * r * r) * jnp.mean(v * t, axis=-1, keepdims=True)
    return dv, jnp.sum(v * r * dh, axis=0, keepdims=True)


def back_middle(part, ypart, m, dyrows, gain, cid):
    def kernel(part, ypart, m, dy, gain, y_out, dm_out, dg_out, da_out, acc, big, mid, small, ss, rs, acc2, big2, mid2, small2, ss2, rs2, gs, gr):
        x, y = lax.axis_index("x"), lax.axis_index("y")
        greet(peers(x=(1, 3), y=(1, 3)))
        run(
            [plane_scatter(part, acc, big.at[h], mid.at[h], small.at[h], h, ss.at[h], rs.at[h]) for h in (0, 1)]
            + [
                plane_scatter(ypart, acc2, big2.at[h], mid2.at[h], small2.at[h], h, ss2.at[h], rs2.at[h])
                for h in (0, 1)
            ]
        )
        mv = m[...]
        dv, dgain = norm_back(mv, gain[...], acc[...])
        dm = dy[...].astype(f32) + dv
        dm_out[...] = dm
        dg_out[...] = dgain
        da_out[x, y] = dm.astype(bf16)
        y_out[...] = (mv + acc2[...]).astype(bf16)
        run(gather_rows(da_out, gs, gr))

    return pl.pallas_call(
        kernel,
        out_shape=[shape((32, D), bf16), shape((32, D)), shape((1, D)), shape((4, 4, 32, D), bf16)],
        in_specs=[VM] * 5,
        out_specs=[VM] * 4,
        scratch_shapes=[pltpu.VMEM((32, D), f32)]
        + SCATTER_SCRATCH
        + [pltpu.VMEM((32, D), f32)]
        + SCATTER_SCRATCH
        + [pltpu.SemaphoreType.DMA((2, 2, 4)), pltpu.SemaphoreType.DMA((2, 2, 4))],
        compiler_params=remote_params(cid),
    )(part, ypart, m, dyrows, gain)


def back_input(part, xrows, dm, gain, cid):
    def kernel(part, xr, dm, gain, dx_out, dg_out, acc, big, mid, small, ss, rs):
        greet(peers(x=(1, 3), y=(1, 3)))
        run(
            plane_scatter(part, acc, big.at[h], mid.at[h], small.at[h], h, ss.at[h], rs.at[h]) for h in (0, 1)
        )
        dv, dgain = norm_back(xr[...].astype(f32), gain[...], acc[...])
        dx_out[...] = (dm[...] + dv).astype(bf16)
        dg_out[...] = dgain

    return pl.pallas_call(
        kernel,
        out_shape=[shape((32, D), bf16), shape((1, D))],
        in_specs=[VM] * 4,
        out_specs=[VM] * 2,
        scratch_shapes=[pltpu.VMEM((32, D), f32)] + SCATTER_SCRATCH,
        compiler_params=remote_params(cid),
    )(part, xrows, dm, gain)


def send_home(order, rows, cid):
    n = len(rows)

    def kernel(order, *refs):
        ins, outs = refs[:n], refs[n : 2 * n]
        gathered = refs[2 * n : 3 * n]
        cols, picks, s1, r1, s2, r2, s3, r3 = refs[3 * n :]
        x, y, z, c = (lax.axis_index(a) for a in "xyzc")
        greet(
            [{"x": at("x", i), "y": at("y", j)} for i in range(4) for j in range(4) if (i, j) != (0, 0)]
            + peers(z=(1, 3), c=(1,))
        )

        def flow(k):
            src, alls = ins[k], gathered[k]
            sends = []
            lane = pl.multiple_of((x * 4 + y) * 128, 128)
            cols[k, x, y] = src[:, pl.ds(lane, 128)]
            t = 0
            for i in range(4):
                for j in range(4):
                    if (i, j) == (0, 0):
                        continue
                    px, py = at("x", i), at("y", j)
                    lane = pl.multiple_of((px * 4 + py) * 128, 128)
                    sends.append(
                        send(src.at[:, pl.ds(lane, 128)], cols.at[k, x, y], s1.at[k, t], r1.at[k, t], {"x": px, "y": py})
                    )
                    t += 1
            yield
            for cp in sends:
                cp.wait_recv()
            alls[z, c] = cols[k].reshape(8, 64, 128)
            yield from zc_gather(
                lambda zz, cc: alls.at[zz, cc],
                lambda zz, cc: (alls.at[zz, cc, 0:4], alls.at[zz, cc, 4:8]),
                s2.at[k],
                r2.at[k],
            )
            for j in range(4):
                for i in range(2):
                    t = j * 2 + i
                    picks[k, j, 64 * i : 64 * (i + 1)] = alls[order[0, t], order[1, t], order[2, t]]
            mine = pl.ds(pl.multiple_of(y * 128, 128), 128)
            last = [
                send(picks.at[k, at("y", j)], outs[k].at[:, mine], s3.at[k, j], r3.at[k, j], {"y": at("y", j)})
                for j in (2, 1, 3)
            ]
            outs[k][:, mine] = picks[k, y]
            yield
            for cp in last:
                cp.wait_recv()
            for cp in sends + last:
                cp.wait_send()

        run(flow(k) for k in range(n))

    return pl.pallas_call(
        kernel,
        out_shape=[shape((128, 512), bf16)] * n,
        in_specs=[SM] + [VM] * n,
        out_specs=[VM] * n,
        scratch_shapes=[pltpu.VMEM((4, 2, 8, 64, 128), bf16)] * n
        + [
            pltpu.VMEM((n, 4, 4, 32, 128), bf16),
            pltpu.VMEM((n, 4, 128, 128), bf16),
            pltpu.SemaphoreType.DMA((n, 15)),
            pltpu.SemaphoreType.DMA((n, 15)),
            pltpu.SemaphoreType.DMA((n, 9)),
            pltpu.SemaphoreType.DMA((n, 9)),
            pltpu.SemaphoreType.DMA((n, 4)),
            pltpu.SemaphoreType.DMA((n, 4)),
        ],
        compiler_params=remote_params(cid),
    )(order, *rows)


def scatter_flow(g, core, bufs, stage, out, ss, rs):
    y, z, c = (lax.axis_index(a) for a in "yzc")
    d = send(g.at[:, :, 1 - c], core, ss.at[0], rs.at[0], {"c": 1 - c})
    yield
    d.wait_recv()

    def add(i, _):
        core[i] = (core[i].astype(f32) + g[i, :, c].astype(f32)).astype(core.dtype)
        return 0

    lax.fori_loop(0, 4, add, 0)

    def emit(s, v):
        stage[2 * s : 2 * s + 2] = v.astype(stage.dtype)

    yield from ring_scatter(
        "z", lambda i, s: core.at[2 * s : 2 * s + 2, i], bufs, emit, ss.at[pl.ds(1, 6)], rs.at[pl.ds(1, 6)]
    )
    sends = [
        send(stage.at[at("y", k)], out.at[y], ss.at[6 + k], rs.at[6 + k], {"y": at("y", k)}) for k in (2, 1, 3)
    ]
    out[y] = stage[y]
    yield
    for cp in sends:
        cp.wait_recv()
    d.wait_send()
    for cp in sends:
        cp.wait_send()


def return_grads(gs, tiny, cid):
    n = len(gs)

    def kernel(*refs):
        ins, outs = refs[: n + 1], refs[n + 1 : 2 * n + 2]
        tot = refs[2 * n + 2]
        rest = refs[2 * n + 3 :]
        cores, bufs, stages = rest[: n + 1], rest[n + 1 : 2 * n + 2], rest[2 * n + 2 : 3 * n + 3]
        xr, ss, rs, xs, xq = rest[3 * n + 3 :]
        x = lax.axis_index("x")
        greet(peers(c=(1,), z=(1, 3), y=(1, 2, 3), x=(1, 2, 3)))

        def last():
            yield from scatter_flow(ins[n], cores[n], bufs[n], stages[n], outs[n], ss.at[n], rs.at[n])
            xr[x] = (outs[n][0].astype(f32) + outs[n][1].astype(f32)) + (outs[n][2].astype(f32) + outs[n][3].astype(f32))
            sends = [send(xr.at[x], xr.at[x], xs.at[k], xq.at[k], {"x": at("x", k)}) for k in (2, 1, 3)]
            yield
            for cp in sends:
                cp.wait_recv()
            tot[...] = (xr[0] + xr[1]) + (xr[2] + xr[3])
            for cp in sends:
                cp.wait_send()

        run(
            [last()]
            + [scatter_flow(ins[i], cores[i], bufs[i], stages[i], outs[i], ss.at[i], rs.at[i]) for i in range(n)]
        )

    arrays = list(gs) + [tiny]
    blocks = [(a.shape[3:], a.dtype) for a in arrays]
    return pl.pallas_call(
        kernel,
        out_shape=[shape((4,) + s, k) for s, k in blocks] + [shape(tiny.shape[3:])],
        in_specs=[VM] * (n + 1),
        out_specs=[VM] * (n + 2),
        scratch_shapes=[pltpu.VMEM((4, 4) + s, k) for s, k in blocks]
        + [pltpu.VMEM((6, 2) + s, k) for s, k in blocks]
        + [pltpu.VMEM((4,) + s, k) for s, k in blocks]
        + [
            pltpu.VMEM((4,) + tiny.shape[3:], f32),
            pltpu.SemaphoreType.DMA((n + 1, 10)),
            pltpu.SemaphoreType.DMA((n + 1, 10)),
            pltpu.SemaphoreType.DMA((4,)),
            pltpu.SemaphoreType.DMA((4,)),
        ],
        compiler_params=remote_params(cid),
    )(*gs, tiny)


def dot(a, b, dims, prec=None):
    return lax.dot_general(a, b, (dims, ((), ())), preferred_element_type=f32, precision=prec)


def lo(a):
    return a.astype(bf16)


def mm(a, b):
    return dot(lo(a), lo(b), ((1,), (0,)))


def mmt(a, b):
    return dot(lo(a), lo(b), ((1,), (1,)))


def tmm(a, b):
    return dot(lo(a), lo(b), ((0,), (0,)))


def halves_of(a):
    h = a.astype(bf16)
    return h, (a - h.astype(f32)).astype(bf16)


def fine(a, b, dims=((1,), (0,))):
    ah, al = halves_of(a)
    bh, bl = halves_of(b)
    return dot(ah, bh, dims) + (dot(ah, bl, dims) + dot(al, bh, dims))


def tri_inverse(a, r, c):
    eye = jnp.where(r == c, 1.0, 0.0)
    n1 = jnp.where((r >> 3) == (c >> 3), -a, 0.0)
    n2 = fine(n1, n1)
    n4 = fine(n2, n2)
    t = eye + n1
    t = t + fine(t, n2)
    t = t + fine(t, n4)
    for level in (3, 4, 5, 6):
        off = ((r >> (level + 1)) == (c >> (level + 1))) & ((r >> level) != (c >> level))
        t = t - fine(t, fine(jnp.where(off, a, 0.0), t))
    return t


def iotas():
    return (
        lax.broadcasted_iota(i32, (CH, CH), 0),
        lax.broadcasted_iota(i32, (CH, CH), 1),
    )


def filtered(z, cw, mc, cols):
    total = z[HALO : HALO + SEG, cols] * cw[3:4, cols]
    for j in range(3):
        total = total + mc[:, j : j + 1] * cw[j : j + 1, cols] * z[HALO - 3 + j : HALO - 3 + j + SEG, cols]
    return total


def silu(v):
    return v * jax.nn.sigmoid(v)


QC, KC, VC = slice(0, 128), slice(128, 256), slice(256, 512)


def decay_of(cc, cr, mask):
    return jnp.exp(jnp.where(mask, cc - cr, 0.0)) * jnp.where(mask, 1.0, 0.0)


def prepare(z, ab, cw, sc, mc, mr):
    def kernel(z, ab, cw, sc, mc, mr, qkv, tm, wu, gb, cr, ti):
        r, c = iotas()
        for cols, scale in ((QC, DK**-0.5), (KC, 1.0)):
            s = silu(filtered(z, cw, mc, cols))
            qkv[:, cols] = (s * lax.rsqrt(jnp.sum(s * s, axis=-1, keepdims=True) + EPS) * scale).astype(bf16)
        qkv[:, VC] = silu(filtered(z, cw, mc, VC)).astype(bf16)
        low = jnp.where(r >= c, 1.0, 0.0)
        eye = jnp.where(r == c, 1.0, 0.0)
        lane = lax.broadcasted_iota(i32, (CH, 128), 1)
        transit = eye
        insert = jnp.zeros((DK, DV), f32)
        for n in range(NCH):
            rows = slice(n * CH, (n + 1) * CH)
            raw = ab[HALO + n * CH : HALO + (n + 1) * CH, :]
            beta = jax.nn.sigmoid(raw[:, 1:2])
            u = raw + sc[0:1, 1:2]
            g = -jnp.exp(sc[0:1, 0:1]) * (jnp.maximum(u, 0.0) + jnp.log1p(jnp.exp(-jnp.abs(u))))
            g = jnp.where(lane == 0, g, 0.0)
            cum = dot(low, g, ((1,), (0,)), HI)[:, 0:1]
            cumr = dot(g, low, ((0,), (1,)), HI)[0:8, :]
            gb[rows, :] = jnp.where(lane == 0, beta, cum)
            cr[:, rows] = cumr
            cumrow = cumr[0:1, :]
            last = cumr[0:1, CH - 1 : CH]
            m = mc[rows, :]
            carried, closing, begin, carry_last = m[:, 3:4], m[:, 4:5], m[:, 5:6], m[0:1, 6:7]
            same = begin == mr[0:1, rows]
            k = qkv[rows, KC]
            kf = k.astype(f32)
            v = qkv[rows, VC].astype(f32)
            a = beta * dot(k, k, ((1,), (1,))) * decay_of(cum, cumrow, same & (r > c))
            t = tri_inverse(a, r, c)
            tm[rows, :] = t
            lead = (beta * jnp.exp(cum) * carried) * kf
            w = fine(t, lead)
            uu = fine(t, beta * v)
            wu[rows, 0:DK] = w
            wu[rows, DK:] = uu
            tail = kf * (jnp.exp(last - cum) * closing)
            keep = jnp.exp(last) * carry_last
            hand = keep * eye - fine(tail, w, ((0,), (0,)))
            insert = fine(hand, insert) + fine(tail, uu, ((0,), (0,)))
            transit = fine(hand, transit)
        ti[:, 0:DK] = transit.astype(bf16)
        ti[:, DK:] = insert.astype(bf16)

    return pl.pallas_call(
        kernel,
        out_shape=[
            shape((SEG, 512), bf16),
            shape((SEG, CH)),
            shape((SEG, DK + DV)),
            shape((SEG, 128)),
            shape((8, SEG)),
            shape((DK, DK + DV), bf16),
        ],
        in_specs=[VM] * 6,
        out_specs=[VM] * 6,
        compiler_params=pltpu.CompilerParams(vmem_limit_bytes=VLIM),
    )(z, ab, cw, sc, mc, mr)


def emit_outputs(where, maps, qkv, wu, gb, cr, mc, mr, gp, hg):
    def kernel(where, maps, qkv, wu, gb, cr, mc, mr, gp, hg, nout, oout, fout, sout):
        r, c = iotas()

        def fold(d, s):
            tr, ins = maps[d, :, 0:DK], maps[d, :, DK:].astype(f32)
            sh, sl = halves_of(s)
            new = dot(tr, sh, ((1,), (0,))) + dot(tr, sl, ((1,), (0,))) + ins
            return jnp.where(d < where[0], new, s)

        s = lax.fori_loop(0, 7, fold, jnp.zeros((DK, DV), f32))
        for n in range(NCH):
            rows = slice(n * CH, (n + 1) * CH)
            m = mc[rows, :]
            carried, closing, begin, carry_last = m[:, 3:4], m[:, 4:5], m[:, 5:6], m[0:1, 6:7]
            cum = gb[rows, 1:2]
            cumrow = cr[0:1, rows]
            last = cr[0:1, n * CH + CH - 1 : n * CH + CH]
            same = begin == mr[0:1, rows]
            q, k = qkv[rows, QC], qkv[rows, KC]
            p = dot(q, k, ((1,), (1,))) * decay_of(cum, cumrow, same & (r >= c))
            fresh = wu[rows, DK:] - fine(wu[rows, 0:DK], s)
            qd = q.astype(f32) * (jnp.exp(cum) * carried)
            o = mm(qd, s) + mm(p, fresh)
            sout[n] = s
            fout[rows, :] = fresh
            oout[rows, :] = o
            x = gp[HALO + n * CH : HALO + (n + 1) * CH, :]
            rn = lax.rsqrt(jnp.mean(o * o, axis=-1, keepdims=True) + EPS)
            nout[rows, :] = (o * rn * hg[0:1, :] * silu(x)).astype(bf16)
            tail = k.astype(f32) * (jnp.exp(last - cum) * closing)
            s = (jnp.exp(last) * carry_last) * s + fine(tail, fresh, ((0,), (0,)))

    return pl.pallas_call(
        kernel,
        out_shape=[shape((SEG, DV), bf16), shape((SEG, DV)), shape((SEG, DV)), shape((NCH, DK, DV))],
        in_specs=[SM] + [VM] * 9,
        out_specs=[VM] * 4,
        compiler_params=pltpu.CompilerParams(vmem_limit_bytes=VLIM),
    )(where, maps, qkv, wu, gb, cr, mc, mr, gp, hg)


def back_emit(dn, o, gp, hg, qkv, wu, gb, cr, mc, mr):
    def kernel(dn, o, gp, hg, qkv, wu, gb, cr, mc, mr, do_out, dgp_out, dhg_out, e_out):
        r, c = iotas()
        dhg = jnp.zeros((1, DV), f32)
        e = jnp.zeros((DK, DV), f32)
        for n in reversed(range(NCH)):
            rows = slice(n * CH, (n + 1) * CH)
            ov, x, dnv = o[rows, :], gp[HALO + n * CH : HALO + (n + 1) * CH, :], dn[rows, :]
            rn = lax.rsqrt(jnp.mean(ov * ov, axis=-1, keepdims=True) + EPS)
            sg = jax.nn.sigmoid(x)
            act = x * sg
            h = hg[0:1, :]
            base = ov * rn
            dhg = dhg + jnp.sum(base * act * dnv, axis=0, keepdims=True)
            dgp_out[rows, :] = (dnv * base * h * (sg * (1.0 + x * (1.0 - sg)))).astype(bf16)
            t = dnv * h * act
            do = rn * t - base * (rn * rn) * jnp.mean(ov * t, axis=-1, keepdims=True)
            do_out[rows, :] = do
            m = mc[rows, :]
            carried, closing, begin, carry_last = m[:, 3:4], m[:, 4:5], m[:, 5:6], m[0:1, 6:7]
            cum = gb[rows, 1:2]
            cumrow = cr[0:1, rows]
            last = cr[0:1, n * CH + CH - 1 : n * CH + CH]
            same = begin == mr[0:1, rows]
            q, k = qkv[rows, QC], qkv[rows, KC]
            p = dot(q, k, ((1,), (1,))) * decay_of(cum, cumrow, same & (r >= c))
            qd = q.astype(f32) * (jnp.exp(cum) * carried)
            tail = k.astype(f32) * (jnp.exp(last - cum) * closing)
            df = tmm(p, do) + mm(tail, e)
            e = tmm(qd, do) + (jnp.exp(last) * carry_last) * e - tmm(wu[rows, 0:DK], df)
        dhg_out[...] = dhg
        e_out[...] = e.astype(bf16)

    return pl.pallas_call(
        kernel,
        out_shape=[shape((SEG, DV)), shape((SEG, DV), bf16), shape((1, DV)), shape((DK, DV), bf16)],
        in_specs=[VM] * 10,
        out_specs=[VM] * 4,
        compiler_params=pltpu.CompilerParams(vmem_limit_bytes=VLIM),
    )(dn, o, gp, hg, qkv, wu, gb, cr, mc, mr)


def back_delta(where, maps, tails, do, fr, st, qkv, tm, wu, gb, cr, z, ab, cw, sc, mc, mr):
    def kernel(
        where, maps, tails, do, fr, st, qkv, tm, wu, gb, cr, z, ab, cw, sc, mc, mr, dz, dab, dcw, dsc, dqkv
    ):
        r, c = iotas()
        low = jnp.where(r >= c, 1.0, 0.0)
        ones = jnp.ones((CH, CH), f32)
        lane = lax.broadcasted_iota(i32, (CH, 128), 1)
        row = lax.broadcasted_iota(i32, (CH, 1), 0)

        def fold(i, e):
            d = 7 - i
            tr, own = maps[d, :, 0:DK], tails[d].astype(f32)
            eh, el = halves_of(e)
            new = dot(tr, eh, ((0,), (0,))) + dot(tr, el, ((0,), (0,))) + own
            return jnp.where(d > where[0], new, e)

        e = lax.fori_loop(0, 7, fold, jnp.zeros((DK, DV), f32))
        acc_a = jnp.zeros((1, 128), f32)
        acc_d = jnp.zeros((1, 128), f32)
        for n in reversed(range(NCH)):
            rows = slice(n * CH, (n + 1) * CH)
            m = mc[rows, :]
            carried, closing, begin, carry_last = m[:, 3:4], m[:, 4:5], m[:, 5:6], m[0:1, 6:7]
            beta, cum = gb[rows, 0:1], gb[rows, 1:2]
            cumrow = cr[0:1, rows]
            last = cr[0:1, n * CH + CH - 1 : n * CH + CH]
            same = begin == mr[0:1, rows]
            q, k = qkv[rows, QC], qkv[rows, KC]
            qf, kf, vf = q.astype(f32), k.astype(f32), qkv[rows, VC].astype(f32)
            dec_i = decay_of(cum, cumrow, same & (r >= c))
            dec_s = jnp.where(r > c, dec_i, 0.0)
            p = dot(q, k, ((1,), (1,))) * dec_i
            kkd = dot(k, k, ((1,), (1,))) * dec_s
            ex = jnp.exp(cum) * carried
            tf = jnp.exp(last - cum) * closing
            keep = jnp.exp(last) * carry_last
            tail = kf * tf
            qd = qf * ex
            dov, fv, sv, tv = do[rows, :], fr[rows, :], st[n], tm[rows, :]
            w, u = wu[rows, 0:DK], wu[rows, DK:]
            df = tmm(p, dov) + mm(tail, e)
            dw = -mmt(df, sv)
            dtail = mmt(fv, e)
            dkeep = jnp.sum(jnp.sum(sv * e, axis=1, keepdims=True), axis=0, keepdims=True)
            dqd = mmt(dov, sv)
            dp = mmt(dov, fv)
            dlead = tmm(tv, dw)
            dbv = tmm(tv, df)
            da = -(mmt(dlead, w) + mmt(dbv, u))
            dakd = da * kkd
            dkk = da * beta * dec_s
            dqk = dp * dec_i
            mix = dakd * beta + dp * p
            dqkv[rows, QC] = mm(dqk, k) + dqd * ex
            dqkv[rows, KC] = (
                tmm(dqk, q) + mm(dkk, k) + tmm(dkk, k) + dlead * (beta * ex) + dtail * tf
            )
            dqkv[rows, VC] = beta * dbv
            lk = jnp.sum(dlead * kf, axis=1, keepdims=True) * ex
            dbeta = jnp.sum(dakd, axis=1, keepdims=True) + lk + jnp.sum(dbv * vf, axis=1, keepdims=True)
            tt = jnp.sum(dtail * tail, axis=1, keepdims=True)
            dcum = jnp.sum(mix, axis=1, keepdims=True) + jnp.sum(dqd * qd, axis=1, keepdims=True) + lk * beta - tt
            dcum = dcum + jnp.where(row == CH - 1, jnp.sum(tt, axis=0, keepdims=True) + dkeep * keep, 0.0)
            full = dcum - dot(mix, ones, ((0,), (0,)), HI)
            dg = dot(low, full, ((0,), (0,)), HI)
            raw = ab[HALO + n * CH : HALO + (n + 1) * CH, :]
            uu = raw + sc[0:1, 1:2]
            rate = -jnp.exp(sc[0:1, 0:1])
            sp = jnp.maximum(uu, 0.0) + jnp.log1p(jnp.exp(-jnp.abs(uu)))
            dal = dg * rate * jax.nn.sigmoid(uu)
            acc_a = acc_a + jnp.sum(dg * rate * sp, axis=0, keepdims=True)
            acc_d = acc_d + jnp.sum(dal, axis=0, keepdims=True)
            dab[rows, :] = jnp.where(
                lane == 0, dal, jnp.where(lane == 1, dbeta * beta * (1.0 - beta), 0.0)
            ).astype(bf16)
            e = tmm(qd, dov) + keep * e - tmm(w, df)
        dsc[0:1, :] = acc_a
        dsc[1:2, :] = acc_d
        dz[0:HALO, :] = jnp.zeros((HALO, 512), f32)
        for cols, scale in ((QC, DK**-0.5), (KC, 1.0), (VC, None)):
            y = filtered(z, cw, mc, cols)
            sg = jax.nn.sigmoid(y)
            ds = dqkv[:, cols]
            if scale is not None:
                s = y * sg
                rn = lax.rsqrt(jnp.sum(s * s, axis=-1, keepdims=True) + EPS)
                ds = scale * (rn * ds - s * (rn * rn * rn) * jnp.sum(s * ds, axis=-1, keepdims=True))
            dy = ds * (sg * (1.0 + y * (1.0 - sg)))
            dz[HALO : HALO + SEG, cols] = dy * cw[3:4, cols]
            dcw[3:4, cols] = jnp.sum(dy * z[HALO : HALO + SEG, cols], axis=0, keepdims=True)
            for j in range(3):
                part = mc[:, j : j + 1] * dy
                away = slice(HALO - 3 + j, HALO - 3 + j + SEG)
                dcw[j : j + 1, cols] = jnp.sum(part * z[away, cols], axis=0, keepdims=True)
                dz[away, cols] = dz[away, cols] + part * cw[j : j + 1, cols]

    return pl.pallas_call(
        kernel,
        out_shape=[shape((ROWS, 512)), shape((SEG, 128), bf16), shape((4, 512)), shape((2, 128))],
        in_specs=[SM] + [VM] * 16,
        out_specs=[VM] * 4,
        scratch_shapes=[pltpu.VMEM((SEG, 512), f32)],
        compiler_params=pltpu.CompilerParams(vmem_limit_bytes=VLIM),
    )(where, maps, tails, do, fr, st, qkv, tm, wu, gb, cr, z, ab, cw, sc, mc, mr)


def wide(a):
    a = jnp.pad(a.astype(bf16), ((0, 0), (0, 4 * FFP - a.shape[1])))
    return a.reshape(a.shape[0], 4, FFP).swapaxes(0, 1)


def body(
    tokens,
    cotangent,
    seq_lengths,
    stretch_order,
    attn_gain,
    w_query,
    w_key,
    w_value,
    w_alpha,
    w_beta,
    conv_query,
    conv_key,
    conv_value,
    a_log,
    dt_bias,
    head_gain,
    w_outgate,
    w_output,
    mlp_gain,
    w_gate,
    w_up,
    w_down,
):
    x, y, z, c = (lax.axis_index(a) for a in "xyzc")
    seg = z * 2 + c
    slot = x * 4 + y
    ff = w_gate.shape[1]

    def by_head(a):
        return a.astype(bf16).swapaxes(0, 1)

    pair = jnp.stack([w_alpha, w_beta], axis=-1).astype(bf16)
    pack_a = jnp.concatenate(
        [
            by_head(w_query),
            by_head(w_key),
            by_head(w_value),
            by_head(w_outgate),
            jnp.pad(pair.swapaxes(0, 1), ((0, 0), (0, 0), (0, 126))),
            w_output.astype(bf16).swapaxes(1, 2),
        ],
        axis=2,
    )
    pack_b = jnp.concatenate([wide(w_gate), wide(w_up), wide(w_down.T)], axis=2)

    def taps(a):
        return a.swapaxes(0, 1).reshape(4, -1)

    def each(a):
        return jnp.broadcast_to(a[None], (4,) + a.shape)

    line = jnp.concatenate(
        [taps(conv_query), taps(conv_key), taps(conv_value), each(head_gain), each(attn_gain), each(mlp_gain)], axis=1
    ).astype(bf16)
    tiny = jnp.broadcast_to(jnp.pad(line, ((0, 0), (0, 256 - line.shape[1])))[:, None], (4, 16, 256))
    tok_all, cot_all, wa, wb, tiny_all = exchange(tokens, cotangent, (pack_a, pack_b, tiny), 1)
    wa = wa.reshape(D, NA)
    wb = wb.reshape(D, NB)
    lines = tiny_all[:, :, :, 0].reshape(32, 256).astype(f32)

    def filters(a):
        return a.reshape(32, 4, -1).swapaxes(0, 1).reshape(4, -1)

    cw = jnp.concatenate([filters(lines[:, 0:16]), filters(lines[:, 16:32]), filters(lines[:, 32:64])], axis=1)
    hg = lines[:, 64:72].reshape(1, DV)
    gain1 = lines[:, 72:136].reshape(1, D)
    gain2 = lines[:, 136:200].reshape(1, D)
    sc = jnp.pad(
        jnp.stack([lax.dynamic_index_in_dim(a_log, y, 0, False), lax.dynamic_index_in_dim(dt_bias, y, 0, False)])[None],
        ((0, 7), (0, 126)),
    )

    blocks = jnp.maximum(seg * 8 - 1 + jnp.arange(9, dtype=i32), 0)
    index = jnp.sum(
        jnp.where(stretch_order[None, :] == blocks[:, None], jnp.arange(64, dtype=i32)[None, :], 0), axis=1, dtype=i32
    )
    xg, dyg = pick_and_gather(index, tok_all.reshape(64, 64, 128), cot_all.reshape(64, 64, 128), 2)
    xs = xg.reshape(16, ROWS, 128).swapaxes(0, 1).reshape(ROWS, D)
    dys = dyg.reshape(16, SEG, 128).swapaxes(0, 1).reshape(SEG, D)
    xrows = lax.dynamic_slice_in_dim(xs, HALO + 32 * slot, 32, 0)
    dyrows = lax.dynamic_slice_in_dim(dys, 32 * slot, 32, 0)

    pos = seg * SEG + jnp.arange(SEG, dtype=i32)
    ends = jnp.cumsum(seq_lengths, dtype=i32)
    begins = ends - seq_lengths
    inside = (pos[:, None] >= begins[None, :]) & (pos[:, None] < ends[None, :])
    begin = jnp.sum(jnp.where(inside, begins[None, :], 0), axis=1, dtype=i32)
    valid = (pos[:, None] - 3 + jnp.arange(3, dtype=i32)[None, :] >= begin[:, None]).astype(f32)
    cb = begin.reshape(NCH, CH)
    first = pos.reshape(NCH, CH)[:, :1]
    carried = (cb < first).astype(f32)
    closing = (cb == cb[:, -1:]).astype(f32)
    carry_last = jnp.broadcast_to(carried[:, -1:], (NCH, CH))
    beginf = begin.astype(f32)
    mc = jnp.concatenate(
        [valid, jnp.stack([carried.reshape(-1), closing.reshape(-1), beginf, carry_last.reshape(-1)], axis=1)], axis=1
    )
    mc = jnp.pad(mc, ((0, 0), (0, 121)))
    mr = jnp.broadcast_to(beginf[None], (8, SEG))
    where = seg.reshape(1).astype(i32)

    xf = xs.astype(f32)
    h1 = (xf * lax.rsqrt(jnp.mean(xf * xf, axis=-1, keepdims=True) + EPS) * gain1).astype(bf16)
    proj = jnp.dot(h1, wa[:, :896], preferred_element_type=f32)
    zq, gp, ab = proj[:, :512], proj[:, 512:768], proj[:, 768:896]
    qkv, tm, wu, gb, cr, ti = prepare(zq, ab, cw, sc, mc, mr)
    maps = zc_all(ti, 3).reshape(8, DK, DK + DV)
    nv, ov, fr, st = emit_outputs(where, maps, qkv, wu, gb, cr, mc, mr, gp, hg)
    wo = wa[:, 896:]
    part = dot(nv, wo, ((1,), (1,))).astype(bf16).reshape(4, 4, 32, D)
    m, h2 = sum_norm_gather(part, xrows, gain2, 4)
    h2 = h2.reshape(SEG, D)
    wg, wu_, wd = wb[:, :FFP], wb[:, FFP : 2 * FFP], wb[:, 2 * FFP :]
    both = jnp.dot(h2, wb[:, : 2 * FFP], preferred_element_type=f32)
    ga, up = both[:, :FFP], both[:, FFP:]
    sg = jax.nn.sigmoid(ga)
    act = ga * sg
    hid = (act * up).astype(bf16)
    ypart = dot(hid, wd, ((1,), (1,))).astype(bf16).reshape(4, 4, 32, D)

    dhid = jnp.dot(dys, wd, preferred_element_type=f32)
    dga = (dhid * up * (sg * (1.0 + ga * (1.0 - sg)))).astype(bf16)
    dup = (dhid * act).astype(bf16)
    dgu = jnp.concatenate([dga, dup], axis=1)
    dh2 = dot(dgu, wb[:, : 2 * FFP], ((1,), (1,))).astype(bf16).reshape(4, 4, 32, D)
    grad_b = jnp.concatenate([dot(h2, dgu, ((0,), (0,))), dot(dys, hid, ((0,), (0,)))], axis=1).astype(bf16)
    yrows, dm, dgain2, da = back_middle(dh2, ypart, m, dyrows, gain2, 5)
    da = da.reshape(SEG, D)
    dn = jnp.dot(da, wo, preferred_element_type=f32)
    do, dgp, dhg, etail = back_emit(dn, ov, gp, hg, qkv, wu, gb, cr, mc, mr)
    tails = zc_all(etail, 6).reshape(8, DK, DV)
    dz, dab, dcw, dsc = back_delta(where, maps, tails, do, fr, st, qkv, tm, wu, gb, cr, zq, ab, cw, sc, mc, mr)
    edge = lax.ppermute(dz[:HALO], ("z", "c"), [(i, i - 1) for i in range(1, 8)])
    dzq = jnp.concatenate([dz[HALO:SEG], dz[SEG:] + edge], axis=0).astype(bf16)
    dproj = jnp.concatenate([dzq, dgp, dab], axis=1)
    dh1 = dot(dproj, wa[:, :896], ((1,), (1,))).astype(bf16).reshape(4, 4, 32, D)
    h1o = h1[HALO:]
    grad_a = jnp.concatenate([dot(h1o, dproj, ((0,), (0,))), dot(da, nv, ((0,), (0,)))], axis=1).astype(bf16)
    dxrows, dgain1 = back_input(dh1, xrows, dm, gain1, 7)
    dp = y * 8 + z * 2 + c
    wanted = stretch_order.reshape(4, 8, 2)
    wanted = lax.dynamic_index_in_dim(wanted, seg, 1, False).reshape(8)
    wanted = jnp.stack([wanted // 16, wanted // 8 % 2, wanted % 8])
    out, dtok = send_home(wanted, (yrows, dxrows), 8)

    def unfilter(a):
        return a.reshape(4, 32, -1).swapaxes(0, 1).reshape(32, -1)

    head = jnp.broadcast_to(dsc[:, 0][None], (32, 2))
    back_line = jnp.concatenate(
        [
            unfilter(dcw[:, QC]),
            unfilter(dcw[:, KC]),
            unfilter(dcw[:, VC]),
            dhg.reshape(32, 8),
            dgain1.reshape(32, 64),
            dgain2.reshape(32, 64),
            head,
        ],
        axis=1,
    )
    back_line = jnp.pad(back_line, ((0, 0), (0, 256 - back_line.shape[1])))
    tiny_back = jnp.pad(back_line[:, None], ((0, 0), (0, 15), (0, 0))).reshape(4, 4, 2, 16, 256).astype(bf16)
    ra, rb, rt, total = return_grads(
        (grad_a.reshape(4, 4, 2, 64, NA), grad_b.reshape(4, 4, 2, 64, NB)), tiny_back, 9
    )
    ra = ra.astype(f32)
    rb = rb.astype(f32)
    rt = rt[:, 0].astype(f32)
    total = total[0]

    def heads(a):
        return a.swapaxes(0, 1)

    def untaps(a):
        return a.reshape(4, 4, -1).swapaxes(0, 1)

    def narrow(a):
        return a.swapaxes(0, 1).reshape(a.shape[1], -1)[:, :ff]

    return (
        out,
        dtok,
        total[72:136],
        heads(ra[:, :, 0:128]),
        heads(ra[:, :, 128:256]),
        heads(ra[:, :, 256:512]),
        heads(ra[:, :, 768]),
        heads(ra[:, :, 769]),
        untaps(rt[:, 0:16]),
        untaps(rt[:, 16:32]),
        untaps(rt[:, 32:64]),
        rt[:, 200],
        rt[:, 201],
        total[64:72],
        heads(ra[:, :, 512:768]),
        ra[:, :, 896:].swapaxes(1, 2),
        total[136:200],
        narrow(rb[:, :, 0:FFP]),
        narrow(rb[:, :, FFP : 2 * FFP]),
        narrow(rb[:, :, 2 * FFP :]).T,
    )


def solution(mesh):
    torus = Mesh(mesh.devices.reshape(4, 4, 2, 4), ("y", "z", "c", "x"))
    dp, tp = ("y", "z", "c"), "x"
    in_specs = (
        P(dp, None),
        P(dp, None),
        P(),
        P(),
        P(dp),
        P(dp, tp, None),
        P(dp, tp, None),
        P(dp, tp, None),
        P(dp, tp),
        P(dp, tp),
        P(None, tp, dp),
        P(None, tp, dp),
        P(None, tp, dp),
        P(tp),
        P(tp),
        P(dp),
        P(dp, tp, None),
        P(tp, None, dp),
        P(dp),
        P(dp, tp),
        P(dp, tp),
        P(tp, dp),
    )
    out_specs = (
        P(dp, tp),
        P(dp, tp),
        P(dp),
        P(dp, tp, None),
        P(dp, tp, None),
        P(dp, tp, None),
        P(dp, tp),
        P(dp, tp),
        P(None, tp, dp),
        P(None, tp, dp),
        P(None, tp, dp),
        P(tp),
        P(tp),
        P(dp),
        P(dp, tp, None),
        P(tp, None, dp),
        P(dp),
        P(dp, tp),
        P(dp, tp),
        P(tp, dp),
    )
    return jax.shard_map(body, mesh=torus, in_specs=in_specs, out_specs=out_specs, check_vma=False)
```

```python
import functools
import math

import jax
import jax.numpy as jnp
from jax import lax
from jax.experimental import pallas as pl
from jax.experimental.pallas import tpu as pltpu
from jax.sharding import Mesh
from jax.sharding import PartitionSpec as P

MESH = pl.DeviceIdType.MESH
bf16, f32, i32 = jnp.bfloat16, jnp.float32, jnp.int32
HI = lax.Precision.HIGHEST
EPS = 1e-6
STRETCH = 64
D, DK, DV, FFP, HALO = 2048, 128, 256, 384, 16
SEG = 512
ROWS = SEG + HALO
CH = 128
NCH = SEG // CH
NA, NB = 1152, 1152
VLIM = 58 * 1024 * 1024


def at(axis, k):
    n = lax.axis_size(axis)
    return lax.rem(lax.axis_index(axis) + k + n, n)


def greet(peers):
    b = pltpu.get_barrier_semaphore()
    for p in peers:
        pl.semaphore_signal(b, inc=1, device_id=p, device_id_type=MESH)
    pl.semaphore_wait(b, len(peers))


def send(src, dst, ss, rs, who):
    cp = pltpu.make_async_remote_copy(
        src_ref=src, dst_ref=dst, send_sem=ss, recv_sem=rs, device_id=who, device_id_type=MESH
    )
    cp.start()
    return cp


def run(flows, plan=""):
    flows = list(flows)
    for i in plan:
        next(flows[int(i)], None)
    for _ in together(flows):
        pass


def together(flows):
    flows = list(flows)
    while flows:
        left = []
        for f in flows:
            try:
                next(f)
                left.append(f)
            except StopIteration:
                pass
        flows = left
        if flows:
            yield


def segment_peers():
    z, c = lax.axis_index("z"), lax.axis_index("c")
    out = []
    for k in range(4):
        for d in range(2):
            if (k, d) != (0, 0):
                out.append({"z": at("z", k), "c": lax.rem(c + d, 2)})
    return out


def plane_peers():
    return [{"x": at("x", i), "y": at("y", j)} for i in range(4) for j in range(4) if (i, j) != (0, 0)]


def peers(**steps):
    return [{ax: at(ax, k)} for ax, ks in steps.items() for k in ks]


def zc_gather(slot, halves, ss, rs):
    z, c = lax.axis_index("z"), lax.axis_index("c")
    other = {"c": 1 - c}
    zp, zm, zf = at("z", 1), at("z", -1), at("z", 2)
    own, (o1, o2) = slot(z, c), halves(z, c)
    a = send(o1, o1, ss.at[0], rs.at[0], {"z": zp})
    b = send(o2, o2, ss.at[1], rs.at[1], {"z": zm})
    a2 = send(o2, o2, ss.at[9], rs.at[9], {"z": zp})
    b2 = send(o1, o1, ss.at[10], rs.at[10], {"z": zm})
    d0 = send(own, own, ss.at[4], rs.at[4], other)
    yield
    a.wait_recv()
    lo = halves(zm, c)[0]
    e = send(lo, lo, ss.at[2], rs.at[2], {"z": zp})
    b.wait_recv()
    hi = halves(zp, c)[1]
    f = send(hi, hi, ss.at[3], rs.at[3], {"z": zm})
    yield
    a2.wait_recv()
    m = slot(zm, c)
    d1 = send(m, m, ss.at[5], rs.at[5], other)
    b2.wait_recv()
    p = slot(zp, c)
    d2 = send(p, p, ss.at[6], rs.at[6], other)
    yield
    e.wait_recv()
    fl = halves(zf, c)[0]
    d3 = send(fl, fl, ss.at[7], rs.at[7], other)
    f.wait_recv()
    fh = halves(zf, c)[1]
    d4 = send(fh, fh, ss.at[8], rs.at[8], other)
    yield
    for cp in (d0, d1, d2, d3, d4):
        cp.wait_recv()
    for cp in (a, b, a2, b2, e, f, d0, d1, d2, d3, d4):
        cp.wait_send()


def trade_flow(src_of, dst, ss, rs):
    y = lax.axis_index("y")
    loc = pltpu.make_async_copy(src_of(y), dst(y), ss.at[3])
    loc.start()
    sends = [
        send(src_of(at("y", k)), dst(y), ss.at[k - 1], rs.at[k - 1], {"y": at("y", k)}) for k in (2, 1, 3)
    ]
    yield
    loc.wait()
    for cp in sends:
        cp.wait_recv()
    for cp in sends:
        cp.wait_send()


def spread_flow(out, ss, rs):
    return zc_gather(
        lambda zz, cc: out.at[:, zz, cc],
        lambda zz, cc: (out.at[0:2, zz, cc], out.at[2:4, zz, cc]),
        ss,
        rs,
    )


def exchange_flow(src_of, out, ss, rs):
    z, c = lax.axis_index("z"), lax.axis_index("c")
    yield from trade_flow(src_of, lambda y: out.at[y, z, c], ss.at[pl.ds(11, 4)], rs.at[pl.ds(11, 4)])
    yield from spread_flow(out, ss, rs)


def torus_gather(a1, a2, block, ss, rs):
    i, j = lax.axis_index(a1), lax.axis_index(a2)
    p1, m1, f1 = (at(a1, k) for k in (1, -1, 2))
    p2, m2 = at(a2, 1), at(a2, -1)
    all_of = []

    def go(ref, who):
        k = len(all_of)
        all_of.append(send(ref, ref, ss.at[k], rs.at[k], who))
        return all_of[-1]

    def along(i1):
        b = block(i1, j, None)
        return go(b, {a2: p2}), go(b, {a2: m2})

    def forward(i1, pair):
        pair[0].wait_recv()
        go(block(i1, m2, 0), {a2: p2})
        pair[1].wait_recv()
        go(block(i1, p2, 1), {a2: m2})

    own = block(i, j, None)
    a, b = go(own, {a1: p1}), go(own, {a1: m1})
    s0 = along(i)
    yield
    a.wait_recv()
    e = go(block(m1, j, 0), {a1: p1})
    b.wait_recv()
    f = go(block(p1, j, 1), {a1: m1})
    s1 = along(m1)
    s2 = along(p1)
    yield
    forward(i, s0)
    yield
    e.wait_recv()
    f.wait_recv()
    s3 = along(f1)
    yield
    forward(m1, s1)
    forward(p1, s2)
    yield
    forward(f1, s3)
    yield
    done = [a, b, e, f] + [cp for pair in (s0, s1, s2, s3) for cp in pair]
    for cp in all_of:
        if not any(cp is d for d in done):
            cp.wait_recv()
    for cp in all_of:
        cp.wait_send()


def lanes(i, j):
    return pl.ds(pl.multiple_of((i * 4 + j) * 128, 128), 128)


def gather_columns(out, skip, ss, rs):
    def half(lo, mid, hi):
        rows = {None: slice(lo, hi), 0: slice(lo, mid), 1: slice(mid, hi)}
        return lambda x, y, part: out.at[rows[part], lanes(x, y)]

    one, two = half(0, skip + 128, skip + 256), half(skip + 256, skip + 384, skip + 512)
    yield from together(
        [
            torus_gather("x", "y", one, ss.at[0], rs.at[0]),
            torus_gather("y", "x", lambda y, x, part: two(x, y, part), ss.at[1], rs.at[1]),
        ]
    )


def gather_rows(out, ss, rs):
    def half(lo):
        cols = {None: slice(lo, lo + 1024), 0: slice(lo, lo + 512), 1: slice(lo + 512, lo + 1024)}
        return lambda x, y, part: out.at[x, y, :, cols[part]]

    one, two = half(0), half(1024)
    yield from together(
        [
            torus_gather("x", "y", one, ss.at[0], rs.at[0]),
            torus_gather("y", "x", lambda y, x, part: two(x, y, part), ss.at[1], rs.at[1]),
        ]
    )


GATHER_SEMS = [pltpu.SemaphoreType.DMA((2, 20)), pltpu.SemaphoreType.DMA((2, 20))]


def ring_scatter(axis, piece, bufs, emit, ss, rs):
    me, p, m, fr = (at(axis, k) for k in (0, 1, -1, 2))
    a = send(piece(fr, 0), bufs.at[0], ss.at[0], rs.at[0], {axis: p})
    c = send(piece(fr, 1), bufs.at[1], ss.at[1], rs.at[1], {axis: m})
    b = send(piece(p, 1), bufs.at[2], ss.at[2], rs.at[2], {axis: p})
    d = send(piece(m, 0), bufs.at[3], ss.at[3], rs.at[3], {axis: m})
    yield
    a.wait_recv()
    bufs[0] = (bufs[0].astype(f32) + piece(p, 0)[...].astype(f32)).astype(bufs.dtype)
    e = send(bufs.at[0], bufs.at[4], ss.at[4], rs.at[4], {axis: p})
    c.wait_recv()
    bufs[1] = (bufs[1].astype(f32) + piece(m, 1)[...].astype(f32)).astype(bufs.dtype)
    f = send(bufs.at[1], bufs.at[5], ss.at[5], rs.at[5], {axis: m})
    yield
    d.wait_recv()
    e.wait_recv()
    emit(0, piece(me, 0)[...].astype(f32) + bufs[3].astype(f32) + bufs[4].astype(f32))
    b.wait_recv()
    f.wait_recv()
    emit(1, piece(me, 1)[...].astype(f32) + bufs[2].astype(f32) + bufs[5].astype(f32))
    for cp in (a, b, c, d, e, f):
        cp.wait_send()


def plane_scatter(part, res, big, mid, small, h, ss, rs):
    base, q = h * 1024, 512

    def keep(s, v):
        mid[:, :, s * q : (s + 1) * q] = v.astype(bf16)

    def final(s, v):
        res[:, base + s * q : base + (s + 1) * q] = v

    cols = [slice(base + s * q, base + (s + 1) * q) for s in (0, 1)]
    sub = [slice(s * q, (s + 1) * q) for s in (0, 1)]
    if h == 0:
        yield from ring_scatter("x", lambda i, s: part.at[i, :, :, cols[s]], big, keep, ss.at[0], rs.at[0])
        yield from ring_scatter("y", lambda i, s: mid.at[i, :, sub[s]], small, final, ss.at[1], rs.at[1])
    else:
        yield from ring_scatter("y", lambda i, s: part.at[:, i, :, cols[s]], big, keep, ss.at[0], rs.at[0])
        yield from ring_scatter("x", lambda i, s: mid.at[i, :, sub[s]], small, final, ss.at[1], rs.at[1])


def plane_sum(part, acc, big, mid, small, ss, rs):
    yield from together(
        plane_scatter(part, acc, big.at[h], mid.at[h], small.at[h], h, ss.at[h], rs.at[h]) for h in (0, 1)
    )


SCATTER_SCRATCH = [
    pltpu.VMEM((2, 6, 4, 32, 512), bf16),
    pltpu.VMEM((2, 4, 32, 1024), bf16),
    pltpu.VMEM((2, 6, 32, 512), bf16),
    pltpu.SemaphoreType.DMA((2, 2, 6)),
    pltpu.SemaphoreType.DMA((2, 2, 6)),
]
VM = pl.BlockSpec(memory_space=pltpu.VMEM)
SM = pl.BlockSpec(memory_space=pltpu.SMEM)
HB = pl.BlockSpec(memory_space=pl.ANY)


def shape(dims, kind=f32):
    return jax.ShapeDtypeStruct(dims, kind)


def remote_params(cid):
    return pltpu.CompilerParams(collective_id=cid, has_side_effects=True, vmem_limit_bytes=VLIM)


def columns(r):
    return lambda yy: r.at[:, :, lanes(lax.axis_index("x"), yy)]


def slots(r):
    return lambda yy: r.at[yy]


def pick_flow(src, every, index, out, skip, es, er, gs, gr):
    x, y = lax.axis_index("x"), lax.axis_index("y")
    yield from exchange_flow(columns(src), every, es, er)
    here = lanes(x, y)

    def block(j):
        a = index[j]
        return every[a >> 4, (a >> 2) & 3, (a >> 1) & 1, a & 1]

    if skip:
        out[0:skip, here] = block(0)[STRETCH - skip : STRETCH]
    for j in range(8):
        out[skip + 64 * j : skip + 64 * (j + 1), here] = block(j + 1)
    yield from gather_columns(out, skip, gs, gr)


PICK_SCRATCH = [
    pltpu.VMEM((4, 4, 2, 2, 64, 128), bf16),
    pltpu.SemaphoreType.DMA((15,)),
    pltpu.SemaphoreType.DMA((15,)),
] + GATHER_SEMS


def spread_gain(line, row, out):
    for i in range(32):
        out[:, 64 * i : 64 * (i + 1)] = line[i // 8, i // 2 % 4, i % 2, row : row + 1, 0:64]


def fetch(order, tokens, pack, tiny, cid):
    def kernel(order, tok, pack, tiny, wa, line, index, gain1, gain2, xr, h1, xo, every, es, er, gs, gr, ss, rs):
        x, y, z, c = (lax.axis_index(a) for a in "xyzc")
        seg = z * 2 + c

        def find(a, found):
            return tuple(jnp.where(order[a] == jnp.maximum(seg * 8 - 1 + j, 0), a, f) for j, f in enumerate(found))

        for j, f in enumerate(lax.fori_loop(0, 64, find, tuple(jnp.int32(0) for _ in range(9)))):
            index[j] = f
        greet(peers(y=(1, 2, 3), z=(1, 3), c=(1,), x=(1, 3)))

        def rows():
            yield from pick_flow(tok, every, index, xo, HALO, es, er, gs, gr)

            def norm(t, _):
                at_rows = pl.ds(pl.multiple_of(t * 16, 16), 16)
                v = xo[at_rows, :].astype(f32)
                r = lax.rsqrt(jnp.mean(v * v, axis=-1, keepdims=True) + EPS)
                h1[at_rows, :] = (v * r * gain1[...]).astype(bf16)
                return 0

            lax.fori_loop(0, ROWS // 16, norm, 0)
            xr[...] = xo[pl.ds(pl.multiple_of(HALO + 32 * (x * 4 + y), 16), 32), :]

        def small():
            yield from exchange_flow(slots(tiny), line, ss.at[0], rs.at[0])
            spread_gain(line, 1, gain1)
            spread_gain(line, 2, gain2)

        run([rows(), small(), exchange_flow(slots(pack), wa, ss.at[1], rs.at[1])], "012" + "01" * 6 + "2" + "02" * 3)

    return pl.pallas_call(
        kernel,
        out_shape=[
            shape((4, 4, 2) + pack.shape[1:], bf16),
            shape((4, 4, 2) + tiny.shape[1:]),
            shape((16,), i32),
            shape((1, D)),
            shape((1, D)),
            shape((32, D), bf16),
            shape((ROWS, D), bf16),
        ],
        in_specs=[SM] + [VM] * 3,
        out_specs=[VM] * 2 + [SM] + [VM] * 4,
        scratch_shapes=[pltpu.VMEM((ROWS, D), bf16)]
        + PICK_SCRATCH
        + [pltpu.SemaphoreType.DMA((2, 15)), pltpu.SemaphoreType.DMA((2, 15))],
        compiler_params=remote_params(cid),
    )(order, tokens, pack, tiny)


def sum_norm_gather(part, xrows, gain, wpart, cid):
    def kernel(part, xr, gain, wp, m_out, h_out, w_out, acc, big, mid, small, ss, rs, gs, gr, ws, wr, ls):
        x, y, z, c = (lax.axis_index(a) for a in "xyzc")
        own = pltpu.make_async_copy(wp, w_out.at[:, z, c], ls)
        own.start()
        greet(peers(x=(1, 3), y=(1, 3), z=(1, 3), c=(1,)))

        def rows():
            yield from plane_sum(part, acc, big, mid, small, ss, rs)
            m = xr[...].astype(f32) + acc[...]
            m_out[...] = m
            r = lax.rsqrt(jnp.mean(m * m, axis=-1, keepdims=True) + EPS)
            h_out[x, y] = (m * r * gain[...]).astype(bf16)
            yield from gather_rows(h_out, gs, gr)

        def weights():
            own.wait()
            yield from spread_flow(w_out, ws, wr)

        run([rows(), weights()], "01000100010")

    return pl.pallas_call(
        kernel,
        out_shape=[
            shape((32, D)),
            shape((4, 4, 32, D), bf16),
            shape((4, 4, 2) + wpart.shape[1:], bf16),
        ],
        in_specs=[VM] * 4,
        out_specs=[VM] * 3,
        scratch_shapes=[pltpu.VMEM((32, D), f32)]
        + SCATTER_SCRATCH
        + GATHER_SEMS
        + [pltpu.SemaphoreType.DMA((11,)), pltpu.SemaphoreType.DMA((11,)), pltpu.SemaphoreType.DMA],
        compiler_params=remote_params(cid),
    )(part, xrows, gain, wpart)


def norm_back(v, gain, dh):
    r = lax.rsqrt(jnp.mean(v * v, axis=-1, keepdims=True) + EPS)
    t = gain * dh
    dv = r * t - v * (r * r * r) * jnp.mean(v * t, axis=-1, keepdims=True)
    return dv, jnp.sum(v * r * dh, axis=0, keepdims=True)


def back_middle(part, m, dyrows, gain, grads, cid):
    n = len(grads)

    def kernel(part, m, dy, gain, *refs):
        gin, (dm_out, dg_out, da_out), gout = refs[:n], refs[n : n + 3], refs[n + 3 : 2 * n + 3]
        acc, big, mid, small, ss, rs, gs, gr = refs[2 * n + 3 : 2 * n + 11]
        rest = refs[2 * n + 11 :]
        x, y = lax.axis_index("x"), lax.axis_index("y")
        greet(peers(x=(1, 3), y=(1, 3), z=(1, 3), c=(1,)))

        def rows():
            yield from plane_sum(part, acc, big, mid, small, ss, rs)
            dv, dgain = norm_back(m[...], gain[...], acc[...])
            dm = dy[...].astype(f32) + dv
            dm_out[...] = dm
            dg_out[...] = dgain
            da_out[x, y] = dm.astype(bf16)
            yield from gather_rows(da_out, gs, gr)

        def sums():
            yield from together(sum_flow(gin[i], gout[i], *rest[4 * i : 4 * i + 4]) for i in range(n))

        run([rows(), sums()], "0100100100")

    return pl.pallas_call(
        kernel,
        out_shape=[shape((32, D)), shape((1, D)), shape((4, 4, 32, D), bf16)]
        + [shape((4,) + g.shape[3:], bf16) for g in grads],
        in_specs=[VM] * (4 + n),
        out_specs=[VM] * (3 + n),
        scratch_shapes=[pltpu.VMEM((32, D), f32)]
        + SCATTER_SCRATCH
        + GATHER_SEMS
        + [r for g in grads for r in sum_scratch(g.shape[3:], bf16)],
        compiler_params=remote_params(cid),
    )(part, m, dyrows, gain, *grads)


def home_flow(src, dst, order, alls, cols, picks, s1, r1, s2, r2, s3, r3):
    x, y, z, c = (lax.axis_index(a) for a in "xyzc")
    sends = []
    cols[x, y] = src[:, pl.ds(pl.multiple_of((x * 4 + y) * 128, 128), 128)]
    t = 0
    for i in range(4):
        for j in range(4):
            if (i, j) == (0, 0):
                continue
            px, py = at("x", i), at("y", j)
            lane = pl.multiple_of((px * 4 + py) * 128, 128)
            sends.append(send(src.at[:, pl.ds(lane, 128)], cols.at[x, y], s1.at[t], r1.at[t], {"x": px, "y": py}))
            t += 1
    yield
    for cp in sends:
        cp.wait_recv()
    alls[z, c] = cols[...].reshape(8, 64, 128)
    yield from zc_gather(
        lambda zz, cc: alls.at[zz, cc], lambda zz, cc: (alls.at[zz, cc, 0:4], alls.at[zz, cc, 4:8]), s2, r2
    )
    for j in range(4):
        for i in range(2):
            b = order[j * 16 + (z * 2 + c) * 2 + i]
            picks[j, 64 * i : 64 * (i + 1)] = alls[b >> 4, (b >> 3) & 1, b & 7]
    mine = pl.ds(pl.multiple_of(y * 128, 128), 128)
    last = [
        send(picks.at[at("y", j)], dst.at[:, mine], s3.at[j], r3.at[j], {"y": at("y", j)}) for j in (2, 1, 3)
    ]
    dst[:, mine] = picks[y]
    yield
    for cp in last:
        cp.wait_recv()
    for cp in sends + last:
        cp.wait_send()


HOME_SCRATCH = [
    pltpu.VMEM((4, 2, 8, 64, 128), bf16),
    pltpu.VMEM((4, 4, 32, 128), bf16),
    pltpu.VMEM((4, 128, 128), bf16),
    pltpu.SemaphoreType.DMA((15,)),
    pltpu.SemaphoreType.DMA((15,)),
    pltpu.SemaphoreType.DMA((11,)),
    pltpu.SemaphoreType.DMA((11,)),
    pltpu.SemaphoreType.DMA((4,)),
    pltpu.SemaphoreType.DMA((4,)),
]


def sum_flow(g, stage, core, bufs, ss, rs):
    c = lax.axis_index("c")
    d = send(g.at[:, :, 1 - c], core, ss.at[0], rs.at[0], {"c": 1 - c})
    yield
    d.wait_recv()

    def add(i, _):
        core[i] = (core[i].astype(f32) + g[i, :, c].astype(f32)).astype(core.dtype)
        return 0

    lax.fori_loop(0, 4, add, 0)

    def emit(s, v):
        stage[2 * s : 2 * s + 2] = v.astype(stage.dtype)

    yield from ring_scatter(
        "z", lambda i, s: core.at[2 * s : 2 * s + 2, i], bufs, emit, ss.at[pl.ds(1, 6)], rs.at[pl.ds(1, 6)]
    )
    d.wait_send()


def sum_scratch(dims, kind):
    return [
        pltpu.VMEM((4, 4) + dims, kind),
        pltpu.VMEM((6, 2) + dims, kind),
        pltpu.SemaphoreType.DMA((7,)),
        pltpu.SemaphoreType.DMA((7,)),
    ]


TRADE_SEMS = [pltpu.SemaphoreType.DMA((4,)), pltpu.SemaphoreType.DMA((4,))]


def scatter_flow(g, out, stage, ts, tr, *sums):
    yield from sum_flow(g, stage, *sums)
    yield from trade_flow(slots(stage), lambda y: out.at[y], ts, tr)


def scatter_scratch(dims, kind):
    return [pltpu.VMEM((4,) + dims, kind)] + TRADE_SEMS + sum_scratch(dims, kind)


def finish(order, part, xrows, dm, gain, grad, tiny, cid):
    nh, ns = len(HOME_SCRATCH), 7

    def kernel(order, part, xr, dm, gain, grad, tiny, dt_out, g_out, t_out, tot, acc, *rest):
        big, mid, small, ss, rs = rest[:5]
        home, rest = rest[5 : 5 + nh], rest[5 + nh :]
        ga, ti, rest = rest[:ns], rest[ns : 2 * ns], rest[2 * ns :]
        line, dx, xr4, xs, xq = rest
        x = lax.axis_index("x")
        greet(plane_peers() + peers(z=(1, 3), c=(1,)))

        def small_grads():
            yield from scatter_flow(line, t_out, *ti)
            xr4[x] = (t_out[0] + t_out[1]) + (t_out[2] + t_out[3])
            sends = [send(xr4.at[x], xr4.at[x], xs.at[k], xq.at[k], {"x": at("x", k)}) for k in (2, 1, 3)]
            yield
            for cp in sends:
                cp.wait_recv()
            tot[...] = (xr4[0] + xr4[1]) + (xr4[2] + xr4[3])
            for cp in sends:
                cp.wait_send()

        def input_grads():
            yield from plane_sum(part, acc, big, mid, small, ss, rs)
            dv, dgain = norm_back(xr[...].astype(f32), gain[...], acc[...])
            dx[...] = (dm[...] + dv).astype(bf16)
            line[...] = tiny[...]
            for i in range(32):
                line[i // 8, i // 2 % 4, i % 2, 1:2, 0:64] = dgain[:, 64 * i : 64 * (i + 1)]
            yield from together([home_flow(dx, dt_out, order, *home), small_grads()])

        run([input_grads(), scatter_flow(grad, g_out, *ga)], "0101001")

    td, gd = tiny.shape[3:], grad.shape[3:]
    return pl.pallas_call(
        kernel,
        out_shape=[shape((128, 512), bf16), shape((4,) + gd, bf16), shape((4,) + td), shape(td)],
        in_specs=[SM] + [VM] * 6,
        out_specs=[VM] * 4,
        scratch_shapes=[pltpu.VMEM((32, D), f32)]
        + SCATTER_SCRATCH
        + HOME_SCRATCH
        + scatter_scratch(gd, bf16)
        + scatter_scratch(td, f32)
        + [
            pltpu.VMEM(tiny.shape, f32),
            pltpu.VMEM((32, D), bf16),
            pltpu.VMEM((4,) + td, f32),
            pltpu.SemaphoreType.DMA((4,)),
            pltpu.SemaphoreType.DMA((4,)),
        ],
        compiler_params=remote_params(cid),
    )(order, part, xrows, dm, gain, grad, tiny)


def dot(a, b, dims, prec=None):
    return lax.dot_general(a, b, (dims, ((), ())), preferred_element_type=f32, precision=prec)


def lo(a):
    return a.astype(bf16)


def mm(a, b):
    return dot(lo(a), lo(b), ((1,), (0,)))


def mmt(a, b):
    return dot(lo(a), lo(b), ((1,), (1,)))


def tmm(a, b):
    return dot(lo(a), lo(b), ((0,), (0,)))


def halves_of(a):
    h = a.astype(bf16)
    return h, (a - h.astype(f32)).astype(bf16)


def fine(a, b, dims=((1,), (0,))):
    ah, al = halves_of(a)
    bh, bl = halves_of(b)
    return dot(ah, bh, dims) + (dot(ah, bl, dims) + dot(al, bh, dims))


def tri_inverse(a, r, c):
    eye = jnp.where(r == c, 1.0, 0.0)
    n1 = jnp.where((r >> 3) == (c >> 3), -a, 0.0)
    n2 = fine(n1, n1)
    n4 = fine(n2, n2)
    t = eye + n1
    t = t + fine(t, n2)
    t = t + fine(t, n4)
    for level in (3, 4, 5, 6):
        off = ((r >> (level + 1)) == (c >> (level + 1))) & ((r >> level) != (c >> level))
        t = t - fine(t, fine(jnp.where(off, a, 0.0), t))
    return t


def iotas():
    return (
        lax.broadcasted_iota(i32, (CH, CH), 0),
        lax.broadcasted_iota(i32, (CH, CH), 1),
    )


def filtered(z, cw, mc, cols):
    total = z[HALO : HALO + SEG, cols] * cw[3:4, cols]
    for j in range(3):
        total = total + mc[:, j : j + 1] * cw[j : j + 1, cols] * z[HALO - 3 + j : HALO - 3 + j + SEG, cols]
    return total


def silu(v):
    return v * jax.nn.sigmoid(v)


QC, KC, VC = slice(0, 128), slice(128, 256), slice(256, 512)


def decay_of(cc, cr, mask):
    return jnp.exp(jnp.where(mask, cc - cr, 0.0)) * jnp.where(mask, 1.0, 0.0)


def prepare(z, ab, cw, sc, mc, mr, qkv, tm, wu, gb, cr, ti):
    r, c = iotas()
    for cols, scale in ((QC, DK**-0.5), (KC, 1.0)):
        s = silu(filtered(z, cw, mc, cols))
        qkv[:, cols] = (s * lax.rsqrt(jnp.sum(s * s, axis=-1, keepdims=True) + EPS) * scale).astype(bf16)
    qkv[:, VC] = silu(filtered(z, cw, mc, VC)).astype(bf16)
    low = jnp.where(r >= c, 1.0, 0.0)
    eye = jnp.where(r == c, 1.0, 0.0)
    lane = lax.broadcasted_iota(i32, (CH, 128), 1)
    transit = eye
    insert = jnp.zeros((DK, DV), f32)
    yield
    for n in range(NCH):
        rows = slice(n * CH, (n + 1) * CH)
        raw = ab[HALO + n * CH : HALO + (n + 1) * CH, :]
        beta = jax.nn.sigmoid(raw[:, 1:2])
        u = raw + sc[0:1, 1:2]
        g = -jnp.exp(sc[0:1, 0:1]) * (jnp.maximum(u, 0.0) + jnp.log1p(jnp.exp(-jnp.abs(u))))
        g = jnp.where(lane == 0, g, 0.0)
        cum = dot(low, g, ((1,), (0,)), HI)[:, 0:1]
        cumr = dot(g, low, ((0,), (1,)), HI)[0:8, :]
        gb[rows, :] = jnp.where(lane == 0, beta, cum)
        cr[:, rows] = cumr
        cumrow = cumr[0:1, :]
        last = cumr[0:1, CH - 1 : CH]
        m = mc[rows, :]
        carried, closing, begin, carry_last = m[:, 3:4], m[:, 4:5], m[:, 5:6], m[0:1, 6:7]
        same = begin == mr[0:1, rows]
        k = qkv[rows, KC]
        kf = k.astype(f32)
        v = qkv[rows, VC].astype(f32)
        a = beta * dot(k, k, ((1,), (1,))) * decay_of(cum, cumrow, same & (r > c))
        t = tri_inverse(a, r, c)
        tm[rows, :] = t
        lead = (beta * jnp.exp(cum) * carried) * kf
        w = fine(t, lead)
        uu = fine(t, beta * v)
        wu[rows, 0:DK] = w
        wu[rows, DK:] = uu
        tail = kf * (jnp.exp(last - cum) * closing)
        keep = jnp.exp(last) * carry_last
        hand = keep * eye - fine(tail, w, ((0,), (0,)))
        insert = fine(hand, insert) + fine(tail, uu, ((0,), (0,)))
        transit = fine(hand, transit)
        yield
    ti[:, 0:DK] = transit.astype(bf16)
    ti[:, DK:] = insert.astype(bf16)


def emit_outputs(seg, maps, qkv, wu, gb, cr, mc, mr, gp, hg, nout, oout, fout, sout):
    r, c = iotas()

    def fold(d, s):
        tr, ins = maps[d, :, 0:DK], maps[d, :, DK:].astype(f32)
        sh, sl = halves_of(s)
        new = dot(tr, sh, ((1,), (0,))) + dot(tr, sl, ((1,), (0,))) + ins
        return jnp.where(d < seg, new, s)

    s = lax.fori_loop(0, 7, fold, jnp.zeros((DK, DV), f32))
    for n in range(NCH):
        rows = slice(n * CH, (n + 1) * CH)
        m = mc[rows, :]
        carried, closing, begin, carry_last = m[:, 3:4], m[:, 4:5], m[:, 5:6], m[0:1, 6:7]
        cum = gb[rows, 1:2]
        cumrow = cr[0:1, rows]
        last = cr[0:1, n * CH + CH - 1 : n * CH + CH]
        same = begin == mr[0:1, rows]
        q, k = qkv[rows, QC], qkv[rows, KC]
        p = dot(q, k, ((1,), (1,))) * decay_of(cum, cumrow, same & (r >= c))
        fresh = wu[rows, DK:] - fine(wu[rows, 0:DK], s)
        qd = q.astype(f32) * (jnp.exp(cum) * carried)
        o = mm(qd, s) + mm(p, fresh)
        sout[n] = s
        fout[rows, :] = fresh
        oout[rows, :] = o
        x = gp[HALO + n * CH : HALO + (n + 1) * CH, :]
        rn = lax.rsqrt(jnp.mean(o * o, axis=-1, keepdims=True) + EPS)
        nout[rows, :] = (o * rn * hg[0:1, :] * silu(x)).astype(bf16)
        tail = k.astype(f32) * (jnp.exp(last - cum) * closing)
        s = (jnp.exp(last) * carry_last) * s + fine(tail, fresh, ((0,), (0,)))
        yield


def back_emit(dn, o, gp, hg, qkv, wu, gb, cr, mc, mr, do_out, dgp_out, dhg_out, e_out):
    r, c = iotas()
    dhg = jnp.zeros((1, DV), f32)
    e = jnp.zeros((DK, DV), f32)
    for n in reversed(range(NCH)):
        rows = slice(n * CH, (n + 1) * CH)
        ov, x, dnv = o[rows, :], gp[HALO + n * CH : HALO + (n + 1) * CH, :], dn[rows, :]
        rn = lax.rsqrt(jnp.mean(ov * ov, axis=-1, keepdims=True) + EPS)
        sg = jax.nn.sigmoid(x)
        act = x * sg
        h = hg[0:1, :]
        base = ov * rn
        dhg = dhg + jnp.sum(base * act * dnv, axis=0, keepdims=True)
        dgp_out[rows, :] = (dnv * base * h * (sg * (1.0 + x * (1.0 - sg)))).astype(bf16)
        t = dnv * h * act
        do = rn * t - base * (rn * rn) * jnp.mean(ov * t, axis=-1, keepdims=True)
        do_out[rows, :] = do
        m = mc[rows, :]
        carried, closing, begin, carry_last = m[:, 3:4], m[:, 4:5], m[:, 5:6], m[0:1, 6:7]
        cum = gb[rows, 1:2]
        cumrow = cr[0:1, rows]
        last = cr[0:1, n * CH + CH - 1 : n * CH + CH]
        same = begin == mr[0:1, rows]
        q, k = qkv[rows, QC], qkv[rows, KC]
        p = dot(q, k, ((1,), (1,))) * decay_of(cum, cumrow, same & (r >= c))
        qd = q.astype(f32) * (jnp.exp(cum) * carried)
        tail = k.astype(f32) * (jnp.exp(last - cum) * closing)
        df = tmm(p, do) + mm(tail, e)
        e = tmm(qd, do) + (jnp.exp(last) * carry_last) * e - tmm(wu[rows, 0:DK], df)
        yield
    dhg_out[...] = dhg
    e_out[...] = e.astype(bf16)


def back_delta(seg, maps, tails, do, fr, st, qkv, tm, wu, gb, cr, z, ab, cw, sc, mc, mr, dz, dab, dcw, dsc, dqkv):
    r, c = iotas()
    low = jnp.where(r >= c, 1.0, 0.0)
    ones = jnp.ones((CH, CH), f32)
    lane = lax.broadcasted_iota(i32, (CH, 128), 1)
    row = lax.broadcasted_iota(i32, (CH, 1), 0)

    def fold(i, e):
        d = 7 - i
        tr, own = maps[d, :, 0:DK], tails[d].astype(f32)
        eh, el = halves_of(e)
        new = dot(tr, eh, ((0,), (0,))) + dot(tr, el, ((0,), (0,))) + own
        return jnp.where(d > seg, new, e)

    e = lax.fori_loop(0, 7, fold, jnp.zeros((DK, DV), f32))
    acc_a = jnp.zeros((1, 128), f32)
    acc_d = jnp.zeros((1, 128), f32)
    for n in reversed(range(NCH)):
        rows = slice(n * CH, (n + 1) * CH)
        m = mc[rows, :]
        carried, closing, begin, carry_last = m[:, 3:4], m[:, 4:5], m[:, 5:6], m[0:1, 6:7]
        beta, cum = gb[rows, 0:1], gb[rows, 1:2]
        cumrow = cr[0:1, rows]
        last = cr[0:1, n * CH + CH - 1 : n * CH + CH]
        same = begin == mr[0:1, rows]
        q, k = qkv[rows, QC], qkv[rows, KC]
        qf, kf, vf = q.astype(f32), k.astype(f32), qkv[rows, VC].astype(f32)
        dec_i = decay_of(cum, cumrow, same & (r >= c))
        dec_s = jnp.where(r > c, dec_i, 0.0)
        p = dot(q, k, ((1,), (1,))) * dec_i
        kkd = dot(k, k, ((1,), (1,))) * dec_s
        ex = jnp.exp(cum) * carried
        tf = jnp.exp(last - cum) * closing
        keep = jnp.exp(last) * carry_last
        tail = kf * tf
        qd = qf * ex
        dov, fv, sv, tv = do[rows, :], fr[rows, :], st[n], tm[rows, :]
        w, u = wu[rows, 0:DK], wu[rows, DK:]
        df = tmm(p, dov) + mm(tail, e)
        dw = -mmt(df, sv)
        dtail = mmt(fv, e)
        dkeep = jnp.sum(jnp.sum(sv * e, axis=1, keepdims=True), axis=0, keepdims=True)
        dqd = mmt(dov, sv)
        dp = mmt(dov, fv)
        dlead = tmm(tv, dw)
        dbv = tmm(tv, df)
        da = -(mmt(dlead, w) + mmt(dbv, u))
        dakd = da * kkd
        dkk = da * beta * dec_s
        dqk = dp * dec_i
        mix = dakd * beta + dp * p
        dqkv[rows, QC] = mm(dqk, k) + dqd * ex
        dqkv[rows, KC] = (
            tmm(dqk, q) + mm(dkk, k) + tmm(dkk, k) + dlead * (beta * ex) + dtail * tf
        )
        dqkv[rows, VC] = beta * dbv
        lk = jnp.sum(dlead * kf, axis=1, keepdims=True) * ex
        dbeta = jnp.sum(dakd, axis=1, keepdims=True) + lk + jnp.sum(dbv * vf, axis=1, keepdims=True)
        tt = jnp.sum(dtail * tail, axis=1, keepdims=True)
        dcum = jnp.sum(mix, axis=1, keepdims=True) + jnp.sum(dqd * qd, axis=1, keepdims=True) + lk * beta - tt
        dcum = dcum + jnp.where(row == CH - 1, jnp.sum(tt, axis=0, keepdims=True) + dkeep * keep, 0.0)
        full = dcum - dot(mix, ones, ((0,), (0,)), HI)
        dg = dot(low, full, ((0,), (0,)), HI)
        raw = ab[HALO + n * CH : HALO + (n + 1) * CH, :]
        uu = raw + sc[0:1, 1:2]
        rate = -jnp.exp(sc[0:1, 0:1])
        sp = jnp.maximum(uu, 0.0) + jnp.log1p(jnp.exp(-jnp.abs(uu)))
        dal = dg * rate * jax.nn.sigmoid(uu)
        acc_a = acc_a + jnp.sum(dg * rate * sp, axis=0, keepdims=True)
        acc_d = acc_d + jnp.sum(dal, axis=0, keepdims=True)
        dab[rows, :] = jnp.where(
            lane == 0, dal, jnp.where(lane == 1, dbeta * beta * (1.0 - beta), 0.0)
        ).astype(bf16)
        e = tmm(qd, dov) + keep * e - tmm(w, df)
        yield
    dsc[0:1, :] = acc_a
    dsc[1:2, :] = acc_d
    dz[0:HALO, :] = jnp.zeros((HALO, 512), f32)
    for cols, scale in ((QC, DK**-0.5), (KC, 1.0), (VC, None)):
        y = filtered(z, cw, mc, cols)
        sg = jax.nn.sigmoid(y)
        ds = dqkv[:, cols]
        if scale is not None:
            s = y * sg
            rn = lax.rsqrt(jnp.sum(s * s, axis=-1, keepdims=True) + EPS)
            ds = scale * (rn * ds - s * (rn * rn * rn) * jnp.sum(s * ds, axis=-1, keepdims=True))
        dy = ds * (sg * (1.0 + y * (1.0 - sg)))
        dz[HALO : HALO + SEG, cols] = dy * cw[3:4, cols]
        dcw[3:4, cols] = jnp.sum(dy * z[HALO : HALO + SEG, cols], axis=0, keepdims=True)
        for j in range(3):
            part = mc[:, j : j + 1] * dy
            away = slice(HALO - 3 + j, HALO - 3 + j + SEG)
            dcw[j : j + 1, cols] = jnp.sum(part * z[away, cols], axis=0, keepdims=True)
            dz[away, cols] = dz[away, cols] + part * cw[j : j + 1, cols]
        yield


def map_gather(own, out, ss, rs):
    z, c = lax.axis_index("z"), lax.axis_index("c")
    out[z, c] = own[...]
    h = own.shape[0] // 2
    yield from zc_gather(
        lambda zz, cc: out.at[zz, cc], lambda zz, cc: (out.at[zz, cc, 0:h], out.at[zz, cc, h : 2 * h]), ss, rs
    )


class Maps:
    def __init__(self, ref):
        self.ref = ref

    def __getitem__(self, key):
        key = key if isinstance(key, tuple) else (key,)
        return self.ref[(key[0] // 2, key[0] % 2) + key[1:]]


def masks(lens, mc, mr):
    base = (lax.axis_index("z") * 2 + lax.axis_index("c")) * SEG
    firsts = [jnp.int32(0)]
    for k in range(3):
        firsts.append(firsts[k] + lens[k])

    def begin_of(pos):
        b = jnp.zeros_like(pos)
        for k in range(1, 4):
            b = jnp.where((pos >= firsts[k]) & (pos < firsts[k] + lens[k]), firsts[k], b)
        return b

    lane = lax.broadcasted_iota(i32, (CH, 128), 1)
    for n in range(NCH):
        first = base + n * CH
        pos = first + lax.broadcasted_iota(i32, (CH, 128), 0)
        b = begin_of(pos)
        last = begin_of(jnp.full((CH, 128), first + CH - 1, i32))

        def one(flag):
            return jnp.where(flag, 1.0, 0.0)

        late = jnp.where(lane == 3, one(b < first), jnp.where(lane == 4, one(b == last), one(last < first)))
        flags = jnp.where(lane < 3, one(pos - 3 + lane >= b), late)
        mc[n * CH : (n + 1) * CH, :] = jnp.where(lane == 5, b.astype(f32), flags)
        mr[:, n * CH : (n + 1) * CH] = begin_of(first + lax.broadcasted_iota(i32, (8, CH), 1)).astype(f32)


def attend(proj, cw, hg, lens, a_log, dt_bias, index, cotangent, pack, cid):
    npk = len(PICK_SCRATCH)

    def kernel(proj, cw, hg, lens, al, dt, index, cot, pack, wp, dyo, dyr, qkv, tm, wu, gb, cr, maps, nout, oout, fout, sout, mc, mr, sc, *refs):
        every, es, er, gs, gr = refs[:npk]
        ti, ms, mq, ts, tr = refs[npk:]
        x, y, z, c = (lax.axis_index(a) for a in "xyzc")
        zq, gp, ab = proj.at[:, 0:512], proj.at[:, 512:768], proj.at[:, 768:896]
        greet(peers(y=(1, 2, 3), z=(1, 3), c=(1,), x=(1, 3)))

        def mixer():
            masks(lens, mc, mr)
            sc[0:8, :] = jnp.where(lax.broadcasted_iota(i32, (8, 128), 1) == 0, al[y], dt[y])
            yield from prepare(zq, ab, cw, sc, mc, mr, qkv, tm, wu, gb, cr, ti)
            yield from map_gather(ti, maps, ms, mq)
            yield from emit_outputs(z * 2 + c, Maps(maps), qkv, wu, gb, cr, mc, mr, gp, hg, nout, oout, fout, sout)

        def cotangents():
            yield from pick_flow(cot, every, index, dyo, 0, es, er, gs, gr)
            dyr[...] = dyo[pl.ds(pl.multiple_of(32 * (x * 4 + y), 32), 32), :]

        run(
            [mixer(), cotangents(), trade_flow(slots(pack), lambda i: wp.at[i], ts, tr)],
            "12" + "01" * 5 + "0011" + "0101" * 4,
        )

    return pl.pallas_call(
        kernel,
        out_shape=[
            shape(pack.shape, bf16),
            shape((SEG, D), bf16),
            shape((32, D), bf16),
            shape((SEG, 512), bf16),
            shape((SEG, CH)),
            shape((SEG, DK + DV)),
            shape((SEG, 128)),
            shape((8, SEG)),
            shape((4, 2, DK, DK + DV), bf16),
            shape((SEG, DV), bf16),
            shape((SEG, DV)),
            shape((SEG, DV)),
            shape((NCH, DK, DV)),
            shape((SEG, 128)),
            shape((8, SEG)),
            shape((8, 128)),
        ],
        in_specs=[VM] * 3 + [SM] * 4 + [VM] * 2,
        out_specs=[VM] * 16,
        scratch_shapes=PICK_SCRATCH
        + [
            pltpu.VMEM((DK, DK + DV), bf16),
            pltpu.SemaphoreType.DMA((11,)),
            pltpu.SemaphoreType.DMA((11,)),
        ]
        + TRADE_SEMS,
        compiler_params=remote_params(cid),
    )(proj, cw, hg, lens, a_log, dt_bias, index, cotangent, pack)


def back_attend(dn, o, proj, hg, qkv, tm, wu, gb, cr, mc, mr, maps, fr, st, cw, sc, m, order, ypart, stages, grad, cid):
    nh, n = len(HOME_SCRATCH), len(stages)

    def kernel(dn, o, proj, hg, qkv, tm, wu, gb, cr, mc, mr, maps, fr, st, cw, sc, m, order, ypart, *refs):
        staged, grad, refs = refs[:n], refs[n], refs[n + 1 :]
        y_out, dproj, dhg, dcw, dsc, g_out = refs[:6]
        s_out, refs = refs[6 : 6 + n], refs[6 + n :]
        do, dgp, e, tails, dz, dab, dqkv, edge, ms, mq, ds, dq, acc, yrow = refs[:14]
        big, mid, small, ss, rs = refs[14:19]
        home, refs = refs[19 : 19 + nh], refs[19 + nh :]
        ga, trades = refs[:7], refs[7:]
        zq, gp, ab = proj.at[:, 0:512], proj.at[:, 512:768], proj.at[:, 768:896]
        seg = lax.axis_index("z") * 2 + lax.axis_index("c")
        greet(plane_peers() + segment_peers())

        def mixer():
            yield from back_emit(dn, o, gp, hg, qkv, wu, gb, cr, mc, mr, do, dgp, dhg, e)
            yield from map_gather(e, tails, ms, mq)
            yield from back_delta(
                seg, Maps(maps), Maps(tails), do, fr, st, qkv, tm, wu, gb, cr, zq, ab, cw, sc, mc, mr, dz, dab, dcw, dsc, dqkv
            )
            before = lax.rem(seg + 7, 8)
            cp = send(dz.at[0:HALO], edge, ds, dq, {"z": before // 2, "c": lax.rem(before, 2)})
            dproj[0 : SEG - HALO, 0:512] = dz[HALO:SEG].astype(bf16)
            dproj[:, 512:768] = dgp[...]
            dproj[:, 768:896] = dab[...]
            yield
            cp.wait_recv()
            dproj[SEG - HALO : SEG, 0:512] = (dz[SEG:ROWS] + jnp.where(seg < 7, edge[...], 0.0)).astype(bf16)
            cp.wait_send()

        def result():
            yield from plane_sum(ypart, acc, big, mid, small, ss, rs)
            yrow[...] = (m[...] + acc[...]).astype(bf16)
            yield from home_flow(yrow, y_out, order, *home)

        def trade(i):
            return trade_flow(slots(staged[i]), lambda y: s_out[i].at[y], trades[2 * i], trades[2 * i + 1])

        run(
            [mixer(), result(), scatter_flow(grad, g_out, *ga)] + [trade(i) for i in range(n)],
            "12" + "0" * 4 + "12" + "0" * 2 + "12" + "0" * 2 + "12" + "34"[:n] + "0" * 2 + "12" + "0" + "12" + "0" + "34"[:n] + "012012012",
        )

    gd = grad.shape[3:]
    return pl.pallas_call(
        kernel,
        out_shape=[
            shape((128, 512), bf16),
            shape((SEG, 896), bf16),
            shape((1, DV)),
            shape((4, 512)),
            shape((2, 128)),
            shape((4,) + gd, bf16),
        ]
        + [shape(t.shape, bf16) for t in stages],
        in_specs=[VM] * 17 + [SM] + [VM] * (2 + n),
        out_specs=[VM] * (6 + n),
        scratch_shapes=[
            pltpu.VMEM((SEG, DV), f32),
            pltpu.VMEM((SEG, DV), bf16),
            pltpu.VMEM((DK, DV), bf16),
            pltpu.VMEM((4, 2, DK, DV), bf16),
            pltpu.VMEM((ROWS, 512), f32),
            pltpu.VMEM((SEG, 128), bf16),
            pltpu.VMEM((SEG, 512), f32),
            pltpu.VMEM((HALO, 512), f32),
            pltpu.SemaphoreType.DMA((11,)),
            pltpu.SemaphoreType.DMA((11,)),
            pltpu.SemaphoreType.DMA,
            pltpu.SemaphoreType.DMA,
            pltpu.VMEM((32, D), f32),
            pltpu.VMEM((32, D), bf16),
        ]
        + SCATTER_SCRATCH
        + HOME_SCRATCH
        + scatter_scratch(gd, bf16)
        + TRADE_SEMS * n,
        compiler_params=remote_params(cid),
    )(dn, o, proj, hg, qkv, tm, wu, gb, cr, mc, mr, maps, fr, st, cw, sc, m, order, ypart, *stages, grad)


def wide(a):
    a = jnp.pad(a.astype(bf16), ((0, 0), (0, 4 * FFP - a.shape[1])))
    return a.reshape(a.shape[0], 4, FFP).swapaxes(0, 1)


def body(
    tokens,
    cotangent,
    seq_lengths,
    stretch_order,
    attn_gain,
    w_query,
    w_key,
    w_value,
    w_alpha,
    w_beta,
    conv_query,
    conv_key,
    conv_value,
    a_log,
    dt_bias,
    head_gain,
    w_outgate,
    w_output,
    mlp_gain,
    w_gate,
    w_up,
    w_down,
):
    ff = w_gate.shape[1]

    def by_head(a):
        return a.astype(bf16).swapaxes(0, 1)

    pair = jnp.stack([w_alpha, w_beta], axis=-1).astype(bf16)
    pack_a = jnp.concatenate(
        [
            by_head(w_query),
            by_head(w_key),
            by_head(w_value),
            by_head(w_outgate),
            jnp.pad(pair.swapaxes(0, 1), ((0, 0), (0, 0), (0, 126))),
            w_output.astype(bf16).swapaxes(1, 2),
        ],
        axis=2,
    )
    pack_b = jnp.concatenate([wide(w_gate), wide(w_up), wide(w_down.T)], axis=2)

    def taps(a):
        return a.swapaxes(0, 1).reshape(4, -1)

    def each(a):
        return jnp.broadcast_to(a[None], (4,) + a.shape)

    line = jnp.concatenate([taps(conv_query), taps(conv_key), taps(conv_value), each(head_gain)], axis=1)
    line = jnp.pad(line, ((0, 0), (0, 128 - line.shape[1])))
    gains = jnp.pad(jnp.stack([attn_gain, mlp_gain]), ((0, 5), (0, 64)))
    tiny = jnp.concatenate([line[:, None], each(gains)], axis=1).astype(bf16).astype(f32)
    wa, lines, index, gain1, gain2, xrows, h1 = fetch(stretch_order, tokens.reshape(2, STRETCH, D), pack_a, tiny, 1)
    wa = wa.reshape(D, NA)
    lines = lines[:, :, :, 0].reshape(32, 128)

    def filters(a):
        return a.reshape(32, 4, -1).swapaxes(0, 1).reshape(4, -1)

    cw = jnp.concatenate([filters(lines[:, 0:16]), filters(lines[:, 16:32]), filters(lines[:, 32:64])], axis=1)
    hg = lines[:, 64:72].reshape(1, DV)

    proj = jnp.dot(h1, wa[:, :896], preferred_element_type=f32)
    wpart, dys, dyrows, qkv, tm, wu, gb, cr, maps, nv, ov, fr, st, mc, mr, sc = attend(
        proj, cw, hg, seq_lengths, a_log, dt_bias, index, cotangent.reshape(2, STRETCH, D), pack_b, 2
    )
    wo = wa[:, 896:]
    part = dot(nv, wo, ((1,), (1,))).astype(bf16).reshape(4, 4, 32, D)
    m, h2, wb = sum_norm_gather(part, xrows, gain2, wpart, 3)
    wb = wb.reshape(D, NB)
    h2 = h2.reshape(SEG, D)
    wg, wu_, wd = wb[:, :FFP], wb[:, FFP : 2 * FFP], wb[:, 2 * FFP :]
    both = jnp.dot(h2, wb[:, : 2 * FFP], preferred_element_type=f32)
    ga, up = both[:, :FFP], both[:, FFP:]
    sg = jax.nn.sigmoid(ga)
    act = ga * sg
    hid = (act * up).astype(bf16)
    ypart = dot(hid, wd, ((1,), (1,))).astype(bf16).reshape(4, 4, 32, D)

    dhid = jnp.dot(dys, wd, preferred_element_type=f32)
    dga = (dhid * up * (sg * (1.0 + ga * (1.0 - sg)))).astype(bf16)
    dup = (dhid * act).astype(bf16)
    dgu = jnp.concatenate([dga, dup], axis=1)
    dh2 = dot(dgu, wb[:, : 2 * FFP], ((1,), (1,))).astype(bf16).reshape(4, 4, 32, D)
    grad_gu = dot(h2, dgu, ((0,), (0,))).astype(bf16).reshape(4, 4, 2, 64, -1)
    grad_d = dot(dys, hid, ((0,), (0,))).astype(bf16).reshape(4, 4, 2, 64, -1)
    dm, dgain2, da, sgu, sd = back_middle(dh2, m, dyrows, gain2, (grad_gu, grad_d), 4)
    da = da.reshape(SEG, D)
    dn = jnp.dot(da, wo, preferred_element_type=f32)
    grad_o = dot(da, nv, ((0,), (0,))).astype(bf16).reshape(4, 4, 2, 64, -1)
    out, dproj, dhg, dcw, dsc, ro, rgu, rd = back_attend(
        dn, ov, proj, hg, qkv, tm, wu, gb, cr, mc, mr, maps, fr, st, cw, sc, m, stretch_order, ypart, (sgu, sd), grad_o, 5
    )
    dh1 = dot(dproj, wa[:, :896], ((1,), (1,))).astype(bf16).reshape(4, 4, 32, D)
    h1o = h1[HALO:]
    grad_a = dot(h1o, dproj, ((0,), (0,))).astype(bf16).reshape(4, 4, 2, 64, -1)
    def unfilter(a):
        return a.reshape(4, 32, -1).swapaxes(0, 1).reshape(32, -1)

    head = jnp.broadcast_to(dsc[:, 0][None], (32, 2))
    back_line = jnp.concatenate(
        [unfilter(dcw[:, QC]), unfilter(dcw[:, KC]), unfilter(dcw[:, VC]), dhg.reshape(32, 8), head], axis=1
    )
    back_line = jnp.pad(back_line, ((0, 0), (0, 128 - back_line.shape[1])))
    gain_line = jnp.pad(dgain2.reshape(32, 64), ((0, 0), (0, 64)))
    blank = jnp.zeros_like(back_line)
    tiny_back = jnp.stack([back_line, blank, gain_line] + [blank] * 5, axis=1).reshape(4, 4, 2, 8, 128)
    dtok, ra, rt, total = finish(
        stretch_order, dh1, xrows, dm, gain1, grad_a, tiny_back, 6
    )
    ra = ra.astype(f32)
    rgu, rd, ro = rgu.astype(f32), rd.astype(f32), ro.astype(f32)
    rt = rt[:, 0]

    def heads(a):
        return a.swapaxes(0, 1)

    def untaps(a):
        return a.reshape(4, 4, -1).swapaxes(0, 1)

    def narrow(a):
        return a.swapaxes(0, 1).reshape(a.shape[1], -1)[:, :ff]

    return (
        out,
        dtok,
        total[1, :64],
        heads(ra[:, :, 0:128]),
        heads(ra[:, :, 128:256]),
        heads(ra[:, :, 256:512]),
        heads(ra[:, :, 768]),
        heads(ra[:, :, 769]),
        untaps(rt[:, 0:16]),
        untaps(rt[:, 16:32]),
        untaps(rt[:, 32:64]),
        rt[:, 72],
        rt[:, 73],
        total[0, 64:72],
        heads(ra[:, :, 512:768]),
        ro.swapaxes(1, 2),
        total[2, :64],
        narrow(rgu[:, :, :FFP]),
        narrow(rgu[:, :, FFP:]),
        narrow(rd).T,
    )


def solution(mesh):
    torus = Mesh(mesh.devices.reshape(4, 4, 2, 4), ("y", "z", "c", "x"))
    dp, tp = ("y", "z", "c"), "x"
    in_specs = (
        P(dp, None),
        P(dp, None),
        P(),
        P(),
        P(dp),
        P(dp, tp, None),
        P(dp, tp, None),
        P(dp, tp, None),
        P(dp, tp),
        P(dp, tp),
        P(None, tp, dp),
        P(None, tp, dp),
        P(None, tp, dp),
        P(tp),
        P(tp),
        P(dp),
        P(dp, tp, None),
        P(tp, None, dp),
        P(dp),
        P(dp, tp),
        P(dp, tp),
        P(tp, dp),
    )
    out_specs = (
        P(dp, tp),
        P(dp, tp),
        P(dp),
        P(dp, tp, None),
        P(dp, tp, None),
        P(dp, tp, None),
        P(dp, tp),
        P(dp, tp),
        P(None, tp, dp),
        P(None, tp, dp),
        P(None, tp, dp),
        P(tp),
        P(tp),
        P(dp),
        P(dp, tp, None),
        P(tp, None, dp),
        P(dp),
        P(dp, tp),
        P(dp, tp),
        P(tp, dp),
    )
    return jax.shard_map(body, mesh=torus, in_specs=in_specs, out_specs=out_specs, check_vma=False)
```

```python
import functools
import math

import jax
import jax.numpy as jnp
from jax import lax
from jax.experimental import pallas as pl
from jax.experimental.pallas import tpu as pltpu
from jax.sharding import Mesh
from jax.sharding import PartitionSpec as P

MESH = pl.DeviceIdType.MESH
bf16, f32, i32 = jnp.bfloat16, jnp.float32, jnp.int32
HI = lax.Precision.HIGHEST
EPS = 1e-6
STRETCH = 64
D, DK, DV, FFP, HALO = 2048, 128, 256, 384, 16
SEG = 512
ROWS = SEG + HALO
CH = 128
NCH = SEG // CH
NA, NB = 1152, 1152
VLIM = 58 * 1024 * 1024


def at(axis, k):
    n = lax.axis_size(axis)
    return lax.rem(lax.axis_index(axis) + k + n, n)


def greet(peers):
    b = pltpu.get_barrier_semaphore()
    for p in peers:
        pl.semaphore_signal(b, inc=1, device_id=p, device_id_type=MESH)
    pl.semaphore_wait(b, len(peers))


def send(src, dst, ss, rs, who):
    cp = pltpu.make_async_remote_copy(
        src_ref=src, dst_ref=dst, send_sem=ss, recv_sem=rs, device_id=who, device_id_type=MESH
    )
    cp.start()
    return cp


def run(flows, plan=""):
    flows = list(flows)
    for i in plan:
        next(flows[int(i)], None)
    for _ in together(flows):
        pass


def together(flows):
    flows = list(flows)
    while flows:
        left = []
        for f in flows:
            try:
                next(f)
                left.append(f)
            except StopIteration:
                pass
        flows = left
        if flows:
            yield


def segment_peers():
    z, c = lax.axis_index("z"), lax.axis_index("c")
    out = []
    for k in range(4):
        for d in range(2):
            if (k, d) != (0, 0):
                out.append({"z": at("z", k), "c": lax.rem(c + d, 2)})
    return out


def plane_peers():
    return [{"x": at("x", i), "y": at("y", j)} for i in range(4) for j in range(4) if (i, j) != (0, 0)]


def peers(**steps):
    return [{ax: at(ax, k)} for ax, ks in steps.items() for k in ks]


def zc_gather(slot, halves, ss, rs):
    z, c = lax.axis_index("z"), lax.axis_index("c")
    other = {"c": 1 - c}
    zp, zm, zf = at("z", 1), at("z", -1), at("z", 2)
    own, (o1, o2) = slot(z, c), halves(z, c)
    a = send(o1, o1, ss.at[0], rs.at[0], {"z": zp})
    b = send(o2, o2, ss.at[1], rs.at[1], {"z": zm})
    a2 = send(o2, o2, ss.at[9], rs.at[9], {"z": zp})
    b2 = send(o1, o1, ss.at[10], rs.at[10], {"z": zm})
    d0 = send(own, own, ss.at[4], rs.at[4], other)
    yield
    a.wait_recv()
    lo = halves(zm, c)[0]
    e = send(lo, lo, ss.at[2], rs.at[2], {"z": zp})
    b.wait_recv()
    hi = halves(zp, c)[1]
    f = send(hi, hi, ss.at[3], rs.at[3], {"z": zm})
    yield
    a2.wait_recv()
    m = slot(zm, c)
    d1 = send(m, m, ss.at[5], rs.at[5], other)
    b2.wait_recv()
    p = slot(zp, c)
    d2 = send(p, p, ss.at[6], rs.at[6], other)
    yield
    e.wait_recv()
    fl = halves(zf, c)[0]
    d3 = send(fl, fl, ss.at[7], rs.at[7], other)
    f.wait_recv()
    fh = halves(zf, c)[1]
    d4 = send(fh, fh, ss.at[8], rs.at[8], other)
    yield
    for cp in (d0, d1, d2, d3, d4):
        cp.wait_recv()
    for cp in (a, b, a2, b2, e, f, d0, d1, d2, d3, d4):
        cp.wait_send()


def zc_direct(slot, ss, rs):
    z, c = lax.axis_index("z"), lax.axis_index("c")
    other = {"c": 1 - c}
    own = slot(z, c)
    far = [send(own, own, ss.at[k - 1], rs.at[k - 1], {"z": at("z", k)}) for k in (2, 1, 3)]
    over = [send(own, own, ss.at[3], rs.at[3], other)]
    yield
    for k, cp in zip((2, 1, 3), far):
        cp.wait_recv()
        got = slot(at("z", -k), c)
        over.append(send(got, got, ss.at[3 + k], rs.at[3 + k], other))
    yield
    for cp in over:
        cp.wait_recv()
    for cp in far + over:
        cp.wait_send()


def trade_flow(src_of, dst, ss, rs):
    y = lax.axis_index("y")
    loc = pltpu.make_async_copy(src_of(y), dst(y), ss.at[3])
    loc.start()
    sends = [
        send(src_of(at("y", k)), dst(y), ss.at[k - 1], rs.at[k - 1], {"y": at("y", k)}) for k in (2, 1, 3)
    ]
    yield
    loc.wait()
    for cp in sends:
        cp.wait_recv()
    for cp in sends:
        cp.wait_send()


def spread_flow(out, ss, rs):
    return zc_gather(
        lambda zz, cc: out.at[:, zz, cc],
        lambda zz, cc: (out.at[0:2, zz, cc], out.at[2:4, zz, cc]),
        ss,
        rs,
    )


def exchange_flow(src_of, out, ss, rs):
    z, c = lax.axis_index("z"), lax.axis_index("c")
    yield from trade_flow(src_of, lambda y: out.at[y, z, c], ss.at[pl.ds(11, 4)], rs.at[pl.ds(11, 4)])
    yield from spread_flow(out, ss, rs)


def torus_gather(a1, a2, block, ss, rs):
    i, j = lax.axis_index(a1), lax.axis_index(a2)
    all_of = []

    def go(ref, who):
        k = len(all_of)
        all_of.append(send(ref, ref, ss.at[k], rs.at[k], who))
        return all_of[-1]

    own = block(i, j)
    first = [(go(own, {a1: at(a1, k)}), k) for k in (2, 1, 3)]
    for k in (2, 1, 3):
        go(own, {a2: at(a2, k)})
    yield
    for cp, k in first:
        cp.wait_recv()
        got = block(at(a1, -k), j)
        for q in (2, 1, 3):
            go(got, {a2: at(a2, q)})
    yield
    for cp in all_of[3:]:
        cp.wait_recv()
    for cp in all_of:
        cp.wait_send()


def lanes(i, j):
    return pl.ds(pl.multiple_of((i * 4 + j) * 128, 128), 128)


def gather_columns(out, skip, ss, rs):
    def half(rows):
        return lambda x, y: out.at[rows, lanes(x, y)]

    one, two = half(slice(0, skip + 256)), half(slice(skip + 256, skip + 512))
    yield from together(
        [
            torus_gather("x", "y", one, ss.at[0], rs.at[0]),
            torus_gather("y", "x", lambda y, x: two(x, y), ss.at[1], rs.at[1]),
        ]
    )


def gather_rows(out, ss, rs, rows=slice(0, 32)):
    def half(cols):
        return lambda x, y: out.at[x, y, rows, cols]

    one, two = half(slice(0, 1024)), half(slice(1024, 2048))
    yield from together(
        [
            torus_gather("x", "y", one, ss.at[0], rs.at[0]),
            torus_gather("y", "x", lambda y, x: two(x, y), ss.at[1], rs.at[1]),
        ]
    )


GATHER_SEMS = [pltpu.SemaphoreType.DMA((2, 15)), pltpu.SemaphoreType.DMA((2, 15))]


def ring_scatter(axis, piece, ready, bufs, emit, ss, rs):
    me, p, m, fr = (at(axis, k) for k in (0, 1, -1, 2))
    ready(fr)
    a = send(piece(fr, 0), bufs.at[0], ss.at[0], rs.at[0], {axis: p})
    c = send(piece(fr, 1), bufs.at[1], ss.at[1], rs.at[1], {axis: m})
    ready(p)
    b = send(piece(p, 1), bufs.at[2], ss.at[2], rs.at[2], {axis: p})
    ready(m)
    d = send(piece(m, 0), bufs.at[3], ss.at[3], rs.at[3], {axis: m})
    ready(me)
    yield
    a.wait_recv()
    bufs[0] = bufs[0] + piece(p, 0)[...]
    e = send(bufs.at[0], bufs.at[4], ss.at[4], rs.at[4], {axis: p})
    c.wait_recv()
    bufs[1] = bufs[1] + piece(m, 1)[...]
    f = send(bufs.at[1], bufs.at[5], ss.at[5], rs.at[5], {axis: m})
    yield
    d.wait_recv()
    e.wait_recv()
    emit(0, piece(me, 0)[...].astype(f32) + bufs[3].astype(f32) + bufs[4].astype(f32))
    b.wait_recv()
    f.wait_recv()
    emit(1, piece(me, 1)[...].astype(f32) + bufs[2].astype(f32) + bufs[5].astype(f32))
    for cp in (a, b, c, d, e, f):
        cp.wait_send()


def plane_scatter(part, rows, res, big, mid, small, h, ss, rs):
    cols = slice(h * 1024, (h + 1) * 1024)
    a1, a2 = ("x", "y") if h == 0 else ("y", "x")
    i, j = lax.axis_index(a1), lax.axis_index(a2)

    def piece(k):
        return part.at[k, :, rows, cols] if h == 0 else part.at[:, k, rows, cols]

    one = [send(piece(at(a1, k)), big.at[k - 1], ss.at[k - 1], rs.at[k - 1], {a1: at(a1, k)}) for k in (2, 1, 3)]
    yield
    for cp in one:
        cp.wait_recv()
    total = piece(i)[...].astype(f32) + big[0].astype(f32)
    mid[...] = (total + (big[1].astype(f32) + big[2].astype(f32))).astype(bf16)
    two = [
        send(mid.at[at(a2, k)], small.at[k - 1], ss.at[k + 2], rs.at[k + 2], {a2: at(a2, k)}) for k in (2, 1, 3)
    ]
    yield
    for cp in two:
        cp.wait_recv()
    res[:, cols] = (mid[j].astype(f32) + small[0].astype(f32)) + (small[1].astype(f32) + small[2].astype(f32))
    for cp in one + two:
        cp.wait_send()


def plane_sum(part, acc, big, mid, small, ss, rs, rows=slice(0, 32)):
    yield from together(
        plane_scatter(part, rows, acc, big.at[h], mid.at[h], small.at[h], h, ss.at[h], rs.at[h]) for h in (0, 1)
    )


def scatter_buffers(rows):
    return [
        pltpu.VMEM((2, 3, 4, rows, 1024), bf16),
        pltpu.VMEM((2, 4, rows, 1024), bf16),
        pltpu.VMEM((2, 3, rows, 1024), bf16),
        pltpu.SemaphoreType.DMA((2, 6)),
        pltpu.SemaphoreType.DMA((2, 6)),
    ]


SCATTER_SCRATCH = scatter_buffers(32)
PLANS = {
    "fetch": "01201021020202",
    "attend": "1201001010010000000",
    "middle": "",
    "back_attend": "12000010200010200341",
    "finish": "1010101",
}
VM = pl.BlockSpec(memory_space=pltpu.VMEM)
SM = pl.BlockSpec(memory_space=pltpu.SMEM)
HB = pl.BlockSpec(memory_space=pl.ANY)


def shape(dims, kind=f32):
    return jax.ShapeDtypeStruct(dims, kind)


def remote_params(cid):
    return pltpu.CompilerParams(collective_id=cid, has_side_effects=True, vmem_limit_bytes=VLIM)


def columns(r):
    return lambda yy: r.at[:, :, lanes(lax.axis_index("x"), yy)]


def slots(r):
    return lambda yy: r.at[yy]


def pick_flow(src, every, index, out, skip, es, er, gs, gr):
    x, y = lax.axis_index("x"), lax.axis_index("y")
    z, c = lax.axis_index("z"), lax.axis_index("c")
    yield from trade_flow(columns(src), lambda i: every.at[i, z, c], es.at[pl.ds(7, 4)], er.at[pl.ds(7, 4)])
    yield from zc_direct(lambda zz, cc: every.at[:, zz, cc], es, er)
    here = lanes(x, y)

    def block(j):
        a = index[j]
        return every[a >> 4, (a >> 2) & 3, (a >> 1) & 1, a & 1]

    if skip:
        out[0:skip, here] = block(0)[STRETCH - skip : STRETCH]
    for j in range(8):
        out[skip + 64 * j : skip + 64 * (j + 1), here] = block(j + 1)
    yield from gather_columns(out, skip, gs, gr)


PICK_SCRATCH = [
    pltpu.VMEM((4, 4, 2, 2, 64, 128), bf16),
    pltpu.SemaphoreType.DMA((15,)),
    pltpu.SemaphoreType.DMA((15,)),
] + GATHER_SEMS


def spread_gain(line, row, out):
    for i in range(32):
        out[:, 64 * i : 64 * (i + 1)] = line[i // 8, i // 2 % 4, i % 2, row : row + 1, 0:64]


def fetch(order, tokens, pack, tiny, cid, plan=PLANS["fetch"]):
    def kernel(order, tok, pack, tiny, wa, line, index, gain1, gain2, xr, h1, xo, every, es, er, gs, gr, ss, rs):
        x, y, z, c = (lax.axis_index(a) for a in "xyzc")
        seg = z * 2 + c

        def find(a, found):
            return tuple(jnp.where(order[a] == jnp.maximum(seg * 8 - 1 + j, 0), a, f) for j, f in enumerate(found))

        for j, f in enumerate(lax.fori_loop(0, 64, find, tuple(jnp.int32(0) for _ in range(9)))):
            index[j] = f
        greet(peers(y=(1, 2, 3), z=(1, 2, 3), c=(1,), x=(1, 2, 3)))

        def rows():
            yield from pick_flow(tok, every, index, xo, HALO, es, er, gs, gr)
            for _ in lines:
                pass

            def norm(t, _):
                at_rows = pl.ds(pl.multiple_of(t * 16, 16), 16)
                v = xo[at_rows, :].astype(f32)
                r = lax.rsqrt(jnp.mean(v * v, axis=-1, keepdims=True) + EPS)
                h1[at_rows, :] = (v * r * gain1[...]).astype(bf16)
                return 0

            lax.fori_loop(0, ROWS // 16, norm, 0)
            xr[...] = xo[pl.ds(pl.multiple_of(HALO + 32 * (x * 4 + y), 16), 32), :]

        def small():
            se, re = ss.at[0], rs.at[0]
            yield from trade_flow(slots(tiny), lambda i: line.at[i, z, c], se.at[pl.ds(7, 4)], re.at[pl.ds(7, 4)])
            yield from zc_direct(lambda zz, cc: line.at[:, zz, cc], se, re)
            spread_gain(line, 1, gain1)
            spread_gain(line, 2, gain2)

        lines = small()
        run([rows(), lines, exchange_flow(slots(pack), wa, ss.at[1], rs.at[1])], plan)

    return pl.pallas_call(
        kernel,
        out_shape=[
            shape((4, 4, 2) + pack.shape[1:], bf16),
            shape((4, 4, 2) + tiny.shape[1:]),
            shape((16,), i32),
            shape((1, D)),
            shape((1, D)),
            shape((32, D), bf16),
            shape((ROWS, D), bf16),
        ],
        in_specs=[SM] + [VM] * 3,
        out_specs=[VM] * 2 + [SM] + [VM] * 4,
        scratch_shapes=[pltpu.VMEM((ROWS, D), bf16)]
        + PICK_SCRATCH
        + [pltpu.SemaphoreType.DMA((2, 15)), pltpu.SemaphoreType.DMA((2, 15))],
        compiler_params=remote_params(cid),
    )(order, tokens, pack, tiny)


def norm_back(v, gain, dh):
    r = lax.rsqrt(jnp.mean(v * v, axis=-1, keepdims=True) + EPS)
    t = gain * dh
    dv = r * t - v * (r * r * r) * jnp.mean(v * t, axis=-1, keepdims=True)
    return dv, jnp.sum(v * r * dh, axis=0, keepdims=True)


def middle(nv, wo, xrows, gain, wpart, dys, cid, plan=PLANS["middle"]):
    def kernel(nv, wo, xr, gain, wp, dys, m_out, dm_out, dg_out, da_out, dn_out, yp_out, sgu, sd, *refs):
        w, part, part2, h2, hid, dgu, ggu, gd, acc, dgs, refs = *refs[:10], refs[10:]
        sums = [refs[5 * i : 5 * i + 5] for i in range(4)]
        refs = refs[20:]
        gathers = [refs[2 * i : 2 * i + 2] for i in range(4)]
        ws, wr, ls = refs[8:11]
        fgu, fd = refs[11:15], refs[15:19]
        x, y, z, c = (lax.axis_index(a) for a in "xyzc")
        own = pltpu.make_async_copy(wp, w.at[:, z, c], ls)
        own.start()
        greet(peers(x=(1, 2, 3), y=(1, 2, 3), z=(1, 3), c=(1,)))

        def spread():
            own.wait()
            yield from spread_flow(w, ws, wr)

        weights = spread()

        def flat(ref, rows):
            v = ref[:, :, rows, :]
            return v.reshape(-1, v.shape[-1])

        def grads():
            def tiles(left, right, out):
                def tile(t, _):
                    cols = pl.ds(pl.multiple_of(t * 256, 256), 256)
                    v = dot(left[:, :, :, cols].reshape(SEG, 256), flat(right, slice(0, 32)), ((0,), (0,))).astype(bf16)
                    for k in range(4):
                        out[t // 2, lax.rem(t, 2) * 2 + k // 2, k % 2] = v[64 * k : 64 * (k + 1)]
                    return 0

                lax.fori_loop(0, 8, tile, 0)

            def first():
                tiles(h2, dgu, ggu)
                yield from sum_flow(ggu, sgu, *fgu)

            def second():
                tiles(dys, hid, gd)
                yield from sum_flow(gd, sd, *fd)

            yield from first()
            yield from second()

        def half(h):
            rows = slice(16 * h, 16 * h + 16)
            nrows = flat(nv, rows)
            for t in range(4):
                cols = slice(512 * t, 512 * (t + 1))
                part[:, :, rows, cols] = dot(nrows, wo[cols, :], ((1,), (1,))).astype(bf16).reshape(4, 4, 16, 512)
            yield from plane_sum(part, acc.at[h], *sums[h], rows)
            m = xr[rows, :].astype(f32) + acc[h]
            m_out[rows, :] = m
            r = lax.rsqrt(jnp.mean(m * m, axis=-1, keepdims=True) + EPS)
            h2[x, y, rows, :] = (m * r * gain[...]).astype(bf16)
            yield from gather_rows(h2, *gathers[h], rows)
            for _ in weights:
                pass
            wv = w[...].reshape(D, NB)
            both = dot(flat(h2, rows), wv[:, : 2 * FFP], ((1,), (0,)))
            ga, up = both[:, :FFP], both[:, FFP:]
            dhid = dot(flat(dys, rows), wv[:, 2 * FFP :], ((1,), (0,)))
            sg = jax.nn.sigmoid(ga)
            act = ga * sg
            hv = (act * up).astype(bf16)
            hid[:, :, rows, :] = hv.reshape(4, 4, 16, FFP)
            dga = (dhid * up * (sg * (1.0 + ga * (1.0 - sg)))).astype(bf16)
            dup = (dhid * act).astype(bf16)
            dgu[:, :, rows, :FFP] = dga.reshape(4, 4, 16, FFP)
            dgu[:, :, rows, FFP:] = dup.reshape(4, 4, 16, FFP)
            dv = jnp.concatenate([dga, dup], axis=1)
            for t in range(4):
                cols = slice(512 * t, 512 * (t + 1))
                part2[:, :, rows, cols] = (
                    dot(dv, wv[cols, : 2 * FFP], ((1,), (1,))).astype(bf16).reshape(4, 4, 16, 512)
                )

            def back():
                yield from plane_sum(part2, acc.at[2 + h], *sums[2 + h], rows)
                dvr, dgain = norm_back(m_out[rows, :], gain[...], acc[2 + h])
                dm = dys[x, y, rows, :].astype(f32) + dvr
                dm_out[rows, :] = dm
                dgs[h : h + 1, :] = dgain
                da_out[x, y, rows, :] = dm.astype(bf16)
                yield from gather_rows(da_out, *gathers[2 + h], rows)
                dn_out[:, :, rows, :] = dot(flat(da_out, rows), wo[...], ((1,), (0,))).reshape(4, 4, 16, DV)

            def result():
                yield
                for t in range(4):
                    cols = slice(512 * t, 512 * (t + 1))
                    yp_out[:, :, rows, cols] = (
                        dot(hv, wv[cols, 2 * FFP :], ((1,), (1,))).astype(bf16).reshape(4, 4, 16, 512)
                    )

            yield from together([back(), result()] + ([grads()] if h else []))

        run([half(0), half(1), weights], plan)
        dg_out[...] = dgs[0:1, :] + dgs[1:2, :]

    gu, gdown = (4, 4, 2, 64, 2 * FFP), (4, 4, 2, 64, FFP)
    return pl.pallas_call(
        kernel,
        out_shape=[
            shape((32, D)),
            shape((32, D)),
            shape((1, D)),
            shape((4, 4, 32, D), bf16),
            shape((4, 4, 32, DV)),
            shape((4, 4, 32, D), bf16),
            shape((4, 64, 2 * FFP), bf16),
            shape((4, 64, FFP), bf16),
        ],
        in_specs=[VM] * 6,
        out_specs=[VM] * 8,
        scratch_shapes=[
            pltpu.VMEM((4, 4, 2, 64, NB), bf16),
            pltpu.VMEM((4, 4, 32, D), bf16),
            pltpu.VMEM((4, 4, 32, D), bf16),
            pltpu.VMEM((4, 4, 32, D), bf16),
            pltpu.VMEM((4, 4, 32, FFP), bf16),
            pltpu.VMEM((4, 4, 32, 2 * FFP), bf16),
            pltpu.VMEM(gu, bf16),
            pltpu.VMEM(gdown, bf16),
            pltpu.VMEM((4, 16, D), f32),
            pltpu.VMEM((2, D), f32),
        ]
        + scatter_buffers(16) * 4
        + GATHER_SEMS * 4
        + [pltpu.SemaphoreType.DMA((11,)), pltpu.SemaphoreType.DMA((11,)), pltpu.SemaphoreType.DMA]
        + sum_scratch(gu[3:], bf16)
        + sum_scratch(gdown[3:], bf16),
        compiler_params=remote_params(cid),
    )(nv, wo, xrows, gain, wpart, dys)


def home_flow(src, dst, order, alls, cols, picks, s1, r1, s2, r2, s3, r3):
    x, y, z, c = (lax.axis_index(a) for a in "xyzc")
    sends = []
    cols[x, y] = src[:, pl.ds(pl.multiple_of((x * 4 + y) * 128, 128), 128)]
    t = 0
    for i in range(4):
        for j in range(4):
            if (i, j) == (0, 0):
                continue
            px, py = at("x", i), at("y", j)
            lane = pl.multiple_of((px * 4 + py) * 128, 128)
            sends.append(send(src.at[:, pl.ds(lane, 128)], cols.at[x, y], s1.at[t], r1.at[t], {"x": px, "y": py}))
            t += 1
    yield
    for cp in sends:
        cp.wait_recv()
    alls[z, c] = cols[...].reshape(8, 64, 128)
    yield from zc_direct(lambda zz, cc: alls.at[zz, cc], s2, r2)
    for j in range(4):
        for i in range(2):
            b = order[j * 16 + (z * 2 + c) * 2 + i]
            picks[j, 64 * i : 64 * (i + 1)] = alls[b >> 4, (b >> 3) & 1, b & 7]
    mine = pl.ds(pl.multiple_of(y * 128, 128), 128)
    last = [
        send(picks.at[at("y", j)], dst.at[:, mine], s3.at[j], r3.at[j], {"y": at("y", j)}) for j in (2, 1, 3)
    ]
    dst[:, mine] = picks[y]
    yield
    for cp in last:
        cp.wait_recv()
    for cp in sends + last:
        cp.wait_send()


HOME_SCRATCH = [
    pltpu.VMEM((4, 2, 8, 64, 128), bf16),
    pltpu.VMEM((4, 4, 32, 128), bf16),
    pltpu.VMEM((4, 128, 128), bf16),
    pltpu.SemaphoreType.DMA((15,)),
    pltpu.SemaphoreType.DMA((15,)),
    pltpu.SemaphoreType.DMA((11,)),
    pltpu.SemaphoreType.DMA((11,)),
    pltpu.SemaphoreType.DMA((4,)),
    pltpu.SemaphoreType.DMA((4,)),
]


def sum_flow(g, stage, core, bufs, ss, rs):
    c = lax.axis_index("c")
    d = send(g.at[:, :, 1 - c], core, ss.at[0], rs.at[0], {"c": 1 - c})
    yield
    d.wait_recv()

    def ready(i):
        for k in range(4):
            core[k, i] = core[k, i] + g[k, i, c]

    def emit(s, v):
        stage[2 * s : 2 * s + 2] = v.astype(stage.dtype)

    def piece(i, s):
        return core.at[2 * s : 2 * s + 2, i]

    yield from ring_scatter("z", piece, ready, bufs, emit, ss.at[pl.ds(1, 6)], rs.at[pl.ds(1, 6)])
    d.wait_send()


def sum_scratch(dims, kind):
    return [
        pltpu.VMEM((4, 4) + dims, kind),
        pltpu.VMEM((6, 2) + dims, kind),
        pltpu.SemaphoreType.DMA((7,)),
        pltpu.SemaphoreType.DMA((7,)),
    ]


TRADE_SEMS = [pltpu.SemaphoreType.DMA((4,)), pltpu.SemaphoreType.DMA((4,))]


def scatter_flow(g, out, stage, ts, tr, *sums):
    yield from sum_flow(g, stage, *sums)
    yield from trade_flow(slots(stage), lambda y: out.at[y], ts, tr)


def scatter_scratch(dims, kind):
    return [pltpu.VMEM((4,) + dims, kind)] + TRADE_SEMS + sum_scratch(dims, kind)


def finish(order, part, xrows, dm, gain, grad, tiny, cid, plan=PLANS["finish"]):
    nh, ns = len(HOME_SCRATCH), 7

    def kernel(order, part, xr, dm, gain, grad, tiny, dt_out, g_out, t_out, tot, acc, *rest):
        big, mid, small, ss, rs = rest[:5]
        home, rest = rest[5 : 5 + nh], rest[5 + nh :]
        ga, ti, rest = rest[:ns], rest[ns : 2 * ns], rest[2 * ns :]
        line, dx, xr4, xs, xq = rest
        x = lax.axis_index("x")
        greet(plane_peers() + peers(z=(1, 2, 3), c=(1,)))

        def small_grads():
            yield from scatter_flow(line, t_out, *ti)
            xr4[x] = (t_out[0] + t_out[1]) + (t_out[2] + t_out[3])
            sends = [send(xr4.at[x], xr4.at[x], xs.at[k], xq.at[k], {"x": at("x", k)}) for k in (2, 1, 3)]
            yield
            for cp in sends:
                cp.wait_recv()
            tot[...] = (xr4[0] + xr4[1]) + (xr4[2] + xr4[3])
            for cp in sends:
                cp.wait_send()

        def input_grads():
            yield from plane_sum(part, acc, big, mid, small, ss, rs)
            dv, dgain = norm_back(xr[...].astype(f32), gain[...], acc[...])
            dx[...] = (dm[...] + dv).astype(bf16)
            line[...] = tiny[...]
            for i in range(32):
                line[i // 8, i // 2 % 4, i % 2, 1:2, 0:64] = dgain[:, 64 * i : 64 * (i + 1)]
            yield from together([home_flow(dx, dt_out, order, *home), small_grads()])

        run([input_grads(), scatter_flow(grad, g_out, *ga)], plan)

    td, gd = tiny.shape[3:], grad.shape[3:]
    return pl.pallas_call(
        kernel,
        out_shape=[shape((128, 512), bf16), shape((4,) + gd, bf16), shape((4,) + td), shape(td)],
        in_specs=[SM] + [VM] * 6,
        out_specs=[VM] * 4,
        scratch_shapes=[pltpu.VMEM((32, D), f32)]
        + SCATTER_SCRATCH
        + HOME_SCRATCH
        + scatter_scratch(gd, bf16)
        + scatter_scratch(td, f32)
        + [
            pltpu.VMEM(tiny.shape, f32),
            pltpu.VMEM((32, D), bf16),
            pltpu.VMEM((4,) + td, f32),
            pltpu.SemaphoreType.DMA((4,)),
            pltpu.SemaphoreType.DMA((4,)),
        ],
        compiler_params=remote_params(cid),
    )(order, part, xrows, dm, gain, grad, tiny)


def dot(a, b, dims, prec=None):
    return lax.dot_general(a, b, (dims, ((), ())), preferred_element_type=f32, precision=prec)


def lo(a):
    return a.astype(bf16)


def mm(a, b):
    return dot(lo(a), lo(b), ((1,), (0,)))


def mmt(a, b):
    return dot(lo(a), lo(b), ((1,), (1,)))


def tmm(a, b):
    return dot(lo(a), lo(b), ((0,), (0,)))


def halves_of(a):
    h = a.astype(bf16)
    return h, (a - h.astype(f32)).astype(bf16)


def fine(a, b, dims=((1,), (0,))):
    ah, al = halves_of(a)
    bh, bl = halves_of(b)
    return dot(ah, bh, dims) + (dot(ah, bl, dims) + dot(al, bh, dims))


def tri_inverse(a, r, c):
    eye = jnp.where(r == c, 1.0, 0.0)
    n1 = jnp.where((r >> 3) == (c >> 3), -a, 0.0)
    n2 = fine(n1, n1)
    n4 = fine(n2, n2)
    t = eye + n1
    t = t + fine(t, n2)
    t = t + fine(t, n4)
    for level in (3, 4, 5, 6):
        off = ((r >> (level + 1)) == (c >> (level + 1))) & ((r >> level) != (c >> level))
        t = t - fine(t, fine(jnp.where(off, a, 0.0), t))
    return t


def iotas():
    return (
        lax.broadcasted_iota(i32, (CH, CH), 0),
        lax.broadcasted_iota(i32, (CH, CH), 1),
    )


def filtered(z, cw, mc, cols):
    total = z[HALO : HALO + SEG, cols] * cw[3:4, cols]
    for j in range(3):
        total = total + mc[:, j : j + 1] * cw[j : j + 1, cols] * z[HALO - 3 + j : HALO - 3 + j + SEG, cols]
    return total


def silu(v):
    return v * jax.nn.sigmoid(v)


QC, KC, VC = slice(0, 128), slice(128, 256), slice(256, 512)


def decay_of(cc, cr, mask):
    return jnp.exp(jnp.where(mask, cc - cr, 0.0)) * jnp.where(mask, 1.0, 0.0)


def prepare(z, ab, cw, sc, mc, mr, qkv, tm, wu, gb, cr, ti):
    r, c = iotas()
    for cols, scale in ((QC, DK**-0.5), (KC, 1.0)):
        s = silu(filtered(z, cw, mc, cols))
        qkv[:, cols] = (s * lax.rsqrt(jnp.sum(s * s, axis=-1, keepdims=True) + EPS) * scale).astype(bf16)
    qkv[:, VC] = silu(filtered(z, cw, mc, VC)).astype(bf16)
    low = jnp.where(r >= c, 1.0, 0.0)
    eye = jnp.where(r == c, 1.0, 0.0)
    lane = lax.broadcasted_iota(i32, (CH, 128), 1)
    transit = eye
    insert = jnp.zeros((DK, DV), f32)
    yield
    for n in range(NCH):
        rows = slice(n * CH, (n + 1) * CH)
        raw = ab[HALO + n * CH : HALO + (n + 1) * CH, :]
        beta = jax.nn.sigmoid(raw[:, 1:2])
        u = raw + sc[0:1, 1:2]
        g = -jnp.exp(sc[0:1, 0:1]) * (jnp.maximum(u, 0.0) + jnp.log1p(jnp.exp(-jnp.abs(u))))
        g = jnp.where(lane == 0, g, 0.0)
        cum = dot(low, g, ((1,), (0,)), HI)[:, 0:1]
        cumr = dot(g, low, ((0,), (1,)), HI)[0:8, :]
        gb[rows, :] = jnp.where(lane == 0, beta, cum)
        cr[:, rows] = cumr
        cumrow = cumr[0:1, :]
        last = cumr[0:1, CH - 1 : CH]
        m = mc[rows, :]
        carried, closing, begin, carry_last = m[:, 3:4], m[:, 4:5], m[:, 5:6], m[0:1, 6:7]
        same = begin == mr[0:1, rows]
        k = qkv[rows, KC]
        kf = k.astype(f32)
        v = qkv[rows, VC].astype(f32)
        a = beta * dot(k, k, ((1,), (1,))) * decay_of(cum, cumrow, same & (r > c))
        t = tri_inverse(a, r, c)
        tm[rows, :] = t
        lead = (beta * jnp.exp(cum) * carried) * kf
        w = fine(t, lead)
        uu = fine(t, beta * v)
        wu[rows, 0:DK] = w
        wu[rows, DK:] = uu
        tail = kf * (jnp.exp(last - cum) * closing)
        keep = jnp.exp(last) * carry_last
        hand = keep * eye - fine(tail, w, ((0,), (0,)))
        insert = fine(hand, insert) + fine(tail, uu, ((0,), (0,)))
        transit = fine(hand, transit)
        yield
    ti[:, 0:DK] = transit.astype(bf16)
    ti[:, DK:] = insert.astype(bf16)


def emit_outputs(seg, maps, qkv, wu, gb, cr, mc, mr, gp, hg, nout, oout, fout, sout):
    r, c = iotas()

    def fold(d, s):
        tr, ins = maps[d, :, 0:DK], maps[d, :, DK:].astype(f32)
        sh, sl = halves_of(s)
        new = dot(tr, sh, ((1,), (0,))) + dot(tr, sl, ((1,), (0,))) + ins
        return jnp.where(d < seg, new, s)

    s = lax.fori_loop(0, 7, fold, jnp.zeros((DK, DV), f32))
    for n in range(NCH):
        rows = slice(n * CH, (n + 1) * CH)
        m = mc[rows, :]
        carried, closing, begin, carry_last = m[:, 3:4], m[:, 4:5], m[:, 5:6], m[0:1, 6:7]
        cum = gb[rows, 1:2]
        cumrow = cr[0:1, rows]
        last = cr[0:1, n * CH + CH - 1 : n * CH + CH]
        same = begin == mr[0:1, rows]
        q, k = qkv[rows, QC], qkv[rows, KC]
        p = dot(q, k, ((1,), (1,))) * decay_of(cum, cumrow, same & (r >= c))
        fresh = wu[rows, DK:] - fine(wu[rows, 0:DK], s)
        qd = q.astype(f32) * (jnp.exp(cum) * carried)
        o = mm(qd, s) + mm(p, fresh)
        sout[n] = s
        fout[rows, :] = fresh
        oout[rows, :] = o
        x = gp[HALO + n * CH : HALO + (n + 1) * CH, :]
        rn = lax.rsqrt(jnp.mean(o * o, axis=-1, keepdims=True) + EPS)
        nout[rows, :] = (o * rn * hg[0:1, :] * silu(x)).astype(bf16)
        tail = k.astype(f32) * (jnp.exp(last - cum) * closing)
        s = (jnp.exp(last) * carry_last) * s + fine(tail, fresh, ((0,), (0,)))
        yield


def back_emit(dn, o, gp, hg, qkv, wu, gb, cr, mc, mr, do_out, dgp_out, dhg_out, e_out):
    r, c = iotas()
    dhg = jnp.zeros((1, DV), f32)
    e = jnp.zeros((DK, DV), f32)
    for n in reversed(range(NCH)):
        rows = slice(n * CH, (n + 1) * CH)
        ov, x, dnv = o[rows, :], gp[HALO + n * CH : HALO + (n + 1) * CH, :], dn[rows, :]
        rn = lax.rsqrt(jnp.mean(ov * ov, axis=-1, keepdims=True) + EPS)
        sg = jax.nn.sigmoid(x)
        act = x * sg
        h = hg[0:1, :]
        base = ov * rn
        dhg = dhg + jnp.sum(base * act * dnv, axis=0, keepdims=True)
        dgp_out[rows, :] = (dnv * base * h * (sg * (1.0 + x * (1.0 - sg)))).astype(bf16)
        t = dnv * h * act
        do = rn * t - base * (rn * rn) * jnp.mean(ov * t, axis=-1, keepdims=True)
        do_out[rows, :] = do
        m = mc[rows, :]
        carried, closing, begin, carry_last = m[:, 3:4], m[:, 4:5], m[:, 5:6], m[0:1, 6:7]
        cum = gb[rows, 1:2]
        cumrow = cr[0:1, rows]
        last = cr[0:1, n * CH + CH - 1 : n * CH + CH]
        same = begin == mr[0:1, rows]
        q, k = qkv[rows, QC], qkv[rows, KC]
        p = dot(q, k, ((1,), (1,))) * decay_of(cum, cumrow, same & (r >= c))
        qd = q.astype(f32) * (jnp.exp(cum) * carried)
        tail = k.astype(f32) * (jnp.exp(last - cum) * closing)
        df = tmm(p, do) + mm(tail, e)
        e = tmm(qd, do) + (jnp.exp(last) * carry_last) * e - tmm(wu[rows, 0:DK], df)
        yield
    dhg_out[...] = dhg
    e_out[...] = e.astype(bf16)


def back_delta(seg, maps, tails, do, fr, st, qkv, tm, wu, gb, cr, z, ab, cw, sc, mc, mr, dz, dab, dcw, dsc, dqkv):
    r, c = iotas()
    low = jnp.where(r >= c, 1.0, 0.0)
    ones = jnp.ones((CH, CH), f32)
    lane = lax.broadcasted_iota(i32, (CH, 128), 1)
    row = lax.broadcasted_iota(i32, (CH, 1), 0)

    def fold(i, e):
        d = 7 - i
        tr, own = maps[d, :, 0:DK], tails[d].astype(f32)
        eh, el = halves_of(e)
        new = dot(tr, eh, ((0,), (0,))) + dot(tr, el, ((0,), (0,))) + own
        return jnp.where(d > seg, new, e)

    e = lax.fori_loop(0, 7, fold, jnp.zeros((DK, DV), f32))
    acc_a = jnp.zeros((1, 128), f32)
    acc_d = jnp.zeros((1, 128), f32)
    for n in reversed(range(NCH)):
        rows = slice(n * CH, (n + 1) * CH)
        m = mc[rows, :]
        carried, closing, begin, carry_last = m[:, 3:4], m[:, 4:5], m[:, 5:6], m[0:1, 6:7]
        beta, cum = gb[rows, 0:1], gb[rows, 1:2]
        cumrow = cr[0:1, rows]
        last = cr[0:1, n * CH + CH - 1 : n * CH + CH]
        same = begin == mr[0:1, rows]
        q, k = qkv[rows, QC], qkv[rows, KC]
        qf, kf, vf = q.astype(f32), k.astype(f32), qkv[rows, VC].astype(f32)
        dec_i = decay_of(cum, cumrow, same & (r >= c))
        dec_s = jnp.where(r > c, dec_i, 0.0)
        p = dot(q, k, ((1,), (1,))) * dec_i
        kkd = dot(k, k, ((1,), (1,))) * dec_s
        ex = jnp.exp(cum) * carried
        tf = jnp.exp(last - cum) * closing
        keep = jnp.exp(last) * carry_last
        tail = kf * tf
        qd = qf * ex
        dov, fv, sv, tv = do[rows, :], fr[rows, :], st[n], tm[rows, :]
        w, u = wu[rows, 0:DK], wu[rows, DK:]
        df = tmm(p, dov) + mm(tail, e)
        dw = -mmt(df, sv)
        dtail = mmt(fv, e)
        dkeep = jnp.sum(jnp.sum(sv * e, axis=1, keepdims=True), axis=0, keepdims=True)
        dqd = mmt(dov, sv)
        dp = mmt(dov, fv)
        dlead = tmm(tv, dw)
        dbv = tmm(tv, df)
        da = -(mmt(dlead, w) + mmt(dbv, u))
        dakd = da * kkd
        dkk = da * beta * dec_s
        dqk = dp * dec_i
        mix = dakd * beta + dp * p
        dqkv[rows, QC] = mm(dqk, k) + dqd * ex
        dqkv[rows, KC] = (
            tmm(dqk, q) + mm(dkk, k) + tmm(dkk, k) + dlead * (beta * ex) + dtail * tf
        )
        dqkv[rows, VC] = beta * dbv
        lk = jnp.sum(dlead * kf, axis=1, keepdims=True) * ex
        dbeta = jnp.sum(dakd, axis=1, keepdims=True) + lk + jnp.sum(dbv * vf, axis=1, keepdims=True)
        tt = jnp.sum(dtail * tail, axis=1, keepdims=True)
        dcum = jnp.sum(mix, axis=1, keepdims=True) + jnp.sum(dqd * qd, axis=1, keepdims=True) + lk * beta - tt
        dcum = dcum + jnp.where(row == CH - 1, jnp.sum(tt, axis=0, keepdims=True) + dkeep * keep, 0.0)
        full = dcum - dot(mix, ones, ((0,), (0,)), HI)
        dg = dot(low, full, ((0,), (0,)), HI)
        raw = ab[HALO + n * CH : HALO + (n + 1) * CH, :]
        uu = raw + sc[0:1, 1:2]
        rate = -jnp.exp(sc[0:1, 0:1])
        sp = jnp.maximum(uu, 0.0) + jnp.log1p(jnp.exp(-jnp.abs(uu)))
        dal = dg * rate * jax.nn.sigmoid(uu)
        acc_a = acc_a + jnp.sum(dg * rate * sp, axis=0, keepdims=True)
        acc_d = acc_d + jnp.sum(dal, axis=0, keepdims=True)
        dab[rows, :] = jnp.where(
            lane == 0, dal, jnp.where(lane == 1, dbeta * beta * (1.0 - beta), 0.0)
        ).astype(bf16)
        e = tmm(qd, dov) + keep * e - tmm(w, df)
        yield
    dsc[0:1, :] = acc_a
    dsc[1:2, :] = acc_d
    dz[0:HALO, :] = jnp.zeros((HALO, 512), f32)
    for cols, scale in ((QC, DK**-0.5), (KC, 1.0), (VC, None)):
        y = filtered(z, cw, mc, cols)
        sg = jax.nn.sigmoid(y)
        ds = dqkv[:, cols]
        if scale is not None:
            s = y * sg
            rn = lax.rsqrt(jnp.sum(s * s, axis=-1, keepdims=True) + EPS)
            ds = scale * (rn * ds - s * (rn * rn * rn) * jnp.sum(s * ds, axis=-1, keepdims=True))
        dy = ds * (sg * (1.0 + y * (1.0 - sg)))
        dz[HALO : HALO + SEG, cols] = dy * cw[3:4, cols]
        dcw[3:4, cols] = jnp.sum(dy * z[HALO : HALO + SEG, cols], axis=0, keepdims=True)
        for j in range(3):
            part = mc[:, j : j + 1] * dy
            away = slice(HALO - 3 + j, HALO - 3 + j + SEG)
            dcw[j : j + 1, cols] = jnp.sum(part * z[away, cols], axis=0, keepdims=True)
            dz[away, cols] = dz[away, cols] + part * cw[j : j + 1, cols]
        yield


def map_gather(own, out, ss, rs):
    z, c = lax.axis_index("z"), lax.axis_index("c")
    out[z, c] = own[...]
    yield from zc_direct(lambda zz, cc: out.at[zz, cc], ss, rs)


class Maps:
    def __init__(self, ref):
        self.ref = ref

    def __getitem__(self, key):
        key = key if isinstance(key, tuple) else (key,)
        return self.ref[(key[0] // 2, key[0] % 2) + key[1:]]


def masks(lens, mc, mr):
    base = (lax.axis_index("z") * 2 + lax.axis_index("c")) * SEG
    firsts = [jnp.int32(0)]
    for k in range(3):
        firsts.append(firsts[k] + lens[k])

    def begin_of(pos):
        b = jnp.zeros_like(pos)
        for k in range(1, 4):
            b = jnp.where((pos >= firsts[k]) & (pos < firsts[k] + lens[k]), firsts[k], b)
        return b

    lane = lax.broadcasted_iota(i32, (CH, 128), 1)
    for n in range(NCH):
        first = base + n * CH
        pos = first + lax.broadcasted_iota(i32, (CH, 128), 0)
        b = begin_of(pos)
        last = begin_of(jnp.full((CH, 128), first + CH - 1, i32))

        def one(flag):
            return jnp.where(flag, 1.0, 0.0)

        late = jnp.where(lane == 3, one(b < first), jnp.where(lane == 4, one(b == last), one(last < first)))
        flags = jnp.where(lane < 3, one(pos - 3 + lane >= b), late)
        mc[n * CH : (n + 1) * CH, :] = jnp.where(lane == 5, b.astype(f32), flags)
        mr[:, n * CH : (n + 1) * CH] = begin_of(first + lax.broadcasted_iota(i32, (8, CH), 1)).astype(f32)


def attend(proj, cw, hg, lens, a_log, dt_bias, index, cotangent, pack, cid, plan=PLANS["attend"]):
    npk = len(PICK_SCRATCH)

    def kernel(proj, cw, hg, lens, al, dt, index, cot, pack, wp, dyo, qkv, tm, wu, gb, cr, maps, nout, oout, fout, sout, mc, mr, sc, *refs):
        every, es, er, gs, gr = refs[:npk]
        ti, ms, mq, ts, tr = refs[npk:]
        x, y, z, c = (lax.axis_index(a) for a in "xyzc")
        zq, gp, ab = proj.at[:, 0:512], proj.at[:, 512:768], proj.at[:, 768:896]
        greet(peers(y=(1, 2, 3), z=(1, 2, 3), c=(1,), x=(1, 2, 3)))

        def mixer():
            masks(lens, mc, mr)
            sc[0:8, :] = jnp.where(lax.broadcasted_iota(i32, (8, 128), 1) == 0, al[y], dt[y])
            yield from prepare(zq, ab, cw, sc, mc, mr, qkv, tm, wu, gb, cr, ti)
            yield from map_gather(ti, maps, ms, mq)
            yield from emit_outputs(z * 2 + c, Maps(maps), qkv, wu, gb, cr, mc, mr, gp, hg, nout, oout, fout, sout)

        run(
            [mixer(), pick_flow(cot, every, index, dyo, 0, es, er, gs, gr), trade_flow(slots(pack), lambda i: wp.at[i], ts, tr)],
            plan,
        )

    return pl.pallas_call(
        kernel,
        out_shape=[
            shape(pack.shape, bf16),
            shape((SEG, D), bf16),
            shape((SEG, 512), bf16),
            shape((SEG, CH)),
            shape((SEG, DK + DV)),
            shape((SEG, 128)),
            shape((8, SEG)),
            shape((4, 2, DK, DK + DV), bf16),
            shape((SEG, DV), bf16),
            shape((SEG, DV)),
            shape((SEG, DV)),
            shape((NCH, DK, DV)),
            shape((SEG, 128)),
            shape((8, SEG)),
            shape((8, 128)),
        ],
        in_specs=[VM] * 3 + [SM] * 4 + [VM] * 2,
        out_specs=[VM] * 15,
        scratch_shapes=PICK_SCRATCH
        + [
            pltpu.VMEM((DK, DK + DV), bf16),
            pltpu.SemaphoreType.DMA((11,)),
            pltpu.SemaphoreType.DMA((11,)),
        ]
        + TRADE_SEMS,
        compiler_params=remote_params(cid),
    )(proj, cw, hg, lens, a_log, dt_bias, index, cotangent, pack)


def back_attend(dn, o, proj, hg, qkv, tm, wu, gb, cr, mc, mr, maps, fr, st, cw, sc, m, order, ypart, stages, grad, cid, plan=PLANS["back_attend"]):
    nh, n = len(HOME_SCRATCH), len(stages)

    def kernel(dn, o, proj, hg, qkv, tm, wu, gb, cr, mc, mr, maps, fr, st, cw, sc, m, order, ypart, *refs):
        staged, grad, refs = refs[:n], refs[n], refs[n + 1 :]
        y_out, dproj, dhg, dcw, dsc, g_out = refs[:6]
        s_out, refs = refs[6 : 6 + n], refs[6 + n :]
        do, dgp, e, tails, dz, dab, dqkv, edge, ms, mq, ds, dq, acc, yrow = refs[:14]
        big, mid, small, ss, rs = refs[14:19]
        home, refs = refs[19 : 19 + nh], refs[19 + nh :]
        ga, trades = refs[:7], refs[7:]
        zq, gp, ab = proj.at[:, 0:512], proj.at[:, 512:768], proj.at[:, 768:896]
        seg = lax.axis_index("z") * 2 + lax.axis_index("c")
        greet(plane_peers() + segment_peers())

        def mixer():
            yield from back_emit(dn, o, gp, hg, qkv, wu, gb, cr, mc, mr, do, dgp, dhg, e)
            yield from map_gather(e, tails, ms, mq)
            yield from back_delta(
                seg, Maps(maps), Maps(tails), do, fr, st, qkv, tm, wu, gb, cr, zq, ab, cw, sc, mc, mr, dz, dab, dcw, dsc, dqkv
            )
            before = lax.rem(seg + 7, 8)
            cp = send(dz.at[0:HALO], edge, ds, dq, {"z": before // 2, "c": lax.rem(before, 2)})
            dproj[0 : SEG - HALO, 0:512] = dz[HALO:SEG].astype(bf16)
            dproj[:, 512:768] = dgp[...]
            dproj[:, 768:896] = dab[...]
            yield
            cp.wait_recv()
            dproj[SEG - HALO : SEG, 0:512] = (dz[SEG:ROWS] + jnp.where(seg < 7, edge[...], 0.0)).astype(bf16)
            cp.wait_send()

        def result():
            yield from plane_sum(ypart, acc, big, mid, small, ss, rs)
            yrow[...] = (m[...] + acc[...]).astype(bf16)
            yield from home_flow(yrow, y_out, order, *home)

        def trade(i):
            return trade_flow(slots(staged[i]), lambda y: s_out[i].at[y], trades[2 * i], trades[2 * i + 1])

        run(
            [mixer(), result(), scatter_flow(grad, g_out, *ga)] + [trade(i) for i in range(n)],
            plan,
        )

    gd = grad.shape[3:]
    return pl.pallas_call(
        kernel,
        out_shape=[
            shape((128, 512), bf16),
            shape((SEG, 896), bf16),
            shape((1, DV)),
            shape((4, 512)),
            shape((2, 128)),
            shape((4,) + gd, bf16),
        ]
        + [shape(t.shape, bf16) for t in stages],
        in_specs=[VM] * 17 + [SM] + [VM] * (2 + n),
        out_specs=[VM] * (6 + n),
        scratch_shapes=[
            pltpu.VMEM((SEG, DV), f32),
            pltpu.VMEM((SEG, DV), bf16),
            pltpu.VMEM((DK, DV), bf16),
            pltpu.VMEM((4, 2, DK, DV), bf16),
            pltpu.VMEM((ROWS, 512), f32),
            pltpu.VMEM((SEG, 128), bf16),
            pltpu.VMEM((SEG, 512), f32),
            pltpu.VMEM((HALO, 512), f32),
            pltpu.SemaphoreType.DMA((11,)),
            pltpu.SemaphoreType.DMA((11,)),
            pltpu.SemaphoreType.DMA,
            pltpu.SemaphoreType.DMA,
            pltpu.VMEM((32, D), f32),
            pltpu.VMEM((32, D), bf16),
        ]
        + SCATTER_SCRATCH
        + HOME_SCRATCH
        + scatter_scratch(gd, bf16)
        + TRADE_SEMS * n,
        compiler_params=remote_params(cid),
    )(dn, o, proj, hg, qkv, tm, wu, gb, cr, mc, mr, maps, fr, st, cw, sc, m, order, ypart, *stages, grad)


def wide(a):
    a = jnp.pad(a.astype(bf16), ((0, 0), (0, 4 * FFP - a.shape[1])))
    return a.reshape(a.shape[0], 4, FFP).swapaxes(0, 1)


def body(
    tokens,
    cotangent,
    seq_lengths,
    stretch_order,
    attn_gain,
    w_query,
    w_key,
    w_value,
    w_alpha,
    w_beta,
    conv_query,
    conv_key,
    conv_value,
    a_log,
    dt_bias,
    head_gain,
    w_outgate,
    w_output,
    mlp_gain,
    w_gate,
    w_up,
    w_down,
):
    ff = w_gate.shape[1]

    def by_head(a):
        return a.astype(bf16).swapaxes(0, 1)

    pair = jnp.stack([w_alpha, w_beta], axis=-1).astype(bf16)
    pack_a = jnp.concatenate(
        [
            by_head(w_query),
            by_head(w_key),
            by_head(w_value),
            by_head(w_outgate),
            jnp.pad(pair.swapaxes(0, 1), ((0, 0), (0, 0), (0, 126))),
            w_output.astype(bf16).swapaxes(1, 2),
        ],
        axis=2,
    )
    pack_b = jnp.concatenate([wide(w_gate), wide(w_up), wide(w_down.T)], axis=2)

    def taps(a):
        return a.swapaxes(0, 1).reshape(4, -1)

    def each(a):
        return jnp.broadcast_to(a[None], (4,) + a.shape)

    line = jnp.concatenate([taps(conv_query), taps(conv_key), taps(conv_value), each(head_gain)], axis=1)
    line = jnp.pad(line, ((0, 0), (0, 128 - line.shape[1])))
    gains = jnp.pad(jnp.stack([attn_gain, mlp_gain]), ((0, 5), (0, 64)))
    tiny = jnp.concatenate([line[:, None], each(gains)], axis=1).astype(bf16).astype(f32)
    wa, lines, index, gain1, gain2, xrows, h1 = fetch(stretch_order, tokens.reshape(2, STRETCH, D), pack_a, tiny, 1)
    wa = wa.reshape(D, NA)
    lines = lines[:, :, :, 0].reshape(32, 128)

    def filters(a):
        return a.reshape(32, 4, -1).swapaxes(0, 1).reshape(4, -1)

    cw = jnp.concatenate([filters(lines[:, 0:16]), filters(lines[:, 16:32]), filters(lines[:, 32:64])], axis=1)
    hg = lines[:, 64:72].reshape(1, DV)

    proj = jnp.dot(h1, wa[:, :896], preferred_element_type=f32)
    wpart, dys, qkv, tm, wu, gb, cr, maps, nv, ov, fr, st, mc, mr, sc = attend(
        proj, cw, hg, seq_lengths, a_log, dt_bias, index, cotangent.reshape(2, STRETCH, D), pack_b, 2
    )
    wo = wa[:, 896:]
    m, dm, dgain2, da, dn, ypart, sgu, sd = middle(
        nv.reshape(4, 4, 32, DV), wo, xrows, gain2, wpart, dys.reshape(4, 4, 32, D), 3
    )
    da, dn = da.reshape(SEG, D), dn.reshape(SEG, DV)

    grad_o = dot(da, nv, ((0,), (0,))).astype(bf16).reshape(4, 4, 2, 64, -1)
    out, dproj, dhg, dcw, dsc, ro, rgu, rd = back_attend(
        dn, ov, proj, hg, qkv, tm, wu, gb, cr, mc, mr, maps, fr, st, cw, sc, m, stretch_order, ypart, (sgu, sd), grad_o, 5
    )
    dh1 = dot(dproj, wa[:, :896], ((1,), (1,))).astype(bf16).reshape(4, 4, 32, D)
    h1o = h1[HALO:]
    grad_a = dot(h1o, dproj, ((0,), (0,))).astype(bf16).reshape(4, 4, 2, 64, -1)
    def unfilter(a):
        return a.reshape(4, 32, -1).swapaxes(0, 1).reshape(32, -1)

    head = jnp.broadcast_to(dsc[:, 0][None], (32, 2))
    back_line = jnp.concatenate(
        [unfilter(dcw[:, QC]), unfilter(dcw[:, KC]), unfilter(dcw[:, VC]), dhg.reshape(32, 8), head], axis=1
    )
    back_line = jnp.pad(back_line, ((0, 0), (0, 128 - back_line.shape[1])))
    gain_line = jnp.pad(dgain2.reshape(32, 64), ((0, 0), (0, 64)))
    blank = jnp.zeros_like(back_line)
    tiny_back = jnp.stack([back_line, blank, gain_line] + [blank] * 5, axis=1).reshape(4, 4, 2, 8, 128)
    dtok, ra, rt, total = finish(
        stretch_order, dh1, xrows, dm, gain1, grad_a, tiny_back, 6
    )
    ra = ra.astype(f32)
    rgu, rd, ro = rgu.astype(f32), rd.astype(f32), ro.astype(f32)
    rt = rt[:, 0]

    def heads(a):
        return a.swapaxes(0, 1)

    def untaps(a):
        return a.reshape(4, 4, -1).swapaxes(0, 1)

    def narrow(a):
        return a.swapaxes(0, 1).reshape(a.shape[1], -1)[:, :ff]

    return (
        out,
        dtok,
        total[1, :64],
        heads(ra[:, :, 0:128]),
        heads(ra[:, :, 128:256]),
        heads(ra[:, :, 256:512]),
        heads(ra[:, :, 768]),
        heads(ra[:, :, 769]),
        untaps(rt[:, 0:16]),
        untaps(rt[:, 16:32]),
        untaps(rt[:, 32:64]),
        rt[:, 72],
        rt[:, 73],
        total[0, 64:72],
        heads(ra[:, :, 512:768]),
        ro.swapaxes(1, 2),
        total[2, :64],
        narrow(rgu[:, :, :FFP]),
        narrow(rgu[:, :, FFP:]),
        narrow(rd).T,
    )


def solution(mesh):
    torus = Mesh(mesh.devices.reshape(4, 4, 2, 4), ("y", "z", "c", "x"))
    dp, tp = ("y", "z", "c"), "x"
    in_specs = (
        P(dp, None),
        P(dp, None),
        P(),
        P(),
        P(dp),
        P(dp, tp, None),
        P(dp, tp, None),
        P(dp, tp, None),
        P(dp, tp),
        P(dp, tp),
        P(None, tp, dp),
        P(None, tp, dp),
        P(None, tp, dp),
        P(tp),
        P(tp),
        P(dp),
        P(dp, tp, None),
        P(tp, None, dp),
        P(dp),
        P(dp, tp),
        P(dp, tp),
        P(tp, dp),
    )
    out_specs = (
        P(dp, tp),
        P(dp, tp),
        P(dp),
        P(dp, tp, None),
        P(dp, tp, None),
        P(dp, tp, None),
        P(dp, tp),
        P(dp, tp),
        P(None, tp, dp),
        P(None, tp, dp),
        P(None, tp, dp),
        P(tp),
        P(tp),
        P(dp),
        P(dp, tp, None),
        P(tp, None, dp),
        P(dp),
        P(dp, tp),
        P(dp, tp),
        P(tp, dp),
    )
    return jax.shard_map(body, mesh=torus, in_specs=in_specs, out_specs=out_specs, check_vma=False)
```

```python
import functools
import math

import jax
import jax.numpy as jnp
from jax import lax
from jax.experimental import pallas as pl
from jax.experimental.pallas import tpu as pltpu
from jax.sharding import Mesh
from jax.sharding import PartitionSpec as P

MESH = pl.DeviceIdType.MESH
bf16, f32, i32 = jnp.bfloat16, jnp.float32, jnp.int32
HI = lax.Precision.HIGHEST
EPS = 1e-6
STRETCH = 64
D, DK, DV, FFP, HALO = 2048, 128, 256, 384, 16
SEG = 512
ROWS = SEG + HALO
CH = 128
NCH = SEG // CH
NA, NB = 1152, 1152
VLIM = 58 * 1024 * 1024


def at(axis, k):
    n = lax.axis_size(axis)
    return lax.rem(lax.axis_index(axis) + k + n, n)


def greet(peers):
    b = pltpu.get_barrier_semaphore()
    for p in peers:
        pl.semaphore_signal(b, inc=1, device_id=p, device_id_type=MESH)
    pl.semaphore_wait(b, len(peers))


def send(src, dst, ss, rs, who):
    cp = pltpu.make_async_remote_copy(
        src_ref=src, dst_ref=dst, send_sem=ss, recv_sem=rs, device_id=who, device_id_type=MESH
    )
    cp.start()
    return cp


def run(flows, plan=""):
    flows = list(flows)
    for i in plan:
        next(flows[int(i)], None)
    for _ in together(flows):
        pass


def together(flows):
    flows = list(flows)
    while flows:
        left = []
        for f in flows:
            try:
                next(f)
                left.append(f)
            except StopIteration:
                pass
        flows = left
        if flows:
            yield


def segment_peers():
    z, c = lax.axis_index("z"), lax.axis_index("c")
    out = []
    for k in range(4):
        for d in range(2):
            if (k, d) != (0, 0):
                out.append({"z": at("z", k), "c": lax.rem(c + d, 2)})
    return out


def plane_peers():
    return [{"x": at("x", i), "y": at("y", j)} for i in range(4) for j in range(4) if (i, j) != (0, 0)]


def peers(**steps):
    return [{ax: at(ax, k)} for ax, ks in steps.items() for k in ks]


def zc_gather(slot, halves, ss, rs):
    z, c = lax.axis_index("z"), lax.axis_index("c")
    other = {"c": 1 - c}
    zp, zm, zf = at("z", 1), at("z", -1), at("z", 2)
    own, (o1, o2) = slot(z, c), halves(z, c)
    a = send(o1, o1, ss.at[0], rs.at[0], {"z": zp})
    b = send(o2, o2, ss.at[1], rs.at[1], {"z": zm})
    a2 = send(o2, o2, ss.at[9], rs.at[9], {"z": zp})
    b2 = send(o1, o1, ss.at[10], rs.at[10], {"z": zm})
    d0 = send(own, own, ss.at[4], rs.at[4], other)
    yield
    a.wait_recv()
    lo = halves(zm, c)[0]
    e = send(lo, lo, ss.at[2], rs.at[2], {"z": zp})
    b.wait_recv()
    hi = halves(zp, c)[1]
    f = send(hi, hi, ss.at[3], rs.at[3], {"z": zm})
    yield
    a2.wait_recv()
    m = slot(zm, c)
    d1 = send(m, m, ss.at[5], rs.at[5], other)
    b2.wait_recv()
    p = slot(zp, c)
    d2 = send(p, p, ss.at[6], rs.at[6], other)
    yield
    e.wait_recv()
    fl = halves(zf, c)[0]
    d3 = send(fl, fl, ss.at[7], rs.at[7], other)
    f.wait_recv()
    fh = halves(zf, c)[1]
    d4 = send(fh, fh, ss.at[8], rs.at[8], other)
    yield
    for cp in (d0, d1, d2, d3, d4):
        cp.wait_recv()
    for cp in (a, b, a2, b2, e, f, d0, d1, d2, d3, d4):
        cp.wait_send()


def zc_direct(slot, ss, rs):
    z, c = lax.axis_index("z"), lax.axis_index("c")
    other = {"c": 1 - c}
    own = slot(z, c)
    far = [send(own, own, ss.at[k - 1], rs.at[k - 1], {"z": at("z", k)}) for k in (2, 1, 3)]
    over = [send(own, own, ss.at[3], rs.at[3], other)]
    yield
    for k, cp in zip((2, 1, 3), far):
        cp.wait_recv()
        got = slot(at("z", -k), c)
        over.append(send(got, got, ss.at[3 + k], rs.at[3 + k], other))
    yield
    for cp in over:
        cp.wait_recv()
    for cp in far + over:
        cp.wait_send()


def trade_flow(src_of, dst, ss, rs):
    y = lax.axis_index("y")
    loc = pltpu.make_async_copy(src_of(y), dst(y), ss.at[3])
    loc.start()
    sends = [
        send(src_of(at("y", k)), dst(y), ss.at[k - 1], rs.at[k - 1], {"y": at("y", k)}) for k in (2, 1, 3)
    ]
    yield
    loc.wait()
    for cp in sends:
        cp.wait_recv()
    for cp in sends:
        cp.wait_send()


def spread_flow(out, ss, rs):
    return zc_gather(
        lambda zz, cc: out.at[:, zz, cc],
        lambda zz, cc: (out.at[0:2, zz, cc], out.at[2:4, zz, cc]),
        ss,
        rs,
    )


def exchange_flow(src_of, out, ss, rs):
    z, c = lax.axis_index("z"), lax.axis_index("c")
    yield from trade_flow(src_of, lambda y: out.at[y, z, c], ss.at[pl.ds(11, 4)], rs.at[pl.ds(11, 4)])
    yield from spread_flow(out, ss, rs)


def torus_gather(a1, a2, block, ss, rs):
    i, j = lax.axis_index(a1), lax.axis_index(a2)
    all_of = []

    def go(ref, who):
        k = len(all_of)
        all_of.append(send(ref, ref, ss.at[k], rs.at[k], who))
        return all_of[-1]

    own = block(i, j)
    first = [(go(own, {a1: at(a1, k)}), k) for k in (2, 1, 3)]
    for k in (2, 1, 3):
        go(own, {a2: at(a2, k)})
    yield
    for cp, k in first:
        cp.wait_recv()
        got = block(at(a1, -k), j)
        for q in (2, 1, 3):
            go(got, {a2: at(a2, q)})
    yield
    for cp in all_of[3:]:
        cp.wait_recv()
    for cp in all_of:
        cp.wait_send()


def lanes(i, j):
    return pl.ds(pl.multiple_of((i * 4 + j) * 128, 128), 128)


def gather_columns(out, skip, ss, rs):
    def half(rows):
        return lambda x, y: out.at[rows, lanes(x, y)]

    one, two = half(slice(0, skip + 256)), half(slice(skip + 256, skip + 512))
    yield from together(
        [
            torus_gather("x", "y", one, ss.at[0], rs.at[0]),
            torus_gather("y", "x", lambda y, x: two(x, y), ss.at[1], rs.at[1]),
        ]
    )


def gather_rows(out, ss, rs, rows=slice(0, 32)):
    def half(cols):
        return lambda x, y: out.at[x, y, rows, cols]

    one, two = half(slice(0, 1024)), half(slice(1024, 2048))
    yield from together(
        [
            torus_gather("x", "y", one, ss.at[0], rs.at[0]),
            torus_gather("y", "x", lambda y, x: two(x, y), ss.at[1], rs.at[1]),
        ]
    )


GATHER_SEMS = [pltpu.SemaphoreType.DMA((2, 15)), pltpu.SemaphoreType.DMA((2, 15))]


def ring_scatter(axis, piece, ready, bufs, emit, ss, rs):
    me, p, m, fr = (at(axis, k) for k in (0, 1, -1, 2))
    ready(fr)
    a = send(piece(fr, 0), bufs.at[0], ss.at[0], rs.at[0], {axis: p})
    c = send(piece(fr, 1), bufs.at[1], ss.at[1], rs.at[1], {axis: m})
    ready(p)
    b = send(piece(p, 1), bufs.at[2], ss.at[2], rs.at[2], {axis: p})
    ready(m)
    d = send(piece(m, 0), bufs.at[3], ss.at[3], rs.at[3], {axis: m})
    ready(me)
    yield
    a.wait_recv()
    bufs[0] = bufs[0] + piece(p, 0)[...]
    e = send(bufs.at[0], bufs.at[4], ss.at[4], rs.at[4], {axis: p})
    c.wait_recv()
    bufs[1] = bufs[1] + piece(m, 1)[...]
    f = send(bufs.at[1], bufs.at[5], ss.at[5], rs.at[5], {axis: m})
    yield
    d.wait_recv()
    e.wait_recv()
    emit(0, piece(me, 0)[...].astype(f32) + bufs[3].astype(f32) + bufs[4].astype(f32))
    b.wait_recv()
    f.wait_recv()
    emit(1, piece(me, 1)[...].astype(f32) + bufs[2].astype(f32) + bufs[5].astype(f32))
    for cp in (a, b, c, d, e, f):
        cp.wait_send()


def plane_scatter(part, rows, res, big, mid, small, h, ss, rs):
    cols = slice(h * 1024, (h + 1) * 1024)
    a1, a2 = ("x", "y") if h == 0 else ("y", "x")
    i, j = lax.axis_index(a1), lax.axis_index(a2)

    def piece(k):
        return part.at[k, :, rows, cols] if h == 0 else part.at[:, k, rows, cols]

    one = [send(piece(at(a1, k)), big.at[k - 1], ss.at[k - 1], rs.at[k - 1], {a1: at(a1, k)}) for k in (2, 1, 3)]
    yield
    for cp in one:
        cp.wait_recv()
    total = piece(i)[...].astype(f32) + big[0].astype(f32)
    mid[...] = (total + (big[1].astype(f32) + big[2].astype(f32))).astype(bf16)
    two = [
        send(mid.at[at(a2, k)], small.at[k - 1], ss.at[k + 2], rs.at[k + 2], {a2: at(a2, k)}) for k in (2, 1, 3)
    ]
    yield
    for cp in two:
        cp.wait_recv()
    res[:, cols] = (mid[j].astype(f32) + small[0].astype(f32)) + (small[1].astype(f32) + small[2].astype(f32))
    for cp in one + two:
        cp.wait_send()


def plane_sum(part, acc, big, mid, small, ss, rs, rows=slice(0, 32)):
    yield from together(
        plane_scatter(part, rows, acc, big.at[h], mid.at[h], small.at[h], h, ss.at[h], rs.at[h]) for h in (0, 1)
    )


def scatter_buffers(rows):
    return [
        pltpu.VMEM((2, 3, 4, rows, 1024), bf16),
        pltpu.VMEM((2, 4, rows, 1024), bf16),
        pltpu.VMEM((2, 3, rows, 1024), bf16),
        pltpu.SemaphoreType.DMA((2, 6)),
        pltpu.SemaphoreType.DMA((2, 6)),
    ]


SCATTER_SCRATCH = scatter_buffers(32)
PLANS = {
    "fetch": "01201021020202",
    "attend": "1201001010010000000",
    "middle": "",
    "back_attend": "1340000020010020012",
    "finish": "011010",
}
VM = pl.BlockSpec(memory_space=pltpu.VMEM)
SM = pl.BlockSpec(memory_space=pltpu.SMEM)
HB = pl.BlockSpec(memory_space=pl.ANY)


def shape(dims, kind=f32):
    return jax.ShapeDtypeStruct(dims, kind)


def remote_params(cid):
    return pltpu.CompilerParams(collective_id=cid, has_side_effects=True, vmem_limit_bytes=VLIM)


def columns(r):
    return lambda yy: r.at[:, :, lanes(lax.axis_index("x"), yy)]


def slots(r):
    return lambda yy: r.at[yy]


def pick_flow(src, every, index, out, skip, es, er, gs, gr):
    x, y = lax.axis_index("x"), lax.axis_index("y")
    z, c = lax.axis_index("z"), lax.axis_index("c")
    yield from trade_flow(columns(src), lambda i: every.at[i, z, c], es.at[pl.ds(7, 4)], er.at[pl.ds(7, 4)])
    yield from zc_direct(lambda zz, cc: every.at[:, zz, cc], es, er)
    here = lanes(x, y)

    def block(j):
        a = index[j]
        return every[a >> 4, (a >> 2) & 3, (a >> 1) & 1, a & 1]

    if skip:
        out[0:skip, here] = block(0)[STRETCH - skip : STRETCH]
    for j in range(8):
        out[skip + 64 * j : skip + 64 * (j + 1), here] = block(j + 1)
    yield from gather_columns(out, skip, gs, gr)


PICK_SCRATCH = [
    pltpu.VMEM((4, 4, 2, 2, 64, 128), bf16),
    pltpu.SemaphoreType.DMA((15,)),
    pltpu.SemaphoreType.DMA((15,)),
] + GATHER_SEMS


def spread_gain(line, row, out):
    for i in range(32):
        out[:, 64 * i : 64 * (i + 1)] = line[i // 8, i // 2 % 4, i % 2, row : row + 1, 0:64]


def fetch(order, tokens, weights, tiny, cid, plan=PLANS["fetch"]):
    def kernel(order, tok, wq, wk, wv, wg, wal, wbe, wou, tiny, wa, line, index, gain1, gain2, xr, h1, pack, xo, every, es, er, gs, gr, ss, rs):
        x, y, z, c = (lax.axis_index(a) for a in "xyzc")
        seg = z * 2 + c

        def find(a, found):
            return tuple(jnp.where(order[a] == jnp.maximum(seg * 8 - 1 + j, 0), a, f) for j, f in enumerate(found))

        diag = lax.broadcasted_iota(i32, (64, 64), 0) == lax.broadcasted_iota(i32, (64, 64), 1)
        lane = lax.broadcasted_iota(i32, (64, 128), 1)
        for i in range(4):
            for ref, cols in ((wq, QC), (wk, KC), (wv, VC), (wg, slice(512, 768))):
                pack[i, :, cols] = ref[:, i, :].astype(bf16)
            al, be = (jnp.sum(jnp.where(diag, r[i : i + 1, :], 0.0), axis=1, keepdims=True) for r in (wal, wbe))
            pack[i, :, 768:896] = jnp.where(lane == 0, al, jnp.where(lane == 1, be, 0.0)).astype(bf16)
            pack[i, :, 896:1152] = wou[i].astype(bf16)

        for j, f in enumerate(lax.fori_loop(0, 64, find, tuple(jnp.int32(0) for _ in range(9)))):
            index[j] = f
        greet(peers(y=(1, 2, 3), z=(1, 2, 3), c=(1,), x=(1, 2, 3)))

        def rows():
            yield from pick_flow(tok, every, index, xo, HALO, es, er, gs, gr)
            for _ in lines:
                pass

            def norm(t, _):
                at_rows = pl.ds(pl.multiple_of(t * 16, 16), 16)
                v = xo[at_rows, :].astype(f32)
                r = lax.rsqrt(jnp.mean(v * v, axis=-1, keepdims=True) + EPS)
                h1[at_rows, :] = (v * r * gain1[...]).astype(bf16)
                return 0

            lax.fori_loop(0, ROWS // 16, norm, 0)
            xr[...] = xo[pl.ds(pl.multiple_of(HALO + 32 * (x * 4 + y), 16), 32), :]

        def small():
            se, re = ss.at[0], rs.at[0]
            yield from trade_flow(slots(tiny), lambda i: line.at[i, z, c], se.at[pl.ds(7, 4)], re.at[pl.ds(7, 4)])
            yield from zc_direct(lambda zz, cc: line.at[:, zz, cc], se, re)
            spread_gain(line, 1, gain1)
            spread_gain(line, 2, gain2)

        lines = small()
        run([rows(), lines, exchange_flow(slots(pack), wa, ss.at[1], rs.at[1])], plan)

    return pl.pallas_call(
        kernel,
        out_shape=[
            shape((4, 4, 2, 64, NA), bf16),
            shape((4, 4, 2) + tiny.shape[1:]),
            shape((16,), i32),
            shape((1, D)),
            shape((1, D)),
            shape((32, D), bf16),
            shape((ROWS, D), bf16),
        ],
        in_specs=[SM] + [VM] * 9,
        out_specs=[VM] * 2 + [SM] + [VM] * 4,
        scratch_shapes=[pltpu.VMEM((4, 64, NA), bf16), pltpu.VMEM((ROWS, D), bf16)]
        + PICK_SCRATCH
        + [pltpu.SemaphoreType.DMA((2, 15)), pltpu.SemaphoreType.DMA((2, 15))],
        compiler_params=remote_params(cid),
    )(order, tokens, *weights, tiny)


def norm_back(v, gain, dh):
    r = lax.rsqrt(jnp.mean(v * v, axis=-1, keepdims=True) + EPS)
    t = gain * dh
    dv = r * t - v * (r * r * r) * jnp.mean(v * t, axis=-1, keepdims=True)
    return dv, jnp.sum(v * r * dh, axis=0, keepdims=True)


def weight_tiles(left, right, out):
    def tile(t, _):
        v = dot(left(pl.ds(pl.multiple_of(t * 256, 256), 256)), right(), ((0,), (0,))).astype(bf16)
        for k in range(4):
            out[t // 2, lax.rem(t, 2) * 2 + k // 2, k % 2] = v[64 * k : 64 * (k + 1)]
        return 0

    lax.fori_loop(0, 8, tile, 0)


def middle(nv, wa, xrows, gain, wpart, dys, cid, plan=PLANS["middle"]):
    def kernel(nv, wa, xr, gain, wp, dys, m_out, dm_out, dg_out, da_out, dn_out, yp_out, sgu, sd, *refs):
        w, part, part2, h2, hid, dgu, ggu, gd, acc, dgs, refs = *refs[:10], refs[10:]
        sums = [refs[5 * i : 5 * i + 5] for i in range(4)]
        refs = refs[20:]
        gathers = [refs[2 * i : 2 * i + 2] for i in range(4)]
        ws, wr, ls = refs[8:11]
        fgu, fd = refs[11:15], refs[15:19]
        x, y, z, c = (lax.axis_index(a) for a in "xyzc")
        wo = wa.at[:, 896:]
        own = pltpu.make_async_copy(wp, w.at[:, z, c], ls)
        own.start()
        greet(peers(x=(1, 2, 3), y=(1, 2, 3), z=(1, 3), c=(1,)))

        def spread():
            own.wait()
            yield from spread_flow(w, ws, wr)

        weights = spread()

        def flat(ref, rows):
            v = ref[:, :, rows, :]
            return v.reshape(-1, v.shape[-1])

        def grads():
            def first():
                weight_tiles(lambda cols: h2[:, :, :, cols].reshape(SEG, 256), lambda: flat(dgu, slice(0, 32)), ggu)
                yield from sum_flow(ggu, sgu, *fgu)

            def second():
                weight_tiles(lambda cols: dys[:, :, :, cols].reshape(SEG, 256), lambda: flat(hid, slice(0, 32)), gd)
                yield from sum_flow(gd, sd, *fd)

            yield from first()
            yield from second()

        def half(h):
            rows = slice(16 * h, 16 * h + 16)
            nrows = flat(nv, rows)
            for t in range(4):
                cols = slice(512 * t, 512 * (t + 1))
                part[:, :, rows, cols] = dot(nrows, wo[cols, :], ((1,), (1,))).astype(bf16).reshape(4, 4, 16, 512)
            yield from plane_sum(part, acc.at[h], *sums[h], rows)
            m = xr[rows, :].astype(f32) + acc[h]
            m_out[rows, :] = m
            r = lax.rsqrt(jnp.mean(m * m, axis=-1, keepdims=True) + EPS)
            h2[x, y, rows, :] = (m * r * gain[...]).astype(bf16)
            yield from gather_rows(h2, *gathers[h], rows)
            for _ in weights:
                pass
            wv = w[...].reshape(D, NB)
            both = dot(flat(h2, rows), wv[:, : 2 * FFP], ((1,), (0,)))
            ga, up = both[:, :FFP], both[:, FFP:]
            dhid = dot(flat(dys, rows), wv[:, 2 * FFP :], ((1,), (0,)))
            sg = jax.nn.sigmoid(ga)
            act = ga * sg
            hv = (act * up).astype(bf16)
            hid[:, :, rows, :] = hv.reshape(4, 4, 16, FFP)
            dga = (dhid * up * (sg * (1.0 + ga * (1.0 - sg)))).astype(bf16)
            dup = (dhid * act).astype(bf16)
            dgu[:, :, rows, :FFP] = dga.reshape(4, 4, 16, FFP)
            dgu[:, :, rows, FFP:] = dup.reshape(4, 4, 16, FFP)
            dv = jnp.concatenate([dga, dup], axis=1)
            for t in range(4):
                cols = slice(512 * t, 512 * (t + 1))
                part2[:, :, rows, cols] = (
                    dot(dv, wv[cols, : 2 * FFP], ((1,), (1,))).astype(bf16).reshape(4, 4, 16, 512)
                )

            def back():
                yield from plane_sum(part2, acc.at[2 + h], *sums[2 + h], rows)
                dvr, dgain = norm_back(m_out[rows, :], gain[...], acc[2 + h])
                dm = dys[x, y, rows, :].astype(f32) + dvr
                dm_out[rows, :] = dm
                dgs[h : h + 1, :] = dgain
                da_out[x, y, rows, :] = dm.astype(bf16)
                yield from gather_rows(da_out, *gathers[2 + h], rows)
                dn_out[:, :, rows, :] = dot(flat(da_out, rows), wo[...], ((1,), (0,))).reshape(4, 4, 16, DV)

            def result():
                yield
                for t in range(4):
                    cols = slice(512 * t, 512 * (t + 1))
                    yp_out[:, :, rows, cols] = (
                        dot(hv, wv[cols, 2 * FFP :], ((1,), (1,))).astype(bf16).reshape(4, 4, 16, 512)
                    )

            yield from together([back(), result()] + ([grads()] if h else []))

        run([half(0), half(1), weights], plan)
        dg_out[...] = dgs[0:1, :] + dgs[1:2, :]

    gu, gdown = (4, 4, 2, 64, 2 * FFP), (4, 4, 2, 64, FFP)
    return pl.pallas_call(
        kernel,
        out_shape=[
            shape((32, D)),
            shape((32, D)),
            shape((1, D)),
            shape((4, 4, 32, D), bf16),
            shape((4, 4, 32, DV)),
            shape((4, 4, 32, D), bf16),
            shape((4, 64, 2 * FFP), bf16),
            shape((4, 64, FFP), bf16),
        ],
        in_specs=[VM] * 6,
        out_specs=[VM] * 8,
        scratch_shapes=[
            pltpu.VMEM((4, 4, 2, 64, NB), bf16),
            pltpu.VMEM((4, 4, 32, D), bf16),
            pltpu.VMEM((4, 4, 32, D), bf16),
            pltpu.VMEM((4, 4, 32, D), bf16),
            pltpu.VMEM((4, 4, 32, FFP), bf16),
            pltpu.VMEM((4, 4, 32, 2 * FFP), bf16),
            pltpu.VMEM(gu, bf16),
            pltpu.VMEM(gdown, bf16),
            pltpu.VMEM((4, 16, D), f32),
            pltpu.VMEM((2, D), f32),
        ]
        + scatter_buffers(16) * 4
        + GATHER_SEMS * 4
        + [pltpu.SemaphoreType.DMA((11,)), pltpu.SemaphoreType.DMA((11,)), pltpu.SemaphoreType.DMA]
        + sum_scratch(gu[3:], bf16)
        + sum_scratch(gdown[3:], bf16),
        compiler_params=remote_params(cid),
    )(nv, wa, xrows, gain, wpart, dys)


def home_flow(src, dst, order, alls, cols, picks, s1, r1, s2, r2, s3, r3):
    x, y, z, c = (lax.axis_index(a) for a in "xyzc")
    n = src.shape[0]
    sends = []
    cols[x, y] = src[:, :, lanes(x, y)]
    t = 0
    for i in range(4):
        for j in range(4):
            if (i, j) == (0, 0):
                continue
            px, py = at("x", i), at("y", j)
            sends.append(send(src.at[:, :, lanes(px, py)], cols.at[x, y], s1.at[t], r1.at[t], {"x": px, "y": py}))
            t += 1
    yield
    for cp in sends:
        cp.wait_recv()
    for k in range(n):
        alls[z, c, k] = cols[:, :, k].reshape(8, 64, 128)
    yield from zc_direct(lambda zz, cc: alls.at[zz, cc], s2, r2)
    for j in range(4):
        for i in range(2):
            b = order[j * 16 + (z * 2 + c) * 2 + i]
            for k in range(n):
                picks[j, k, 64 * i : 64 * (i + 1)] = alls[b >> 4, (b >> 3) & 1, k, b & 7]
    mine = pl.ds(pl.multiple_of(y * 128, 128), 128)
    last = [
        send(picks.at[at("y", j)], dst.at[:, :, mine], s3.at[j], r3.at[j], {"y": at("y", j)}) for j in (2, 1, 3)
    ]
    dst[:, :, mine] = picks[y]
    yield
    for cp in last:
        cp.wait_recv()
    for cp in sends + last:
        cp.wait_send()


HOME_SCRATCH = [
    pltpu.VMEM((4, 2, 2, 8, 64, 128), bf16),
    pltpu.VMEM((4, 4, 2, 32, 128), bf16),
    pltpu.VMEM((4, 2, 128, 128), bf16),
    pltpu.SemaphoreType.DMA((15,)),
    pltpu.SemaphoreType.DMA((15,)),
    pltpu.SemaphoreType.DMA((7,)),
    pltpu.SemaphoreType.DMA((7,)),
    pltpu.SemaphoreType.DMA((4,)),
    pltpu.SemaphoreType.DMA((4,)),
]


def sum_flow(g, stage, core, bufs, ss, rs):
    c = lax.axis_index("c")
    d = send(g.at[:, :, 1 - c], core, ss.at[0], rs.at[0], {"c": 1 - c})
    yield
    d.wait_recv()

    def ready(i):
        for k in range(4):
            core[k, i] = core[k, i] + g[k, i, c]

    def emit(s, v):
        stage[2 * s : 2 * s + 2] = v.astype(stage.dtype)

    def piece(i, s):
        return core.at[2 * s : 2 * s + 2, i]

    yield from ring_scatter("z", piece, ready, bufs, emit, ss.at[pl.ds(1, 6)], rs.at[pl.ds(1, 6)])
    d.wait_send()


def sum_scratch(dims, kind):
    return [
        pltpu.VMEM((4, 4) + dims, kind),
        pltpu.VMEM((6, 2) + dims, kind),
        pltpu.SemaphoreType.DMA((7,)),
        pltpu.SemaphoreType.DMA((7,)),
    ]


TRADE_SEMS = [pltpu.SemaphoreType.DMA((4,)), pltpu.SemaphoreType.DMA((4,))]


def scatter_flow(g, out, stage, ts, tr, *sums):
    yield from sum_flow(g, stage, *sums)
    yield from trade_flow(slots(stage), lambda y: out.at[y], ts, tr)


def scatter_scratch(dims, kind):
    return [pltpu.VMEM((4,) + dims, kind)] + TRADE_SEMS + sum_scratch(dims, kind)


def finish(order, part, xrows, dm, gain, h1, dproj, dcw, dsc, dhg, dgain2, yrows, cid, plan=PLANS["finish"]):
    nh, ns = len(HOME_SCRATCH), 7

    def kernel(order, part, xr, dm, gain, h1, dproj, dcw, dsc, dhg, dgain2, yr, both, g_out, t_out, tot, acc, *rest):
        big, mid, small, ss, rs = rest[:5]
        home, rest = rest[5 : 5 + nh], rest[5 + nh :]
        ga, ti, rest = rest[:ns], rest[ns : 2 * ns], rest[2 * ns :]
        grad, line, rows, xr4, xs, xq = rest
        x = lax.axis_index("x")
        greet(plane_peers() + peers(z=(1, 2, 3), c=(1,)))

        def small_grads():
            yield from scatter_flow(line, t_out, *ti)
            xr4[x] = (t_out[0] + t_out[1]) + (t_out[2] + t_out[3])
            sends = [send(xr4.at[x], xr4.at[x], xs.at[k], xq.at[k], {"x": at("x", k)}) for k in (2, 1, 3)]
            yield
            for cp in sends:
                cp.wait_recv()
            tot[...] = (xr4[0] + xr4[1]) + (xr4[2] + xr4[3])
            for cp in sends:
                cp.wait_send()

        def spread(v, wide, first):
            n = 32 * wide
            owner = lax.broadcasted_iota(i32, (32, n), 0) == lax.broadcasted_iota(i32, (32, n), 1) // wide
            place = lax.broadcasted_iota(i32, (n, 128), 1) == first + lax.rem(lax.broadcasted_iota(i32, (n, 128), 0), wide)
            return dot(jnp.where(owner, v, 0.0), jnp.where(place, 1.0, 0.0), ((1,), (0,)), HI)

        def fill_lines():
            lane = lax.broadcasted_iota(i32, (32, 128), 1)
            top = jnp.where(lane == 72, dsc[0:1, 0:1], 0.0) + jnp.where(lane == 73, dsc[1:2, 0:1], 0.0)
            for j in range(4):
                top = top + spread(dcw[j : j + 1, QC], 4, 4 * j) + spread(dcw[j : j + 1, KC], 4, 16 + 4 * j)
                top = top + spread(dcw[j : j + 1, VC], 8, 32 + 8 * j)
            top = top + spread(dhg[...], 8, 64)
            line[...] = jnp.zeros(line.shape, f32)
            for i in range(32):
                line[i // 8, i // 2 % 4, i % 2, 0:1, :] = top[i : i + 1]
                line[i // 8, i // 2 % 4, i % 2, 2:3, 0:64] = dgain2[:, 64 * i : 64 * (i + 1)]

        def input_grads():
            sums = plane_sum(part, acc, big, mid, small, ss, rs)
            next(sums)
            fill_lines()
            yield
            yield from sums
            dvr, dgain = norm_back(xr[...].astype(f32), gain[...], acc[...])
            rows[0] = yr[...]
            rows[1] = (dm[...] + dvr).astype(bf16)
            for i in range(32):
                line[i // 8, i // 2 % 4, i % 2, 1:2, 0:64] = dgain[:, 64 * i : 64 * (i + 1)]
            yield from together([home_flow(rows, both, order, *home), small_grads()])

        def weight_grads():
            weight_tiles(lambda cols: h1[HALO:, cols], lambda: dproj[...], grad)
            yield from scatter_flow(grad, g_out, *ga)

        run([input_grads(), weight_grads()], plan)

    td, gd = (8, 128), (64, 896)
    return pl.pallas_call(
        kernel,
        out_shape=[
            shape((2, 128, 512), bf16),
            shape((4,) + gd, bf16),
            shape((4,) + td),
            shape(td),
        ],
        in_specs=[SM] + [VM] * 11,
        out_specs=[VM] * 4,
        scratch_shapes=[pltpu.VMEM((32, D), f32)]
        + SCATTER_SCRATCH
        + HOME_SCRATCH
        + scatter_scratch(gd, bf16)
        + scatter_scratch(td, f32)
        + [
            pltpu.VMEM((4, 4, 2) + gd, bf16),
            pltpu.VMEM((4, 4, 2) + td, f32),
            pltpu.VMEM((2, 32, D), bf16),
            pltpu.VMEM((4,) + td, f32),
            pltpu.SemaphoreType.DMA((4,)),
            pltpu.SemaphoreType.DMA((4,)),
        ],
        compiler_params=remote_params(cid),
    )(order, part, xrows, dm, gain, h1, dproj, dcw, dsc, dhg, dgain2, yrows)


def dot(a, b, dims, prec=None):
    return lax.dot_general(a, b, (dims, ((), ())), preferred_element_type=f32, precision=prec)


def lo(a):
    return a.astype(bf16)


def mm(a, b):
    return dot(lo(a), lo(b), ((1,), (0,)))


def mmt(a, b):
    return dot(lo(a), lo(b), ((1,), (1,)))


def tmm(a, b):
    return dot(lo(a), lo(b), ((0,), (0,)))


def halves_of(a):
    h = a.astype(bf16)
    return h, (a - h.astype(f32)).astype(bf16)


def fine(a, b, dims=((1,), (0,))):
    ah, al = halves_of(a)
    bh, bl = halves_of(b)
    return dot(ah, bh, dims) + (dot(ah, bl, dims) + dot(al, bh, dims))


def tri_inverse(a, r, c):
    eye = jnp.where(r == c, 1.0, 0.0)
    n1 = jnp.where((r >> 3) == (c >> 3), -a, 0.0)
    n2 = fine(n1, n1)
    n4 = fine(n2, n2)
    t = eye + n1
    t = t + fine(t, n2)
    t = t + fine(t, n4)
    for level in (3, 4, 5, 6):
        off = ((r >> (level + 1)) == (c >> (level + 1))) & ((r >> level) != (c >> level))
        t = t - fine(t, fine(jnp.where(off, a, 0.0), t))
    return t


def iotas():
    return (
        lax.broadcasted_iota(i32, (CH, CH), 0),
        lax.broadcasted_iota(i32, (CH, CH), 1),
    )


def filtered(z, cw, mc, cols):
    total = z[HALO : HALO + SEG, cols] * cw[3:4, cols]
    for j in range(3):
        total = total + mc[:, j : j + 1] * cw[j : j + 1, cols] * z[HALO - 3 + j : HALO - 3 + j + SEG, cols]
    return total


def silu(v):
    return v * jax.nn.sigmoid(v)


QC, KC, VC = slice(0, 128), slice(128, 256), slice(256, 512)


def decay_of(cc, cr, mask):
    return jnp.exp(jnp.where(mask, cc - cr, 0.0)) * jnp.where(mask, 1.0, 0.0)


def prepare(z, ab, cw, sc, mc, mr, qkv, tm, wu, gb, cr, ti):
    r, c = iotas()
    for cols, scale in ((QC, DK**-0.5), (KC, 1.0)):
        s = silu(filtered(z, cw, mc, cols))
        qkv[:, cols] = (s * lax.rsqrt(jnp.sum(s * s, axis=-1, keepdims=True) + EPS) * scale).astype(bf16)
    qkv[:, VC] = silu(filtered(z, cw, mc, VC)).astype(bf16)
    low = jnp.where(r >= c, 1.0, 0.0)
    eye = jnp.where(r == c, 1.0, 0.0)
    lane = lax.broadcasted_iota(i32, (CH, 128), 1)
    transit = eye
    insert = jnp.zeros((DK, DV), f32)
    yield
    for n in range(NCH):
        rows = slice(n * CH, (n + 1) * CH)
        raw = ab[HALO + n * CH : HALO + (n + 1) * CH, :]
        beta = jax.nn.sigmoid(raw[:, 1:2])
        u = raw + sc[0:1, 1:2]
        g = -jnp.exp(sc[0:1, 0:1]) * (jnp.maximum(u, 0.0) + jnp.log1p(jnp.exp(-jnp.abs(u))))
        g = jnp.where(lane == 0, g, 0.0)
        cum = dot(low, g, ((1,), (0,)), HI)[:, 0:1]
        cumr = dot(g, low, ((0,), (1,)), HI)[0:8, :]
        gb[rows, :] = jnp.where(lane == 0, beta, cum)
        cr[:, rows] = cumr
        cumrow = cumr[0:1, :]
        last = cumr[0:1, CH - 1 : CH]
        m = mc[rows, :]
        carried, closing, begin, carry_last = m[:, 3:4], m[:, 4:5], m[:, 5:6], m[0:1, 6:7]
        same = begin == mr[0:1, rows]
        k = qkv[rows, KC]
        kf = k.astype(f32)
        v = qkv[rows, VC].astype(f32)
        a = beta * dot(k, k, ((1,), (1,))) * decay_of(cum, cumrow, same & (r > c))
        t = tri_inverse(a, r, c)
        tm[rows, :] = t
        lead = (beta * jnp.exp(cum) * carried) * kf
        w = fine(t, lead)
        uu = fine(t, beta * v)
        wu[rows, 0:DK] = w
        wu[rows, DK:] = uu
        tail = kf * (jnp.exp(last - cum) * closing)
        keep = jnp.exp(last) * carry_last
        hand = keep * eye - fine(tail, w, ((0,), (0,)))
        insert = fine(hand, insert) + fine(tail, uu, ((0,), (0,)))
        transit = fine(hand, transit)
        yield
    ti[:, 0:DK] = transit.astype(bf16)
    ti[:, DK:] = insert.astype(bf16)


def emit_outputs(seg, maps, qkv, wu, gb, cr, mc, mr, gp, hg, nout, oout, fout, sout):
    r, c = iotas()

    def fold(d, s):
        tr, ins = maps[d, :, 0:DK], maps[d, :, DK:].astype(f32)
        sh, sl = halves_of(s)
        new = dot(tr, sh, ((1,), (0,))) + dot(tr, sl, ((1,), (0,))) + ins
        return jnp.where(d < seg, new, s)

    s = lax.fori_loop(0, 7, fold, jnp.zeros((DK, DV), f32))
    for n in range(NCH):
        rows = slice(n * CH, (n + 1) * CH)
        m = mc[rows, :]
        carried, closing, begin, carry_last = m[:, 3:4], m[:, 4:5], m[:, 5:6], m[0:1, 6:7]
        cum = gb[rows, 1:2]
        cumrow = cr[0:1, rows]
        last = cr[0:1, n * CH + CH - 1 : n * CH + CH]
        same = begin == mr[0:1, rows]
        q, k = qkv[rows, QC], qkv[rows, KC]
        p = dot(q, k, ((1,), (1,))) * decay_of(cum, cumrow, same & (r >= c))
        fresh = wu[rows, DK:] - fine(wu[rows, 0:DK], s)
        qd = q.astype(f32) * (jnp.exp(cum) * carried)
        o = mm(qd, s) + mm(p, fresh)
        sout[n] = s
        fout[rows, :] = fresh
        oout[rows, :] = o
        x = gp[HALO + n * CH : HALO + (n + 1) * CH, :]
        rn = lax.rsqrt(jnp.mean(o * o, axis=-1, keepdims=True) + EPS)
        nout[rows, :] = (o * rn * hg[0:1, :] * silu(x)).astype(bf16)
        tail = k.astype(f32) * (jnp.exp(last - cum) * closing)
        s = (jnp.exp(last) * carry_last) * s + fine(tail, fresh, ((0,), (0,)))
        yield


def back_emit(dn, o, gp, hg, qkv, wu, gb, cr, mc, mr, do_out, dgp_out, dhg_out, e_out):
    r, c = iotas()
    dhg = jnp.zeros((1, DV), f32)
    e = jnp.zeros((DK, DV), f32)
    for n in reversed(range(NCH)):
        rows = slice(n * CH, (n + 1) * CH)
        ov, x, dnv = o[rows, :], gp[HALO + n * CH : HALO + (n + 1) * CH, :], dn[rows, :]
        rn = lax.rsqrt(jnp.mean(ov * ov, axis=-1, keepdims=True) + EPS)
        sg = jax.nn.sigmoid(x)
        act = x * sg
        h = hg[0:1, :]
        base = ov * rn
        dhg = dhg + jnp.sum(base * act * dnv, axis=0, keepdims=True)
        dgp_out[rows, :] = (dnv * base * h * (sg * (1.0 + x * (1.0 - sg)))).astype(bf16)
        t = dnv * h * act
        do = rn * t - base * (rn * rn) * jnp.mean(ov * t, axis=-1, keepdims=True)
        do_out[rows, :] = do
        m = mc[rows, :]
        carried, closing, begin, carry_last = m[:, 3:4], m[:, 4:5], m[:, 5:6], m[0:1, 6:7]
        cum = gb[rows, 1:2]
        cumrow = cr[0:1, rows]
        last = cr[0:1, n * CH + CH - 1 : n * CH + CH]
        same = begin == mr[0:1, rows]
        q, k = qkv[rows, QC], qkv[rows, KC]
        p = dot(q, k, ((1,), (1,))) * decay_of(cum, cumrow, same & (r >= c))
        qd = q.astype(f32) * (jnp.exp(cum) * carried)
        tail = k.astype(f32) * (jnp.exp(last - cum) * closing)
        df = tmm(p, do) + mm(tail, e)
        e = tmm(qd, do) + (jnp.exp(last) * carry_last) * e - tmm(wu[rows, 0:DK], df)
        yield
    dhg_out[...] = dhg
    e_out[...] = e.astype(bf16)


def back_delta(seg, maps, tails, do, fr, st, qkv, tm, wu, gb, cr, z, ab, cw, sc, mc, mr, dz, dab, dcw, dsc, dqkv):
    r, c = iotas()
    low = jnp.where(r >= c, 1.0, 0.0)
    ones = jnp.ones((CH, CH), f32)
    lane = lax.broadcasted_iota(i32, (CH, 128), 1)
    row = lax.broadcasted_iota(i32, (CH, 1), 0)

    def fold(i, e):
        d = 7 - i
        tr, own = maps[d, :, 0:DK], tails[d].astype(f32)
        eh, el = halves_of(e)
        new = dot(tr, eh, ((0,), (0,))) + dot(tr, el, ((0,), (0,))) + own
        return jnp.where(d > seg, new, e)

    e = lax.fori_loop(0, 7, fold, jnp.zeros((DK, DV), f32))
    acc_a = jnp.zeros((1, 128), f32)
    acc_d = jnp.zeros((1, 128), f32)
    for n in reversed(range(NCH)):
        rows = slice(n * CH, (n + 1) * CH)
        m = mc[rows, :]
        carried, closing, begin, carry_last = m[:, 3:4], m[:, 4:5], m[:, 5:6], m[0:1, 6:7]
        beta, cum = gb[rows, 0:1], gb[rows, 1:2]
        cumrow = cr[0:1, rows]
        last = cr[0:1, n * CH + CH - 1 : n * CH + CH]
        same = begin == mr[0:1, rows]
        q, k = qkv[rows, QC], qkv[rows, KC]
        qf, kf, vf = q.astype(f32), k.astype(f32), qkv[rows, VC].astype(f32)
        dec_i = decay_of(cum, cumrow, same & (r >= c))
        dec_s = jnp.where(r > c, dec_i, 0.0)
        p = dot(q, k, ((1,), (1,))) * dec_i
        kkd = dot(k, k, ((1,), (1,))) * dec_s
        ex = jnp.exp(cum) * carried
        tf = jnp.exp(last - cum) * closing
        keep = jnp.exp(last) * carry_last
        tail = kf * tf
        qd = qf * ex
        dov, fv, sv, tv = do[rows, :], fr[rows, :], st[n], tm[rows, :]
        w, u = wu[rows, 0:DK], wu[rows, DK:]
        df = tmm(p, dov) + mm(tail, e)
        dw = -mmt(df, sv)
        dtail = mmt(fv, e)
        dkeep = jnp.sum(jnp.sum(sv * e, axis=1, keepdims=True), axis=0, keepdims=True)
        dqd = mmt(dov, sv)
        dp = mmt(dov, fv)
        dlead = tmm(tv, dw)
        dbv = tmm(tv, df)
        da = -(mmt(dlead, w) + mmt(dbv, u))
        dakd = da * kkd
        dkk = da * beta * dec_s
        dqk = dp * dec_i
        mix = dakd * beta + dp * p
        dqkv[rows, QC] = mm(dqk, k) + dqd * ex
        dqkv[rows, KC] = (
            tmm(dqk, q) + mm(dkk, k) + tmm(dkk, k) + dlead * (beta * ex) + dtail * tf
        )
        dqkv[rows, VC] = beta * dbv
        lk = jnp.sum(dlead * kf, axis=1, keepdims=True) * ex
        dbeta = jnp.sum(dakd, axis=1, keepdims=True) + lk + jnp.sum(dbv * vf, axis=1, keepdims=True)
        tt = jnp.sum(dtail * tail, axis=1, keepdims=True)
        dcum = jnp.sum(mix, axis=1, keepdims=True) + jnp.sum(dqd * qd, axis=1, keepdims=True) + lk * beta - tt
        dcum = dcum + jnp.where(row == CH - 1, jnp.sum(tt, axis=0, keepdims=True) + dkeep * keep, 0.0)
        full = dcum - dot(mix, ones, ((0,), (0,)), HI)
        dg = dot(low, full, ((0,), (0,)), HI)
        raw = ab[HALO + n * CH : HALO + (n + 1) * CH, :]
        uu = raw + sc[0:1, 1:2]
        rate = -jnp.exp(sc[0:1, 0:1])
        sp = jnp.maximum(uu, 0.0) + jnp.log1p(jnp.exp(-jnp.abs(uu)))
        dal = dg * rate * jax.nn.sigmoid(uu)
        acc_a = acc_a + jnp.sum(dg * rate * sp, axis=0, keepdims=True)
        acc_d = acc_d + jnp.sum(dal, axis=0, keepdims=True)
        dab[rows, :] = jnp.where(
            lane == 0, dal, jnp.where(lane == 1, dbeta * beta * (1.0 - beta), 0.0)
        ).astype(bf16)
        e = tmm(qd, dov) + keep * e - tmm(w, df)
        yield
    dsc[0:1, :] = acc_a
    dsc[1:2, :] = acc_d
    dz[0:HALO, :] = jnp.zeros((HALO, 512), f32)
    for cols, scale in ((QC, DK**-0.5), (KC, 1.0), (VC, None)):
        y = filtered(z, cw, mc, cols)
        sg = jax.nn.sigmoid(y)
        ds = dqkv[:, cols]
        if scale is not None:
            s = y * sg
            rn = lax.rsqrt(jnp.sum(s * s, axis=-1, keepdims=True) + EPS)
            ds = scale * (rn * ds - s * (rn * rn * rn) * jnp.sum(s * ds, axis=-1, keepdims=True))
        dy = ds * (sg * (1.0 + y * (1.0 - sg)))
        dz[HALO : HALO + SEG, cols] = dy * cw[3:4, cols]
        dcw[3:4, cols] = jnp.sum(dy * z[HALO : HALO + SEG, cols], axis=0, keepdims=True)
        for j in range(3):
            part = mc[:, j : j + 1] * dy
            away = slice(HALO - 3 + j, HALO - 3 + j + SEG)
            dcw[j : j + 1, cols] = jnp.sum(part * z[away, cols], axis=0, keepdims=True)
            dz[away, cols] = dz[away, cols] + part * cw[j : j + 1, cols]
        yield


def map_gather(own, out, ss, rs):
    z, c = lax.axis_index("z"), lax.axis_index("c")
    out[z, c] = own[...]
    yield from zc_direct(lambda zz, cc: out.at[zz, cc], ss, rs)


class Maps:
    def __init__(self, ref):
        self.ref = ref

    def __getitem__(self, key):
        key = key if isinstance(key, tuple) else (key,)
        return self.ref[(key[0] // 2, key[0] % 2) + key[1:]]


def masks(lens, mc, mr):
    base = (lax.axis_index("z") * 2 + lax.axis_index("c")) * SEG
    firsts = [jnp.int32(0)]
    for k in range(3):
        firsts.append(firsts[k] + lens[k])

    def begin_of(pos):
        b = jnp.zeros_like(pos)
        for k in range(1, 4):
            b = jnp.where((pos >= firsts[k]) & (pos < firsts[k] + lens[k]), firsts[k], b)
        return b

    lane = lax.broadcasted_iota(i32, (CH, 128), 1)
    for n in range(NCH):
        first = base + n * CH
        pos = first + lax.broadcasted_iota(i32, (CH, 128), 0)
        b = begin_of(pos)
        last = begin_of(jnp.full((CH, 128), first + CH - 1, i32))

        def one(flag):
            return jnp.where(flag, 1.0, 0.0)

        late = jnp.where(lane == 3, one(b < first), jnp.where(lane == 4, one(b == last), one(last < first)))
        flags = jnp.where(lane < 3, one(pos - 3 + lane >= b), late)
        mc[n * CH : (n + 1) * CH, :] = jnp.where(lane == 5, b.astype(f32), flags)
        mr[:, n * CH : (n + 1) * CH] = begin_of(first + lax.broadcasted_iota(i32, (8, CH), 1)).astype(f32)


def attend(proj, cw, hg, lens, a_log, dt_bias, index, cotangent, weights, cid, plan=PLANS["attend"]):
    npk = len(PICK_SCRATCH)

    def kernel(proj, cw, hg, lens, al, dt, index, cot, wga, wup, wdo, wp, dyo, qkv, tm, wu, gb, cr, maps, nout, oout, fout, sout, mc, mr, sc, *refs):
        every, es, er, gs, gr = refs[:npk]
        pack, ti, ms, mq, ts, tr = refs[npk:]
        x, y, z, c = (lax.axis_index(a) for a in "xyzc")
        zq, gp, ab = proj.at[:, 0:512], proj.at[:, 512:768], proj.at[:, 768:896]
        greet(peers(y=(1, 2, 3), z=(1, 2, 3), c=(1,), x=(1, 2, 3)))

        ff = wga.shape[1]
        for i in range(4):
            n = min(FFP, ff - FFP * i)
            cols = slice(FFP * i, FFP * i + n)
            for k, v in enumerate((wga[:, cols], wup[:, cols], wdo[:, cols])):
                pack[i, :, FFP * k : FFP * k + n] = v.astype(bf16)
                if n < FFP:
                    pack[i, :, FFP * k + n : FFP * (k + 1)] = jnp.zeros((64, FFP - n), bf16)

        def mixer():
            masks(lens, mc, mr)
            sc[0:8, :] = jnp.where(lax.broadcasted_iota(i32, (8, 128), 1) == 0, al[y], dt[y])
            yield from prepare(zq, ab, cw, sc, mc, mr, qkv, tm, wu, gb, cr, ti)
            yield from map_gather(ti, maps, ms, mq)
            yield from emit_outputs(z * 2 + c, Maps(maps), qkv, wu, gb, cr, mc, mr, gp, hg, nout, oout, fout, sout)

        run(
            [mixer(), pick_flow(cot, every, index, dyo, 0, es, er, gs, gr), trade_flow(slots(pack), lambda i: wp.at[i], ts, tr)],
            plan,
        )

    return pl.pallas_call(
        kernel,
        out_shape=[
            shape((4, 64, NB), bf16),
            shape((SEG, D), bf16),
            shape((SEG, 512), bf16),
            shape((SEG, CH)),
            shape((SEG, DK + DV)),
            shape((SEG, 128)),
            shape((8, SEG)),
            shape((4, 2, DK, DK + DV), bf16),
            shape((SEG, DV), bf16),
            shape((SEG, DV)),
            shape((SEG, DV)),
            shape((NCH, DK, DV)),
            shape((SEG, 128)),
            shape((8, SEG)),
            shape((8, 128)),
        ],
        in_specs=[VM] * 3 + [SM] * 4 + [VM] * 4,
        out_specs=[VM] * 15,
        scratch_shapes=PICK_SCRATCH
        + [
            pltpu.VMEM((4, 64, NB), bf16),
            pltpu.VMEM((DK, DK + DV), bf16),
            pltpu.SemaphoreType.DMA((11,)),
            pltpu.SemaphoreType.DMA((11,)),
        ]
        + TRADE_SEMS,
        compiler_params=remote_params(cid),
    )(proj, cw, hg, lens, a_log, dt_bias, index, cotangent, *weights)


def back_attend(dn, o, proj, hg, qkv, tm, wu, gb, cr, mc, mr, maps, fr, st, cw, sc, m, ypart, stages, da, nv, cid, plan=PLANS["back_attend"]):
    def kernel(
        dn, o, proj, hg, qkv, tm, wu, gb, cr, mc, mr, maps, fr, st, cw, sc, m, ypart, sgu, sd, da, nv,
        yrow, dproj, dhg, dcw, dsc, ro, rgu, rd,
        do, dgp, e, tails, dz, dab, dqkv, edge, ms, mq, ds, dq, acc, grad, *refs,
    ):
        big, mid, small, ss, rs = refs[:5]
        ga, trades = refs[5:12], refs[12:]
        zq, gp, ab = proj.at[:, 0:512], proj.at[:, 512:768], proj.at[:, 768:896]
        seg = lax.axis_index("z") * 2 + lax.axis_index("c")
        greet(peers(x=(1, 2, 3), y=(1, 2, 3)) + segment_peers())

        def mixer():
            yield from back_emit(dn, o, gp, hg, qkv, wu, gb, cr, mc, mr, do, dgp, dhg, e)
            yield from map_gather(e, tails, ms, mq)
            yield from back_delta(
                seg, Maps(maps), Maps(tails), do, fr, st, qkv, tm, wu, gb, cr, zq, ab, cw, sc, mc, mr, dz, dab, dcw, dsc, dqkv
            )
            before = lax.rem(seg + 7, 8)
            cp = send(dz.at[0:HALO], edge, ds, dq, {"z": before // 2, "c": lax.rem(before, 2)})
            dproj[0 : SEG - HALO, 0:512] = dz[HALO:SEG].astype(bf16)
            dproj[:, 512:768] = dgp[...]
            dproj[:, 768:896] = dab[...]
            yield
            cp.wait_recv()
            dproj[SEG - HALO : SEG, 0:512] = (dz[SEG:ROWS] + jnp.where(seg < 7, edge[...], 0.0)).astype(bf16)
            cp.wait_send()

        def result():
            yield from plane_sum(ypart, acc, big, mid, small, ss, rs)
            yrow[...] = (m[...] + acc[...]).astype(bf16)

        def output_grads():
            weight_tiles(lambda cols: da[:, cols], lambda: nv[...], grad)
            yield from scatter_flow(grad, ro, *ga)

        def trade(staged, out, sems):
            yield from trade_flow(slots(staged), lambda y: out.at[y], *sems)

        run(
            [
                mixer(),
                result(),
                output_grads(),
                trade(sgu, rgu, trades[0:2]),
                trade(sd, rd, trades[2:4]),
            ],
            plan,
        )

    sgu, sd = stages
    gd = (64, DV)
    return pl.pallas_call(
        kernel,
        out_shape=[
            shape((32, D), bf16),
            shape((SEG, 896), bf16),
            shape((1, DV)),
            shape((4, 512)),
            shape((2, 128)),
            shape((4,) + gd, bf16),
            shape(sgu.shape, bf16),
            shape(sd.shape, bf16),
        ],
        in_specs=[VM] * 22,
        out_specs=[VM] * 8,
        scratch_shapes=[
            pltpu.VMEM((SEG, DV), f32),
            pltpu.VMEM((SEG, DV), bf16),
            pltpu.VMEM((DK, DV), bf16),
            pltpu.VMEM((4, 2, DK, DV), bf16),
            pltpu.VMEM((ROWS, 512), f32),
            pltpu.VMEM((SEG, 128), bf16),
            pltpu.VMEM((SEG, 512), f32),
            pltpu.VMEM((HALO, 512), f32),
            pltpu.SemaphoreType.DMA((11,)),
            pltpu.SemaphoreType.DMA((11,)),
            pltpu.SemaphoreType.DMA,
            pltpu.SemaphoreType.DMA,
            pltpu.VMEM((32, D), f32),
            pltpu.VMEM((4, 4, 2) + gd, bf16),
        ]
        + SCATTER_SCRATCH
        + scatter_scratch(gd, bf16)
        + TRADE_SEMS * 2,
        compiler_params=remote_params(cid),
    )(dn, o, proj, hg, qkv, tm, wu, gb, cr, mc, mr, maps, fr, st, cw, sc, m, ypart, sgu, sd, da, nv)


def lay_out(both, ra, ro, rgu, rd, lines, ff):
    def kernel(both, ra, ro, rgu, rd, lines, out, dt, dq, dk, dv, dg, da, db, do, gg, gu, gd, cq, ck, cv):
        out[...] = both[0]
        dt[...] = both[1]
        diag = lax.broadcasted_iota(i32, (64, 64), 0) == lax.broadcasted_iota(i32, (64, 64), 1)
        for i in range(4):
            for ref, cols in ((dq, QC), (dk, KC), (dv, VC), (dg, slice(512, 768))):
                ref[:, i, :] = ra[i, :, cols].astype(f32)
            do[i] = ro[i].astype(f32)
            n = min(FFP, ff - FFP * i)
            cols = slice(FFP * i, FFP * i + n)
            gg[:, cols] = rgu[i, :, 0:n].astype(f32)
            gu[:, cols] = rgu[i, :, FFP : FFP + n].astype(f32)
            gd[:, cols] = rd[i, :, 0:n].astype(f32)
            for k, ref in enumerate((da, db)):
                col = ra[i, :, 768 + k : 769 + k].astype(f32)
                ref[i : i + 1, :] = jnp.sum(jnp.where(diag, col, 0.0), axis=0, keepdims=True)
            for j in range(4):
                cq[j, i : i + 1, :] = lines[i, 0:1, 4 * j : 4 * j + 4]
                ck[j, i : i + 1, :] = lines[i, 0:1, 16 + 4 * j : 20 + 4 * j]
                cv[j, i : i + 1, :] = lines[i, 0:1, 32 + 8 * j : 40 + 8 * j]

    return pl.pallas_call(
        kernel,
        out_shape=[shape((128, 512), bf16)] * 2
        + [shape((64, 4, DK))] * 2
        + [shape((64, 4, DV))] * 2
        + [shape((4, 64))] * 2
        + [shape((4, 64, DV))]
        + [shape((64, ff))] * 3
        + [shape((4, 4, 4)), shape((4, 4, 4)), shape((4, 4, 8))],
        in_specs=[VM] * 6,
        out_specs=[VM] * 15,
        compiler_params=pltpu.CompilerParams(vmem_limit_bytes=VLIM),
    )(both, ra, ro, rgu, rd, lines)


def body(
    tokens,
    cotangent,
    seq_lengths,
    stretch_order,
    attn_gain,
    w_query,
    w_key,
    w_value,
    w_alpha,
    w_beta,
    conv_query,
    conv_key,
    conv_value,
    a_log,
    dt_bias,
    head_gain,
    w_outgate,
    w_output,
    mlp_gain,
    w_gate,
    w_up,
    w_down,
):

    def taps(a):
        return a.swapaxes(0, 1).reshape(4, -1)

    def each(a):
        return jnp.broadcast_to(a[None], (4,) + a.shape)

    line = jnp.concatenate([taps(conv_query), taps(conv_key), taps(conv_value), each(head_gain)], axis=1)
    line = jnp.pad(line, ((0, 0), (0, 128 - line.shape[1])))
    gains = jnp.pad(jnp.stack([attn_gain, mlp_gain]), ((0, 5), (0, 64)))
    tiny = jnp.concatenate([line[:, None], each(gains)], axis=1).astype(bf16).astype(f32)
    wa, lines, index, gain1, gain2, xrows, h1 = fetch(
        stretch_order,
        tokens.reshape(2, STRETCH, D),
        (w_query, w_key, w_value, w_outgate, w_alpha.T, w_beta.T, w_output.swapaxes(1, 2)),
        tiny,
        1,
    )
    wa = wa.reshape(D, NA)
    lines = lines[:, :, :, 0].reshape(32, 128)

    def filters(a):
        return a.reshape(32, 4, -1).swapaxes(0, 1).reshape(4, -1)

    cw = jnp.concatenate([filters(lines[:, 0:16]), filters(lines[:, 16:32]), filters(lines[:, 32:64])], axis=1)
    hg = lines[:, 64:72].reshape(1, DV)

    proj = jnp.dot(h1, wa[:, :896], preferred_element_type=f32)
    wpart, dys, qkv, tm, wu, gb, cr, maps, nv, ov, fr, st, mc, mr, sc = attend(
        proj, cw, hg, seq_lengths, a_log, dt_bias, index, cotangent.reshape(2, STRETCH, D), (w_gate, w_up, w_down.T), 2
    )
    m, dm, dgain2, da, dn, ypart, sgu, sd = middle(
        nv.reshape(4, 4, 32, DV), wa, xrows, gain2, wpart, dys.reshape(4, 4, 32, D), 3
    )
    da, dn = da.reshape(SEG, D), dn.reshape(SEG, DV)

    yrows, dproj, dhg, dcw, dsc, ro, rgu, rd = back_attend(
        dn, ov, proj, hg, qkv, tm, wu, gb, cr, mc, mr, maps, fr, st, cw, sc, m, ypart, (sgu, sd), da, nv, 4
    )
    dh1 = dot(dproj, wa[:, :896], ((1,), (1,))).astype(bf16).reshape(4, 4, 32, D)
    both, ra, rt, total = finish(
        stretch_order, dh1, xrows, dm, gain1, h1, dproj, dcw, dsc, dhg, dgain2, yrows, 5
    )
    out, dtok, d_query, d_key, d_value, d_outgate, d_alpha, d_beta, d_output, d_gate, d_up, d_down, cq, ck, cv = lay_out(
        both, ra, ro, rgu, rd, rt, w_gate.shape[1]
    )
    return (
        out,
        dtok,
        total[1, :64],
        d_query,
        d_key,
        d_value,
        d_alpha.T,
        d_beta.T,
        cq,
        ck,
        cv,
        rt[:, 0, 72],
        rt[:, 0, 73],
        total[0, 64:72],
        d_outgate,
        d_output.swapaxes(1, 2),
        total[2, :64],
        d_gate,
        d_up,
        d_down.T,
    )


def solution(mesh):
    torus = Mesh(mesh.devices.reshape(4, 4, 2, 4), ("y", "z", "c", "x"))
    dp, tp = ("y", "z", "c"), "x"
    in_specs = (
        P(dp, None),
        P(dp, None),
        P(),
        P(),
        P(dp),
        P(dp, tp, None),
        P(dp, tp, None),
        P(dp, tp, None),
        P(dp, tp),
        P(dp, tp),
        P(None, tp, dp),
        P(None, tp, dp),
        P(None, tp, dp),
        P(tp),
        P(tp),
        P(dp),
        P(dp, tp, None),
        P(tp, None, dp),
        P(dp),
        P(dp, tp),
        P(dp, tp),
        P(tp, dp),
    )
    out_specs = (
        P(dp, tp),
        P(dp, tp),
        P(dp),
        P(dp, tp, None),
        P(dp, tp, None),
        P(dp, tp, None),
        P(dp, tp),
        P(dp, tp),
        P(None, tp, dp),
        P(None, tp, dp),
        P(None, tp, dp),
        P(tp),
        P(tp),
        P(dp),
        P(dp, tp, None),
        P(tp, None, dp),
        P(dp),
        P(dp, tp),
        P(dp, tp),
        P(tp, dp),
    )
    return jax.shard_map(body, mesh=torus, in_specs=in_specs, out_specs=out_specs, check_vma=False)
```

```python
import functools
import math

import jax
import jax.numpy as jnp
from jax import lax
from jax.experimental import pallas as pl
from jax.experimental.pallas import tpu as pltpu
from jax.sharding import Mesh
from jax.sharding import PartitionSpec as P

MESH = pl.DeviceIdType.MESH
bf16, f32, i32 = jnp.bfloat16, jnp.float32, jnp.int32
HI = lax.Precision.HIGHEST
EPS = 1e-6
STRETCH = 64
D, DK, DV, FFP, HALO = 2048, 128, 256, 384, 16
SEG = 512
ROWS = SEG + HALO
CH = 128
NCH = SEG // CH
NA, NB = 1152, 1152
VLIM = 58 * 1024 * 1024


def at(axis, k):
    n = lax.axis_size(axis)
    return lax.rem(lax.axis_index(axis) + k + n, n)


def greet(peers):
    b = pltpu.get_barrier_semaphore()
    for p in peers:
        pl.semaphore_signal(b, inc=1, device_id=p, device_id_type=MESH)
    pl.semaphore_wait(b, len(peers))


def send(src, dst, ss, rs, who):
    cp = pltpu.make_async_remote_copy(
        src_ref=src, dst_ref=dst, send_sem=ss, recv_sem=rs, device_id=who, device_id_type=MESH
    )
    cp.start()
    return cp


def run(flows, plan=""):
    flows = list(flows)
    for i in plan:
        next(flows[int(i)], None)
    for _ in together(flows):
        pass


def together(flows):
    flows = list(flows)
    while flows:
        left = []
        for f in flows:
            try:
                next(f)
                left.append(f)
            except StopIteration:
                pass
        flows = left
        if flows:
            yield


def segment_peers():
    z, c = lax.axis_index("z"), lax.axis_index("c")
    out = []
    for k in range(4):
        for d in range(2):
            if (k, d) != (0, 0):
                out.append({"z": at("z", k), "c": lax.rem(c + d, 2)})
    return out


def plane_peers():
    return [{"x": at("x", i), "y": at("y", j)} for i in range(4) for j in range(4) if (i, j) != (0, 0)]


def peers(**steps):
    return [{ax: at(ax, k)} for ax, ks in steps.items() for k in ks]


def zc_gather(slot, halves, ss, rs):
    z, c = lax.axis_index("z"), lax.axis_index("c")
    other = {"c": 1 - c}
    zp, zm, zf = at("z", 1), at("z", -1), at("z", 2)
    own, (o1, o2) = slot(z, c), halves(z, c)
    a = send(o1, o1, ss.at[0], rs.at[0], {"z": zp})
    b = send(o2, o2, ss.at[1], rs.at[1], {"z": zm})
    a2 = send(o2, o2, ss.at[9], rs.at[9], {"z": zp})
    b2 = send(o1, o1, ss.at[10], rs.at[10], {"z": zm})
    d0 = send(own, own, ss.at[4], rs.at[4], other)
    yield
    a.wait_recv()
    lo = halves(zm, c)[0]
    e = send(lo, lo, ss.at[2], rs.at[2], {"z": zp})
    b.wait_recv()
    hi = halves(zp, c)[1]
    f = send(hi, hi, ss.at[3], rs.at[3], {"z": zm})
    yield
    a2.wait_recv()
    m = slot(zm, c)
    d1 = send(m, m, ss.at[5], rs.at[5], other)
    b2.wait_recv()
    p = slot(zp, c)
    d2 = send(p, p, ss.at[6], rs.at[6], other)
    yield
    e.wait_recv()
    fl = halves(zf, c)[0]
    d3 = send(fl, fl, ss.at[7], rs.at[7], other)
    f.wait_recv()
    fh = halves(zf, c)[1]
    d4 = send(fh, fh, ss.at[8], rs.at[8], other)
    yield
    for cp in (d0, d1, d2, d3, d4):
        cp.wait_recv()
    for cp in (a, b, a2, b2, e, f, d0, d1, d2, d3, d4):
        cp.wait_send()


def zc_direct(slot, ss, rs):
    z, c = lax.axis_index("z"), lax.axis_index("c")
    other = {"c": 1 - c}
    own = slot(z, c)
    far = [send(own, own, ss.at[k - 1], rs.at[k - 1], {"z": at("z", k)}) for k in (2, 1, 3)]
    over = [send(own, own, ss.at[3], rs.at[3], other)]
    yield
    for k, cp in zip((2, 1, 3), far):
        cp.wait_recv()
        got = slot(at("z", -k), c)
        over.append(send(got, got, ss.at[3 + k], rs.at[3 + k], other))
    yield
    for cp in over:
        cp.wait_recv()
    for cp in far + over:
        cp.wait_send()


def trade_flow(src_of, dst, ss, rs):
    y = lax.axis_index("y")
    loc = pltpu.make_async_copy(src_of(y), dst(y), ss.at[3])
    loc.start()
    sends = [
        send(src_of(at("y", k)), dst(y), ss.at[k - 1], rs.at[k - 1], {"y": at("y", k)}) for k in (2, 1, 3)
    ]
    yield
    loc.wait()
    for cp in sends:
        cp.wait_recv()
    for cp in sends:
        cp.wait_send()


def spread_flow(out, ss, rs):
    return zc_gather(
        lambda zz, cc: out.at[:, zz, cc],
        lambda zz, cc: (out.at[0:2, zz, cc], out.at[2:4, zz, cc]),
        ss,
        rs,
    )


def exchange_flow(src_of, out, ss, rs):
    z, c = lax.axis_index("z"), lax.axis_index("c")
    yield from trade_flow(src_of, lambda y: out.at[y, z, c], ss.at[pl.ds(11, 4)], rs.at[pl.ds(11, 4)])
    yield from spread_flow(out, ss, rs)


def torus_gather(a1, a2, block, ss, rs):
    i, j = lax.axis_index(a1), lax.axis_index(a2)
    all_of = []

    def go(ref, who):
        k = len(all_of)
        all_of.append(send(ref, ref, ss.at[k], rs.at[k], who))
        return all_of[-1]

    own = block(i, j)
    first = [(go(own, {a1: at(a1, k)}), k) for k in (2, 1, 3)]
    for k in (2, 1, 3):
        go(own, {a2: at(a2, k)})
    yield
    for cp, k in first:
        cp.wait_recv()
        got = block(at(a1, -k), j)
        for q in (2, 1, 3):
            go(got, {a2: at(a2, q)})
    yield
    for cp in all_of[3:]:
        cp.wait_recv()
    for cp in all_of:
        cp.wait_send()


def lanes(i, j):
    return pl.ds(pl.multiple_of((i * 4 + j) * 128, 128), 128)


def gather_columns(out, skip, ss, rs):
    def half(rows):
        return lambda x, y: out.at[rows, lanes(x, y)]

    one, two = half(slice(0, skip + 256)), half(slice(skip + 256, skip + 512))
    yield from together(
        [
            torus_gather("x", "y", one, ss.at[0], rs.at[0]),
            torus_gather("y", "x", lambda y, x: two(x, y), ss.at[1], rs.at[1]),
        ]
    )


def gather_rows(out, ss, rs, rows=slice(0, 32)):
    def half(cols):
        return lambda x, y: out.at[x, y, rows, cols]

    one, two = half(slice(0, 1024)), half(slice(1024, 2048))
    yield from together(
        [
            torus_gather("x", "y", one, ss.at[0], rs.at[0]),
            torus_gather("y", "x", lambda y, x: two(x, y), ss.at[1], rs.at[1]),
        ]
    )


GATHER_SEMS = [pltpu.SemaphoreType.DMA((2, 15)), pltpu.SemaphoreType.DMA((2, 15))]


def ring_scatter(axis, piece, ready, bufs, emit, ss, rs):
    me, p, m, fr = (at(axis, k) for k in (0, 1, -1, 2))
    ready(fr)
    a = send(piece(fr, 0), bufs.at[0], ss.at[0], rs.at[0], {axis: p})
    c = send(piece(fr, 1), bufs.at[1], ss.at[1], rs.at[1], {axis: m})
    ready(p)
    b = send(piece(p, 1), bufs.at[2], ss.at[2], rs.at[2], {axis: p})
    ready(m)
    d = send(piece(m, 0), bufs.at[3], ss.at[3], rs.at[3], {axis: m})
    ready(me)
    yield
    a.wait_recv()
    bufs[0] = bufs[0] + piece(p, 0)[...]
    e = send(bufs.at[0], bufs.at[4], ss.at[4], rs.at[4], {axis: p})
    c.wait_recv()
    bufs[1] = bufs[1] + piece(m, 1)[...]
    f = send(bufs.at[1], bufs.at[5], ss.at[5], rs.at[5], {axis: m})
    yield
    d.wait_recv()
    e.wait_recv()
    emit(0, piece(me, 0)[...].astype(f32) + bufs[3].astype(f32) + bufs[4].astype(f32))
    b.wait_recv()
    f.wait_recv()
    emit(1, piece(me, 1)[...].astype(f32) + bufs[2].astype(f32) + bufs[5].astype(f32))
    for cp in (a, b, c, d, e, f):
        cp.wait_send()


def plane_scatter(part, rows, res, big, mid, small, h, ss, rs):
    cols = slice(h * 1024, (h + 1) * 1024)
    a1, a2 = ("x", "y") if h == 0 else ("y", "x")
    i, j = lax.axis_index(a1), lax.axis_index(a2)

    def piece(k):
        return part.at[k, :, rows, cols] if h == 0 else part.at[:, k, rows, cols]

    one = [send(piece(at(a1, k)), big.at[k - 1], ss.at[k - 1], rs.at[k - 1], {a1: at(a1, k)}) for k in (2, 1, 3)]
    yield
    for cp in one:
        cp.wait_recv()
    total = piece(i)[...].astype(f32) + big[0].astype(f32)
    mid[...] = (total + (big[1].astype(f32) + big[2].astype(f32))).astype(bf16)
    two = [
        send(mid.at[at(a2, k)], small.at[k - 1], ss.at[k + 2], rs.at[k + 2], {a2: at(a2, k)}) for k in (2, 1, 3)
    ]
    yield
    for cp in two:
        cp.wait_recv()
    res[:, cols] = (mid[j].astype(f32) + small[0].astype(f32)) + (small[1].astype(f32) + small[2].astype(f32))
    for cp in one + two:
        cp.wait_send()


def plane_sum(part, acc, big, mid, small, ss, rs, rows=slice(0, 32)):
    yield from together(
        plane_scatter(part, rows, acc, big.at[h], mid.at[h], small.at[h], h, ss.at[h], rs.at[h]) for h in (0, 1)
    )


def scatter_buffers(rows):
    return [
        pltpu.VMEM((2, 3, 4, rows, 1024), bf16),
        pltpu.VMEM((2, 4, rows, 1024), bf16),
        pltpu.VMEM((2, 3, rows, 1024), bf16),
        pltpu.SemaphoreType.DMA((2, 6)),
        pltpu.SemaphoreType.DMA((2, 6)),
    ]


SCATTER_SCRATCH = scatter_buffers(32)
PLANS = {
    "front": "012010210203402030030300300000000",
    "middle": "",
    "back": "1340000020010020012",
}
VM = pl.BlockSpec(memory_space=pltpu.VMEM)
SM = pl.BlockSpec(memory_space=pltpu.SMEM)
HB = pl.BlockSpec(memory_space=pl.ANY)


def shape(dims, kind=f32):
    return jax.ShapeDtypeStruct(dims, kind)


def remote_params(cid):
    return pltpu.CompilerParams(collective_id=cid, has_side_effects=True, vmem_limit_bytes=VLIM)


def columns(r):
    return lambda yy: r.at[:, :, lanes(lax.axis_index("x"), yy)]


def slots(r):
    return lambda yy: r.at[yy]


def pick_flow(src, every, index, out, skip, es, er, gs, gr):
    x, y = lax.axis_index("x"), lax.axis_index("y")
    z, c = lax.axis_index("z"), lax.axis_index("c")
    yield from trade_flow(columns(src), lambda i: every.at[i, z, c], es.at[pl.ds(7, 4)], er.at[pl.ds(7, 4)])
    yield from zc_direct(lambda zz, cc: every.at[:, zz, cc], es, er)
    here = lanes(x, y)

    def block(j):
        a = index[j]
        return every[a >> 4, (a >> 2) & 3, (a >> 1) & 1, a & 1]

    if skip:
        out[0:skip, here] = block(0)[STRETCH - skip : STRETCH]
    for j in range(8):
        out[skip + 64 * j : skip + 64 * (j + 1), here] = block(j + 1)
    yield from gather_columns(out, skip, gs, gr)


PICK_SCRATCH = [
    pltpu.VMEM((4, 4, 2, 2, 64, 128), bf16),
    pltpu.SemaphoreType.DMA((15,)),
    pltpu.SemaphoreType.DMA((15,)),
] + GATHER_SEMS


def spread_gain(line, row, out):
    for i in range(32):
        out[:, 64 * i : 64 * (i + 1)] = line[i // 8, i // 2 % 4, i % 2, row : row + 1, 0:64]


def norm_back(v, gain, dh):
    r = lax.rsqrt(jnp.mean(v * v, axis=-1, keepdims=True) + EPS)
    t = gain * dh
    dv = r * t - v * (r * r * r) * jnp.mean(v * t, axis=-1, keepdims=True)
    return dv, jnp.sum(v * r * dh, axis=0, keepdims=True)


def weight_tiles(left, right, out):
    def tile(t, _):
        v = dot(left(pl.ds(pl.multiple_of(t * 256, 256), 256)), right(), ((0,), (0,))).astype(bf16)
        for k in range(4):
            out[t // 2, lax.rem(t, 2) * 2 + k // 2, k % 2] = v[64 * k : 64 * (k + 1)]
        return 0

    lax.fori_loop(0, 8, tile, 0)


def middle(nv, wa, xrows, gain, wpart, dys, cid, plan=PLANS["middle"]):
    def kernel(nv, wa, xr, gain, wp, dys, m_out, dm_out, dg_out, da_out, dn_out, yp_out, sgu, sd, *refs):
        w, part, part2, h2, hid, dgu, ggu, gd, acc, dgs, refs = *refs[:10], refs[10:]
        sums = [refs[5 * i : 5 * i + 5] for i in range(4)]
        refs = refs[20:]
        gathers = [refs[2 * i : 2 * i + 2] for i in range(4)]
        ws, wr, ls = refs[8:11]
        fgu, fd = refs[11:15], refs[15:19]
        x, y, z, c = (lax.axis_index(a) for a in "xyzc")
        wo = wa.at[:, 896:]
        own = pltpu.make_async_copy(wp, w.at[:, z, c], ls)
        own.start()
        greet(peers(x=(1, 2, 3), y=(1, 2, 3), z=(1, 3), c=(1,)))

        def spread():
            own.wait()
            yield from spread_flow(w, ws, wr)

        weights = spread()

        def flat(ref, rows):
            v = ref[:, :, rows, :]
            return v.reshape(-1, v.shape[-1])

        def grads():
            def first():
                weight_tiles(lambda cols: h2[:, :, :, cols].reshape(SEG, 256), lambda: flat(dgu, slice(0, 32)), ggu)
                yield from sum_flow(ggu, sgu, *fgu)

            def second():
                weight_tiles(lambda cols: dys[:, :, :, cols].reshape(SEG, 256), lambda: flat(hid, slice(0, 32)), gd)
                yield from sum_flow(gd, sd, *fd)

            yield from first()
            yield from second()

        def half(h):
            rows = slice(16 * h, 16 * h + 16)
            nrows = flat(nv, rows)
            for t in range(4):
                cols = slice(512 * t, 512 * (t + 1))
                part[:, :, rows, cols] = dot(nrows, wo[cols, :], ((1,), (1,))).astype(bf16).reshape(4, 4, 16, 512)
            yield from plane_sum(part, acc.at[h], *sums[h], rows)
            m = xr[rows, :].astype(f32) + acc[h]
            m_out[rows, :] = m
            r = lax.rsqrt(jnp.mean(m * m, axis=-1, keepdims=True) + EPS)
            h2[x, y, rows, :] = (m * r * gain[...]).astype(bf16)
            yield from gather_rows(h2, *gathers[h], rows)
            for _ in weights:
                pass
            wv = w[...].reshape(D, NB)
            both = dot(flat(h2, rows), wv[:, : 2 * FFP], ((1,), (0,)))
            ga, up = both[:, :FFP], both[:, FFP:]
            dhid = dot(flat(dys, rows), wv[:, 2 * FFP :], ((1,), (0,)))
            sg = jax.nn.sigmoid(ga)
            act = ga * sg
            hv = (act * up).astype(bf16)
            hid[:, :, rows, :] = hv.reshape(4, 4, 16, FFP)
            dga = (dhid * up * (sg * (1.0 + ga * (1.0 - sg)))).astype(bf16)
            dup = (dhid * act).astype(bf16)
            dgu[:, :, rows, :FFP] = dga.reshape(4, 4, 16, FFP)
            dgu[:, :, rows, FFP:] = dup.reshape(4, 4, 16, FFP)
            dv = jnp.concatenate([dga, dup], axis=1)
            for t in range(4):
                cols = slice(512 * t, 512 * (t + 1))
                part2[:, :, rows, cols] = (
                    dot(dv, wv[cols, : 2 * FFP], ((1,), (1,))).astype(bf16).reshape(4, 4, 16, 512)
                )

            def back():
                yield from plane_sum(part2, acc.at[2 + h], *sums[2 + h], rows)
                dvr, dgain = norm_back(m_out[rows, :], gain[...], acc[2 + h])
                dm = dys[x, y, rows, :].astype(f32) + dvr
                dm_out[rows, :] = dm
                dgs[h : h + 1, :] = dgain
                da_out[x, y, rows, :] = dm.astype(bf16)
                yield from gather_rows(da_out, *gathers[2 + h], rows)
                dn_out[:, :, rows, :] = dot(flat(da_out, rows), wo[...], ((1,), (0,))).reshape(4, 4, 16, DV)

            def result():
                yield
                for t in range(4):
                    cols = slice(512 * t, 512 * (t + 1))
                    yp_out[:, :, rows, cols] = (
                        dot(hv, wv[cols, 2 * FFP :], ((1,), (1,))).astype(bf16).reshape(4, 4, 16, 512)
                    )

            yield from together([back(), result()] + ([grads()] if h else []))

        run([half(0), half(1), weights], plan)
        dg_out[...] = dgs[0:1, :] + dgs[1:2, :]

    gu, gdown = (4, 4, 2, 64, 2 * FFP), (4, 4, 2, 64, FFP)
    return pl.pallas_call(
        kernel,
        out_shape=[
            shape((32, D)),
            shape((32, D)),
            shape((1, D)),
            shape((4, 4, 32, D), bf16),
            shape((4, 4, 32, DV)),
            shape((4, 4, 32, D), bf16),
            shape((4, 64, 2 * FFP), bf16),
            shape((4, 64, FFP), bf16),
        ],
        in_specs=[VM] * 6,
        out_specs=[VM] * 8,
        scratch_shapes=[
            pltpu.VMEM((4, 4, 2, 64, NB), bf16),
            pltpu.VMEM((4, 4, 32, D), bf16),
            pltpu.VMEM((4, 4, 32, D), bf16),
            pltpu.VMEM((4, 4, 32, D), bf16),
            pltpu.VMEM((4, 4, 32, FFP), bf16),
            pltpu.VMEM((4, 4, 32, 2 * FFP), bf16),
            pltpu.VMEM(gu, bf16),
            pltpu.VMEM(gdown, bf16),
            pltpu.VMEM((4, 16, D), f32),
            pltpu.VMEM((2, D), f32),
        ]
        + scatter_buffers(16) * 4
        + GATHER_SEMS * 4
        + [pltpu.SemaphoreType.DMA((11,)), pltpu.SemaphoreType.DMA((11,)), pltpu.SemaphoreType.DMA]
        + sum_scratch(gu[3:], bf16)
        + sum_scratch(gdown[3:], bf16),
        compiler_params=remote_params(cid),
    )(nv, wa, xrows, gain, wpart, dys)


def home_flow(src, dst, order, alls, cols, picks, s1, r1, s2, r2, s3, r3):
    x, y, z, c = (lax.axis_index(a) for a in "xyzc")
    n = src.shape[0]
    sends = []
    cols[x, y] = src[:, :, lanes(x, y)]
    t = 0
    for i in range(4):
        for j in range(4):
            if (i, j) == (0, 0):
                continue
            px, py = at("x", i), at("y", j)
            sends.append(send(src.at[:, :, lanes(px, py)], cols.at[x, y], s1.at[t], r1.at[t], {"x": px, "y": py}))
            t += 1
    yield
    for cp in sends:
        cp.wait_recv()
    for k in range(n):
        alls[z, c, k] = cols[:, :, k].reshape(8, 64, 128)
    yield from zc_direct(lambda zz, cc: alls.at[zz, cc], s2, r2)
    for j in range(4):
        for i in range(2):
            b = order[j * 16 + (z * 2 + c) * 2 + i]
            for k in range(n):
                picks[j, k, 64 * i : 64 * (i + 1)] = alls[b >> 4, (b >> 3) & 1, k, b & 7]
    mine = pl.ds(pl.multiple_of(y * 128, 128), 128)
    last = [
        send(picks.at[at("y", j)], dst.at[:, :, mine], s3.at[j], r3.at[j], {"y": at("y", j)}) for j in (2, 1, 3)
    ]
    dst[:, :, mine] = picks[y]
    yield
    for cp in last:
        cp.wait_recv()
    for cp in sends + last:
        cp.wait_send()


HOME_SCRATCH = [
    pltpu.VMEM((4, 2, 2, 8, 64, 128), bf16),
    pltpu.VMEM((4, 4, 2, 32, 128), bf16),
    pltpu.VMEM((4, 2, 128, 128), bf16),
    pltpu.SemaphoreType.DMA((15,)),
    pltpu.SemaphoreType.DMA((15,)),
    pltpu.SemaphoreType.DMA((7,)),
    pltpu.SemaphoreType.DMA((7,)),
    pltpu.SemaphoreType.DMA((4,)),
    pltpu.SemaphoreType.DMA((4,)),
]


def sum_flow(g, stage, core, bufs, ss, rs):
    c = lax.axis_index("c")
    d = send(g.at[:, :, 1 - c], core, ss.at[0], rs.at[0], {"c": 1 - c})
    yield
    d.wait_recv()

    def ready(i):
        for k in range(4):
            core[k, i] = core[k, i] + g[k, i, c]

    def emit(s, v):
        stage[2 * s : 2 * s + 2] = v.astype(stage.dtype)

    def piece(i, s):
        return core.at[2 * s : 2 * s + 2, i]

    yield from ring_scatter("z", piece, ready, bufs, emit, ss.at[pl.ds(1, 6)], rs.at[pl.ds(1, 6)])
    d.wait_send()


def sum_scratch(dims, kind):
    return [
        pltpu.VMEM((4, 4) + dims, kind),
        pltpu.VMEM((6, 2) + dims, kind),
        pltpu.SemaphoreType.DMA((7,)),
        pltpu.SemaphoreType.DMA((7,)),
    ]


TRADE_SEMS = [pltpu.SemaphoreType.DMA((4,)), pltpu.SemaphoreType.DMA((4,))]


def scatter_flow(g, out, stage, ts, tr, *sums):
    yield from sum_flow(g, stage, *sums)
    yield from trade_flow(slots(stage), lambda y: out.at[y], ts, tr)


def scatter_scratch(dims, kind):
    return [pltpu.VMEM((4,) + dims, kind)] + TRADE_SEMS + sum_scratch(dims, kind)


def dot(a, b, dims, prec=None):
    return lax.dot_general(a, b, (dims, ((), ())), preferred_element_type=f32, precision=prec)


def lo(a):
    return a.astype(bf16)


def mm(a, b):
    return dot(lo(a), lo(b), ((1,), (0,)))


def mmt(a, b):
    return dot(lo(a), lo(b), ((1,), (1,)))


def tmm(a, b):
    return dot(lo(a), lo(b), ((0,), (0,)))


def halves_of(a):
    h = a.astype(bf16)
    return h, (a - h.astype(f32)).astype(bf16)


def fine(a, b, dims=((1,), (0,))):
    ah, al = halves_of(a)
    bh, bl = halves_of(b)
    return dot(ah, bh, dims) + (dot(ah, bl, dims) + dot(al, bh, dims))


def tri_inverse(a, r, c):
    eye = jnp.where(r == c, 1.0, 0.0)
    n1 = jnp.where((r >> 3) == (c >> 3), -a, 0.0)
    n2 = fine(n1, n1)
    n4 = fine(n2, n2)
    t = eye + n1
    t = t + fine(t, n2)
    t = t + fine(t, n4)
    for level in (3, 4, 5, 6):
        off = ((r >> (level + 1)) == (c >> (level + 1))) & ((r >> level) != (c >> level))
        t = t - fine(t, fine(jnp.where(off, a, 0.0), t))
    return t


def iotas():
    return (
        lax.broadcasted_iota(i32, (CH, CH), 0),
        lax.broadcasted_iota(i32, (CH, CH), 1),
    )


def filtered(z, cw, mc, cols):
    total = z[HALO : HALO + SEG, cols] * cw[3:4, cols]
    for j in range(3):
        total = total + mc[:, j : j + 1] * cw[j : j + 1, cols] * z[HALO - 3 + j : HALO - 3 + j + SEG, cols]
    return total


def silu(v):
    return v * jax.nn.sigmoid(v)


QC, KC, VC = slice(0, 128), slice(128, 256), slice(256, 512)


def decay_of(cc, cr, mask):
    return jnp.exp(jnp.where(mask, cc - cr, 0.0)) * jnp.where(mask, 1.0, 0.0)


def prepare(z, ab, cw, sc, mc, mr, qkv, tm, wu, gb, cr, ti):
    r, c = iotas()
    for cols, scale in ((QC, DK**-0.5), (KC, 1.0)):
        s = silu(filtered(z, cw, mc, cols))
        qkv[:, cols] = (s * lax.rsqrt(jnp.sum(s * s, axis=-1, keepdims=True) + EPS) * scale).astype(bf16)
    qkv[:, VC] = silu(filtered(z, cw, mc, VC)).astype(bf16)
    low = jnp.where(r >= c, 1.0, 0.0)
    eye = jnp.where(r == c, 1.0, 0.0)
    lane = lax.broadcasted_iota(i32, (CH, 128), 1)
    transit = eye
    insert = jnp.zeros((DK, DV), f32)
    yield
    for n in range(NCH):
        rows = slice(n * CH, (n + 1) * CH)
        raw = ab[HALO + n * CH : HALO + (n + 1) * CH, :]
        beta = jax.nn.sigmoid(raw[:, 1:2])
        u = raw + sc[0:1, 1:2]
        g = -jnp.exp(sc[0:1, 0:1]) * (jnp.maximum(u, 0.0) + jnp.log1p(jnp.exp(-jnp.abs(u))))
        g = jnp.where(lane == 0, g, 0.0)
        cum = dot(low, g, ((1,), (0,)), HI)[:, 0:1]
        cumr = dot(g, low, ((0,), (1,)), HI)[0:8, :]
        gb[rows, :] = jnp.where(lane == 0, beta, cum)
        cr[:, rows] = cumr
        cumrow = cumr[0:1, :]
        last = cumr[0:1, CH - 1 : CH]
        m = mc[rows, :]
        carried, closing, begin, carry_last = m[:, 3:4], m[:, 4:5], m[:, 5:6], m[0:1, 6:7]
        same = begin == mr[0:1, rows]
        k = qkv[rows, KC]
        kf = k.astype(f32)
        v = qkv[rows, VC].astype(f32)
        a = beta * dot(k, k, ((1,), (1,))) * decay_of(cum, cumrow, same & (r > c))
        t = tri_inverse(a, r, c)
        tm[rows, :] = t
        lead = (beta * jnp.exp(cum) * carried) * kf
        w = fine(t, lead)
        uu = fine(t, beta * v)
        wu[rows, 0:DK] = w
        wu[rows, DK:] = uu
        tail = kf * (jnp.exp(last - cum) * closing)
        keep = jnp.exp(last) * carry_last
        hand = keep * eye - fine(tail, w, ((0,), (0,)))
        insert = fine(hand, insert) + fine(tail, uu, ((0,), (0,)))
        transit = fine(hand, transit)
        yield
    ti[:, 0:DK] = transit.astype(bf16)
    ti[:, DK:] = insert.astype(bf16)


def emit_outputs(seg, maps, qkv, wu, gb, cr, mc, mr, gp, hg, nout, oout, fout, sout):
    r, c = iotas()

    def fold(d, s):
        tr, ins = maps[d, :, 0:DK], maps[d, :, DK:].astype(f32)
        sh, sl = halves_of(s)
        new = dot(tr, sh, ((1,), (0,))) + dot(tr, sl, ((1,), (0,))) + ins
        return jnp.where(d < seg, new, s)

    s = lax.fori_loop(0, 7, fold, jnp.zeros((DK, DV), f32))
    for n in range(NCH):
        rows = slice(n * CH, (n + 1) * CH)
        m = mc[rows, :]
        carried, closing, begin, carry_last = m[:, 3:4], m[:, 4:5], m[:, 5:6], m[0:1, 6:7]
        cum = gb[rows, 1:2]
        cumrow = cr[0:1, rows]
        last = cr[0:1, n * CH + CH - 1 : n * CH + CH]
        same = begin == mr[0:1, rows]
        q, k = qkv[rows, QC], qkv[rows, KC]
        p = dot(q, k, ((1,), (1,))) * decay_of(cum, cumrow, same & (r >= c))
        fresh = wu[rows, DK:] - fine(wu[rows, 0:DK], s)
        qd = q.astype(f32) * (jnp.exp(cum) * carried)
        o = mm(qd, s) + mm(p, fresh)
        sout[n] = s
        fout[rows, :] = fresh
        oout[rows, :] = o
        x = gp[HALO + n * CH : HALO + (n + 1) * CH, :]
        rn = lax.rsqrt(jnp.mean(o * o, axis=-1, keepdims=True) + EPS)
        nout[rows, :] = (o * rn * hg[0:1, :] * silu(x)).astype(bf16)
        tail = k.astype(f32) * (jnp.exp(last - cum) * closing)
        s = (jnp.exp(last) * carry_last) * s + fine(tail, fresh, ((0,), (0,)))
        yield


def back_emit(dn, o, gp, hg, qkv, wu, gb, cr, mc, mr, do_out, dgp_out, dhg_out, e_out):
    r, c = iotas()
    dhg = jnp.zeros((1, DV), f32)
    e = jnp.zeros((DK, DV), f32)
    for n in reversed(range(NCH)):
        rows = slice(n * CH, (n + 1) * CH)
        ov, x, dnv = o[rows, :], gp[HALO + n * CH : HALO + (n + 1) * CH, :], dn[rows, :]
        rn = lax.rsqrt(jnp.mean(ov * ov, axis=-1, keepdims=True) + EPS)
        sg = jax.nn.sigmoid(x)
        act = x * sg
        h = hg[0:1, :]
        base = ov * rn
        dhg = dhg + jnp.sum(base * act * dnv, axis=0, keepdims=True)
        dgp_out[rows, :] = (dnv * base * h * (sg * (1.0 + x * (1.0 - sg)))).astype(bf16)
        t = dnv * h * act
        do = rn * t - base * (rn * rn) * jnp.mean(ov * t, axis=-1, keepdims=True)
        do_out[rows, :] = do
        m = mc[rows, :]
        carried, closing, begin, carry_last = m[:, 3:4], m[:, 4:5], m[:, 5:6], m[0:1, 6:7]
        cum = gb[rows, 1:2]
        cumrow = cr[0:1, rows]
        last = cr[0:1, n * CH + CH - 1 : n * CH + CH]
        same = begin == mr[0:1, rows]
        q, k = qkv[rows, QC], qkv[rows, KC]
        p = dot(q, k, ((1,), (1,))) * decay_of(cum, cumrow, same & (r >= c))
        qd = q.astype(f32) * (jnp.exp(cum) * carried)
        tail = k.astype(f32) * (jnp.exp(last - cum) * closing)
        df = tmm(p, do) + mm(tail, e)
        e = tmm(qd, do) + (jnp.exp(last) * carry_last) * e - tmm(wu[rows, 0:DK], df)
        yield
    dhg_out[...] = dhg
    e_out[...] = e.astype(bf16)


def back_delta(seg, maps, tails, do, fr, st, qkv, tm, wu, gb, cr, z, ab, cw, sc, mc, mr, dz, dab, dcw, dsc, dqkv):
    r, c = iotas()
    low = jnp.where(r >= c, 1.0, 0.0)
    ones = jnp.ones((CH, CH), f32)
    lane = lax.broadcasted_iota(i32, (CH, 128), 1)
    row = lax.broadcasted_iota(i32, (CH, 1), 0)

    def fold(i, e):
        d = 7 - i
        tr, own = maps[d, :, 0:DK], tails[d].astype(f32)
        eh, el = halves_of(e)
        new = dot(tr, eh, ((0,), (0,))) + dot(tr, el, ((0,), (0,))) + own
        return jnp.where(d > seg, new, e)

    e = lax.fori_loop(0, 7, fold, jnp.zeros((DK, DV), f32))
    acc_a = jnp.zeros((1, 128), f32)
    acc_d = jnp.zeros((1, 128), f32)
    for n in reversed(range(NCH)):
        rows = slice(n * CH, (n + 1) * CH)
        m = mc[rows, :]
        carried, closing, begin, carry_last = m[:, 3:4], m[:, 4:5], m[:, 5:6], m[0:1, 6:7]
        beta, cum = gb[rows, 0:1], gb[rows, 1:2]
        cumrow = cr[0:1, rows]
        last = cr[0:1, n * CH + CH - 1 : n * CH + CH]
        same = begin == mr[0:1, rows]
        q, k = qkv[rows, QC], qkv[rows, KC]
        qf, kf, vf = q.astype(f32), k.astype(f32), qkv[rows, VC].astype(f32)
        dec_i = decay_of(cum, cumrow, same & (r >= c))
        dec_s = jnp.where(r > c, dec_i, 0.0)
        p = dot(q, k, ((1,), (1,))) * dec_i
        kkd = dot(k, k, ((1,), (1,))) * dec_s
        ex = jnp.exp(cum) * carried
        tf = jnp.exp(last - cum) * closing
        keep = jnp.exp(last) * carry_last
        tail = kf * tf
        qd = qf * ex
        dov, fv, sv, tv = do[rows, :], fr[rows, :], st[n], tm[rows, :]
        w, u = wu[rows, 0:DK], wu[rows, DK:]
        df = tmm(p, dov) + mm(tail, e)
        dw = -mmt(df, sv)
        dtail = mmt(fv, e)
        dkeep = jnp.sum(jnp.sum(sv * e, axis=1, keepdims=True), axis=0, keepdims=True)
        dqd = mmt(dov, sv)
        dp = mmt(dov, fv)
        dlead = tmm(tv, dw)
        dbv = tmm(tv, df)
        da = -(mmt(dlead, w) + mmt(dbv, u))
        dakd = da * kkd
        dkk = da * beta * dec_s
        dqk = dp * dec_i
        mix = dakd * beta + dp * p
        dqkv[rows, QC] = mm(dqk, k) + dqd * ex
        dqkv[rows, KC] = (
            tmm(dqk, q) + mm(dkk, k) + tmm(dkk, k) + dlead * (beta * ex) + dtail * tf
        )
        dqkv[rows, VC] = beta * dbv
        lk = jnp.sum(dlead * kf, axis=1, keepdims=True) * ex
        dbeta = jnp.sum(dakd, axis=1, keepdims=True) + lk + jnp.sum(dbv * vf, axis=1, keepdims=True)
        tt = jnp.sum(dtail * tail, axis=1, keepdims=True)
        dcum = jnp.sum(mix, axis=1, keepdims=True) + jnp.sum(dqd * qd, axis=1, keepdims=True) + lk * beta - tt
        dcum = dcum + jnp.where(row == CH - 1, jnp.sum(tt, axis=0, keepdims=True) + dkeep * keep, 0.0)
        full = dcum - dot(mix, ones, ((0,), (0,)), HI)
        dg = dot(low, full, ((0,), (0,)), HI)
        raw = ab[HALO + n * CH : HALO + (n + 1) * CH, :]
        uu = raw + sc[0:1, 1:2]
        rate = -jnp.exp(sc[0:1, 0:1])
        sp = jnp.maximum(uu, 0.0) + jnp.log1p(jnp.exp(-jnp.abs(uu)))
        dal = dg * rate * jax.nn.sigmoid(uu)
        acc_a = acc_a + jnp.sum(dg * rate * sp, axis=0, keepdims=True)
        acc_d = acc_d + jnp.sum(dal, axis=0, keepdims=True)
        dab[rows, :] = jnp.where(
            lane == 0, dal, jnp.where(lane == 1, dbeta * beta * (1.0 - beta), 0.0)
        ).astype(bf16)
        e = tmm(qd, dov) + keep * e - tmm(w, df)
        yield
    dsc[0:1, :] = acc_a
    dsc[1:2, :] = acc_d
    dz[0:HALO, :] = jnp.zeros((HALO, 512), f32)
    for cols, scale in ((QC, DK**-0.5), (KC, 1.0), (VC, None)):
        y = filtered(z, cw, mc, cols)
        sg = jax.nn.sigmoid(y)
        ds = dqkv[:, cols]
        if scale is not None:
            s = y * sg
            rn = lax.rsqrt(jnp.sum(s * s, axis=-1, keepdims=True) + EPS)
            ds = scale * (rn * ds - s * (rn * rn * rn) * jnp.sum(s * ds, axis=-1, keepdims=True))
        dy = ds * (sg * (1.0 + y * (1.0 - sg)))
        dz[HALO : HALO + SEG, cols] = dy * cw[3:4, cols]
        dcw[3:4, cols] = jnp.sum(dy * z[HALO : HALO + SEG, cols], axis=0, keepdims=True)
        for j in range(3):
            part = mc[:, j : j + 1] * dy
            away = slice(HALO - 3 + j, HALO - 3 + j + SEG)
            dcw[j : j + 1, cols] = jnp.sum(part * z[away, cols], axis=0, keepdims=True)
            dz[away, cols] = dz[away, cols] + part * cw[j : j + 1, cols]
        yield


def map_gather(own, out, ss, rs):
    z, c = lax.axis_index("z"), lax.axis_index("c")
    out[z, c] = own[...]
    yield from zc_direct(lambda zz, cc: out.at[zz, cc], ss, rs)


class Maps:
    def __init__(self, ref):
        self.ref = ref

    def __getitem__(self, key):
        key = key if isinstance(key, tuple) else (key,)
        return self.ref[(key[0] // 2, key[0] % 2) + key[1:]]


def masks(lens, mc, mr):
    base = (lax.axis_index("z") * 2 + lax.axis_index("c")) * SEG
    firsts = [jnp.int32(0)]
    for k in range(3):
        firsts.append(firsts[k] + lens[k])

    def begin_of(pos):
        b = jnp.zeros_like(pos)
        for k in range(1, 4):
            b = jnp.where((pos >= firsts[k]) & (pos < firsts[k] + lens[k]), firsts[k], b)
        return b

    lane = lax.broadcasted_iota(i32, (CH, 128), 1)
    for n in range(NCH):
        first = base + n * CH
        pos = first + lax.broadcasted_iota(i32, (CH, 128), 0)
        b = begin_of(pos)
        last = begin_of(jnp.full((CH, 128), first + CH - 1, i32))

        def one(flag):
            return jnp.where(flag, 1.0, 0.0)

        late = jnp.where(lane == 3, one(b < first), jnp.where(lane == 4, one(b == last), one(last < first)))
        flags = jnp.where(lane < 3, one(pos - 3 + lane >= b), late)
        mc[n * CH : (n + 1) * CH, :] = jnp.where(lane == 5, b.astype(f32), flags)
        mr[:, n * CH : (n + 1) * CH] = begin_of(first + lax.broadcasted_iota(i32, (8, CH), 1)).astype(f32)


def spread_lanes(v, wide, first):
    n = 32 * wide
    owner = lax.broadcasted_iota(i32, (32, n), 0) == lax.broadcasted_iota(i32, (32, n), 1) // wide
    place = lax.broadcasted_iota(i32, (n, 128), 1) == first + lax.rem(lax.broadcasted_iota(i32, (n, 128), 0), wide)
    return dot(jnp.where(owner, v, 0.0), jnp.where(place, 1.0, 0.0), ((1,), (0,)), HI)


def gather_lanes(rows, wide, first):
    n = 32 * wide
    owner = lax.broadcasted_iota(i32, (32, n), 0) == lax.broadcasted_iota(i32, (32, n), 1) // wide
    place = lax.broadcasted_iota(i32, (128, n), 0) == first + lax.rem(lax.broadcasted_iota(i32, (128, n), 1), wide)
    every = dot(rows, jnp.where(place, 1.0, 0.0), ((1,), (0,)), HI)
    return jnp.sum(jnp.where(owner, every, 0.0), axis=0, keepdims=True)


def front(order, lens, a_log, dt_bias, tokens, cotangent, weights, wide_weights, convs, gains, cid, plan=PLANS["front"]):
    npk = len(PICK_SCRATCH)

    def kernel(
        order, lens, al, dt, tok, cot, wq, wk, wv, wg, wal, wbe, wou, wga, wup, wdo, cvq, cvk, cvv, hgi, g1i, g2i,
        wa, gain1, gain2, xr, h1, proj, cw, hg, wp, dyo, qkv, tm, wu, gb, cr, maps, nout, oout, fout, sout, mc, mr, sc,
        pack, pack_b, tiny, line, tops, xo, ti, index, *refs,
    ):
        pick_x, pick_y, refs = refs[:npk], refs[npk : 2 * npk], refs[2 * npk :]
        ss, rs, ms, mq, ts, tr = refs
        x, y, z, c = (lax.axis_index(a) for a in "xyzc")
        seg = z * 2 + c
        zq, gp, ab = proj.at[:, 0:512], proj.at[:, 512:768], proj.at[:, 768:896]

        diag = lax.broadcasted_iota(i32, (64, 64), 0) == lax.broadcasted_iota(i32, (64, 64), 1)
        lane = lax.broadcasted_iota(i32, (64, 128), 1)
        for i in range(4):
            for ref, cols in ((wq, QC), (wk, KC), (wv, VC), (wg, slice(512, 768))):
                pack[i, :, cols] = ref[:, i, :].astype(bf16)
            alpha, beta = (jnp.sum(jnp.where(diag, r[i : i + 1, :], 0.0), axis=1, keepdims=True) for r in (wal, wbe))
            pack[i, :, 768:896] = jnp.where(lane == 0, alpha, jnp.where(lane == 1, beta, 0.0)).astype(bf16)
            pack[i, :, 896:1152] = wou[i].astype(bf16)
        tiny[...] = jnp.zeros(tiny.shape, f32)
        for i in range(4):
            for ref, n, first in ((cvq, 4, 0), (cvk, 4, 16), (cvv, 8, 32)):
                for j in range(4):
                    tiny[i, 0:1, first + n * j : first + n * (j + 1)] = ref[j, i : i + 1, :]
            tiny[i, 0:1, 64:72] = hgi[...]
            tiny[i, 1:2, 0:64] = g1i[...]
            tiny[i, 2:3, 0:64] = g2i[...]
        tiny[...] = tiny[...].astype(bf16).astype(f32)

        def find(a, found):
            return tuple(jnp.where(order[a] == jnp.maximum(seg * 8 - 1 + j, 0), a, f) for j, f in enumerate(found))

        for j, f in enumerate(lax.fori_loop(0, 64, find, tuple(jnp.int32(0) for _ in range(9)))):
            index[j] = f
        greet(peers(y=(1, 2, 3), z=(1, 2, 3), c=(1,), x=(1, 2, 3)))

        def small():
            se, re = ss.at[0], rs.at[0]
            yield from trade_flow(slots(tiny), lambda i: line.at[i, z, c], se.at[pl.ds(7, 4)], re.at[pl.ds(7, 4)])
            yield from zc_direct(lambda zz, cc: line.at[:, zz, cc], se, re)
            spread_gain(line, 1, gain1)
            spread_gain(line, 2, gain2)
            for i in range(32):
                tops[i : i + 1, :] = line[i // 8, i // 2 % 4, i % 2, 0:1, :]
            top = tops[...]
            for j in range(4):
                cw[j : j + 1, QC] = gather_lanes(top, 4, 4 * j)
                cw[j : j + 1, KC] = gather_lanes(top, 4, 16 + 4 * j)
                cw[j : j + 1, VC] = gather_lanes(top, 8, 32 + 8 * j)
            hg[...] = gather_lanes(top, 8, 64)

        def main():
            yield from pick_flow(tok, pick_x[0], index, xo, HALO, *pick_x[1:])
            for _ in lines:
                pass

            def norm(t, _):
                at_rows = pl.ds(pl.multiple_of(t * 16, 16), 16)
                v = xo[at_rows, :].astype(f32)
                r = lax.rsqrt(jnp.mean(v * v, axis=-1, keepdims=True) + EPS)
                h1[at_rows, :] = (v * r * gain1[...]).astype(bf16)
                return 0

            lax.fori_loop(0, ROWS // 16, norm, 0)
            xr[...] = xo[pl.ds(pl.multiple_of(HALO + 32 * (x * 4 + y), 16), 32), :]
            masks(lens, mc, mr)
            sc[0:8, :] = jnp.where(lax.broadcasted_iota(i32, (8, 128), 1) == 0, al[y], dt[y])
            yield
            for _ in fetched:
                pass
            for cols in (slice(0, 256), slice(256, 512), slice(512, 768), slice(768, 896)):
                w = wa[:, :, :, :, cols]
                proj[:, cols] = dot(h1[...], w.reshape(D, w.shape[-1]), ((1,), (0,)))
            yield
            yield from prepare(zq, ab, cw, sc, mc, mr, qkv, tm, wu, gb, cr, ti)
            yield from map_gather(ti, maps, ms, mq)
            yield from emit_outputs(seg, Maps(maps), qkv, wu, gb, cr, mc, mr, gp, hg, nout, oout, fout, sout)

        def trade_wide():
            ff = wga.shape[1]
            for i in range(4):
                n = min(FFP, ff - FFP * i)
                cols = slice(FFP * i, FFP * i + n)
                for k, v in enumerate((wga[:, cols], wup[:, cols], wdo[:, cols])):
                    pack_b[i, :, FFP * k : FFP * k + n] = v.astype(bf16)
                    if n < FFP:
                        pack_b[i, :, FFP * k + n : FFP * (k + 1)] = jnp.zeros((64, FFP - n), bf16)
            yield from trade_flow(slots(pack_b), lambda i: wp.at[i], ts, tr)

        lines, fetched = small(), exchange_flow(slots(pack), wa, ss.at[1], rs.at[1])
        run([main(), lines, fetched, pick_flow(cot, pick_y[0], index, dyo, 0, *pick_y[1:]), trade_wide()], plan)

    return pl.pallas_call(
        kernel,
        out_shape=[
            shape((4, 4, 2, 64, NA), bf16),
            shape((1, D)),
            shape((1, D)),
            shape((32, D), bf16),
            shape((ROWS, D), bf16),
            shape((ROWS, 896)),
            shape((4, 512)),
            shape((1, DV)),
            shape((4, 64, NB), bf16),
            shape((SEG, D), bf16),
            shape((SEG, 512), bf16),
            shape((SEG, CH)),
            shape((SEG, DK + DV)),
            shape((SEG, 128)),
            shape((8, SEG)),
            shape((4, 2, DK, DK + DV), bf16),
            shape((SEG, DV), bf16),
            shape((SEG, DV)),
            shape((SEG, DV)),
            shape((NCH, DK, DV)),
            shape((SEG, 128)),
            shape((8, SEG)),
            shape((8, 128)),
        ],
        in_specs=[SM] * 4 + [VM] * 18,
        out_specs=[VM] * 23,
        scratch_shapes=[
            pltpu.VMEM((4, 64, NA), bf16),
            pltpu.VMEM((4, 64, NB), bf16),
            pltpu.VMEM((4, 8, 128), f32),
            pltpu.VMEM((4, 4, 2, 8, 128), f32),
            pltpu.VMEM((32, 128), f32),
            pltpu.VMEM((ROWS, D), bf16),
            pltpu.VMEM((DK, DK + DV), bf16),
            pltpu.SMEM((16,), i32),
        ]
        + PICK_SCRATCH * 2
        + [
            pltpu.SemaphoreType.DMA((2, 15)),
            pltpu.SemaphoreType.DMA((2, 15)),
            pltpu.SemaphoreType.DMA((11,)),
            pltpu.SemaphoreType.DMA((11,)),
        ]
        + TRADE_SEMS,
        compiler_params=remote_params(cid),
    )(order, lens, a_log, dt_bias, tokens, cotangent, *weights, *wide_weights, *convs, *gains)


def in_order(flows, plan):
    for i in plan:
        next(flows[int(i)], None)
        yield
    yield from together(flows)


def back(dn, o, proj, hg, qkv, tm, wu, gb, cr, mc, mr, maps, fr, st, cw, sc, m, ypart, sgu, sd, da, nv, order, xrows, dm, gain, h1, wa, dgain2, cid, plan=PLANS["back"]):
    nh, ns, nc = len(HOME_SCRATCH), 7, len(SCATTER_SCRATCH)

    def kernel(
        dn, o, proj, hg, qkv, tm, wu, gb, cr, mc, mr, maps, fr, st, cw, sc, m, ypart, sgu, sd, da, nv, order, xr, dm, gain, h1, wa, dgain2,
        both, g_out, ro, rgu, rd, t_out, tot,
        dproj, dhg, dcw, dsc, do, dgp, e, tails, dz, dab, dqkv, edge, ms, mq, ds, dq, acc, grad_o, part, acc2, grad, line, rows, xr4, xs, xq, *refs,
    ):
        sum_y, sum_x, refs = refs[:nc], refs[nc : 2 * nc], refs[2 * nc :]
        home, refs = refs[:nh], refs[nh:]
        so, sg, st_, trades = refs[:ns], refs[ns : 2 * ns], refs[2 * ns : 3 * ns], refs[3 * ns :]
        zq, gp, ab = proj.at[:, 0:512], proj.at[:, 512:768], proj.at[:, 768:896]
        x = lax.axis_index("x")
        seg = lax.axis_index("z") * 2 + lax.axis_index("c")
        greet(plane_peers() + segment_peers())

        def main():
            yield from back_emit(dn, o, gp, hg, qkv, wu, gb, cr, mc, mr, do, dgp, dhg, e)
            yield from map_gather(e, tails, ms, mq)
            yield from back_delta(
                seg, Maps(maps), Maps(tails), do, fr, st, qkv, tm, wu, gb, cr, zq, ab, cw, sc, mc, mr, dz, dab, dcw, dsc, dqkv
            )
            before = lax.rem(seg + 7, 8)
            cp = send(dz.at[0:HALO], edge, ds, dq, {"z": before // 2, "c": lax.rem(before, 2)})
            dproj[0 : SEG - HALO, 0:512] = dz[HALO:SEG].astype(bf16)
            dproj[:, 512:768] = dgp[...]
            dproj[:, 768:896] = dab[...]
            yield
            cp.wait_recv()
            dproj[SEG - HALO : SEG, 0:512] = (dz[SEG:ROWS] + jnp.where(seg < 7, edge[...], 0.0)).astype(bf16)
            cp.wait_send()
            for t in range(4):
                cols = slice(512 * t, 512 * (t + 1))
                part[:, :, :, cols] = dot(dproj[...], wa[cols, 0:896], ((1,), (1,))).astype(bf16).reshape(4, 4, 32, 512)
            yield from in_order([input_grads(), weight_grads()], "011010")

        def result():
            yield from plane_sum(ypart, acc, *sum_y)
            rows[0] = (m[...] + acc[...]).astype(bf16)

        def output_grads():
            weight_tiles(lambda cols: da[:, cols], lambda: nv[...], grad_o)
            yield from scatter_flow(grad_o, ro, *so)

        def weight_grads():
            weight_tiles(lambda cols: h1[HALO:, cols], lambda: dproj[...], grad)
            yield from scatter_flow(grad, g_out, *sg)

        def small_grads():
            yield from scatter_flow(line, t_out, *st_)
            xr4[x] = (t_out[0] + t_out[1]) + (t_out[2] + t_out[3])
            sends = [send(xr4.at[x], xr4.at[x], xs.at[k], xq.at[k], {"x": at("x", k)}) for k in (2, 1, 3)]
            yield
            for cp in sends:
                cp.wait_recv()
            tot[...] = (xr4[0] + xr4[1]) + (xr4[2] + xr4[3])
            for cp in sends:
                cp.wait_send()

        def fill_lines():
            lane = lax.broadcasted_iota(i32, (32, 128), 1)
            top = jnp.where(lane == 72, dsc[0:1, 0:1], 0.0) + jnp.where(lane == 73, dsc[1:2, 0:1], 0.0)
            for j in range(4):
                top = top + spread_lanes(dcw[j : j + 1, QC], 4, 4 * j) + spread_lanes(dcw[j : j + 1, KC], 4, 16 + 4 * j)
                top = top + spread_lanes(dcw[j : j + 1, VC], 8, 32 + 8 * j)
            top = top + spread_lanes(dhg[...], 8, 64)
            line[...] = jnp.zeros(line.shape, f32)
            for i in range(32):
                line[i // 8, i // 2 % 4, i % 2, 0:1, :] = top[i : i + 1]
                line[i // 8, i // 2 % 4, i % 2, 2:3, 0:64] = dgain2[:, 64 * i : 64 * (i + 1)]

        def input_grads():
            sums = plane_sum(part, acc2, *sum_x)
            next(sums)
            fill_lines()
            yield
            yield from sums
            dvr, dgain = norm_back(xr[...].astype(f32), gain[...], acc2[...])
            for _ in outcome:
                pass
            rows[1] = (dm[...] + dvr).astype(bf16)
            for i in range(32):
                line[i // 8, i // 2 % 4, i % 2, 1:2, 0:64] = dgain[:, 64 * i : 64 * (i + 1)]
            yield from together([home_flow(rows, both, order, *home), small_grads()])

        def trade(staged, out, sems):
            yield from trade_flow(slots(staged), lambda y: out.at[y], *sems)

        outcome = result()
        run([main(), outcome, output_grads(), trade(sgu, rgu, trades[0:2]), trade(sd, rd, trades[2:4])], plan)

    td, gd, god = (8, 128), (64, 896), (64, DV)
    return pl.pallas_call(
        kernel,
        out_shape=[
            shape((2, 128, 512), bf16),
            shape((4,) + gd, bf16),
            shape((4,) + god, bf16),
            shape(sgu.shape, bf16),
            shape(sd.shape, bf16),
            shape((4,) + td),
            shape(td),
        ],
        in_specs=[VM] * 22 + [SM] + [VM] * 6,
        out_specs=[VM] * 7,
        scratch_shapes=[
            pltpu.VMEM((SEG, 896), bf16),
            pltpu.VMEM((1, DV), f32),
            pltpu.VMEM((4, 512), f32),
            pltpu.VMEM((2, 128), f32),
            pltpu.VMEM((SEG, DV), f32),
            pltpu.VMEM((SEG, DV), bf16),
            pltpu.VMEM((DK, DV), bf16),
            pltpu.VMEM((4, 2, DK, DV), bf16),
            pltpu.VMEM((ROWS, 512), f32),
            pltpu.VMEM((SEG, 128), bf16),
            pltpu.VMEM((SEG, 512), f32),
            pltpu.VMEM((HALO, 512), f32),
            pltpu.SemaphoreType.DMA((11,)),
            pltpu.SemaphoreType.DMA((11,)),
            pltpu.SemaphoreType.DMA,
            pltpu.SemaphoreType.DMA,
            pltpu.VMEM((32, D), f32),
            pltpu.VMEM((4, 4, 2) + god, bf16),
            pltpu.VMEM((4, 4, 32, D), bf16),
            pltpu.VMEM((32, D), f32),
            pltpu.VMEM((4, 4, 2) + gd, bf16),
            pltpu.VMEM((4, 4, 2) + td, f32),
            pltpu.VMEM((2, 32, D), bf16),
            pltpu.VMEM((4,) + td, f32),
            pltpu.SemaphoreType.DMA((4,)),
            pltpu.SemaphoreType.DMA((4,)),
        ]
        + SCATTER_SCRATCH * 2
        + HOME_SCRATCH
        + scatter_scratch(god, bf16)
        + scatter_scratch(gd, bf16)
        + scatter_scratch(td, f32)
        + TRADE_SEMS * 2,
        compiler_params=remote_params(cid),
    )(dn, o, proj, hg, qkv, tm, wu, gb, cr, mc, mr, maps, fr, st, cw, sc, m, ypart, sgu, sd, da, nv, order, xrows, dm, gain, h1, wa, dgain2)


def lay_out(both, ra, ro, rgu, rd, lines, ff):
    def kernel(both, ra, ro, rgu, rd, lines, out, dt, dq, dk, dv, dg, da, db, do, gg, gu, gd, cq, ck, cv):
        out[...] = both[0]
        dt[...] = both[1]
        diag = lax.broadcasted_iota(i32, (64, 64), 0) == lax.broadcasted_iota(i32, (64, 64), 1)
        for i in range(4):
            for ref, cols in ((dq, QC), (dk, KC), (dv, VC), (dg, slice(512, 768))):
                ref[:, i, :] = ra[i, :, cols].astype(f32)
            do[i] = ro[i].astype(f32)
            n = min(FFP, ff - FFP * i)
            cols = slice(FFP * i, FFP * i + n)
            gg[:, cols] = rgu[i, :, 0:n].astype(f32)
            gu[:, cols] = rgu[i, :, FFP : FFP + n].astype(f32)
            gd[:, cols] = rd[i, :, 0:n].astype(f32)
            for k, ref in enumerate((da, db)):
                col = ra[i, :, 768 + k : 769 + k].astype(f32)
                ref[i : i + 1, :] = jnp.sum(jnp.where(diag, col, 0.0), axis=0, keepdims=True)
            for j in range(4):
                cq[j, i : i + 1, :] = lines[i, 0:1, 4 * j : 4 * j + 4]
                ck[j, i : i + 1, :] = lines[i, 0:1, 16 + 4 * j : 20 + 4 * j]
                cv[j, i : i + 1, :] = lines[i, 0:1, 32 + 8 * j : 40 + 8 * j]

    return pl.pallas_call(
        kernel,
        out_shape=[shape((128, 512), bf16)] * 2
        + [shape((64, 4, DK))] * 2
        + [shape((64, 4, DV))] * 2
        + [shape((4, 64))] * 2
        + [shape((4, 64, DV))]
        + [shape((64, ff))] * 3
        + [shape((4, 4, 4)), shape((4, 4, 4)), shape((4, 4, 8))],
        in_specs=[VM] * 6,
        out_specs=[VM] * 15,
        compiler_params=pltpu.CompilerParams(vmem_limit_bytes=VLIM),
    )(both, ra, ro, rgu, rd, lines)


def body(
    tokens,
    cotangent,
    seq_lengths,
    stretch_order,
    attn_gain,
    w_query,
    w_key,
    w_value,
    w_alpha,
    w_beta,
    conv_query,
    conv_key,
    conv_value,
    a_log,
    dt_bias,
    head_gain,
    w_outgate,
    w_output,
    mlp_gain,
    w_gate,
    w_up,
    w_down,
):

    wa, gain1, gain2, xrows, h1, proj, cw, hg, wpart, dys, qkv, tm, wu, gb, cr, maps, nv, ov, fr, st, mc, mr, sc = front(
        stretch_order,
        seq_lengths,
        a_log,
        dt_bias,
        tokens.reshape(2, STRETCH, D),
        cotangent.reshape(2, STRETCH, D),
        (w_query, w_key, w_value, w_outgate, w_alpha.T, w_beta.T, w_output.swapaxes(1, 2)),
        (w_gate, w_up, w_down.T),
        (conv_query, conv_key, conv_value),
        (head_gain[None], attn_gain[None], mlp_gain[None]),
        1,
    )
    wa = wa.reshape(D, NA)
    m, dm, dgain2, da, dn, ypart, sgu, sd = middle(
        nv.reshape(4, 4, 32, DV), wa, xrows, gain2, wpart, dys.reshape(4, 4, 32, D), 2
    )
    da, dn = da.reshape(SEG, D), dn.reshape(SEG, DV)

    both, ra, ro, rgu, rd, rt, total = back(
        dn, ov, proj, hg, qkv, tm, wu, gb, cr, mc, mr, maps, fr, st, cw, sc, m, ypart, sgu, sd, da, nv,
        stretch_order, xrows, dm, gain1, h1, wa, dgain2, 3,
    )
    out, dtok, d_query, d_key, d_value, d_outgate, d_alpha, d_beta, d_output, d_gate, d_up, d_down, cq, ck, cv = lay_out(
        both, ra, ro, rgu, rd, rt, w_gate.shape[1]
    )
    return (
        out,
        dtok,
        total[1, :64],
        d_query,
        d_key,
        d_value,
        d_alpha.T,
        d_beta.T,
        cq,
        ck,
        cv,
        rt[:, 0, 72],
        rt[:, 0, 73],
        total[0, 64:72],
        d_outgate,
        d_output.swapaxes(1, 2),
        total[2, :64],
        d_gate,
        d_up,
        d_down.T,
    )


def solution(mesh):
    torus = Mesh(mesh.devices.reshape(4, 4, 2, 4), ("y", "z", "c", "x"))
    dp, tp = ("y", "z", "c"), "x"
    in_specs = (
        P(dp, None),
        P(dp, None),
        P(),
        P(),
        P(dp),
        P(dp, tp, None),
        P(dp, tp, None),
        P(dp, tp, None),
        P(dp, tp),
        P(dp, tp),
        P(None, tp, dp),
        P(None, tp, dp),
        P(None, tp, dp),
        P(tp),
        P(tp),
        P(dp),
        P(dp, tp, None),
        P(tp, None, dp),
        P(dp),
        P(dp, tp),
        P(dp, tp),
        P(tp, dp),
    )
    out_specs = (
        P(dp, tp),
        P(dp, tp),
        P(dp),
        P(dp, tp, None),
        P(dp, tp, None),
        P(dp, tp, None),
        P(dp, tp),
        P(dp, tp),
        P(None, tp, dp),
        P(None, tp, dp),
        P(None, tp, dp),
        P(tp),
        P(tp),
        P(dp),
        P(dp, tp, None),
        P(tp, None, dp),
        P(dp),
        P(dp, tp),
        P(dp, tp),
        P(tp, dp),
    )
    return jax.shard_map(body, mesh=torus, in_specs=in_specs, out_specs=out_specs, check_vma=False)
```

```python
import functools
import math

import jax
import jax.numpy as jnp
from jax import lax
from jax.experimental import pallas as pl
from jax.experimental.pallas import tpu as pltpu
from jax.sharding import Mesh
from jax.sharding import PartitionSpec as P

MESH = pl.DeviceIdType.MESH
bf16, f32, i32 = jnp.bfloat16, jnp.float32, jnp.int32
HI = lax.Precision.HIGHEST
EPS = 1e-6
STRETCH = 64
D, DK, DV, FFP, HALO = 2048, 128, 256, 384, 16
SEG = 512
ROWS = SEG + HALO
CH = 128
NCH = SEG // CH
NA, NB = 1152, 1152
VLIM = 58 * 1024 * 1024


def at(axis, k):
    n = lax.axis_size(axis)
    return lax.rem(lax.axis_index(axis) + k + n, n)


def hail(peers):
    b = pltpu.get_barrier_semaphore()
    for p in peers:
        pl.semaphore_signal(b, inc=1, device_id=p, device_id_type=MESH)
    return lambda: pl.semaphore_wait(b, len(peers))


def send(src, dst, ss, rs, who):
    cp = pltpu.make_async_remote_copy(
        src_ref=src, dst_ref=dst, send_sem=ss, recv_sem=rs, device_id=who, device_id_type=MESH
    )
    cp.start()
    return cp


def run(flows, plan=""):
    flows = list(flows)
    for i in plan:
        next(flows[int(i)], None)
    for _ in together(flows):
        pass


def together(flows):
    flows = list(flows)
    while flows:
        left = []
        for f in flows:
            try:
                next(f)
                left.append(f)
            except StopIteration:
                pass
        flows = left
        if flows:
            yield


def segment_peers():
    z, c = lax.axis_index("z"), lax.axis_index("c")
    out = []
    for k in range(4):
        for d in range(2):
            if (k, d) != (0, 0):
                out.append({"z": at("z", k), "c": lax.rem(c + d, 2)})
    return out


def plane_peers():
    return [{"x": at("x", i), "y": at("y", j)} for i in range(4) for j in range(4) if (i, j) != (0, 0)]


def peers(**steps):
    return [{ax: at(ax, k)} for ax, ks in steps.items() for k in ks]


def zc_gather(slot, halves, ss, rs):
    z, c = lax.axis_index("z"), lax.axis_index("c")
    other = {"c": 1 - c}
    zp, zm, zf = at("z", 1), at("z", -1), at("z", 2)
    own, (o1, o2) = slot(z, c), halves(z, c)
    a = send(o1, o1, ss.at[0], rs.at[0], {"z": zp})
    b = send(o2, o2, ss.at[1], rs.at[1], {"z": zm})
    a2 = send(o2, o2, ss.at[9], rs.at[9], {"z": zp})
    b2 = send(o1, o1, ss.at[10], rs.at[10], {"z": zm})
    d0 = send(own, own, ss.at[4], rs.at[4], other)
    yield
    a.wait_recv()
    lo = halves(zm, c)[0]
    e = send(lo, lo, ss.at[2], rs.at[2], {"z": zp})
    b.wait_recv()
    hi = halves(zp, c)[1]
    f = send(hi, hi, ss.at[3], rs.at[3], {"z": zm})
    yield
    a2.wait_recv()
    m = slot(zm, c)
    d1 = send(m, m, ss.at[5], rs.at[5], other)
    b2.wait_recv()
    p = slot(zp, c)
    d2 = send(p, p, ss.at[6], rs.at[6], other)
    yield
    e.wait_recv()
    fl = halves(zf, c)[0]
    d3 = send(fl, fl, ss.at[7], rs.at[7], other)
    f.wait_recv()
    fh = halves(zf, c)[1]
    d4 = send(fh, fh, ss.at[8], rs.at[8], other)
    yield
    for cp in (d0, d1, d2, d3, d4):
        cp.wait_recv()
    for cp in (a, b, a2, b2, e, f, d0, d1, d2, d3, d4):
        cp.wait_send()


def zc_direct(slot, ss, rs):
    z, c = lax.axis_index("z"), lax.axis_index("c")
    other = {"c": 1 - c}
    own = slot(z, c)
    far = [send(own, own, ss.at[k - 1], rs.at[k - 1], {"z": at("z", k)}) for k in (2, 1, 3)]
    over = [send(own, own, ss.at[3], rs.at[3], other)]
    yield
    for k, cp in zip((2, 1, 3), far):
        cp.wait_recv()
        got = slot(at("z", -k), c)
        over.append(send(got, got, ss.at[3 + k], rs.at[3 + k], other))
    yield
    for cp in over:
        cp.wait_recv()
    for cp in far + over:
        cp.wait_send()


def trade_flow(src_of, dst, ss, rs):
    y = lax.axis_index("y")
    loc = pltpu.make_async_copy(src_of(y), dst(y), ss.at[3])
    loc.start()
    sends = [
        send(src_of(at("y", k)), dst(y), ss.at[k - 1], rs.at[k - 1], {"y": at("y", k)}) for k in (2, 1, 3)
    ]
    yield
    loc.wait()
    for cp in sends:
        cp.wait_recv()
    for cp in sends:
        cp.wait_send()


def spread_flow(out, ss, rs):
    return zc_gather(
        lambda zz, cc: out.at[:, zz, cc],
        lambda zz, cc: (out.at[0:2, zz, cc], out.at[2:4, zz, cc]),
        ss,
        rs,
    )


def exchange_flow(src_of, out, ss, rs):
    z, c = lax.axis_index("z"), lax.axis_index("c")
    yield from trade_flow(src_of, lambda y: out.at[y, z, c], ss.at[pl.ds(11, 4)], rs.at[pl.ds(11, 4)])
    yield from spread_flow(out, ss, rs)


def torus_gather(a1, a2, block, ss, rs):
    i, j = lax.axis_index(a1), lax.axis_index(a2)
    all_of = []

    def go(ref, who):
        k = len(all_of)
        all_of.append(send(ref, ref, ss.at[k], rs.at[k], who))
        return all_of[-1]

    own = block(i, j)
    first = [(go(own, {a1: at(a1, k)}), k) for k in (2, 1, 3)]
    for k in (2, 1, 3):
        go(own, {a2: at(a2, k)})
    yield
    for cp, k in first:
        cp.wait_recv()
        got = block(at(a1, -k), j)
        for q in (2, 1, 3):
            go(got, {a2: at(a2, q)})
    yield
    for cp in all_of[3:]:
        cp.wait_recv()
    for cp in all_of:
        cp.wait_send()


def lanes(i, j):
    return pl.ds(pl.multiple_of((i * 4 + j) * 128, 128), 128)


def gather_columns(out, skip, ss, rs):
    def half(rows):
        return lambda x, y: out.at[rows, lanes(x, y)]

    one, two = half(slice(0, skip + 256)), half(slice(skip + 256, skip + 512))
    yield from together(
        [
            torus_gather("x", "y", one, ss.at[0], rs.at[0]),
            torus_gather("y", "x", lambda y, x: two(x, y), ss.at[1], rs.at[1]),
        ]
    )


def gather_rows(out, ss, rs, rows=slice(0, 32)):
    def half(cols):
        return lambda x, y: out.at[x, y, rows, cols]

    one, two = half(slice(0, 1024)), half(slice(1024, 2048))
    yield from together(
        [
            torus_gather("x", "y", one, ss.at[0], rs.at[0]),
            torus_gather("y", "x", lambda y, x: two(x, y), ss.at[1], rs.at[1]),
        ]
    )


GATHER_SEMS = [pltpu.SemaphoreType.DMA((2, 15)), pltpu.SemaphoreType.DMA((2, 15))]


def ring_scatter(axis, piece, ready, bufs, emit, ss, rs):
    me, p, m, fr = (at(axis, k) for k in (0, 1, -1, 2))
    ready(fr)
    a = send(piece(fr, 0), bufs.at[0], ss.at[0], rs.at[0], {axis: p})
    c = send(piece(fr, 1), bufs.at[1], ss.at[1], rs.at[1], {axis: m})
    ready(p)
    b = send(piece(p, 1), bufs.at[2], ss.at[2], rs.at[2], {axis: p})
    ready(m)
    d = send(piece(m, 0), bufs.at[3], ss.at[3], rs.at[3], {axis: m})
    ready(me)
    yield
    a.wait_recv()
    bufs[0] = bufs[0] + piece(p, 0)[...]
    e = send(bufs.at[0], bufs.at[4], ss.at[4], rs.at[4], {axis: p})
    c.wait_recv()
    bufs[1] = bufs[1] + piece(m, 1)[...]
    f = send(bufs.at[1], bufs.at[5], ss.at[5], rs.at[5], {axis: m})
    yield
    d.wait_recv()
    e.wait_recv()
    emit(0, piece(me, 0)[...].astype(f32) + bufs[3].astype(f32) + bufs[4].astype(f32))
    b.wait_recv()
    f.wait_recv()
    emit(1, piece(me, 1)[...].astype(f32) + bufs[2].astype(f32) + bufs[5].astype(f32))
    for cp in (a, b, c, d, e, f):
        cp.wait_send()


def plane_scatter(part, rows, res, big, mid, small, h, ss, rs):
    cols = slice(h * 1024, (h + 1) * 1024)
    a1, a2 = ("x", "y") if h == 0 else ("y", "x")
    i, j = lax.axis_index(a1), lax.axis_index(a2)

    def piece(k):
        return part.at[k, :, rows, cols] if h == 0 else part.at[:, k, rows, cols]

    one = [send(piece(at(a1, k)), big.at[k - 1], ss.at[k - 1], rs.at[k - 1], {a1: at(a1, k)}) for k in (2, 1, 3)]
    yield
    for cp in one:
        cp.wait_recv()
    total = piece(i)[...].astype(f32) + big[0].astype(f32)
    mid[...] = (total + (big[1].astype(f32) + big[2].astype(f32))).astype(bf16)
    two = [
        send(mid.at[at(a2, k)], small.at[k - 1], ss.at[k + 2], rs.at[k + 2], {a2: at(a2, k)}) for k in (2, 1, 3)
    ]
    yield
    for cp in two:
        cp.wait_recv()
    res[:, cols] = (mid[j].astype(f32) + small[0].astype(f32)) + (small[1].astype(f32) + small[2].astype(f32))
    for cp in one + two:
        cp.wait_send()


def plane_sum(part, acc, big, mid, small, ss, rs, rows=slice(0, 32)):
    yield from together(
        plane_scatter(part, rows, acc, big.at[h], mid.at[h], small.at[h], h, ss.at[h], rs.at[h]) for h in (0, 1)
    )


def scatter_buffers(rows):
    return [
        pltpu.VMEM((2, 3, 4, rows, 1024), bf16),
        pltpu.VMEM((2, 4, rows, 1024), bf16),
        pltpu.VMEM((2, 3, rows, 1024), bf16),
        pltpu.SemaphoreType.DMA((2, 6)),
        pltpu.SemaphoreType.DMA((2, 6)),
    ]


SCATTER_SCRATCH = scatter_buffers(32)
PLANS = {
    "front": "012010012020134202030030300300000000",
    "middle": "2",
    "back": "1340000020010020012",
}
VM = pl.BlockSpec(memory_space=pltpu.VMEM)
SM = pl.BlockSpec(memory_space=pltpu.SMEM)
HB = pl.BlockSpec(memory_space=pl.ANY)


def shape(dims, kind=f32):
    return jax.ShapeDtypeStruct(dims, kind)


def remote_params(cid):
    return pltpu.CompilerParams(collective_id=cid, has_side_effects=True, vmem_limit_bytes=VLIM)


def columns(r):
    return lambda yy: r.at[:, :, lanes(lax.axis_index("x"), yy)]


def slots(r):
    return lambda yy: r.at[yy]


def pick_flow(src, every, index, out, skip, es, er, gs, gr):
    x, y = lax.axis_index("x"), lax.axis_index("y")
    z, c = lax.axis_index("z"), lax.axis_index("c")
    yield from trade_flow(columns(src), lambda i: every.at[i, z, c], es.at[pl.ds(7, 4)], er.at[pl.ds(7, 4)])
    yield from zc_direct(lambda zz, cc: every.at[:, zz, cc], es, er)
    here = lanes(x, y)

    def block(j):
        a = index[j]
        return every[a >> 4, (a >> 2) & 3, (a >> 1) & 1, a & 1]

    if skip:
        out[0:skip, here] = block(0)[STRETCH - skip : STRETCH]
    for j in range(8):
        out[skip + 64 * j : skip + 64 * (j + 1), here] = block(j + 1)
    yield from gather_columns(out, skip, gs, gr)


PICK_SCRATCH = [
    pltpu.VMEM((4, 4, 2, 2, 64, 128), bf16),
    pltpu.SemaphoreType.DMA((15,)),
    pltpu.SemaphoreType.DMA((15,)),
] + GATHER_SEMS


def spread_gain(line, row, out):
    for i in range(32):
        out[:, 64 * i : 64 * (i + 1)] = line[i // 8, i // 2 % 4, i % 2, row : row + 1, 0:64]


def norm_back(v, gain, dh):
    r = lax.rsqrt(jnp.mean(v * v, axis=-1, keepdims=True) + EPS)
    t = gain * dh
    dv = r * t - v * (r * r * r) * jnp.mean(v * t, axis=-1, keepdims=True)
    return dv, jnp.sum(v * r * dh, axis=0, keepdims=True)


def weight_tiles(left, right, out):
    def tile(t, _):
        v = dot(left(pl.ds(pl.multiple_of(t * 256, 256), 256)), right(), ((0,), (0,))).astype(bf16)
        for k in range(4):
            out[t // 2, lax.rem(t, 2) * 2 + k // 2, k % 2] = v[64 * k : 64 * (k + 1)]
        return 0

    lax.fori_loop(0, 8, tile, 0)


def middle(nv, wa, xrows, gain, wpart, dys, cid, plan=PLANS["middle"]):
    def kernel(nv, wa, xr, gain, wp, dys, m_out, dm_out, dg_out, da_out, dn_out, yp_out, sgu, sd, *refs):
        w, part, part2, h2, hid, dgu, ggu, gd, acc, dgs, refs = *refs[:10], refs[10:]
        sums = [refs[5 * i : 5 * i + 5] for i in range(4)]
        refs = refs[20:]
        gathers = [refs[2 * i : 2 * i + 2] for i in range(4)]
        ws, wr, ls = refs[8:11]
        fgu, fd = refs[11:15], refs[15:19]
        x, y, z, c = (lax.axis_index(a) for a in "xyzc")
        wo = wa.at[:, 896:]
        own = pltpu.make_async_copy(wp, w.at[:, z, c], ls)
        own.start()
        ready = hail(peers(x=(1, 2, 3), y=(1, 2, 3), z=(1, 3), c=(1,)))

        def spread():
            own.wait()
            yield from spread_flow(w, ws, wr)

        weights = spread()

        def flat(ref, rows):
            v = ref[:, :, rows, :]
            return v.reshape(-1, v.shape[-1])

        def grads():
            def first():
                weight_tiles(lambda cols: h2[:, :, :, cols].reshape(SEG, 256), lambda: flat(dgu, slice(0, 32)), ggu)
                yield from sum_flow(ggu, sgu, *fgu)

            def second():
                weight_tiles(lambda cols: dys[:, :, :, cols].reshape(SEG, 256), lambda: flat(hid, slice(0, 32)), gd)
                yield from sum_flow(gd, sd, *fd)

            yield from first()
            yield from second()

        def half(h):
            rows = slice(16 * h, 16 * h + 16)
            nrows = flat(nv, rows)
            for t in range(4):
                cols = slice(512 * t, 512 * (t + 1))
                part[:, :, rows, cols] = dot(nrows, wo[cols, :], ((1,), (1,))).astype(bf16).reshape(4, 4, 16, 512)
            yield
            yield from plane_sum(part, acc.at[h], *sums[h], rows)
            m = xr[rows, :].astype(f32) + acc[h]
            m_out[rows, :] = m
            r = lax.rsqrt(jnp.mean(m * m, axis=-1, keepdims=True) + EPS)
            h2[x, y, rows, :] = (m * r * gain[...]).astype(bf16)
            yield from gather_rows(h2, *gathers[h], rows)
            for _ in weights:
                pass
            wv = w[...].reshape(D, NB)
            both = dot(flat(h2, rows), wv[:, : 2 * FFP], ((1,), (0,)))
            ga, up = both[:, :FFP], both[:, FFP:]
            dhid = dot(flat(dys, rows), wv[:, 2 * FFP :], ((1,), (0,)))
            sg = jax.nn.sigmoid(ga)
            act = ga * sg
            hv = (act * up).astype(bf16)
            hid[:, :, rows, :] = hv.reshape(4, 4, 16, FFP)
            dga = (dhid * up * (sg * (1.0 + ga * (1.0 - sg)))).astype(bf16)
            dup = (dhid * act).astype(bf16)
            dgu[:, :, rows, :FFP] = dga.reshape(4, 4, 16, FFP)
            dgu[:, :, rows, FFP:] = dup.reshape(4, 4, 16, FFP)
            dv = jnp.concatenate([dga, dup], axis=1)
            for t in range(4):
                cols = slice(512 * t, 512 * (t + 1))
                part2[:, :, rows, cols] = (
                    dot(dv, wv[cols, : 2 * FFP], ((1,), (1,))).astype(bf16).reshape(4, 4, 16, 512)
                )

            def back():
                yield from plane_sum(part2, acc.at[2 + h], *sums[2 + h], rows)
                dvr, dgain = norm_back(m_out[rows, :], gain[...], acc[2 + h])
                dm = dys[x, y, rows, :].astype(f32) + dvr
                dm_out[rows, :] = dm
                dgs[h : h + 1, :] = dgain
                da_out[x, y, rows, :] = dm.astype(bf16)
                yield from gather_rows(da_out, *gathers[2 + h], rows)
                dn_out[:, :, rows, :] = dot(flat(da_out, rows), wo[...], ((1,), (0,))).reshape(4, 4, 16, DV)

            def result():
                yield
                for t in range(4):
                    cols = slice(512 * t, 512 * (t + 1))
                    yp_out[:, :, rows, cols] = (
                        dot(hv, wv[cols, 2 * FFP :], ((1,), (1,))).astype(bf16).reshape(4, 4, 16, 512)
                    )

            def later(f, n):
                for _ in range(n):
                    yield
                yield from f

            yield from together([back(), later(result(), 1)] + ([grads()] if h else []))

        halves = half(0), half(1)
        next(halves[0])
        ready()
        next(halves[0])
        next(halves[1])
        next(halves[1])
        run([*halves, weights], plan)
        dg_out[...] = dgs[0:1, :] + dgs[1:2, :]

    gu, gdown = (4, 4, 2, 64, 2 * FFP), (4, 4, 2, 64, FFP)
    return pl.pallas_call(
        kernel,
        out_shape=[
            shape((32, D)),
            shape((32, D)),
            shape((1, D)),
            shape((4, 4, 32, D), bf16),
            shape((4, 4, 32, DV)),
            shape((4, 4, 32, D), bf16),
            shape((4, 64, 2 * FFP), bf16),
            shape((4, 64, FFP), bf16),
        ],
        in_specs=[VM] * 6,
        out_specs=[VM] * 8,
        scratch_shapes=[
            pltpu.VMEM((4, 4, 2, 64, NB), bf16),
            pltpu.VMEM((4, 4, 32, D), bf16),
            pltpu.VMEM((4, 4, 32, D), bf16),
            pltpu.VMEM((4, 4, 32, D), bf16),
            pltpu.VMEM((4, 4, 32, FFP), bf16),
            pltpu.VMEM((4, 4, 32, 2 * FFP), bf16),
            pltpu.VMEM(gu, bf16),
            pltpu.VMEM(gdown, bf16),
            pltpu.VMEM((4, 16, D), f32),
            pltpu.VMEM((2, D), f32),
        ]
        + scatter_buffers(16) * 4
        + GATHER_SEMS * 4
        + [pltpu.SemaphoreType.DMA((11,)), pltpu.SemaphoreType.DMA((11,)), pltpu.SemaphoreType.DMA]
        + sum_scratch(gu[3:], bf16)
        + sum_scratch(gdown[3:], bf16),
        compiler_params=remote_params(cid),
    )(nv, wa, xrows, gain, wpart, dys)


def home_flow(src, dst, order, alls, cols, picks, s1, r1, s2, r2, s3, r3):
    x, y, z, c = (lax.axis_index(a) for a in "xyzc")
    n = src.shape[0]
    sends = []
    cols[x, y] = src[:, :, lanes(x, y)]
    t = 0
    for i in range(4):
        for j in range(4):
            if (i, j) == (0, 0):
                continue
            px, py = at("x", i), at("y", j)
            sends.append(send(src.at[:, :, lanes(px, py)], cols.at[x, y], s1.at[t], r1.at[t], {"x": px, "y": py}))
            t += 1
    yield
    for cp in sends:
        cp.wait_recv()
    for k in range(n):
        alls[z, c, k] = cols[:, :, k].reshape(8, 64, 128)
    yield from zc_direct(lambda zz, cc: alls.at[zz, cc], s2, r2)
    for j in range(4):
        for i in range(2):
            b = order[j * 16 + (z * 2 + c) * 2 + i]
            for k in range(n):
                picks[j, k, 64 * i : 64 * (i + 1)] = alls[b >> 4, (b >> 3) & 1, k, b & 7]
    mine = pl.ds(pl.multiple_of(y * 128, 128), 128)
    last = [
        send(picks.at[at("y", j)], dst.at[:, :, mine], s3.at[j], r3.at[j], {"y": at("y", j)}) for j in (2, 1, 3)
    ]
    dst[:, :, mine] = picks[y]
    yield
    for cp in last:
        cp.wait_recv()
    for cp in sends + last:
        cp.wait_send()


HOME_SCRATCH = [
    pltpu.VMEM((4, 2, 2, 8, 64, 128), bf16),
    pltpu.VMEM((4, 4, 2, 32, 128), bf16),
    pltpu.VMEM((4, 2, 128, 128), bf16),
    pltpu.SemaphoreType.DMA((15,)),
    pltpu.SemaphoreType.DMA((15,)),
    pltpu.SemaphoreType.DMA((7,)),
    pltpu.SemaphoreType.DMA((7,)),
    pltpu.SemaphoreType.DMA((4,)),
    pltpu.SemaphoreType.DMA((4,)),
]


def sum_flow(g, stage, core, bufs, ss, rs):
    c = lax.axis_index("c")
    d = send(g.at[:, :, 1 - c], core, ss.at[0], rs.at[0], {"c": 1 - c})
    yield
    d.wait_recv()

    def ready(i):
        for k in range(4):
            core[k, i] = core[k, i] + g[k, i, c]

    def emit(s, v):
        stage[2 * s : 2 * s + 2] = v.astype(stage.dtype)

    def piece(i, s):
        return core.at[2 * s : 2 * s + 2, i]

    yield from ring_scatter("z", piece, ready, bufs, emit, ss.at[pl.ds(1, 6)], rs.at[pl.ds(1, 6)])
    d.wait_send()


def sum_scratch(dims, kind):
    return [
        pltpu.VMEM((4, 4) + dims, kind),
        pltpu.VMEM((6, 2) + dims, kind),
        pltpu.SemaphoreType.DMA((7,)),
        pltpu.SemaphoreType.DMA((7,)),
    ]


TRADE_SEMS = [pltpu.SemaphoreType.DMA((4,)), pltpu.SemaphoreType.DMA((4,))]


def scatter_flow(g, out, stage, ts, tr, *sums):
    yield from sum_flow(g, stage, *sums)
    yield from trade_flow(slots(stage), lambda y: out.at[y], ts, tr)


def scatter_scratch(dims, kind):
    return [pltpu.VMEM((4,) + dims, kind)] + TRADE_SEMS + sum_scratch(dims, kind)


def dot(a, b, dims, prec=None):
    return lax.dot_general(a, b, (dims, ((), ())), preferred_element_type=f32, precision=prec)


def lo(a):
    return a.astype(bf16)


def mm(a, b):
    return dot(lo(a), lo(b), ((1,), (0,)))


def mmt(a, b):
    return dot(lo(a), lo(b), ((1,), (1,)))


def tmm(a, b):
    return dot(lo(a), lo(b), ((0,), (0,)))


def halves_of(a):
    h = a.astype(bf16)
    return h, (a - h.astype(f32)).astype(bf16)


def fine(a, b, dims=((1,), (0,))):
    ah, al = halves_of(a)
    bh, bl = halves_of(b)
    return dot(ah, bh, dims) + (dot(ah, bl, dims) + dot(al, bh, dims))


def tri_inverse(a, r, c):
    eye = jnp.where(r == c, 1.0, 0.0)
    n1 = jnp.where((r >> 3) == (c >> 3), -a, 0.0)
    n2 = fine(n1, n1)
    n4 = fine(n2, n2)
    t = eye + n1
    t = t + fine(t, n2)
    t = t + fine(t, n4)
    for level in (3, 4, 5, 6):
        off = ((r >> (level + 1)) == (c >> (level + 1))) & ((r >> level) != (c >> level))
        t = t - fine(t, fine(jnp.where(off, a, 0.0), t))
    return t


def iotas():
    return (
        lax.broadcasted_iota(i32, (CH, CH), 0),
        lax.broadcasted_iota(i32, (CH, CH), 1),
    )


def filtered(z, cw, mc, cols):
    total = z[HALO : HALO + SEG, cols] * cw[3:4, cols]
    for j in range(3):
        total = total + mc[:, j : j + 1] * cw[j : j + 1, cols] * z[HALO - 3 + j : HALO - 3 + j + SEG, cols]
    return total


def silu(v):
    return v * jax.nn.sigmoid(v)


QC, KC, VC = slice(0, 128), slice(128, 256), slice(256, 512)


def decay_of(cc, cr, mask):
    return jnp.exp(jnp.where(mask, cc - cr, 0.0)) * jnp.where(mask, 1.0, 0.0)


def prepare(z, ab, cw, sc, mc, mr, qkv, tm, wu, gb, cr, ti):
    r, c = iotas()
    for cols, scale in ((QC, DK**-0.5), (KC, 1.0)):
        s = silu(filtered(z, cw, mc, cols))
        qkv[:, cols] = (s * lax.rsqrt(jnp.sum(s * s, axis=-1, keepdims=True) + EPS) * scale).astype(bf16)
    qkv[:, VC] = silu(filtered(z, cw, mc, VC)).astype(bf16)
    low = jnp.where(r >= c, 1.0, 0.0)
    eye = jnp.where(r == c, 1.0, 0.0)
    lane = lax.broadcasted_iota(i32, (CH, 128), 1)
    transit = eye
    insert = jnp.zeros((DK, DV), f32)
    yield
    for n in range(NCH):
        rows = slice(n * CH, (n + 1) * CH)
        raw = ab[HALO + n * CH : HALO + (n + 1) * CH, :]
        beta = jax.nn.sigmoid(raw[:, 1:2])
        u = raw + sc[0:1, 1:2]
        g = -jnp.exp(sc[0:1, 0:1]) * (jnp.maximum(u, 0.0) + jnp.log1p(jnp.exp(-jnp.abs(u))))
        g = jnp.where(lane == 0, g, 0.0)
        cum = dot(low, g, ((1,), (0,)), HI)[:, 0:1]
        cumr = dot(g, low, ((0,), (1,)), HI)[0:8, :]
        gb[rows, :] = jnp.where(lane == 0, beta, cum)
        cr[:, rows] = cumr
        cumrow = cumr[0:1, :]
        last = cumr[0:1, CH - 1 : CH]
        m = mc[rows, :]
        carried, closing, begin, carry_last = m[:, 3:4], m[:, 4:5], m[:, 5:6], m[0:1, 6:7]
        same = begin == mr[0:1, rows]
        k = qkv[rows, KC]
        kf = k.astype(f32)
        v = qkv[rows, VC].astype(f32)
        a = beta * dot(k, k, ((1,), (1,))) * decay_of(cum, cumrow, same & (r > c))
        t = tri_inverse(a, r, c)
        tm[rows, :] = t
        lead = (beta * jnp.exp(cum) * carried) * kf
        w = fine(t, lead)
        uu = fine(t, beta * v)
        wu[rows, 0:DK] = w
        wu[rows, DK:] = uu
        tail = kf * (jnp.exp(last - cum) * closing)
        keep = jnp.exp(last) * carry_last
        hand = keep * eye - fine(tail, w, ((0,), (0,)))
        insert = fine(hand, insert) + fine(tail, uu, ((0,), (0,)))
        transit = fine(hand, transit)
        yield
    ti[:, 0:DK] = transit.astype(bf16)
    ti[:, DK:] = insert.astype(bf16)


def emit_outputs(seg, maps, qkv, wu, gb, cr, mc, mr, gp, hg, nout, oout, fout, sout):
    r, c = iotas()

    def fold(d, s):
        tr, ins = maps[d, :, 0:DK], maps[d, :, DK:].astype(f32)
        sh, sl = halves_of(s)
        new = dot(tr, sh, ((1,), (0,))) + dot(tr, sl, ((1,), (0,))) + ins
        return jnp.where(d < seg, new, s)

    s = lax.fori_loop(0, 7, fold, jnp.zeros((DK, DV), f32))
    for n in range(NCH):
        rows = slice(n * CH, (n + 1) * CH)
        m = mc[rows, :]
        carried, closing, begin, carry_last = m[:, 3:4], m[:, 4:5], m[:, 5:6], m[0:1, 6:7]
        cum = gb[rows, 1:2]
        cumrow = cr[0:1, rows]
        last = cr[0:1, n * CH + CH - 1 : n * CH + CH]
        same = begin == mr[0:1, rows]
        q, k = qkv[rows, QC], qkv[rows, KC]
        p = dot(q, k, ((1,), (1,))) * decay_of(cum, cumrow, same & (r >= c))
        fresh = wu[rows, DK:] - fine(wu[rows, 0:DK], s)
        qd = q.astype(f32) * (jnp.exp(cum) * carried)
        o = mm(qd, s) + mm(p, fresh)
        sout[n] = s
        fout[rows, :] = fresh
        oout[rows, :] = o
        x = gp[HALO + n * CH : HALO + (n + 1) * CH, :]
        rn = lax.rsqrt(jnp.mean(o * o, axis=-1, keepdims=True) + EPS)
        nout[rows, :] = (o * rn * hg[0:1, :] * silu(x)).astype(bf16)
        tail = k.astype(f32) * (jnp.exp(last - cum) * closing)
        s = (jnp.exp(last) * carry_last) * s + fine(tail, fresh, ((0,), (0,)))
        yield


def back_emit(dn, o, gp, hg, qkv, wu, gb, cr, mc, mr, do_out, dgp_out, dhg_out, e_out):
    r, c = iotas()
    dhg = jnp.zeros((1, DV), f32)
    e = jnp.zeros((DK, DV), f32)
    for n in reversed(range(NCH)):
        rows = slice(n * CH, (n + 1) * CH)
        ov, x, dnv = o[rows, :], gp[HALO + n * CH : HALO + (n + 1) * CH, :], dn[rows, :]
        rn = lax.rsqrt(jnp.mean(ov * ov, axis=-1, keepdims=True) + EPS)
        sg = jax.nn.sigmoid(x)
        act = x * sg
        h = hg[0:1, :]
        base = ov * rn
        dhg = dhg + jnp.sum(base * act * dnv, axis=0, keepdims=True)
        dgp_out[rows, :] = (dnv * base * h * (sg * (1.0 + x * (1.0 - sg)))).astype(bf16)
        t = dnv * h * act
        do = rn * t - base * (rn * rn) * jnp.mean(ov * t, axis=-1, keepdims=True)
        do_out[rows, :] = do
        m = mc[rows, :]
        carried, closing, begin, carry_last = m[:, 3:4], m[:, 4:5], m[:, 5:6], m[0:1, 6:7]
        cum = gb[rows, 1:2]
        cumrow = cr[0:1, rows]
        last = cr[0:1, n * CH + CH - 1 : n * CH + CH]
        same = begin == mr[0:1, rows]
        q, k = qkv[rows, QC], qkv[rows, KC]
        p = dot(q, k, ((1,), (1,))) * decay_of(cum, cumrow, same & (r >= c))
        qd = q.astype(f32) * (jnp.exp(cum) * carried)
        tail = k.astype(f32) * (jnp.exp(last - cum) * closing)
        df = tmm(p, do) + mm(tail, e)
        e = tmm(qd, do) + (jnp.exp(last) * carry_last) * e - tmm(wu[rows, 0:DK], df)
        yield
    dhg_out[...] = dhg
    e_out[...] = e.astype(bf16)


def back_delta(seg, maps, tails, do, fr, st, qkv, tm, wu, gb, cr, z, ab, cw, sc, mc, mr, dz, dab, dcw, dsc, dqkv):
    r, c = iotas()
    low = jnp.where(r >= c, 1.0, 0.0)
    ones = jnp.ones((CH, CH), f32)
    lane = lax.broadcasted_iota(i32, (CH, 128), 1)
    row = lax.broadcasted_iota(i32, (CH, 1), 0)

    def fold(i, e):
        d = 7 - i
        tr, own = maps[d, :, 0:DK], tails[d].astype(f32)
        eh, el = halves_of(e)
        new = dot(tr, eh, ((0,), (0,))) + dot(tr, el, ((0,), (0,))) + own
        return jnp.where(d > seg, new, e)

    e = lax.fori_loop(0, 7, fold, jnp.zeros((DK, DV), f32))
    acc_a = jnp.zeros((1, 128), f32)
    acc_d = jnp.zeros((1, 128), f32)
    for n in reversed(range(NCH)):
        rows = slice(n * CH, (n + 1) * CH)
        m = mc[rows, :]
        carried, closing, begin, carry_last = m[:, 3:4], m[:, 4:5], m[:, 5:6], m[0:1, 6:7]
        beta, cum = gb[rows, 0:1], gb[rows, 1:2]
        cumrow = cr[0:1, rows]
        last = cr[0:1, n * CH + CH - 1 : n * CH + CH]
        same = begin == mr[0:1, rows]
        q, k = qkv[rows, QC], qkv[rows, KC]
        qf, kf, vf = q.astype(f32), k.astype(f32), qkv[rows, VC].astype(f32)
        dec_i = decay_of(cum, cumrow, same & (r >= c))
        dec_s = jnp.where(r > c, dec_i, 0.0)
        p = dot(q, k, ((1,), (1,))) * dec_i
        kkd = dot(k, k, ((1,), (1,))) * dec_s
        ex = jnp.exp(cum) * carried
        tf = jnp.exp(last - cum) * closing
        keep = jnp.exp(last) * carry_last
        tail = kf * tf
        qd = qf * ex
        dov, fv, sv, tv = do[rows, :], fr[rows, :], st[n], tm[rows, :]
        w, u = wu[rows, 0:DK], wu[rows, DK:]
        df = tmm(p, dov) + mm(tail, e)
        dw = -mmt(df, sv)
        dtail = mmt(fv, e)
        dkeep = jnp.sum(jnp.sum(sv * e, axis=1, keepdims=True), axis=0, keepdims=True)
        dqd = mmt(dov, sv)
        dp = mmt(dov, fv)
        dlead = tmm(tv, dw)
        dbv = tmm(tv, df)
        da = -(mmt(dlead, w) + mmt(dbv, u))
        dakd = da * kkd
        dkk = da * beta * dec_s
        dqk = dp * dec_i
        mix = dakd * beta + dp * p
        dqkv[rows, QC] = mm(dqk, k) + dqd * ex
        dqkv[rows, KC] = (
            tmm(dqk, q) + mm(dkk, k) + tmm(dkk, k) + dlead * (beta * ex) + dtail * tf
        )
        dqkv[rows, VC] = beta * dbv
        lk = jnp.sum(dlead * kf, axis=1, keepdims=True) * ex
        dbeta = jnp.sum(dakd, axis=1, keepdims=True) + lk + jnp.sum(dbv * vf, axis=1, keepdims=True)
        tt = jnp.sum(dtail * tail, axis=1, keepdims=True)
        dcum = jnp.sum(mix, axis=1, keepdims=True) + jnp.sum(dqd * qd, axis=1, keepdims=True) + lk * beta - tt
        dcum = dcum + jnp.where(row == CH - 1, jnp.sum(tt, axis=0, keepdims=True) + dkeep * keep, 0.0)
        full = dcum - dot(mix, ones, ((0,), (0,)), HI)
        dg = dot(low, full, ((0,), (0,)), HI)
        raw = ab[HALO + n * CH : HALO + (n + 1) * CH, :]
        uu = raw + sc[0:1, 1:2]
        rate = -jnp.exp(sc[0:1, 0:1])
        sp = jnp.maximum(uu, 0.0) + jnp.log1p(jnp.exp(-jnp.abs(uu)))
        dal = dg * rate * jax.nn.sigmoid(uu)
        acc_a = acc_a + jnp.sum(dg * rate * sp, axis=0, keepdims=True)
        acc_d = acc_d + jnp.sum(dal, axis=0, keepdims=True)
        dab[rows, :] = jnp.where(
            lane == 0, dal, jnp.where(lane == 1, dbeta * beta * (1.0 - beta), 0.0)
        ).astype(bf16)
        e = tmm(qd, dov) + keep * e - tmm(w, df)
        yield
    dsc[0:1, :] = acc_a
    dsc[1:2, :] = acc_d
    dz[0:HALO, :] = jnp.zeros((HALO, 512), f32)
    for cols, scale in ((QC, DK**-0.5), (KC, 1.0), (VC, None)):
        y = filtered(z, cw, mc, cols)
        sg = jax.nn.sigmoid(y)
        ds = dqkv[:, cols]
        if scale is not None:
            s = y * sg
            rn = lax.rsqrt(jnp.sum(s * s, axis=-1, keepdims=True) + EPS)
            ds = scale * (rn * ds - s * (rn * rn * rn) * jnp.sum(s * ds, axis=-1, keepdims=True))
        dy = ds * (sg * (1.0 + y * (1.0 - sg)))
        dz[HALO : HALO + SEG, cols] = dy * cw[3:4, cols]
        dcw[3:4, cols] = jnp.sum(dy * z[HALO : HALO + SEG, cols], axis=0, keepdims=True)
        for j in range(3):
            part = mc[:, j : j + 1] * dy
            away = slice(HALO - 3 + j, HALO - 3 + j + SEG)
            dcw[j : j + 1, cols] = jnp.sum(part * z[away, cols], axis=0, keepdims=True)
            dz[away, cols] = dz[away, cols] + part * cw[j : j + 1, cols]
        yield


def map_gather(own, out, ss, rs):
    z, c = lax.axis_index("z"), lax.axis_index("c")
    out[z, c] = own[...]
    yield from zc_direct(lambda zz, cc: out.at[zz, cc], ss, rs)


class Maps:
    def __init__(self, ref):
        self.ref = ref

    def __getitem__(self, key):
        key = key if isinstance(key, tuple) else (key,)
        return self.ref[(key[0] // 2, key[0] % 2) + key[1:]]


def masks(lens, mc, mr):
    base = (lax.axis_index("z") * 2 + lax.axis_index("c")) * SEG
    firsts = [jnp.int32(0)]
    for k in range(3):
        firsts.append(firsts[k] + lens[k])

    def begin_of(pos):
        b = jnp.zeros_like(pos)
        for k in range(1, 4):
            b = jnp.where((pos >= firsts[k]) & (pos < firsts[k] + lens[k]), firsts[k], b)
        return b

    lane = lax.broadcasted_iota(i32, (CH, 128), 1)
    for n in range(NCH):
        first = base + n * CH
        pos = first + lax.broadcasted_iota(i32, (CH, 128), 0)
        b = begin_of(pos)
        last = begin_of(jnp.full((CH, 128), first + CH - 1, i32))

        def one(flag):
            return jnp.where(flag, 1.0, 0.0)

        late = jnp.where(lane == 3, one(b < first), jnp.where(lane == 4, one(b == last), one(last < first)))
        flags = jnp.where(lane < 3, one(pos - 3 + lane >= b), late)
        mc[n * CH : (n + 1) * CH, :] = jnp.where(lane == 5, b.astype(f32), flags)
        mr[:, n * CH : (n + 1) * CH] = begin_of(first + lax.broadcasted_iota(i32, (8, CH), 1)).astype(f32)


def spread_lanes(v, wide, first):
    n = 32 * wide
    owner = lax.broadcasted_iota(i32, (32, n), 0) == lax.broadcasted_iota(i32, (32, n), 1) // wide
    place = lax.broadcasted_iota(i32, (n, 128), 1) == first + lax.rem(lax.broadcasted_iota(i32, (n, 128), 0), wide)
    return dot(jnp.where(owner, v, 0.0), jnp.where(place, 1.0, 0.0), ((1,), (0,)), HI)


def gather_lanes(rows, wide, first):
    n = 32 * wide
    owner = lax.broadcasted_iota(i32, (32, n), 0) == lax.broadcasted_iota(i32, (32, n), 1) // wide
    place = lax.broadcasted_iota(i32, (128, n), 0) == first + lax.rem(lax.broadcasted_iota(i32, (128, n), 1), wide)
    every = dot(rows, jnp.where(place, 1.0, 0.0), ((1,), (0,)), HI)
    return jnp.sum(jnp.where(owner, every, 0.0), axis=0, keepdims=True)


def front(order, lens, a_log, dt_bias, tokens, cotangent, weights, wide_weights, convs, gains, cid, plan=PLANS["front"]):
    npk = len(PICK_SCRATCH)

    def kernel(
        order, lens, al, dt, tok, cot, wq, wk, wv, wg, wal, wbe, wou, wga, wup, wdo, cvq, cvk, cvv, hgi, g1i, g2i,
        wa, gain1, gain2, xr, h1, proj, cw, hg, wp, dyo, qkv, tm, wu, gb, cr, maps, nout, oout, fout, sout, mc, mr, sc,
        pack, pack_b, tiny, line, tops, xo, ti, index, *refs,
    ):
        pick_x, pick_y, refs = refs[:npk], refs[npk : 2 * npk], refs[2 * npk :]
        ss, rs, ms, mq, ts, tr = refs
        x, y, z, c = (lax.axis_index(a) for a in "xyzc")
        seg = z * 2 + c
        zq, gp, ab = proj.at[:, 0:512], proj.at[:, 512:768], proj.at[:, 768:896]
        ready = hail(peers(y=(1, 2, 3), z=(1, 2, 3), c=(1,), x=(1, 2, 3)))

        diag = lax.broadcasted_iota(i32, (64, 64), 0) == lax.broadcasted_iota(i32, (64, 64), 1)
        lane = lax.broadcasted_iota(i32, (64, 128), 1)
        for i in range(4):
            for ref, cols in ((wq, QC), (wk, KC), (wv, VC), (wg, slice(512, 768))):
                pack[i, :, cols] = ref[:, i, :].astype(bf16)
            alpha, beta = (jnp.sum(jnp.where(diag, r[i : i + 1, :], 0.0), axis=1, keepdims=True) for r in (wal, wbe))
            pack[i, :, 768:896] = jnp.where(lane == 0, alpha, jnp.where(lane == 1, beta, 0.0)).astype(bf16)
            pack[i, :, 896:1152] = wou[i].astype(bf16)
        tiny[...] = jnp.zeros(tiny.shape, f32)
        for i in range(4):
            for ref, n, first in ((cvq, 4, 0), (cvk, 4, 16), (cvv, 8, 32)):
                for j in range(4):
                    tiny[i, 0:1, first + n * j : first + n * (j + 1)] = ref[j, i : i + 1, :]
            tiny[i, 0:1, 64:72] = hgi[...]
            tiny[i, 1:2, 0:64] = g1i[...]
            tiny[i, 2:3, 0:64] = g2i[...]
        tiny[...] = tiny[...].astype(bf16).astype(f32)

        def find(a, found):
            return tuple(jnp.where(order[a] == jnp.maximum(seg * 8 - 1 + j, 0), a, f) for j, f in enumerate(found))

        for j, f in enumerate(lax.fori_loop(0, 64, find, tuple(jnp.int32(0) for _ in range(9)))):
            index[j] = f
        ready()

        def small():
            se, re = ss.at[0], rs.at[0]
            yield from trade_flow(slots(tiny), lambda i: line.at[i, z, c], se.at[pl.ds(7, 4)], re.at[pl.ds(7, 4)])
            yield from zc_direct(lambda zz, cc: line.at[:, zz, cc], se, re)
            spread_gain(line, 1, gain1)
            spread_gain(line, 2, gain2)
            for i in range(32):
                tops[i : i + 1, :] = line[i // 8, i // 2 % 4, i % 2, 0:1, :]
            top = tops[...]
            for j in range(4):
                cw[j : j + 1, QC] = gather_lanes(top, 4, 4 * j)
                cw[j : j + 1, KC] = gather_lanes(top, 4, 16 + 4 * j)
                cw[j : j + 1, VC] = gather_lanes(top, 8, 32 + 8 * j)
            hg[...] = gather_lanes(top, 8, 64)

        def main():
            yield from pick_flow(tok, pick_x[0], index, xo, HALO, *pick_x[1:])
            for _ in lines:
                pass

            def norm(t, _):
                at_rows = pl.ds(pl.multiple_of(t * 16, 16), 16)
                v = xo[at_rows, :].astype(f32)
                r = lax.rsqrt(jnp.mean(v * v, axis=-1, keepdims=True) + EPS)
                h1[at_rows, :] = (v * r * gain1[...]).astype(bf16)
                return 0

            lax.fori_loop(0, ROWS // 16, norm, 0)
            xr[...] = xo[pl.ds(pl.multiple_of(HALO + 32 * (x * 4 + y), 16), 32), :]
            masks(lens, mc, mr)
            sc[0:8, :] = jnp.where(lax.broadcasted_iota(i32, (8, 128), 1) == 0, al[y], dt[y])
            yield
            for _ in fetched:
                pass
            for cols in (slice(0, 256), slice(256, 512), slice(512, 768), slice(768, 896)):
                w = wa[:, :, :, :, cols]
                proj[:, cols] = dot(h1[...], w.reshape(D, w.shape[-1]), ((1,), (0,)))
            yield
            yield from prepare(zq, ab, cw, sc, mc, mr, qkv, tm, wu, gb, cr, ti)
            yield from map_gather(ti, maps, ms, mq)
            yield from emit_outputs(seg, Maps(maps), qkv, wu, gb, cr, mc, mr, gp, hg, nout, oout, fout, sout)

        def trade_wide():
            ff = wga.shape[1]
            for i in range(4):
                n = min(FFP, ff - FFP * i)
                cols = slice(FFP * i, FFP * i + n)
                for k, v in enumerate((wga[:, cols], wup[:, cols], wdo[:, cols])):
                    pack_b[i, :, FFP * k : FFP * k + n] = v.astype(bf16)
                    if n < FFP:
                        pack_b[i, :, FFP * k + n : FFP * (k + 1)] = jnp.zeros((64, FFP - n), bf16)
            yield from trade_flow(slots(pack_b), lambda i: wp.at[i], ts, tr)

        lines, fetched = small(), exchange_flow(slots(pack), wa, ss.at[1], rs.at[1])
        run([main(), lines, fetched, pick_flow(cot, pick_y[0], index, dyo, 0, *pick_y[1:]), trade_wide()], plan)

    return pl.pallas_call(
        kernel,
        out_shape=[
            shape((4, 4, 2, 64, NA), bf16),
            shape((1, D)),
            shape((1, D)),
            shape((32, D), bf16),
            shape((ROWS, D), bf16),
            shape((ROWS, 896)),
            shape((4, 512)),
            shape((1, DV)),
            shape((4, 64, NB), bf16),
            shape((SEG, D), bf16),
            shape((SEG, 512), bf16),
            shape((SEG, CH)),
            shape((SEG, DK + DV)),
            shape((SEG, 128)),
            shape((8, SEG)),
            shape((4, 2, DK, DK + DV), bf16),
            shape((SEG, DV), bf16),
            shape((SEG, DV)),
            shape((SEG, DV)),
            shape((NCH, DK, DV)),
            shape((SEG, 128)),
            shape((8, SEG)),
            shape((8, 128)),
        ],
        in_specs=[SM] * 4 + [VM] * 18,
        out_specs=[VM] * 23,
        scratch_shapes=[
            pltpu.VMEM((4, 64, NA), bf16),
            pltpu.VMEM((4, 64, NB), bf16),
            pltpu.VMEM((4, 8, 128), f32),
            pltpu.VMEM((4, 4, 2, 8, 128), f32),
            pltpu.VMEM((32, 128), f32),
            pltpu.VMEM((ROWS, D), bf16),
            pltpu.VMEM((DK, DK + DV), bf16),
            pltpu.SMEM((16,), i32),
        ]
        + PICK_SCRATCH * 2
        + [
            pltpu.SemaphoreType.DMA((2, 15)),
            pltpu.SemaphoreType.DMA((2, 15)),
            pltpu.SemaphoreType.DMA((11,)),
            pltpu.SemaphoreType.DMA((11,)),
        ]
        + TRADE_SEMS,
        compiler_params=remote_params(cid),
    )(order, lens, a_log, dt_bias, tokens, cotangent, *weights, *wide_weights, *convs, *gains)


def in_order(flows, plan):
    for i in plan:
        next(flows[int(i)], None)
        yield
    yield from together(flows)


def back(dn, o, proj, hg, qkv, tm, wu, gb, cr, mc, mr, maps, fr, st, cw, sc, m, ypart, sgu, sd, da, nv, order, xrows, dm, gain, h1, wa, dgain2, cid, plan=PLANS["back"], plan2="011010"):
    nh, ns, nc = len(HOME_SCRATCH), 7, len(SCATTER_SCRATCH)

    def kernel(
        dn, o, proj, hg, qkv, tm, wu, gb, cr, mc, mr, maps, fr, st, cw, sc, m, ypart, sgu, sd, da, nv, order, xr, dm, gain, h1, wa, dgain2,
        both, g_out, ro, rgu, rd, t_out, tot,
        dproj, dhg, dcw, dsc, do, dgp, e, tails, dz, dab, dqkv, edge, ms, mq, ds, dq, acc, grad_o, part, acc2, grad, line, rows, xr4, xs, xq, *refs,
    ):
        sum_y, sum_x, refs = refs[:nc], refs[nc : 2 * nc], refs[2 * nc :]
        home, refs = refs[:nh], refs[nh:]
        so, sg, st_, trades = refs[:ns], refs[ns : 2 * ns], refs[2 * ns : 3 * ns], refs[3 * ns :]
        zq, gp, ab = proj.at[:, 0:512], proj.at[:, 512:768], proj.at[:, 768:896]
        x = lax.axis_index("x")
        seg = lax.axis_index("z") * 2 + lax.axis_index("c")
        ready = hail(plane_peers() + segment_peers())

        def main():
            yield from back_emit(dn, o, gp, hg, qkv, wu, gb, cr, mc, mr, do, dgp, dhg, e)
            yield from map_gather(e, tails, ms, mq)
            yield from back_delta(
                seg, Maps(maps), Maps(tails), do, fr, st, qkv, tm, wu, gb, cr, zq, ab, cw, sc, mc, mr, dz, dab, dcw, dsc, dqkv
            )
            before = lax.rem(seg + 7, 8)
            cp = send(dz.at[0:HALO], edge, ds, dq, {"z": before // 2, "c": lax.rem(before, 2)})
            dproj[0 : SEG - HALO, 0:512] = dz[HALO:SEG].astype(bf16)
            dproj[:, 512:768] = dgp[...]
            dproj[:, 768:896] = dab[...]
            yield
            cp.wait_recv()
            dproj[SEG - HALO : SEG, 0:512] = (dz[SEG:ROWS] + jnp.where(seg < 7, edge[...], 0.0)).astype(bf16)
            cp.wait_send()
            for t in range(4):
                cols = slice(512 * t, 512 * (t + 1))
                part[:, :, :, cols] = dot(dproj[...], wa[cols, 0:896], ((1,), (1,))).astype(bf16).reshape(4, 4, 32, 512)
            yield from in_order([input_grads(), weight_grads()], plan2)

        def result():
            yield from plane_sum(ypart, acc, *sum_y)
            rows[0] = (m[...] + acc[...]).astype(bf16)

        def output_grads():
            weight_tiles(lambda cols: da[:, cols], lambda: nv[...], grad_o)
            yield from scatter_flow(grad_o, ro, *so)

        def weight_grads():
            weight_tiles(lambda cols: h1[HALO:, cols], lambda: dproj[...], grad)
            yield from scatter_flow(grad, g_out, *sg)

        def small_grads():
            yield from scatter_flow(line, t_out, *st_)
            xr4[x] = (t_out[0] + t_out[1]) + (t_out[2] + t_out[3])
            sends = [send(xr4.at[x], xr4.at[x], xs.at[k], xq.at[k], {"x": at("x", k)}) for k in (2, 1, 3)]
            yield
            for cp in sends:
                cp.wait_recv()
            tot[...] = (xr4[0] + xr4[1]) + (xr4[2] + xr4[3])
            for cp in sends:
                cp.wait_send()

        def fill_lines():
            lane = lax.broadcasted_iota(i32, (32, 128), 1)
            top = jnp.where(lane == 72, dsc[0:1, 0:1], 0.0) + jnp.where(lane == 73, dsc[1:2, 0:1], 0.0)
            for j in range(4):
                top = top + spread_lanes(dcw[j : j + 1, QC], 4, 4 * j) + spread_lanes(dcw[j : j + 1, KC], 4, 16 + 4 * j)
                top = top + spread_lanes(dcw[j : j + 1, VC], 8, 32 + 8 * j)
            top = top + spread_lanes(dhg[...], 8, 64)
            line[...] = jnp.zeros(line.shape, f32)
            for i in range(32):
                line[i // 8, i // 2 % 4, i % 2, 0:1, :] = top[i : i + 1]
                line[i // 8, i // 2 % 4, i % 2, 2:3, 0:64] = dgain2[:, 64 * i : 64 * (i + 1)]

        def input_grads():
            sums = plane_sum(part, acc2, *sum_x)
            next(sums)
            fill_lines()
            yield
            yield from sums
            dvr, dgain = norm_back(xr[...].astype(f32), gain[...], acc2[...])
            for _ in outcome:
                pass
            rows[1] = (dm[...] + dvr).astype(bf16)
            for i in range(32):
                line[i // 8, i // 2 % 4, i % 2, 1:2, 0:64] = dgain[:, 64 * i : 64 * (i + 1)]
            yield from together([home_flow(rows, both, order, *home), small_grads()])

        def trade(staged, out, sems):
            yield from trade_flow(slots(staged), lambda y: out.at[y], *sems)

        outcome, chain = result(), main()
        for _ in range(4):
            next(chain)
        ready()
        run([chain, outcome, output_grads(), trade(sgu, rgu, trades[0:2]), trade(sd, rd, trades[2:4])], plan)

    td, gd, god = (8, 128), (64, 896), (64, DV)
    return pl.pallas_call(
        kernel,
        out_shape=[
            shape((2, 128, 512), bf16),
            shape((4,) + gd, bf16),
            shape((4,) + god, bf16),
            shape(sgu.shape, bf16),
            shape(sd.shape, bf16),
            shape((4,) + td),
            shape(td),
        ],
        in_specs=[VM] * 22 + [SM] + [VM] * 6,
        out_specs=[VM] * 7,
        scratch_shapes=[
            pltpu.VMEM((SEG, 896), bf16),
            pltpu.VMEM((1, DV), f32),
            pltpu.VMEM((4, 512), f32),
            pltpu.VMEM((2, 128), f32),
            pltpu.VMEM((SEG, DV), f32),
            pltpu.VMEM((SEG, DV), bf16),
            pltpu.VMEM((DK, DV), bf16),
            pltpu.VMEM((4, 2, DK, DV), bf16),
            pltpu.VMEM((ROWS, 512), f32),
            pltpu.VMEM((SEG, 128), bf16),
            pltpu.VMEM((SEG, 512), f32),
            pltpu.VMEM((HALO, 512), f32),
            pltpu.SemaphoreType.DMA((11,)),
            pltpu.SemaphoreType.DMA((11,)),
            pltpu.SemaphoreType.DMA,
            pltpu.SemaphoreType.DMA,
            pltpu.VMEM((32, D), f32),
            pltpu.VMEM((4, 4, 2) + god, bf16),
            pltpu.VMEM((4, 4, 32, D), bf16),
            pltpu.VMEM((32, D), f32),
            pltpu.VMEM((4, 4, 2) + gd, bf16),
            pltpu.VMEM((4, 4, 2) + td, f32),
            pltpu.VMEM((2, 32, D), bf16),
            pltpu.VMEM((4,) + td, f32),
            pltpu.SemaphoreType.DMA((4,)),
            pltpu.SemaphoreType.DMA((4,)),
        ]
        + SCATTER_SCRATCH * 2
        + HOME_SCRATCH
        + scatter_scratch(god, bf16)
        + scatter_scratch(gd, bf16)
        + scatter_scratch(td, f32)
        + TRADE_SEMS * 2,
        compiler_params=remote_params(cid),
    )(dn, o, proj, hg, qkv, tm, wu, gb, cr, mc, mr, maps, fr, st, cw, sc, m, ypart, sgu, sd, da, nv, order, xrows, dm, gain, h1, wa, dgain2)


def lay_out(both, ra, ro, rgu, rd, lines, total, ff):
    def kernel(both, ra, ro, rgu, rd, lines, total, out, dt, dq, dk, dv, dg, da, db, do, gg, gu, gd, cq, ck, cv, g1, g2, hg, al, bi):
        out[...] = both[0]
        dt[...] = both[1]
        g1[...] = total[1:2, 0:64]
        g2[...] = total[2:3, 0:64]
        hg[...] = total[0:1, 64:72]
        diag = lax.broadcasted_iota(i32, (64, 64), 0) == lax.broadcasted_iota(i32, (64, 64), 1)
        for i in range(4):
            for ref, cols in ((dq, QC), (dk, KC), (dv, VC), (dg, slice(512, 768))):
                ref[:, i, :] = ra[i, :, cols].astype(f32)
            do[i] = ro[i].astype(f32)
            n = min(FFP, ff - FFP * i)
            cols = slice(FFP * i, FFP * i + n)
            gg[:, cols] = rgu[i, :, 0:n].astype(f32)
            gu[:, cols] = rgu[i, :, FFP : FFP + n].astype(f32)
            gd[:, cols] = rd[i, :, 0:n].astype(f32)
            for k, ref in enumerate((da, db)):
                col = ra[i, :, 768 + k : 769 + k].astype(f32)
                ref[i : i + 1, :] = jnp.sum(jnp.where(diag, col, 0.0), axis=0, keepdims=True)
            al[:, i : i + 1] = lines[i, 0:1, 72:73]
            bi[:, i : i + 1] = lines[i, 0:1, 73:74]
            for j in range(4):
                cq[j, i : i + 1, :] = lines[i, 0:1, 4 * j : 4 * j + 4]
                ck[j, i : i + 1, :] = lines[i, 0:1, 16 + 4 * j : 20 + 4 * j]
                cv[j, i : i + 1, :] = lines[i, 0:1, 32 + 8 * j : 40 + 8 * j]

    return pl.pallas_call(
        kernel,
        out_shape=[shape((128, 512), bf16)] * 2
        + [shape((64, 4, DK))] * 2
        + [shape((64, 4, DV))] * 2
        + [shape((4, 64))] * 2
        + [shape((4, 64, DV))]
        + [shape((64, ff))] * 3
        + [shape((4, 4, 4)), shape((4, 4, 4)), shape((4, 4, 8))]
        + [shape((1, n)) for n in (64, 64, 8, 4, 4)],
        in_specs=[VM] * 7,
        out_specs=[VM] * 20,
        compiler_params=pltpu.CompilerParams(vmem_limit_bytes=VLIM),
    )(both, ra, ro, rgu, rd, lines, total)


def body(
    tokens,
    cotangent,
    seq_lengths,
    stretch_order,
    attn_gain,
    w_query,
    w_key,
    w_value,
    w_alpha,
    w_beta,
    conv_query,
    conv_key,
    conv_value,
    a_log,
    dt_bias,
    head_gain,
    w_outgate,
    w_output,
    mlp_gain,
    w_gate,
    w_up,
    w_down,
):

    wa, gain1, gain2, xrows, h1, proj, cw, hg, wpart, dys, qkv, tm, wu, gb, cr, maps, nv, ov, fr, st, mc, mr, sc = front(
        stretch_order,
        seq_lengths,
        a_log,
        dt_bias,
        tokens.reshape(2, STRETCH, D),
        cotangent.reshape(2, STRETCH, D),
        (w_query, w_key, w_value, w_outgate, w_alpha.T, w_beta.T, w_output.swapaxes(1, 2)),
        (w_gate, w_up, w_down.T),
        (conv_query, conv_key, conv_value),
        (head_gain[None], attn_gain[None], mlp_gain[None]),
        1,
    )
    wa = wa.reshape(D, NA)
    m, dm, dgain2, da, dn, ypart, sgu, sd = middle(
        nv.reshape(4, 4, 32, DV), wa, xrows, gain2, wpart, dys.reshape(4, 4, 32, D), 2
    )
    da, dn = da.reshape(SEG, D), dn.reshape(SEG, DV)

    both, ra, ro, rgu, rd, rt, total = back(
        dn, ov, proj, hg, qkv, tm, wu, gb, cr, mc, mr, maps, fr, st, cw, sc, m, ypart, sgu, sd, da, nv,
        stretch_order, xrows, dm, gain1, h1, wa, dgain2, 3,
    )
    out, dtok, d_query, d_key, d_value, d_outgate, d_alpha, d_beta, d_output, d_gate, d_up, d_down, cq, ck, cv, g1, g2, hgain, al, bias = lay_out(
        both, ra, ro, rgu, rd, rt, total, w_gate.shape[1]
    )
    return (
        out,
        dtok,
        g1[0],
        d_query,
        d_key,
        d_value,
        d_alpha.T,
        d_beta.T,
        cq,
        ck,
        cv,
        al[0],
        bias[0],
        hgain[0],
        d_outgate,
        d_output.swapaxes(1, 2),
        g2[0],
        d_gate,
        d_up,
        d_down.T,
    )


def solution(mesh):
    torus = Mesh(mesh.devices.reshape(4, 4, 2, 4), ("y", "z", "c", "x"))
    dp, tp = ("y", "z", "c"), "x"
    in_specs = (
        P(dp, None),
        P(dp, None),
        P(),
        P(),
        P(dp),
        P(dp, tp, None),
        P(dp, tp, None),
        P(dp, tp, None),
        P(dp, tp),
        P(dp, tp),
        P(None, tp, dp),
        P(None, tp, dp),
        P(None, tp, dp),
        P(tp),
        P(tp),
        P(dp),
        P(dp, tp, None),
        P(tp, None, dp),
        P(dp),
        P(dp, tp),
        P(dp, tp),
        P(tp, dp),
    )
    out_specs = (
        P(dp, tp),
        P(dp, tp),
        P(dp),
        P(dp, tp, None),
        P(dp, tp, None),
        P(dp, tp, None),
        P(dp, tp),
        P(dp, tp),
        P(None, tp, dp),
        P(None, tp, dp),
        P(None, tp, dp),
        P(tp),
        P(tp),
        P(dp),
        P(dp, tp, None),
        P(tp, None, dp),
        P(dp),
        P(dp, tp),
        P(dp, tp),
        P(tp, dp),
    )
    return jax.shard_map(body, mesh=torus, in_specs=in_specs, out_specs=out_specs, check_vma=False)
```

```python
import functools
import math

import jax
import jax.numpy as jnp
from jax import lax
from jax.experimental import pallas as pl
from jax.experimental.pallas import tpu as pltpu
from jax.sharding import Mesh
from jax.sharding import PartitionSpec as P

MESH = pl.DeviceIdType.MESH
bf16, f32, i32 = jnp.bfloat16, jnp.float32, jnp.int32
HI = lax.Precision.HIGHEST
EPS = 1e-6
STRETCH = 64
D, DK, DV, FFP, HALO = 2048, 128, 256, 384, 16
SEG = 512
ROWS = SEG + HALO
CH = 128
NCH = SEG // CH
NA, NB = 1152, 1152
VLIM = 58 * 1024 * 1024


def at(axis, k):
    n = lax.axis_size(axis)
    return lax.rem(lax.axis_index(axis) + k + n, n)


def hail(peers):
    b = pltpu.get_barrier_semaphore()
    for p in peers:
        pl.semaphore_signal(b, inc=1, device_id=p, device_id_type=MESH)
    return lambda: pl.semaphore_wait(b, len(peers))


def send(src, dst, ss, rs, who):
    cp = pltpu.make_async_remote_copy(
        src_ref=src, dst_ref=dst, send_sem=ss, recv_sem=rs, device_id=who, device_id_type=MESH
    )
    cp.start()
    return cp


def run(flows, plan=""):
    flows = list(flows)
    for i in plan:
        next(flows[int(i)], None)
    for _ in together(flows):
        pass


def together(flows):
    flows = list(flows)
    while flows:
        left = []
        for f in flows:
            try:
                next(f)
                left.append(f)
            except StopIteration:
                pass
        flows = left
        if flows:
            yield


def segment_peers():
    z, c = lax.axis_index("z"), lax.axis_index("c")
    out = []
    for k in range(4):
        for d in range(2):
            if (k, d) != (0, 0):
                out.append({"z": at("z", k), "c": lax.rem(c + d, 2)})
    return out


def plane_peers():
    return [{"x": at("x", i), "y": at("y", j)} for i in range(4) for j in range(4) if (i, j) != (0, 0)]


def peers(**steps):
    return [{ax: at(ax, k)} for ax, ks in steps.items() for k in ks]


def zc_gather(slot, halves, ss, rs):
    z, c = lax.axis_index("z"), lax.axis_index("c")
    other = {"c": 1 - c}
    zp, zm, zf = at("z", 1), at("z", -1), at("z", 2)
    own, (o1, o2) = slot(z, c), halves(z, c)
    a = send(o1, o1, ss.at[0], rs.at[0], {"z": zp})
    b = send(o2, o2, ss.at[1], rs.at[1], {"z": zm})
    a2 = send(o2, o2, ss.at[9], rs.at[9], {"z": zp})
    b2 = send(o1, o1, ss.at[10], rs.at[10], {"z": zm})
    d0 = send(own, own, ss.at[4], rs.at[4], other)
    yield
    a.wait_recv()
    lo = halves(zm, c)[0]
    e = send(lo, lo, ss.at[2], rs.at[2], {"z": zp})
    b.wait_recv()
    hi = halves(zp, c)[1]
    f = send(hi, hi, ss.at[3], rs.at[3], {"z": zm})
    yield
    a2.wait_recv()
    m = slot(zm, c)
    d1 = send(m, m, ss.at[5], rs.at[5], other)
    b2.wait_recv()
    p = slot(zp, c)
    d2 = send(p, p, ss.at[6], rs.at[6], other)
    yield
    e.wait_recv()
    fl = halves(zf, c)[0]
    d3 = send(fl, fl, ss.at[7], rs.at[7], other)
    f.wait_recv()
    fh = halves(zf, c)[1]
    d4 = send(fh, fh, ss.at[8], rs.at[8], other)
    yield
    for cp in (d0, d1, d2, d3, d4):
        cp.wait_recv()
    for cp in (a, b, a2, b2, e, f, d0, d1, d2, d3, d4):
        cp.wait_send()


def zc_direct(slot, ss, rs):
    z, c = lax.axis_index("z"), lax.axis_index("c")
    other = {"c": 1 - c}
    own = slot(z, c)
    far = [send(own, own, ss.at[k - 1], rs.at[k - 1], {"z": at("z", k)}) for k in (2, 1, 3)]
    over = [send(own, own, ss.at[3], rs.at[3], other)]
    yield
    for k, cp in zip((2, 1, 3), far):
        cp.wait_recv()
        got = slot(at("z", -k), c)
        over.append(send(got, got, ss.at[3 + k], rs.at[3 + k], other))
    yield
    for cp in over:
        cp.wait_recv()
    for cp in far + over:
        cp.wait_send()


def trade_flow(src_of, dst, ss, rs):
    y = lax.axis_index("y")
    loc = pltpu.make_async_copy(src_of(y), dst(y), ss.at[3])
    loc.start()
    sends = [
        send(src_of(at("y", k)), dst(y), ss.at[k - 1], rs.at[k - 1], {"y": at("y", k)}) for k in (2, 1, 3)
    ]
    yield
    loc.wait()
    for cp in sends:
        cp.wait_recv()
    for cp in sends:
        cp.wait_send()


def spread_flow(out, ss, rs):
    return zc_gather(
        lambda zz, cc: out.at[:, zz, cc],
        lambda zz, cc: (out.at[0:2, zz, cc], out.at[2:4, zz, cc]),
        ss,
        rs,
    )


def exchange_flow(src_of, out, ss, rs):
    z, c = lax.axis_index("z"), lax.axis_index("c")
    yield from trade_flow(src_of, lambda y: out.at[y, z, c], ss.at[pl.ds(11, 4)], rs.at[pl.ds(11, 4)])
    yield from spread_flow(out, ss, rs)


def torus_gather(a1, a2, block, ss, rs):
    i, j = lax.axis_index(a1), lax.axis_index(a2)
    all_of = []

    def go(ref, who):
        k = len(all_of)
        all_of.append(send(ref, ref, ss.at[k], rs.at[k], who))
        return all_of[-1]

    own = block(i, j)
    first = [(go(own, {a1: at(a1, k)}), k) for k in (2, 1, 3)]
    for k in (2, 1, 3):
        go(own, {a2: at(a2, k)})
    yield
    for cp, k in first:
        cp.wait_recv()
        got = block(at(a1, -k), j)
        for q in (2, 1, 3):
            go(got, {a2: at(a2, q)})
    yield
    for cp in all_of[3:]:
        cp.wait_recv()
    for cp in all_of:
        cp.wait_send()


def lanes(i, j):
    return pl.ds(pl.multiple_of((i * 4 + j) * 128, 128), 128)


def gather_columns(out, skip, ss, rs):
    def half(rows):
        return lambda x, y: out.at[rows, lanes(x, y)]

    one, two = half(slice(0, skip + 256)), half(slice(skip + 256, skip + 512))
    yield from together(
        [
            torus_gather("x", "y", one, ss.at[0], rs.at[0]),
            torus_gather("y", "x", lambda y, x: two(x, y), ss.at[1], rs.at[1]),
        ]
    )


def gather_rows(out, ss, rs, rows=slice(0, 32)):
    def half(cols):
        return lambda x, y: out.at[x, y, rows, cols]

    one, two = half(slice(0, 1024)), half(slice(1024, 2048))
    yield from together(
        [
            torus_gather("x", "y", one, ss.at[0], rs.at[0]),
            torus_gather("y", "x", lambda y, x: two(x, y), ss.at[1], rs.at[1]),
        ]
    )


GATHER_SEMS = [pltpu.SemaphoreType.DMA((2, 15)), pltpu.SemaphoreType.DMA((2, 15))]


def ring_scatter(axis, piece, ready, bufs, emit, ss, rs):
    me, p, m, fr = (at(axis, k) for k in (0, 1, -1, 2))
    ready(fr)
    a = send(piece(fr, 0), bufs.at[0], ss.at[0], rs.at[0], {axis: p})
    c = send(piece(fr, 1), bufs.at[1], ss.at[1], rs.at[1], {axis: m})
    ready(p)
    b = send(piece(p, 1), bufs.at[2], ss.at[2], rs.at[2], {axis: p})
    ready(m)
    d = send(piece(m, 0), bufs.at[3], ss.at[3], rs.at[3], {axis: m})
    ready(me)
    yield
    a.wait_recv()
    bufs[0] = bufs[0] + piece(p, 0)[...]
    e = send(bufs.at[0], bufs.at[4], ss.at[4], rs.at[4], {axis: p})
    c.wait_recv()
    bufs[1] = bufs[1] + piece(m, 1)[...]
    f = send(bufs.at[1], bufs.at[5], ss.at[5], rs.at[5], {axis: m})
    yield
    d.wait_recv()
    e.wait_recv()
    emit(0, piece(me, 0)[...].astype(f32) + bufs[3].astype(f32) + bufs[4].astype(f32))
    b.wait_recv()
    f.wait_recv()
    emit(1, piece(me, 1)[...].astype(f32) + bufs[2].astype(f32) + bufs[5].astype(f32))
    for cp in (a, b, c, d, e, f):
        cp.wait_send()


def plane_scatter(part, rows, res, big, mid, small, h, ss, rs):
    cols = slice(h * 1024, (h + 1) * 1024)
    a1, a2 = ("x", "y") if h == 0 else ("y", "x")
    i, j = lax.axis_index(a1), lax.axis_index(a2)

    def piece(k):
        return part.at[k, :, rows, cols] if h == 0 else part.at[:, k, rows, cols]

    one = [send(piece(at(a1, k)), big.at[k - 1], ss.at[k - 1], rs.at[k - 1], {a1: at(a1, k)}) for k in (2, 1, 3)]
    yield
    for cp in one:
        cp.wait_recv()
    total = piece(i)[...].astype(f32) + big[0].astype(f32)
    mid[...] = (total + (big[1].astype(f32) + big[2].astype(f32))).astype(bf16)
    two = [
        send(mid.at[at(a2, k)], small.at[k - 1], ss.at[k + 2], rs.at[k + 2], {a2: at(a2, k)}) for k in (2, 1, 3)
    ]
    yield
    for cp in two:
        cp.wait_recv()
    res[:, cols] = (mid[j].astype(f32) + small[0].astype(f32)) + (small[1].astype(f32) + small[2].astype(f32))
    for cp in one + two:
        cp.wait_send()


def plane_sum(part, acc, big, mid, small, ss, rs, rows=slice(0, 32)):
    yield from together(
        plane_scatter(part, rows, acc, big.at[h], mid.at[h], small.at[h], h, ss.at[h], rs.at[h]) for h in (0, 1)
    )


def scatter_buffers(rows):
    return [
        pltpu.VMEM((2, 3, 4, rows, 1024), bf16),
        pltpu.VMEM((2, 4, rows, 1024), bf16),
        pltpu.VMEM((2, 3, rows, 1024), bf16),
        pltpu.SemaphoreType.DMA((2, 6)),
        pltpu.SemaphoreType.DMA((2, 6)),
    ]


SCATTER_SCRATCH = scatter_buffers(32)
PLANS = {
    "front": "012010012020134202030030300300000000",
    "middle": "2",
    "back": "1340000020010020012",
}
VM = pl.BlockSpec(memory_space=pltpu.VMEM)
SM = pl.BlockSpec(memory_space=pltpu.SMEM)
HB = pl.BlockSpec(memory_space=pl.ANY)


def shape(dims, kind=f32):
    return jax.ShapeDtypeStruct(dims, kind)


def remote_params(cid):
    return pltpu.CompilerParams(collective_id=cid, has_side_effects=True, vmem_limit_bytes=VLIM)


def columns(r):
    return lambda yy: r.at[:, :, lanes(lax.axis_index("x"), yy)]


def slots(r):
    return lambda yy: r.at[yy]


def pick_flow(src, every, index, out, skip, es, er, gs, gr):
    x, y = lax.axis_index("x"), lax.axis_index("y")
    z, c = lax.axis_index("z"), lax.axis_index("c")
    yield from trade_flow(columns(src), lambda i: every.at[i, z, c], es.at[pl.ds(7, 4)], er.at[pl.ds(7, 4)])
    yield from zc_direct(lambda zz, cc: every.at[:, zz, cc], es, er)
    here = lanes(x, y)

    def block(j):
        a = index[j]
        return every[a >> 4, (a >> 2) & 3, (a >> 1) & 1, a & 1]

    if skip:
        out[0:skip, here] = block(0)[STRETCH - skip : STRETCH]
    for j in range(8):
        out[skip + 64 * j : skip + 64 * (j + 1), here] = block(j + 1)
    yield from gather_columns(out, skip, gs, gr)


PICK_SCRATCH = [
    pltpu.VMEM((4, 4, 2, 2, 64, 128), bf16),
    pltpu.SemaphoreType.DMA((15,)),
    pltpu.SemaphoreType.DMA((15,)),
] + GATHER_SEMS


def spread_gain(line, row, out):
    for i in range(32):
        out[:, 64 * i : 64 * (i + 1)] = line[i // 8, i // 2 % 4, i % 2, row : row + 1, 0:64]


def norm_back(v, gain, dh):
    r = lax.rsqrt(jnp.mean(v * v, axis=-1, keepdims=True) + EPS)
    t = gain * dh
    dv = r * t - v * (r * r * r) * jnp.mean(v * t, axis=-1, keepdims=True)
    return dv, jnp.sum(v * r * dh, axis=0, keepdims=True)


def weight_tiles(left, right, out):
    def tile(t, _):
        v = dot(left(pl.ds(pl.multiple_of(t * 256, 256), 256)), right(), ((0,), (0,))).astype(bf16)
        for k in range(4):
            out[t // 2, lax.rem(t, 2) * 2 + k // 2, k % 2] = v[64 * k : 64 * (k + 1)]
        return 0

    lax.fori_loop(0, 8, tile, 0)


def middle(nv, wa, xrows, gain, wpart, dys, cid, plan=PLANS["middle"]):
    def kernel(nv, wa, xr, gain, wp, dys, m_out, dm_out, dg_out, da_out, dn_out, yp_out, sgu, sd, *refs):
        w, part, part2, h2, hid, dgu, ggu, gd, acc, dgs, refs = *refs[:10], refs[10:]
        sums = [refs[5 * i : 5 * i + 5] for i in range(4)]
        refs = refs[20:]
        gathers = [refs[2 * i : 2 * i + 2] for i in range(4)]
        ws, wr, ls = refs[8:11]
        fgu, fd = refs[11:15], refs[15:19]
        x, y, z, c = (lax.axis_index(a) for a in "xyzc")
        wo = wa.at[:, 896:]
        own = pltpu.make_async_copy(wp, w.at[:, z, c], ls)
        own.start()
        ready = hail(peers(x=(1, 2, 3), y=(1, 2, 3), z=(1, 3), c=(1,)))

        def spread():
            own.wait()
            yield from spread_flow(w, ws, wr)

        weights = spread()

        def flat(ref, rows):
            v = ref[:, :, rows, :]
            return v.reshape(-1, v.shape[-1])

        def grads():
            def first():
                weight_tiles(lambda cols: h2[:, :, :, cols].reshape(SEG, 256), lambda: flat(dgu, slice(0, 32)), ggu)
                yield from sum_flow(ggu, sgu, *fgu)

            def second():
                weight_tiles(lambda cols: dys[:, :, :, cols].reshape(SEG, 256), lambda: flat(hid, slice(0, 32)), gd)
                yield from sum_flow(gd, sd, *fd)

            yield from first()
            yield from second()

        def half(h):
            rows = slice(16 * h, 16 * h + 16)
            nrows = flat(nv, rows)
            for t in range(4):
                cols = slice(512 * t, 512 * (t + 1))
                part[:, :, rows, cols] = dot(nrows, wo[cols, :], ((1,), (1,))).astype(bf16).reshape(4, 4, 16, 512)
            yield
            yield from plane_sum(part, acc.at[h], *sums[h], rows)
            m = xr[rows, :].astype(f32) + acc[h]
            m_out[rows, :] = m
            r = lax.rsqrt(jnp.mean(m * m, axis=-1, keepdims=True) + EPS)
            h2[x, y, rows, :] = (m * r * gain[...]).astype(bf16)
            yield from gather_rows(h2, *gathers[h], rows)
            for _ in weights:
                pass
            wv = w[...].reshape(D, NB)
            both = dot(flat(h2, rows), wv[:, : 2 * FFP], ((1,), (0,)))
            ga, up = both[:, :FFP], both[:, FFP:]
            dhid = dot(flat(dys, rows), wv[:, 2 * FFP :], ((1,), (0,)))
            sg = jax.nn.sigmoid(ga)
            act = ga * sg
            hv = (act * up).astype(bf16)
            hid[:, :, rows, :] = hv.reshape(4, 4, 16, FFP)
            dga = (dhid * up * (sg * (1.0 + ga * (1.0 - sg)))).astype(bf16)
            dup = (dhid * act).astype(bf16)
            dgu[:, :, rows, :FFP] = dga.reshape(4, 4, 16, FFP)
            dgu[:, :, rows, FFP:] = dup.reshape(4, 4, 16, FFP)
            dv = jnp.concatenate([dga, dup], axis=1)
            for t in range(4):
                cols = slice(512 * t, 512 * (t + 1))
                part2[:, :, rows, cols] = (
                    dot(dv, wv[cols, : 2 * FFP], ((1,), (1,))).astype(bf16).reshape(4, 4, 16, 512)
                )

            def back():
                yield from plane_sum(part2, acc.at[2 + h], *sums[2 + h], rows)
                dvr, dgain = norm_back(m_out[rows, :], gain[...], acc[2 + h])
                dm = dys[x, y, rows, :].astype(f32) + dvr
                dm_out[rows, :] = dm
                dgs[h : h + 1, :] = dgain
                da_out[x, y, rows, :] = dm.astype(bf16)
                yield from gather_rows(da_out, *gathers[2 + h], rows)
                dn_out[:, :, rows, :] = dot(flat(da_out, rows), wo[...], ((1,), (0,))).reshape(4, 4, 16, DV)

            def result():
                yield
                for t in range(4):
                    cols = slice(512 * t, 512 * (t + 1))
                    yp_out[:, :, rows, cols] = (
                        dot(hv, wv[cols, 2 * FFP :], ((1,), (1,))).astype(bf16).reshape(4, 4, 16, 512)
                    )

            def later(f, n):
                for _ in range(n):
                    yield
                yield from f

            yield from together([back(), later(result(), 1)] + ([grads()] if h else []))

        halves = half(0), half(1)
        next(halves[0])
        ready()
        next(halves[0])
        next(halves[1])
        next(halves[1])
        run([*halves, weights], plan)
        dg_out[...] = dgs[0:1, :] + dgs[1:2, :]

    gu, gdown = (4, 4, 2, 64, 2 * FFP), (4, 4, 2, 64, FFP)
    return pl.pallas_call(
        kernel,
        out_shape=[
            shape((32, D)),
            shape((32, D)),
            shape((1, D)),
            shape((4, 4, 32, D), bf16),
            shape((4, 4, 32, DV)),
            shape((4, 4, 32, D), bf16),
            shape((4, 64, 2 * FFP), bf16),
            shape((4, 64, FFP), bf16),
        ],
        in_specs=[VM] * 6,
        out_specs=[VM] * 8,
        scratch_shapes=[
            pltpu.VMEM((4, 4, 2, 64, NB), bf16),
            pltpu.VMEM((4, 4, 32, D), bf16),
            pltpu.VMEM((4, 4, 32, D), bf16),
            pltpu.VMEM((4, 4, 32, D), bf16),
            pltpu.VMEM((4, 4, 32, FFP), bf16),
            pltpu.VMEM((4, 4, 32, 2 * FFP), bf16),
            pltpu.VMEM(gu, bf16),
            pltpu.VMEM(gdown, bf16),
            pltpu.VMEM((4, 16, D), f32),
            pltpu.VMEM((2, D), f32),
        ]
        + scatter_buffers(16) * 4
        + GATHER_SEMS * 4
        + [pltpu.SemaphoreType.DMA((11,)), pltpu.SemaphoreType.DMA((11,)), pltpu.SemaphoreType.DMA]
        + sum_scratch(gu[3:], bf16)
        + sum_scratch(gdown[3:], bf16),
        compiler_params=remote_params(cid),
    )(nv, wa, xrows, gain, wpart, dys)


def home_flow(src, dst, order, alls, cols, picks, s1, r1, s2, r2, s3, r3):
    x, y, z, c = (lax.axis_index(a) for a in "xyzc")
    n = src.shape[0]
    sends = []
    cols[x, y] = src[:, :, lanes(x, y)]
    t = 0
    for i in range(4):
        for j in range(4):
            if (i, j) == (0, 0):
                continue
            px, py = at("x", i), at("y", j)
            sends.append(send(src.at[:, :, lanes(px, py)], cols.at[x, y], s1.at[t], r1.at[t], {"x": px, "y": py}))
            t += 1
    yield
    for cp in sends:
        cp.wait_recv()
    for k in range(n):
        alls[z, c, k] = cols[:, :, k].reshape(8, 64, 128)
    yield from zc_direct(lambda zz, cc: alls.at[zz, cc], s2, r2)
    for j in range(4):
        for i in range(2):
            b = order[j * 16 + (z * 2 + c) * 2 + i]
            for k in range(n):
                picks[j, k, 64 * i : 64 * (i + 1)] = alls[b >> 4, (b >> 3) & 1, k, b & 7]
    mine = pl.ds(pl.multiple_of(y * 128, 128), 128)
    last = [
        send(picks.at[at("y", j)], dst.at[:, :, mine], s3.at[j], r3.at[j], {"y": at("y", j)}) for j in (2, 1, 3)
    ]
    dst[:, :, mine] = picks[y]
    yield
    for cp in last:
        cp.wait_recv()
    for cp in sends + last:
        cp.wait_send()


HOME_SCRATCH = [
    pltpu.VMEM((4, 2, 2, 8, 64, 128), bf16),
    pltpu.VMEM((4, 4, 2, 32, 128), bf16),
    pltpu.VMEM((4, 2, 128, 128), bf16),
    pltpu.SemaphoreType.DMA((15,)),
    pltpu.SemaphoreType.DMA((15,)),
    pltpu.SemaphoreType.DMA((7,)),
    pltpu.SemaphoreType.DMA((7,)),
    pltpu.SemaphoreType.DMA((4,)),
    pltpu.SemaphoreType.DMA((4,)),
]


def sum_flow(g, stage, core, bufs, ss, rs):
    c = lax.axis_index("c")
    d = send(g.at[:, :, 1 - c], core, ss.at[0], rs.at[0], {"c": 1 - c})
    yield
    d.wait_recv()

    def ready(i):
        for k in range(4):
            core[k, i] = core[k, i] + g[k, i, c]

    def emit(s, v):
        stage[2 * s : 2 * s + 2] = v.astype(stage.dtype)

    def piece(i, s):
        return core.at[2 * s : 2 * s + 2, i]

    yield from ring_scatter("z", piece, ready, bufs, emit, ss.at[pl.ds(1, 6)], rs.at[pl.ds(1, 6)])
    d.wait_send()


def sum_scratch(dims, kind):
    return [
        pltpu.VMEM((4, 4) + dims, kind),
        pltpu.VMEM((6, 2) + dims, kind),
        pltpu.SemaphoreType.DMA((7,)),
        pltpu.SemaphoreType.DMA((7,)),
    ]


TRADE_SEMS = [pltpu.SemaphoreType.DMA((4,)), pltpu.SemaphoreType.DMA((4,))]


def scatter_flow(g, out, stage, ts, tr, *sums):
    yield from sum_flow(g, stage, *sums)
    yield from trade_flow(slots(stage), lambda y: out.at[y], ts, tr)


def scatter_scratch(dims, kind):
    return [pltpu.VMEM((4,) + dims, kind)] + TRADE_SEMS + sum_scratch(dims, kind)


def dot(a, b, dims, prec=None):
    return lax.dot_general(a, b, (dims, ((), ())), preferred_element_type=f32, precision=prec)


def lo(a):
    return a.astype(bf16)


def mm(a, b):
    return dot(lo(a), lo(b), ((1,), (0,)))


def mmt(a, b):
    return dot(lo(a), lo(b), ((1,), (1,)))


def tmm(a, b):
    return dot(lo(a), lo(b), ((0,), (0,)))


def halves_of(a):
    h = a.astype(bf16)
    return h, (a - h.astype(f32)).astype(bf16)


def fine(a, b, dims=((1,), (0,))):
    ah, al = halves_of(a)
    bh, bl = halves_of(b)
    return dot(ah, bh, dims) + (dot(ah, bl, dims) + dot(al, bh, dims))


def tri_inverses(every, r, c):
    eye = jnp.where(r == c, 1.0, 0.0)
    n1 = [jnp.where((r >> 3) == (c >> 3), -a, 0.0) for a in every]
    n2 = [fine(n, n) for n in n1]
    ts = [eye + n for n in n1]
    ts = [t + fine(t, n) for t, n in zip(ts, n2)]
    n4 = [fine(n, n) for n in n2]
    ts = [t + fine(t, n) for t, n in zip(ts, n4)]
    for level in (3, 4, 5, 6):
        off = ((r >> (level + 1)) == (c >> (level + 1))) & ((r >> level) != (c >> level))
        us = [fine(jnp.where(off, a, 0.0), t) for a, t in zip(every, ts)]
        ts = [t - fine(t, u) for t, u in zip(ts, us)]
    return ts


def iotas():
    return (
        lax.broadcasted_iota(i32, (CH, CH), 0),
        lax.broadcasted_iota(i32, (CH, CH), 1),
    )


def filtered(z, cw, mc, cols):
    total = z[HALO : HALO + SEG, cols] * cw[3:4, cols]
    for j in range(3):
        total = total + mc[:, j : j + 1] * cw[j : j + 1, cols] * z[HALO - 3 + j : HALO - 3 + j + SEG, cols]
    return total


def silu(v):
    return v * jax.nn.sigmoid(v)


QC, KC, VC = slice(0, 128), slice(128, 256), slice(256, 512)


def decay_of(cc, cr, mask):
    return jnp.exp(jnp.where(mask, cc - cr, 0.0)) * jnp.where(mask, 1.0, 0.0)


def prepare(z, ab, cw, sc, mc, mr, qkv, tm, wu, gb, cr, ti):
    r, c = iotas()
    for cols, scale in ((QC, DK**-0.5), (KC, 1.0)):
        s = silu(filtered(z, cw, mc, cols))
        qkv[:, cols] = (s * lax.rsqrt(jnp.sum(s * s, axis=-1, keepdims=True) + EPS) * scale).astype(bf16)
    qkv[:, VC] = silu(filtered(z, cw, mc, VC)).astype(bf16)
    low = jnp.where(r >= c, 1.0, 0.0)
    eye = jnp.where(r == c, 1.0, 0.0)
    lane = lax.broadcasted_iota(i32, (CH, 128), 1)
    yield
    systems, rights, tails = [], [], []
    for n in range(NCH):
        rows = slice(n * CH, (n + 1) * CH)
        raw = ab[HALO + n * CH : HALO + (n + 1) * CH, :]
        beta = jax.nn.sigmoid(raw[:, 1:2])
        u = raw + sc[0:1, 1:2]
        g = -jnp.exp(sc[0:1, 0:1]) * (jnp.maximum(u, 0.0) + jnp.log1p(jnp.exp(-jnp.abs(u))))
        g = jnp.where(lane == 0, g, 0.0)
        cum = dot(low, g, ((1,), (0,)), HI)[:, 0:1]
        cumr = dot(g, low, ((0,), (1,)), HI)[0:8, :]
        gb[rows, :] = jnp.where(lane == 0, beta, cum)
        cr[:, rows] = cumr
        cumrow = cumr[0:1, :]
        last = cumr[0:1, CH - 1 : CH]
        m = mc[rows, :]
        carried, closing, begin, carry_last = m[:, 3:4], m[:, 4:5], m[:, 5:6], m[0:1, 6:7]
        same = begin == mr[0:1, rows]
        k = qkv[rows, KC]
        kf = k.astype(f32)
        v = qkv[rows, VC].astype(f32)
        systems.append(beta * dot(k, k, ((1,), (1,))) * decay_of(cum, cumrow, same & (r > c)))
        rights.append(jnp.concatenate([(beta * jnp.exp(cum) * carried) * kf, beta * v], axis=1))
        tails.append((kf * (jnp.exp(last - cum) * closing), jnp.exp(last) * carry_last))
    yield
    inverses = tri_inverses(systems, r, c)
    yield
    solved = [fine(t, right) for t, right in zip(inverses, rights)]
    hands, injects = [], []
    for n in range(NCH):
        rows = slice(n * CH, (n + 1) * CH)
        tm[rows, :] = inverses[n]
        wu[rows, :] = solved[n]
        tail, keep = tails[n]
        both = fine(tail, solved[n], ((0,), (0,)))
        hands.append(keep * eye - both[:, 0:DK])
        injects.append(both[:, DK:])
    yield
    total = jnp.concatenate([hands[0], injects[0]], axis=1)
    for n in range(1, NCH):
        total = fine(hands[n], total) + jnp.concatenate([jnp.zeros((DK, DK), f32), injects[n]], axis=1)
    ti[...] = total.astype(bf16)
    yield


def emit_outputs(seg, maps, qkv, wu, gb, cr, mc, mr, gp, hg, nout, oout, fout, sout):
    r, c = iotas()

    def fold(d, s):
        tr, ins = maps[d, :, 0:DK], maps[d, :, DK:].astype(f32)
        sh, sl = halves_of(s)
        new = dot(tr, sh, ((1,), (0,))) + dot(tr, sl, ((1,), (0,))) + ins
        return jnp.where(d < seg, new, s)

    s = lax.fori_loop(0, 7, fold, jnp.zeros((DK, DV), f32))
    for n in range(NCH):
        rows = slice(n * CH, (n + 1) * CH)
        m = mc[rows, :]
        carried, closing, begin, carry_last = m[:, 3:4], m[:, 4:5], m[:, 5:6], m[0:1, 6:7]
        cum = gb[rows, 1:2]
        cumrow = cr[0:1, rows]
        last = cr[0:1, n * CH + CH - 1 : n * CH + CH]
        same = begin == mr[0:1, rows]
        q, k = qkv[rows, QC], qkv[rows, KC]
        p = dot(q, k, ((1,), (1,))) * decay_of(cum, cumrow, same & (r >= c))
        fresh = wu[rows, DK:] - fine(wu[rows, 0:DK], s)
        qd = q.astype(f32) * (jnp.exp(cum) * carried)
        o = mm(qd, s) + mm(p, fresh)
        sout[n] = s
        fout[rows, :] = fresh
        oout[rows, :] = o
        x = gp[HALO + n * CH : HALO + (n + 1) * CH, :]
        rn = lax.rsqrt(jnp.mean(o * o, axis=-1, keepdims=True) + EPS)
        nout[rows, :] = (o * rn * hg[0:1, :] * silu(x)).astype(bf16)
        tail = k.astype(f32) * (jnp.exp(last - cum) * closing)
        s = (jnp.exp(last) * carry_last) * s + fine(tail, fresh, ((0,), (0,)))
        yield


def back_emit(dn, o, gp, hg, qkv, wu, gb, cr, mc, mr, do_out, dgp_out, dhg_out, e_out):
    r, c = iotas()
    dhg = jnp.zeros((1, DV), f32)
    e = jnp.zeros((DK, DV), f32)
    for n in reversed(range(NCH)):
        rows = slice(n * CH, (n + 1) * CH)
        ov, x, dnv = o[rows, :], gp[HALO + n * CH : HALO + (n + 1) * CH, :], dn[rows, :]
        rn = lax.rsqrt(jnp.mean(ov * ov, axis=-1, keepdims=True) + EPS)
        sg = jax.nn.sigmoid(x)
        act = x * sg
        h = hg[0:1, :]
        base = ov * rn
        dhg = dhg + jnp.sum(base * act * dnv, axis=0, keepdims=True)
        dgp_out[rows, :] = (dnv * base * h * (sg * (1.0 + x * (1.0 - sg)))).astype(bf16)
        t = dnv * h * act
        do = rn * t - base * (rn * rn) * jnp.mean(ov * t, axis=-1, keepdims=True)
        do_out[rows, :] = do
        m = mc[rows, :]
        carried, closing, begin, carry_last = m[:, 3:4], m[:, 4:5], m[:, 5:6], m[0:1, 6:7]
        cum = gb[rows, 1:2]
        cumrow = cr[0:1, rows]
        last = cr[0:1, n * CH + CH - 1 : n * CH + CH]
        same = begin == mr[0:1, rows]
        q, k = qkv[rows, QC], qkv[rows, KC]
        p = dot(q, k, ((1,), (1,))) * decay_of(cum, cumrow, same & (r >= c))
        qd = q.astype(f32) * (jnp.exp(cum) * carried)
        tail = k.astype(f32) * (jnp.exp(last - cum) * closing)
        df = tmm(p, do) + mm(tail, e)
        e = tmm(qd, do) + (jnp.exp(last) * carry_last) * e - tmm(wu[rows, 0:DK], df)
        yield
    dhg_out[...] = dhg
    e_out[...] = e.astype(bf16)


def back_delta(seg, maps, tails, do, fr, st, qkv, tm, wu, gb, cr, z, ab, cw, sc, mc, mr, dz, dab, dcw, dsc, dqkv):
    r, c = iotas()
    low = jnp.where(r >= c, 1.0, 0.0)
    ones = jnp.ones((CH, CH), f32)
    lane = lax.broadcasted_iota(i32, (CH, 128), 1)
    row = lax.broadcasted_iota(i32, (CH, 1), 0)

    def fold(i, e):
        d = 7 - i
        tr, own = maps[d, :, 0:DK], tails[d].astype(f32)
        eh, el = halves_of(e)
        new = dot(tr, eh, ((0,), (0,))) + dot(tr, el, ((0,), (0,))) + own
        return jnp.where(d > seg, new, e)

    e = lax.fori_loop(0, 7, fold, jnp.zeros((DK, DV), f32))
    acc_a = jnp.zeros((1, 128), f32)
    acc_d = jnp.zeros((1, 128), f32)
    for n in reversed(range(NCH)):
        rows = slice(n * CH, (n + 1) * CH)
        m = mc[rows, :]
        carried, closing, begin, carry_last = m[:, 3:4], m[:, 4:5], m[:, 5:6], m[0:1, 6:7]
        beta, cum = gb[rows, 0:1], gb[rows, 1:2]
        cumrow = cr[0:1, rows]
        last = cr[0:1, n * CH + CH - 1 : n * CH + CH]
        same = begin == mr[0:1, rows]
        q, k = qkv[rows, QC], qkv[rows, KC]
        qf, kf, vf = q.astype(f32), k.astype(f32), qkv[rows, VC].astype(f32)
        dec_i = decay_of(cum, cumrow, same & (r >= c))
        dec_s = jnp.where(r > c, dec_i, 0.0)
        p = dot(q, k, ((1,), (1,))) * dec_i
        kkd = dot(k, k, ((1,), (1,))) * dec_s
        ex = jnp.exp(cum) * carried
        tf = jnp.exp(last - cum) * closing
        keep = jnp.exp(last) * carry_last
        tail = kf * tf
        qd = qf * ex
        dov, fv, sv, tv = do[rows, :], fr[rows, :], st[n], tm[rows, :]
        w, u = wu[rows, 0:DK], wu[rows, DK:]
        df = tmm(p, dov) + mm(tail, e)
        dw = -mmt(df, sv)
        dtail = mmt(fv, e)
        dkeep = jnp.sum(jnp.sum(sv * e, axis=1, keepdims=True), axis=0, keepdims=True)
        dqd = mmt(dov, sv)
        dp = mmt(dov, fv)
        dlead = tmm(tv, dw)
        dbv = tmm(tv, df)
        da = -(mmt(dlead, w) + mmt(dbv, u))
        dakd = da * kkd
        dkk = da * beta * dec_s
        dqk = dp * dec_i
        mix = dakd * beta + dp * p
        dqkv[rows, QC] = mm(dqk, k) + dqd * ex
        dqkv[rows, KC] = (
            tmm(dqk, q) + mm(dkk, k) + tmm(dkk, k) + dlead * (beta * ex) + dtail * tf
        )
        dqkv[rows, VC] = beta * dbv
        lk = jnp.sum(dlead * kf, axis=1, keepdims=True) * ex
        dbeta = jnp.sum(dakd, axis=1, keepdims=True) + lk + jnp.sum(dbv * vf, axis=1, keepdims=True)
        tt = jnp.sum(dtail * tail, axis=1, keepdims=True)
        dcum = jnp.sum(mix, axis=1, keepdims=True) + jnp.sum(dqd * qd, axis=1, keepdims=True) + lk * beta - tt
        dcum = dcum + jnp.where(row == CH - 1, jnp.sum(tt, axis=0, keepdims=True) + dkeep * keep, 0.0)
        full = dcum - dot(mix, ones, ((0,), (0,)), HI)
        dg = dot(low, full, ((0,), (0,)), HI)
        raw = ab[HALO + n * CH : HALO + (n + 1) * CH, :]
        uu = raw + sc[0:1, 1:2]
        rate = -jnp.exp(sc[0:1, 0:1])
        sp = jnp.maximum(uu, 0.0) + jnp.log1p(jnp.exp(-jnp.abs(uu)))
        dal = dg * rate * jax.nn.sigmoid(uu)
        acc_a = acc_a + jnp.sum(dg * rate * sp, axis=0, keepdims=True)
        acc_d = acc_d + jnp.sum(dal, axis=0, keepdims=True)
        dab[rows, :] = jnp.where(
            lane == 0, dal, jnp.where(lane == 1, dbeta * beta * (1.0 - beta), 0.0)
        ).astype(bf16)
        e = tmm(qd, dov) + keep * e - tmm(w, df)
        yield
    dsc[0:1, :] = acc_a
    dsc[1:2, :] = acc_d
    dz[0:HALO, :] = jnp.zeros((HALO, 512), f32)
    for cols, scale in ((QC, DK**-0.5), (KC, 1.0), (VC, None)):
        y = filtered(z, cw, mc, cols)
        sg = jax.nn.sigmoid(y)
        ds = dqkv[:, cols]
        if scale is not None:
            s = y * sg
            rn = lax.rsqrt(jnp.sum(s * s, axis=-1, keepdims=True) + EPS)
            ds = scale * (rn * ds - s * (rn * rn * rn) * jnp.sum(s * ds, axis=-1, keepdims=True))
        dy = ds * (sg * (1.0 + y * (1.0 - sg)))
        dz[HALO : HALO + SEG, cols] = dy * cw[3:4, cols]
        dcw[3:4, cols] = jnp.sum(dy * z[HALO : HALO + SEG, cols], axis=0, keepdims=True)
        for j in range(3):
            part = mc[:, j : j + 1] * dy
            away = slice(HALO - 3 + j, HALO - 3 + j + SEG)
            dcw[j : j + 1, cols] = jnp.sum(part * z[away, cols], axis=0, keepdims=True)
            dz[away, cols] = dz[away, cols] + part * cw[j : j + 1, cols]
        yield


def map_gather(own, out, ss, rs):
    z, c = lax.axis_index("z"), lax.axis_index("c")
    out[z, c] = own[...]
    yield from zc_direct(lambda zz, cc: out.at[zz, cc], ss, rs)


class Maps:
    def __init__(self, ref):
        self.ref = ref

    def __getitem__(self, key):
        key = key if isinstance(key, tuple) else (key,)
        return self.ref[(key[0] // 2, key[0] % 2) + key[1:]]


def masks(lens, mc, mr):
    base = (lax.axis_index("z") * 2 + lax.axis_index("c")) * SEG
    firsts = [jnp.int32(0)]
    for k in range(3):
        firsts.append(firsts[k] + lens[k])

    def begin_of(pos):
        b = jnp.zeros_like(pos)
        for k in range(1, 4):
            b = jnp.where((pos >= firsts[k]) & (pos < firsts[k] + lens[k]), firsts[k], b)
        return b

    lane = lax.broadcasted_iota(i32, (CH, 128), 1)
    for n in range(NCH):
        first = base + n * CH
        pos = first + lax.broadcasted_iota(i32, (CH, 128), 0)
        b = begin_of(pos)
        last = begin_of(jnp.full((CH, 128), first + CH - 1, i32))

        def one(flag):
            return jnp.where(flag, 1.0, 0.0)

        late = jnp.where(lane == 3, one(b < first), jnp.where(lane == 4, one(b == last), one(last < first)))
        flags = jnp.where(lane < 3, one(pos - 3 + lane >= b), late)
        mc[n * CH : (n + 1) * CH, :] = jnp.where(lane == 5, b.astype(f32), flags)
        mr[:, n * CH : (n + 1) * CH] = begin_of(first + lax.broadcasted_iota(i32, (8, CH), 1)).astype(f32)


def spread_lanes(v, wide, first):
    n = 32 * wide
    owner = lax.broadcasted_iota(i32, (32, n), 0) == lax.broadcasted_iota(i32, (32, n), 1) // wide
    place = lax.broadcasted_iota(i32, (n, 128), 1) == first + lax.rem(lax.broadcasted_iota(i32, (n, 128), 0), wide)
    return dot(jnp.where(owner, v, 0.0), jnp.where(place, 1.0, 0.0), ((1,), (0,)), HI)


def gather_lanes(rows, wide, first):
    n = 32 * wide
    owner = lax.broadcasted_iota(i32, (32, n), 0) == lax.broadcasted_iota(i32, (32, n), 1) // wide
    place = lax.broadcasted_iota(i32, (128, n), 0) == first + lax.rem(lax.broadcasted_iota(i32, (128, n), 1), wide)
    every = dot(rows, jnp.where(place, 1.0, 0.0), ((1,), (0,)), HI)
    return jnp.sum(jnp.where(owner, every, 0.0), axis=0, keepdims=True)


def front(order, lens, a_log, dt_bias, tokens, cotangent, weights, wide_weights, convs, gains, cid, plan=PLANS["front"]):
    npk = len(PICK_SCRATCH)

    def kernel(
        order, lens, al, dt, tok, cot, wq, wk, wv, wg, wal, wbe, wou, wga, wup, wdo, cvq, cvk, cvv, hgi, g1i, g2i,
        wa, gain1, gain2, xr, h1, proj, cw, hg, wp, dyo, qkv, tm, wu, gb, cr, maps, nout, oout, fout, sout, mc, mr, sc,
        pack, pack_b, tiny, line, tops, xo, ti, index, *refs,
    ):
        pick_x, pick_y, refs = refs[:npk], refs[npk : 2 * npk], refs[2 * npk :]
        ss, rs, ms, mq, ts, tr = refs
        x, y, z, c = (lax.axis_index(a) for a in "xyzc")
        seg = z * 2 + c
        zq, gp, ab = proj.at[:, 0:512], proj.at[:, 512:768], proj.at[:, 768:896]
        ready = hail(peers(y=(1, 2, 3), z=(1, 2, 3), c=(1,), x=(1, 2, 3)))

        diag = lax.broadcasted_iota(i32, (64, 64), 0) == lax.broadcasted_iota(i32, (64, 64), 1)
        lane = lax.broadcasted_iota(i32, (64, 128), 1)
        for i in range(4):
            for ref, cols in ((wq, QC), (wk, KC), (wv, VC), (wg, slice(512, 768))):
                pack[i, :, cols] = ref[:, i, :].astype(bf16)
            alpha, beta = (jnp.sum(jnp.where(diag, r[i : i + 1, :], 0.0), axis=1, keepdims=True) for r in (wal, wbe))
            pack[i, :, 768:896] = jnp.where(lane == 0, alpha, jnp.where(lane == 1, beta, 0.0)).astype(bf16)
            pack[i, :, 896:1152] = wou[i].astype(bf16)
        tiny[...] = jnp.zeros(tiny.shape, f32)
        for i in range(4):
            for ref, n, first in ((cvq, 4, 0), (cvk, 4, 16), (cvv, 8, 32)):
                for j in range(4):
                    tiny[i, 0:1, first + n * j : first + n * (j + 1)] = ref[j, i : i + 1, :]
            tiny[i, 0:1, 64:72] = hgi[...]
            tiny[i, 1:2, 0:64] = g1i[...]
            tiny[i, 2:3, 0:64] = g2i[...]
        tiny[...] = tiny[...].astype(bf16).astype(f32)

        def find(a, found):
            return tuple(jnp.where(order[a] == jnp.maximum(seg * 8 - 1 + j, 0), a, f) for j, f in enumerate(found))

        for j, f in enumerate(lax.fori_loop(0, 64, find, tuple(jnp.int32(0) for _ in range(9)))):
            index[j] = f
        ready()

        def small():
            se, re = ss.at[0], rs.at[0]
            yield from trade_flow(slots(tiny), lambda i: line.at[i, z, c], se.at[pl.ds(7, 4)], re.at[pl.ds(7, 4)])
            yield from zc_direct(lambda zz, cc: line.at[:, zz, cc], se, re)
            spread_gain(line, 1, gain1)
            spread_gain(line, 2, gain2)
            for i in range(32):
                tops[i : i + 1, :] = line[i // 8, i // 2 % 4, i % 2, 0:1, :]
            top = tops[...]
            for j in range(4):
                cw[j : j + 1, QC] = gather_lanes(top, 4, 4 * j)
                cw[j : j + 1, KC] = gather_lanes(top, 4, 16 + 4 * j)
                cw[j : j + 1, VC] = gather_lanes(top, 8, 32 + 8 * j)
            hg[...] = gather_lanes(top, 8, 64)

        def main():
            yield from pick_flow(tok, pick_x[0], index, xo, HALO, *pick_x[1:])
            for _ in lines:
                pass

            def norm(t, _):
                at_rows = pl.ds(pl.multiple_of(t * 16, 16), 16)
                v = xo[at_rows, :].astype(f32)
                r = lax.rsqrt(jnp.mean(v * v, axis=-1, keepdims=True) + EPS)
                h1[at_rows, :] = (v * r * gain1[...]).astype(bf16)
                return 0

            lax.fori_loop(0, ROWS // 16, norm, 0)
            xr[...] = xo[pl.ds(pl.multiple_of(HALO + 32 * (x * 4 + y), 16), 32), :]
            masks(lens, mc, mr)
            sc[0:8, :] = jnp.where(lax.broadcasted_iota(i32, (8, 128), 1) == 0, al[y], dt[y])
            yield
            for _ in fetched:
                pass
            for cols in (slice(0, 256), slice(256, 512), slice(512, 768), slice(768, 896)):
                w = wa[:, :, :, :, cols]
                proj[:, cols] = dot(h1[...], w.reshape(D, w.shape[-1]), ((1,), (0,)))
            yield
            yield from prepare(zq, ab, cw, sc, mc, mr, qkv, tm, wu, gb, cr, ti)
            yield from map_gather(ti, maps, ms, mq)
            yield from emit_outputs(seg, Maps(maps), qkv, wu, gb, cr, mc, mr, gp, hg, nout, oout, fout, sout)

        def trade_wide():
            ff = wga.shape[1]
            for i in range(4):
                n = min(FFP, ff - FFP * i)
                cols = slice(FFP * i, FFP * i + n)
                for k, v in enumerate((wga[:, cols], wup[:, cols], wdo[:, cols])):
                    pack_b[i, :, FFP * k : FFP * k + n] = v.astype(bf16)
                    if n < FFP:
                        pack_b[i, :, FFP * k + n : FFP * (k + 1)] = jnp.zeros((64, FFP - n), bf16)
            yield from trade_flow(slots(pack_b), lambda i: wp.at[i], ts, tr)

        lines, fetched = small(), exchange_flow(slots(pack), wa, ss.at[1], rs.at[1])
        run([main(), lines, fetched, pick_flow(cot, pick_y[0], index, dyo, 0, *pick_y[1:]), trade_wide()], plan)

    return pl.pallas_call(
        kernel,
        out_shape=[
            shape((4, 4, 2, 64, NA), bf16),
            shape((1, D)),
            shape((1, D)),
            shape((32, D), bf16),
            shape((ROWS, D), bf16),
            shape((ROWS, 896)),
            shape((4, 512)),
            shape((1, DV)),
            shape((4, 64, NB), bf16),
            shape((SEG, D), bf16),
            shape((SEG, 512), bf16),
            shape((SEG, CH)),
            shape((SEG, DK + DV)),
            shape((SEG, 128)),
            shape((8, SEG)),
            shape((4, 2, DK, DK + DV), bf16),
            shape((SEG, DV), bf16),
            shape((SEG, DV)),
            shape((SEG, DV)),
            shape((NCH, DK, DV)),
            shape((SEG, 128)),
            shape((8, SEG)),
            shape((8, 128)),
        ],
        in_specs=[SM] * 4 + [VM] * 18,
        out_specs=[VM] * 23,
        scratch_shapes=[
            pltpu.VMEM((4, 64, NA), bf16),
            pltpu.VMEM((4, 64, NB), bf16),
            pltpu.VMEM((4, 8, 128), f32),
            pltpu.VMEM((4, 4, 2, 8, 128), f32),
            pltpu.VMEM((32, 128), f32),
            pltpu.VMEM((ROWS, D), bf16),
            pltpu.VMEM((DK, DK + DV), bf16),
            pltpu.SMEM((16,), i32),
        ]
        + PICK_SCRATCH * 2
        + [
            pltpu.SemaphoreType.DMA((2, 15)),
            pltpu.SemaphoreType.DMA((2, 15)),
            pltpu.SemaphoreType.DMA((11,)),
            pltpu.SemaphoreType.DMA((11,)),
        ]
        + TRADE_SEMS,
        compiler_params=remote_params(cid),
    )(order, lens, a_log, dt_bias, tokens, cotangent, *weights, *wide_weights, *convs, *gains)


def in_order(flows, plan):
    for i in plan:
        next(flows[int(i)], None)
        yield
    yield from together(flows)


def back(dn, o, proj, hg, qkv, tm, wu, gb, cr, mc, mr, maps, fr, st, cw, sc, m, ypart, sgu, sd, da, nv, order, xrows, dm, gain, h1, wa, dgain2, cid, plan=PLANS["back"], plan2="011010"):
    nh, ns, nc = len(HOME_SCRATCH), 7, len(SCATTER_SCRATCH)

    def kernel(
        dn, o, proj, hg, qkv, tm, wu, gb, cr, mc, mr, maps, fr, st, cw, sc, m, ypart, sgu, sd, da, nv, order, xr, dm, gain, h1, wa, dgain2,
        both, g_out, ro, rgu, rd, t_out, tot,
        dproj, dhg, dcw, dsc, do, dgp, e, tails, dz, dab, dqkv, edge, ms, mq, ds, dq, acc, grad_o, part, acc2, grad, line, rows, xr4, xs, xq, *refs,
    ):
        sum_y, sum_x, refs = refs[:nc], refs[nc : 2 * nc], refs[2 * nc :]
        home, refs = refs[:nh], refs[nh:]
        so, sg, st_, trades = refs[:ns], refs[ns : 2 * ns], refs[2 * ns : 3 * ns], refs[3 * ns :]
        zq, gp, ab = proj.at[:, 0:512], proj.at[:, 512:768], proj.at[:, 768:896]
        x = lax.axis_index("x")
        seg = lax.axis_index("z") * 2 + lax.axis_index("c")
        ready = hail(plane_peers() + segment_peers())

        def main():
            yield from back_emit(dn, o, gp, hg, qkv, wu, gb, cr, mc, mr, do, dgp, dhg, e)
            yield from map_gather(e, tails, ms, mq)
            yield from back_delta(
                seg, Maps(maps), Maps(tails), do, fr, st, qkv, tm, wu, gb, cr, zq, ab, cw, sc, mc, mr, dz, dab, dcw, dsc, dqkv
            )
            before = lax.rem(seg + 7, 8)
            cp = send(dz.at[0:HALO], edge, ds, dq, {"z": before // 2, "c": lax.rem(before, 2)})
            dproj[0 : SEG - HALO, 0:512] = dz[HALO:SEG].astype(bf16)
            dproj[:, 512:768] = dgp[...]
            dproj[:, 768:896] = dab[...]
            yield
            cp.wait_recv()
            dproj[SEG - HALO : SEG, 0:512] = (dz[SEG:ROWS] + jnp.where(seg < 7, edge[...], 0.0)).astype(bf16)
            cp.wait_send()
            for t in range(4):
                cols = slice(512 * t, 512 * (t + 1))
                part[:, :, :, cols] = dot(dproj[...], wa[cols, 0:896], ((1,), (1,))).astype(bf16).reshape(4, 4, 32, 512)
            yield from in_order([input_grads(), weight_grads()], plan2)

        def result():
            yield from plane_sum(ypart, acc, *sum_y)
            rows[0] = (m[...] + acc[...]).astype(bf16)

        def output_grads():
            weight_tiles(lambda cols: da[:, cols], lambda: nv[...], grad_o)
            yield from scatter_flow(grad_o, ro, *so)

        def weight_grads():
            weight_tiles(lambda cols: h1[HALO:, cols], lambda: dproj[...], grad)
            yield from scatter_flow(grad, g_out, *sg)

        def small_grads():
            yield from scatter_flow(line, t_out, *st_)
            xr4[x] = (t_out[0] + t_out[1]) + (t_out[2] + t_out[3])
            sends = [send(xr4.at[x], xr4.at[x], xs.at[k], xq.at[k], {"x": at("x", k)}) for k in (2, 1, 3)]
            yield
            for cp in sends:
                cp.wait_recv()
            tot[...] = (xr4[0] + xr4[1]) + (xr4[2] + xr4[3])
            for cp in sends:
                cp.wait_send()

        def fill_lines():
            lane = lax.broadcasted_iota(i32, (32, 128), 1)
            top = jnp.where(lane == 72, dsc[0:1, 0:1], 0.0) + jnp.where(lane == 73, dsc[1:2, 0:1], 0.0)
            for j in range(4):
                top = top + spread_lanes(dcw[j : j + 1, QC], 4, 4 * j) + spread_lanes(dcw[j : j + 1, KC], 4, 16 + 4 * j)
                top = top + spread_lanes(dcw[j : j + 1, VC], 8, 32 + 8 * j)
            top = top + spread_lanes(dhg[...], 8, 64)
            line[...] = jnp.zeros(line.shape, f32)
            for i in range(32):
                line[i // 8, i // 2 % 4, i % 2, 0:1, :] = top[i : i + 1]
                line[i // 8, i // 2 % 4, i % 2, 2:3, 0:64] = dgain2[:, 64 * i : 64 * (i + 1)]

        def input_grads():
            sums = plane_sum(part, acc2, *sum_x)
            next(sums)
            fill_lines()
            yield
            yield from sums
            dvr, dgain = norm_back(xr[...].astype(f32), gain[...], acc2[...])
            for _ in outcome:
                pass
            rows[1] = (dm[...] + dvr).astype(bf16)
            for i in range(32):
                line[i // 8, i // 2 % 4, i % 2, 1:2, 0:64] = dgain[:, 64 * i : 64 * (i + 1)]
            yield from together([home_flow(rows, both, order, *home), small_grads()])

        def trade(staged, out, sems):
            yield from trade_flow(slots(staged), lambda y: out.at[y], *sems)

        outcome, chain = result(), main()
        for _ in range(4):
            next(chain)
        ready()
        run([chain, outcome, output_grads(), trade(sgu, rgu, trades[0:2]), trade(sd, rd, trades[2:4])], plan)

    td, gd, god = (8, 128), (64, 896), (64, DV)
    return pl.pallas_call(
        kernel,
        out_shape=[
            shape((2, 128, 512), bf16),
            shape((4,) + gd, bf16),
            shape((4,) + god, bf16),
            shape(sgu.shape, bf16),
            shape(sd.shape, bf16),
            shape((4,) + td),
            shape(td),
        ],
        in_specs=[VM] * 22 + [SM] + [VM] * 6,
        out_specs=[VM] * 7,
        scratch_shapes=[
            pltpu.VMEM((SEG, 896), bf16),
            pltpu.VMEM((1, DV), f32),
            pltpu.VMEM((4, 512), f32),
            pltpu.VMEM((2, 128), f32),
            pltpu.VMEM((SEG, DV), f32),
            pltpu.VMEM((SEG, DV), bf16),
            pltpu.VMEM((DK, DV), bf16),
            pltpu.VMEM((4, 2, DK, DV), bf16),
            pltpu.VMEM((ROWS, 512), f32),
            pltpu.VMEM((SEG, 128), bf16),
            pltpu.VMEM((SEG, 512), f32),
            pltpu.VMEM((HALO, 512), f32),
            pltpu.SemaphoreType.DMA((11,)),
            pltpu.SemaphoreType.DMA((11,)),
            pltpu.SemaphoreType.DMA,
            pltpu.SemaphoreType.DMA,
            pltpu.VMEM((32, D), f32),
            pltpu.VMEM((4, 4, 2) + god, bf16),
            pltpu.VMEM((4, 4, 32, D), bf16),
            pltpu.VMEM((32, D), f32),
            pltpu.VMEM((4, 4, 2) + gd, bf16),
            pltpu.VMEM((4, 4, 2) + td, f32),
            pltpu.VMEM((2, 32, D), bf16),
            pltpu.VMEM((4,) + td, f32),
            pltpu.SemaphoreType.DMA((4,)),
            pltpu.SemaphoreType.DMA((4,)),
        ]
        + SCATTER_SCRATCH * 2
        + HOME_SCRATCH
        + scatter_scratch(god, bf16)
        + scatter_scratch(gd, bf16)
        + scatter_scratch(td, f32)
        + TRADE_SEMS * 2,
        compiler_params=remote_params(cid),
    )(dn, o, proj, hg, qkv, tm, wu, gb, cr, mc, mr, maps, fr, st, cw, sc, m, ypart, sgu, sd, da, nv, order, xrows, dm, gain, h1, wa, dgain2)


def lay_out(both, ra, ro, rgu, rd, lines, total, ff):
    def kernel(both, ra, ro, rgu, rd, lines, total, out, dt, dq, dk, dv, dg, da, db, do, gg, gu, gd, cq, ck, cv, g1, g2, hg, al, bi):
        out[...] = both[0]
        dt[...] = both[1]
        g1[...] = total[1:2, 0:64]
        g2[...] = total[2:3, 0:64]
        hg[...] = total[0:1, 64:72]
        diag = lax.broadcasted_iota(i32, (64, 64), 0) == lax.broadcasted_iota(i32, (64, 64), 1)
        for i in range(4):
            for ref, cols in ((dq, QC), (dk, KC), (dv, VC), (dg, slice(512, 768))):
                ref[:, i, :] = ra[i, :, cols].astype(f32)
            do[i] = ro[i].astype(f32)
            n = min(FFP, ff - FFP * i)
            cols = slice(FFP * i, FFP * i + n)
            gg[:, cols] = rgu[i, :, 0:n].astype(f32)
            gu[:, cols] = rgu[i, :, FFP : FFP + n].astype(f32)
            gd[:, cols] = rd[i, :, 0:n].astype(f32)
            for k, ref in enumerate((da, db)):
                col = ra[i, :, 768 + k : 769 + k].astype(f32)
                ref[i : i + 1, :] = jnp.sum(jnp.where(diag, col, 0.0), axis=0, keepdims=True)
            al[:, i : i + 1] = lines[i, 0:1, 72:73]
            bi[:, i : i + 1] = lines[i, 0:1, 73:74]
            for j in range(4):
                cq[j, i : i + 1, :] = lines[i, 0:1, 4 * j : 4 * j + 4]
                ck[j, i : i + 1, :] = lines[i, 0:1, 16 + 4 * j : 20 + 4 * j]
                cv[j, i : i + 1, :] = lines[i, 0:1, 32 + 8 * j : 40 + 8 * j]

    return pl.pallas_call(
        kernel,
        out_shape=[shape((128, 512), bf16)] * 2
        + [shape((64, 4, DK))] * 2
        + [shape((64, 4, DV))] * 2
        + [shape((4, 64))] * 2
        + [shape((4, 64, DV))]
        + [shape((64, ff))] * 3
        + [shape((4, 4, 4)), shape((4, 4, 4)), shape((4, 4, 8))]
        + [shape((1, n)) for n in (64, 64, 8, 4, 4)],
        in_specs=[VM] * 7,
        out_specs=[VM] * 20,
        compiler_params=pltpu.CompilerParams(vmem_limit_bytes=VLIM),
    )(both, ra, ro, rgu, rd, lines, total)


def body(
    tokens,
    cotangent,
    seq_lengths,
    stretch_order,
    attn_gain,
    w_query,
    w_key,
    w_value,
    w_alpha,
    w_beta,
    conv_query,
    conv_key,
    conv_value,
    a_log,
    dt_bias,
    head_gain,
    w_outgate,
    w_output,
    mlp_gain,
    w_gate,
    w_up,
    w_down,
):

    wa, gain1, gain2, xrows, h1, proj, cw, hg, wpart, dys, qkv, tm, wu, gb, cr, maps, nv, ov, fr, st, mc, mr, sc = front(
        stretch_order,
        seq_lengths,
        a_log,
        dt_bias,
        tokens.reshape(2, STRETCH, D),
        cotangent.reshape(2, STRETCH, D),
        (w_query, w_key, w_value, w_outgate, w_alpha.T, w_beta.T, w_output.swapaxes(1, 2)),
        (w_gate, w_up, w_down.T),
        (conv_query, conv_key, conv_value),
        (head_gain[None], attn_gain[None], mlp_gain[None]),
        1,
    )
    wa = wa.reshape(D, NA)
    m, dm, dgain2, da, dn, ypart, sgu, sd = middle(
        nv.reshape(4, 4, 32, DV), wa, xrows, gain2, wpart, dys.reshape(4, 4, 32, D), 2
    )
    da, dn = da.reshape(SEG, D), dn.reshape(SEG, DV)

    both, ra, ro, rgu, rd, rt, total = back(
        dn, ov, proj, hg, qkv, tm, wu, gb, cr, mc, mr, maps, fr, st, cw, sc, m, ypart, sgu, sd, da, nv,
        stretch_order, xrows, dm, gain1, h1, wa, dgain2, 3,
    )
    out, dtok, d_query, d_key, d_value, d_outgate, d_alpha, d_beta, d_output, d_gate, d_up, d_down, cq, ck, cv, g1, g2, hgain, al, bias = lay_out(
        both, ra, ro, rgu, rd, rt, total, w_gate.shape[1]
    )
    return (
        out,
        dtok,
        g1[0],
        d_query,
        d_key,
        d_value,
        d_alpha.T,
        d_beta.T,
        cq,
        ck,
        cv,
        al[0],
        bias[0],
        hgain[0],
        d_outgate,
        d_output.swapaxes(1, 2),
        g2[0],
        d_gate,
        d_up,
        d_down.T,
    )


def solution(mesh):
    torus = Mesh(mesh.devices.reshape(4, 4, 2, 4), ("y", "z", "c", "x"))
    dp, tp = ("y", "z", "c"), "x"
    in_specs = (
        P(dp, None),
        P(dp, None),
        P(),
        P(),
        P(dp),
        P(dp, tp, None),
        P(dp, tp, None),
        P(dp, tp, None),
        P(dp, tp),
        P(dp, tp),
        P(None, tp, dp),
        P(None, tp, dp),
        P(None, tp, dp),
        P(tp),
        P(tp),
        P(dp),
        P(dp, tp, None),
        P(tp, None, dp),
        P(dp),
        P(dp, tp),
        P(dp, tp),
        P(tp, dp),
    )
    out_specs = (
        P(dp, tp),
        P(dp, tp),
        P(dp),
        P(dp, tp, None),
        P(dp, tp, None),
        P(dp, tp, None),
        P(dp, tp),
        P(dp, tp),
        P(None, tp, dp),
        P(None, tp, dp),
        P(None, tp, dp),
        P(tp),
        P(tp),
        P(dp),
        P(dp, tp, None),
        P(tp, None, dp),
        P(dp),
        P(dp, tp),
        P(dp, tp),
        P(tp, dp),
    )
    return jax.shard_map(body, mesh=torus, in_specs=in_specs, out_specs=out_specs, check_vma=False)
```
